32 devices in a mesh: grp: 2 (over x), fsdp: 4 (over z), item: 4 (over y, core).
Axes of the slice: x: 2, y: 2, z: 4, core: 2. Of those that a mesh axis runs over, the one named last changes fastest.
Arguments:
- hidden_states: bfloat16 [2048, 16, 4096], P(('grp', 'fsdp', 'item')), may hold values from -6 to 6
- positives: bfloat16 [2048, 1024], P(('grp', 'fsdp', 'item')), may hold values from -6 to 6
- negatives: int32 [2048, 32], P(('grp', 'fsdp', 'item')), may hold values from 0 to 4095, as said below
- lengths: int32 [2048], P(('grp', 'fsdp', 'item')), may hold values from 1 to 16, as said below
- norm_gain: bfloat16 [4096], replicated, may hold values from 0.25 to 1.75
- proj_weight: bfloat16 [4096, 1024], P('fsdp'), may hold values from -0.09375 to 0.09375
- pool_query: float32 [1024], replicated, may hold values from -6 to 6
- slab: bfloat16 [4096, 1024], P('item'), may hold values from -6 to 6
Outputs:
- grad_proj: float32 [4096, 1024], P('fsdp')
- grad_query: float32 [1024], replicated
- mean_loss: float32 [], replicated
The draws below stay inside these ranges and needn't reach their ends.
Inputs may be any that keep to these rules, and one draw needn't show every extreme that they name: `negatives`: entries 8 o to 8 (o + 1) - 1 of each query's list are rows of owner block o, the slab rows 1024 o to 1024 (o + 1) - 1; a row may repeat. The first lengths[q] token slots of query q are valid.
All inputs are finite; a program needn't handle non-finite values.
Results may differ from the reference program's by a relative error of at most 0.0043.
Values may be sent and summed in bfloat16 or wider, within the bound.
No kernel may reach another device: no remote copies, remote signals or barrier semaphores. Data moves between devices by JAX's collectives and lax.ppermute only.
A program may use at most 128 MiB of HBM per device.

```python
import math
import jax
import jax.numpy as jnp
from jax import lax

D = 4096
P_SIZE = 1024
SEQ = 16
NEG_OWN = 8
Q_DEV = 64
SLAB_DEV = 1024
QUERIES = 2048
NEG = 32
SLAB = 4096


def draw_negatives(key, part):
    owners = NEG // NEG_OWN
    picked_rows = jax.random.randint(key, (QUERIES, owners, NEG_OWN), 0, SLAB_DEV)
    owner_base = jnp.arange(owners, dtype=jnp.int32)[None, :, None] * SLAB_DEV
    values = (picked_rows + owner_base).reshape(QUERIES, NEG)
    values = values.at[0, 0].set(0).at[0, NEG - 1].set(SLAB - 1)
    return values.astype(jnp.int32)


def draw_lengths(key, part):
    lengths_drawn = jax.random.randint(key, (QUERIES,), 1, SEQ + 1)
    lengths_drawn = lengths_drawn.at[0].set(SEQ).at[1].set(1)
    return lengths_drawn.astype(jnp.int32)


def level_of(own_key, extent, pieces, smallest, top_value):
    gain = 1.0
    for dim, parts in pieces:
        draws = jax.random.uniform(jax.random.fold_in(jax.random.fold_in(own_key, 6), dim), (parts,), jnp.float32, smallest / len(pieces), top_value / len(pieces))
        gain = gain * jnp.repeat(jnp.exp(draws), extent[dim] // parts).reshape((-1,) + (1,) * (len(extent) - 1 - dim))
    return gain


def normal_values(own_key, extent, spread, reach, shards=(), kind=jnp.bfloat16):
    values = spread * jax.random.normal(own_key, extent, jnp.float32)
    if shards:
        values = values * level_of(own_key, extent, shards, -0.22, 0.18)
    return jnp.clip(values, -reach, reach).astype(kind)


def setup_inputs(seed: int = 0) -> dict:
    streams_of = jax.random.split(jax.random.key(seed), 9)
    hidden_states = normal_values(streams_of[0], (QUERIES, SEQ, D), 1.0, 6.0, ((0, 32),))
    positives = normal_values(streams_of[1], (QUERIES, P_SIZE), 1.0, 6.0, ((0, 32),))
    negatives = draw_negatives(jax.random.fold_in(streams_of[8], 71), 0)
    lengths = draw_lengths(jax.random.fold_in(streams_of[8], 71), 0)
    norm_gain = jnp.clip(1.0 + 0.15 * jax.random.normal(streams_of[4], (D,), jnp.float32), 0.25, 1.75).astype(jnp.bfloat16)
    proj_weight = normal_values(streams_of[5], (D, P_SIZE), D ** -0.5, 0.09375, ((0, 4),))
    pool_query = normal_values(streams_of[6], (P_SIZE,), 1.0, 6.0, (), jnp.float32)
    slab = normal_values(streams_of[7], (SLAB, P_SIZE), 1.0, 6.0, ((0, 4),))
    return {"hidden_states": hidden_states, "positives": positives, "negatives": negatives, "lengths": lengths, "norm_gain": norm_gain, "proj_weight": proj_weight, "pool_query": pool_query, "slab": slab}


sharpness_divisor = 0.05
norm_eps = 1e-05
embed_eps = 1e-06

def normalize(states, norm_gain):
    flat_states = states.reshape(-1, states.shape[-1]).astype(jnp.float32)
    inv_rms = lax.rsqrt(lax.optimization_barrier(jnp.mean(flat_states * flat_states, axis=1, keepdims=True)) + norm_eps)
    return (flat_states * inv_rms * norm_gain.astype(jnp.float32)).astype(jnp.bfloat16)

def gated_pool(token_proj, lengths, pool_query, seq_len):
    queries = lengths.shape[0]
    proj_width = token_proj.shape[1]
    tokens = token_proj.reshape(queries, seq_len, proj_width)
    gate_vals = jax.nn.sigmoid(jnp.einsum('qsp,p->qs', tokens, pool_query, precision=lax.Precision.HIGHEST) / math.sqrt(proj_width))
    position = lax.broadcasted_iota(jnp.int32, (queries, seq_len), 1)
    weight = jnp.where(position < lengths[:, None], 1.0, 0.0).astype(jnp.float32) / lengths[:, None].astype(jnp.float32)
    pooled = jnp.einsum('qs,qsp->qp', weight * gate_vals, tokens, precision=lax.Precision.HIGHEST)
    return (pooled, gate_vals, weight)

def unit_embed(pooled):
    proj_width = pooled.shape[1]
    unit_scale = lax.rsqrt(lax.optimization_barrier(jnp.mean(pooled * pooled, axis=1, keepdims=True)) + embed_eps) / math.sqrt(proj_width)
    return ((pooled * unit_scale).astype(jnp.bfloat16), unit_scale)

def contrast(embedded, positives, neg_rows):
    proj_width = embedded.shape[1]
    encoded_vector_fullprec = embedded.astype(jnp.float32)
    matching_vector_fullprec = positives.astype(jnp.float32)
    sample_vectors_fullprec = neg_rows.astype(jnp.float32)
    matching_multiplier = lax.rsqrt(lax.optimization_barrier(jnp.mean(matching_vector_fullprec * matching_vector_fullprec, axis=1)) + embed_eps) / math.sqrt(proj_width)
    matching_score = jnp.einsum('au,au->a', encoded_vector_fullprec, matching_vector_fullprec, precision=lax.Precision.HIGHEST) * matching_multiplier / sharpness_divisor
    row_sq = jnp.einsum('qnp,qnp->qn', sample_vectors_fullprec, sample_vectors_fullprec, precision=lax.Precision.HIGHEST)
    sample_multiplier = lax.rsqrt(row_sq / proj_width + embed_eps) / math.sqrt(proj_width)
    distractor_score = jnp.einsum('ir,isr->is', encoded_vector_fullprec, sample_vectors_fullprec, precision=lax.Precision.HIGHEST) * sample_multiplier / sharpness_divisor
    logits = jnp.concatenate([matching_score[:, None], distractor_score], axis=1)
    exp_logits = jnp.exp(logits)
    denom_sum = lax.optimization_barrier(jnp.sum(exp_logits, axis=1, keepdims=True))
    prob = exp_logits / denom_sum
    loss_sum = jnp.sum(jnp.log(denom_sum[:, 0]) - matching_score)
    column = lax.broadcasted_iota(jnp.int32, logits.shape, 1)
    score_derivative = prob - jnp.where(column == 0, 1.0, 0.0).astype(jnp.float32)
    matching_contribution = (score_derivative[:, 0] * matching_multiplier / sharpness_divisor)[:, None] * matching_vector_fullprec
    distractor_probability = (score_derivative[:, 1:] * sample_multiplier / sharpness_divisor).astype(jnp.bfloat16)
    grad_embed = matching_contribution + jnp.einsum('qn,qnp->qp', distractor_probability.astype(jnp.float32), sample_vectors_fullprec, precision=lax.Precision.HIGHEST)
    return (loss_sum, grad_embed)

def backward(token_proj, pooled, unit_scale, grad_embed, gate_vals, weight, pool_query, seq_len):
    queries, proj_width = pooled.shape
    tokens = token_proj.reshape(queries, seq_len, proj_width)
    mean_sq = lax.optimization_barrier(jnp.mean(pooled * pooled, axis=1, keepdims=True))
    radial = lax.optimization_barrier(jnp.sum(pooled * grad_embed, axis=1, keepdims=True))
    grad_pooled = unit_scale * grad_embed - pooled * radial * unit_scale / (proj_width * (mean_sq + embed_eps))
    proj_dot = jnp.einsum('qsp,qp->qs', tokens, grad_pooled, precision=lax.Precision.HIGHEST)
    gate_slope = weight * gate_vals * (1.0 - gate_vals) * proj_dot / math.sqrt(proj_width)
    grad_tokens = (weight * gate_vals)[:, :, None] * grad_pooled[:, None, :] + gate_slope[:, :, None] * pool_query[None, None, :]
    grad_query = jnp.einsum('qs,qsp->p', gate_slope, tokens, precision=lax.Precision.HIGHEST)
    return (grad_tokens.reshape(queries * seq_len, proj_width).astype(jnp.bfloat16), grad_query)

def reference(hidden_states, positives, negatives, lengths, norm_gain, proj_weight, pool_query, slab):
    queries, seq_len, model_width = hidden_states.shape
    proj_width = proj_weight.shape[1]
    blocks = queries // Q_DEV

    def one_block(carried, block_data):
        grad_weight, grad_pool_sum, loss_total = carried
        states, block_pos, block_negs, block_lengths = block_data
        normed = normalize(states, norm_gain)
        token_proj = jnp.dot(normed, proj_weight, preferred_element_type=jnp.float32)
        pooled, gate_vals, weight = gated_pool(token_proj, block_lengths, pool_query, seq_len)
        embedded, unit_scale = unit_embed(pooled)
        neg_rows = jnp.take(slab, block_negs, axis=0)
        loss_part, grad_embed = contrast(embedded, block_pos, neg_rows)
        grad_tokens, query_part = backward(token_proj, pooled, unit_scale, grad_embed, gate_vals, weight, pool_query, seq_len)
        grad_weight = grad_weight + lax.dot_general(normed, grad_tokens, (((0,), (0,)), ((), ())), preferred_element_type=jnp.float32)
        return ((grad_weight, grad_pool_sum + query_part, loss_total + loss_part), None)
    initial = (jnp.zeros((model_width, proj_width), jnp.float32), jnp.zeros((proj_width,), jnp.float32), jnp.zeros((), jnp.float32))
    block_inputs = (hidden_states.reshape(blocks, Q_DEV, seq_len, model_width), positives.reshape(blocks, Q_DEV, proj_width), negatives.reshape(blocks, Q_DEV, negatives.shape[1]), lengths.reshape(blocks, Q_DEV))
    (grad_proj, grad_query, loss_total), _ = lax.scan(one_block, initial, block_inputs)
    return (grad_proj, grad_query, loss_total / queries)
```

```python
import math

import jax
import jax.numpy as jnp
from jax import lax
from jax.sharding import PartitionSpec as P

sharpness_divisor = 0.05
norm_eps = 1e-05
embed_eps = 1e-06

EVERY = ("fsdp", "grp", "item")
PLANE = ("grp", "item")
F32 = jnp.float32
BF16 = jnp.bfloat16


def split_bf16(values):
    high = values.astype(BF16)
    low = (values - high.astype(F32)).astype(BF16)
    return high, low


def exact_rows(left, right, dims):
    high, low = split_bf16(left)
    both = lax.dot_general(
        jnp.concatenate([high, low], axis=0), right, (dims, ((), ())), preferred_element_type=F32
    )
    rows = left.shape[0]
    return both[:rows] + both[rows:]


def gather_small(piece, axis):
    n = lax.axis_size(axis)
    me = lax.axis_index(axis)
    whole = jnp.zeros((n,) + piece.shape, piece.dtype)
    whole = lax.dynamic_update_index_in_dim(whole, piece, me, 0)
    for k in range(1, n):
        got = lax.ppermute(piece, axis, [(i, (i + k) % n) for i in range(n)])
        whole = lax.dynamic_update_index_in_dim(whole, got, lax.rem(me - k + n, n), 0)
    return whole


def body(hidden_states, positives, negatives, lengths, norm_gain, proj_weight, pool_query, slab):
    queries, seq, width = hidden_states.shape
    proj_width = proj_weight.shape[1]
    neg_count = negatives.shape[1]
    n_item = lax.axis_size("item")
    n_plane = lax.axis_size("grp") * n_item
    n_all = n_plane * lax.axis_size("fsdp")
    me_item = lax.axis_index("item")
    root = math.sqrt(proj_width)

    share = proj_weight.shape[0] // n_plane
    place = lax.axis_index("grp") * n_item + me_item
    weight_share = lax.dynamic_slice_in_dim(proj_weight, place * share, share, 0)
    weight = lax.all_gather(weight_share, EVERY, axis=0, tiled=True)

    block_u = jnp.sum(proj_weight.astype(F32) * pool_query[None, :], axis=1)
    u = gather_small(block_u, "fsdp").reshape(width)

    own = neg_count // n_item
    lists = lax.all_to_all(negatives.reshape(queries, n_item, own), "item", 1, 0, tiled=True)
    lists = lists.reshape(n_item * queries, own) - me_item * slab.shape[0]
    row_ids = lax.broadcasted_iota(jnp.int32, (1, slab.shape[0]), 1)
    counts = jnp.zeros((n_item * queries, slab.shape[0]), F32)
    for k in range(own):
        counts = counts + jnp.where(lists[:, k : k + 1] == row_ids, 1.0, 0.0)
    slab_f32 = slab.astype(F32)
    slab_scale = (
        lax.rsqrt(jnp.mean(slab_f32 * slab_f32, axis=1) + embed_eps) / root / sharpness_divisor
    )
    pos_f32 = positives.astype(F32)
    pos_scale = lax.rsqrt(jnp.mean(pos_f32 * pos_f32, axis=1) + embed_eps) / root / sharpness_divisor

    states = hidden_states.astype(F32)
    inv_rms = lax.rsqrt(jnp.mean(states * states, axis=2, keepdims=True) + norm_eps)
    normed = (states * inv_rms * norm_gain.astype(F32)).astype(BF16)
    normed_f32 = normed.astype(F32)
    gate = jax.nn.sigmoid(jnp.sum(normed_f32 * u, axis=2) / root)
    position = lax.broadcasted_iota(jnp.int32, (queries, seq), 1)
    valid = jnp.where(position < lengths[:, None], 1.0, 0.0).astype(F32) / lengths[:, None].astype(F32)
    gated = valid * gate
    pool_rows = jnp.sum(gated[:, :, None] * normed_f32, axis=1)

    rows_slice = lax.all_to_all(pool_rows.astype(BF16), EVERY, 1, 0, tiled=True)

    pooled = exact_rows(pool_rows, weight, ((1,), (0,)))
    mean_sq = jnp.mean(pooled * pooled, axis=1, keepdims=True)
    unit_scale = lax.rsqrt(mean_sq + embed_eps) / root
    embedded = (pooled * unit_scale).astype(BF16)

    all_embedded = gather_small(embedded, "item").reshape(n_item * queries, proj_width)
    score = (
        lax.dot_general(all_embedded, slab, (((1,), (1,)), ((), ())), preferred_element_type=F32)
        * slab_scale[None, :]
    )
    heavy = counts * jnp.exp(score)
    part_denom = jnp.sum(heavy, axis=1, keepdims=True)
    part_grad = jnp.dot((heavy * slab_scale[None, :]).astype(BF16), slab, preferred_element_type=F32)
    part = jnp.concatenate([part_grad, jnp.broadcast_to(part_denom, (n_item * queries, 128))], axis=1)
    part = part.reshape(n_item, queries, proj_width + 128)
    total = lax.dynamic_index_in_dim(part, me_item, 0, keepdims=False)
    for k in range(1, n_item):
        piece = lax.dynamic_index_in_dim(part, lax.rem(me_item + k, n_item), 0, keepdims=False)
        total = total + lax.ppermute(piece, "item", [(i, (i + k) % n_item) for i in range(n_item)])
    pos_score = jnp.sum(embedded.astype(F32) * pos_f32, axis=1) * pos_scale
    pos_exp = jnp.exp(pos_score)
    denom = total[:, proj_width] + pos_exp
    loss_part = jnp.sum(jnp.log(denom) - pos_score)
    grad_embed = (
        (total[:, :proj_width] / denom[:, None])
        + ((pos_exp / denom - 1.0) * pos_scale)[:, None] * pos_f32
    )

    radial = jnp.sum(pooled * grad_embed, axis=1, keepdims=True)
    grad_pooled = unit_scale * grad_embed - pooled * radial * unit_scale / (
        proj_width * (mean_sq + embed_eps)
    )
    all_grad = lax.all_gather(grad_pooled.astype(BF16), EVERY, axis=0, tiled=True)

    back = exact_rows(grad_pooled, weight, ((1,), (1,)))
    slope = gated * (1.0 - gate) * jnp.sum(normed_f32 * back[:, None, :], axis=2) / root
    slope_rows = jnp.sum(slope[:, :, None] * normed_f32, axis=(0, 1))
    slope_sum, loss_total = lax.psum((slope_rows, loss_part), EVERY)
    grad_query = exact_rows(slope_sum[None, :], weight, ((1,), (0,)))[0]

    my_slope = lax.dynamic_slice_in_dim(
        slope_sum, lax.axis_index("fsdp") * proj_weight.shape[0] + place * share, share, 0
    )
    grad_slice = lax.dot_general(
        rows_slice, all_grad, (((0,), (0,)), ((), ())), preferred_element_type=F32
    ) + my_slope[:, None] * pool_query[None, :]
    grad_proj = lax.all_gather(grad_slice.astype(BF16), PLANE, axis=0, tiled=True).astype(F32)
    return (grad_proj, grad_query, loss_total / (queries * n_all))


def solution(mesh):
    return jax.shard_map(
        body,
        mesh=mesh,
        in_specs=(
            P(("grp", "fsdp", "item"), None, None),
            P(("grp", "fsdp", "item"), None),
            P(("grp", "fsdp", "item"), None),
            P(("grp", "fsdp", "item")),
            P(),
            P("fsdp", None),
            P(),
            P("item", None),
        ),
        out_specs=(P("fsdp", None), P(), P()),
        check_vma=False,
    )
```

```python
import functools
import math

import jax
import jax.numpy as jnp
from jax import lax
from jax.experimental import pallas as pl
from jax.experimental.pallas import tpu as pltpu
from jax.sharding import PartitionSpec as P

sharpness_divisor = 0.05
norm_eps = 1e-05
embed_eps = 1e-06

EVERY = ("fsdp", "grp", "item")
PLANE = ("grp", "item")
F32 = jnp.float32
BF16 = jnp.bfloat16
LANES = 128
MIB = 1024 * 1024
VMEM = pl.BlockSpec(memory_space=pltpu.VMEM)
SMEM = pl.BlockSpec(memory_space=pltpu.SMEM)


def shape(dims, dtype):
    return jax.ShapeDtypeStruct(dims, dtype)


def call(kernel, outs, ins, name, flops=0, scratch=(), smem=0):
    moved = sum(math.prod(a.shape) * a.dtype.itemsize for a in list(ins) + list(outs))
    return pl.pallas_call(
        kernel,
        out_shape=outs,
        in_specs=[SMEM] * smem + [VMEM] * (len(ins) - smem),
        out_specs=[VMEM] * len(outs),
        scratch_shapes=scratch,
        cost_estimate=pl.CostEstimate(flops=flops, bytes_accessed=moved, transcendentals=0),
        compiler_params=pltpu.CompilerParams(vmem_limit_bytes=44 * MIB),
        name=name,
    )(*ins)


def shift(values, axis, k):
    n = lax.axis_size(axis)
    return lax.ppermute(values, axis, [(i, (i + k) % n) for i in range(n)])


def split_bf16(values):
    high = values.astype(BF16)
    low = (values - high.astype(F32)).astype(BF16)
    return high, low


def nt(left, right):
    return lax.dot_general(left, right, (((1,), (1,)), ((), ())), preferred_element_type=F32)


def tn(left, right):
    return lax.dot_general(left, right, (((0,), (0,)), ((), ())), preferred_element_type=F32)


def gate_kernel(seq, root, blocks, z_ref, normed_ref, u_ref, len_ref, *rest):
    out_refs, gated_ref, curve_ref, rows_ref = rest[:blocks], rest[blocks], rest[blocks + 1], rest[-1]
    step = pl.program_id(0)
    tokens = normed_ref.shape[0]
    count = tokens // seq
    normed = normed_ref[...]
    logit = jnp.sum(normed.astype(F32) * u_ref[...], axis=1, keepdims=True) / root
    gate = 1.0 / (1.0 + jnp.exp(-logit))
    slot = lax.rem(lax.broadcasted_iota(jnp.int32, (tokens, 1), 0), seq)
    valid = jnp.where(slot < len_ref[...], 1.0, 0.0) / len_ref[...].astype(F32)
    gated = valid * gate
    gated_ref[...] = gated
    curve_ref[...] = gated * (1.0 - gate) / root
    owner = lax.broadcasted_iota(jnp.int32, (tokens, count), 0) // seq
    mine = owner == lax.broadcasted_iota(jnp.int32, (tokens, count), 1)
    high, low = split_bf16(jnp.where(mine, gated, 0.0))
    both = tn(jnp.concatenate([high, low], axis=1), normed)
    rows_ref[pl.ds(pl.multiple_of(step * count, count), count), :] = both[:count] + both[count:]

    @pl.when(step == pl.num_programs(0) - 1)
    def _():
        width = out_refs[0].shape[1]
        for k in range(blocks):
            at = lax.rem(z_ref[0] + k, blocks) * width
            out_refs[k][...] = rows_ref[:, pl.ds(pl.multiple_of(at, LANES), width)].astype(BF16)


def gate_rows(z, normed, u, token_lengths, seq, root, blocks):
    tokens, width = normed.shape
    queries = tokens // seq
    group = 8 if queries % 8 == 0 else queries
    step_tokens = group * seq
    outs = [shape((queries, width // blocks), BF16)] * blocks + [shape((tokens, 1), F32)] * 2
    column = pl.BlockSpec((step_tokens, 1), lambda i: (i, 0))
    return pl.pallas_call(
        functools.partial(gate_kernel, seq, root, blocks),
        grid=(queries // group,),
        out_shape=outs,
        in_specs=[
            SMEM,
            pl.BlockSpec((step_tokens, width), lambda i: (i, 0)),
            pl.BlockSpec((1, width), lambda i: (0, 0)),
            column,
        ],
        out_specs=[pl.BlockSpec((queries, width // blocks), lambda i: (0, 0))] * blocks + [column] * 2,
        scratch_shapes=[pltpu.VMEM((queries, width), F32)],
        cost_estimate=pl.CostEstimate(
            flops=4 * tokens * width, bytes_accessed=2 * tokens * width, transcendentals=0
        ),
        compiler_params=pltpu.CompilerParams(vmem_limit_bytes=44 * MIB),
        name="gate_rows",
    )(z, normed, u, token_lengths)


def block_kernel(n, back, *refs):
    pieces, weight_ref, outs = refs[:n], refs[n], refs[n + 1 : 2 * n + 1]
    rows = pieces[0].shape[0]
    stack = jnp.concatenate([p[...] for p in pieces], axis=0)
    if len(refs) > 2 * n + 1:
        refs[-1][...] = stack
    product = nt(stack, weight_ref[...]) if back else jnp.dot(
        stack, weight_ref[...], preferred_element_type=F32
    )
    for k in range(n):
        outs[k][...] = product[k * rows : (k + 1) * rows].astype(outs[k].dtype)


def block_product(pieces, weight, back, keep):
    n = len(pieces)
    rows, depth = pieces[0].shape
    width = weight.shape[0] if back else weight.shape[1]
    outs = [shape((rows, width), F32)] + [shape((rows, width), BF16)] * (n - 1)
    if keep:
        outs.append(shape((n * rows, depth), BF16))
    return call(
        functools.partial(block_kernel, n, back), outs, list(pieces) + [weight],
        "block_back" if back else "block_forward", flops=2 * n * rows * depth * width,
    )


def embed_kernel(root, *refs):
    parts, (pooled_ref, unit_ref, embedded_ref) = refs[:-3], refs[-3:]
    pooled = parts[0][...]
    for part in parts[1:]:
        pooled = pooled + part[...].astype(F32)
    unit = lax.rsqrt(jnp.mean(pooled * pooled, axis=1, keepdims=True) + embed_eps) / root
    pooled_ref[...] = pooled
    unit_ref[...] = unit
    embedded_ref[...] = (pooled * unit).astype(BF16)


def count_kernel(n, at_ref, lists_ref, counts_ref):
    queries = counts_ref.shape[0] // n
    ids = lax.broadcasted_iota(jnp.int32, (queries, counts_ref.shape[1]), 1)
    for k in range(n):
        at = pl.multiple_of(at_ref[k] * queries, queries)
        lists = lists_ref[pl.ds(at, queries), :] - at_ref[n]
        total = jnp.zeros(ids.shape, F32)
        for entry in range(lists.shape[1]):
            total = total + jnp.where(lists[:, entry : entry + 1] == ids, 1.0, 0.0)
        counts_ref[k * queries : (k + 1) * queries, :] = total


def contrast_kernel(n, *refs):
    pieces, (slab_ref, scale_ref, counts_ref), outs = refs[:n], refs[n : n + 3], refs[n + 3 :]
    queries, width = pieces[0].shape
    embedded = jnp.concatenate([p[...] for p in pieces], axis=0)
    slab = slab_ref[...]
    scale = scale_ref[...]
    heavy = counts_ref[...] * jnp.exp(nt(embedded, slab) * scale)
    denom = jnp.sum(heavy, axis=1, keepdims=True)
    grad = jnp.dot((heavy * scale).astype(BF16), slab, preferred_element_type=F32)
    high, low = split_bf16(denom)
    lane = lax.broadcasted_iota(jnp.int32, (queries, LANES), 1)
    for k in range(n):
        part = slice(k * queries, (k + 1) * queries)
        outs[k][:, :width] = grad[part].astype(outs[k].dtype)
        if k == 0:
            tail = jnp.where(lane == 0, denom[part], 0.0)
        else:
            tail = jnp.where(lane == 0, high[part].astype(F32), jnp.where(lane == 1, low[part].astype(F32), 0.0))
        outs[k][:, width:] = tail.astype(outs[k].dtype)


def grad_kernel(n, root, *refs):
    parts = refs[:n]
    pos_ref, pooled_ref, unit_ref, embedded_ref, grad_ref, columns_ref, loss_ref = refs[n:]
    queries, width = pos_ref.shape
    total = parts[0][:, :width]
    denom = jnp.sum(parts[0][:, width:], axis=1, keepdims=True)
    for part in parts[1:]:
        total = total + part[:, :width].astype(F32)
        denom = denom + jnp.sum(part[:, width:].astype(F32), axis=1, keepdims=True)
    positive = pos_ref[...].astype(F32)
    scale = (
        lax.rsqrt(jnp.mean(positive * positive, axis=1, keepdims=True) + embed_eps)
        / root
        / sharpness_divisor
    )
    score = jnp.sum(embedded_ref[...].astype(F32) * positive, axis=1, keepdims=True) * scale
    pos_exp = jnp.exp(score)
    denom = denom + pos_exp
    loss_ref[...] = jnp.broadcast_to(jnp.sum(jnp.log(denom) - score), loss_ref.shape)
    grad_embed = total / denom + (pos_exp / denom - 1.0) * scale * positive
    pooled, unit = pooled_ref[...], unit_ref[...]
    mean_sq = jnp.mean(pooled * pooled, axis=1, keepdims=True)
    radial = jnp.sum(pooled * grad_embed, axis=1, keepdims=True)
    grad = unit * grad_embed - pooled * (radial * unit / (width * (mean_sq + embed_eps)))
    grad = grad.astype(BF16)
    grad_ref[...] = grad
    places = width // columns_ref.shape[2]
    cols = columns_ref.shape[2]
    for j in range(columns_ref.shape[0]):
        at = (j % places) * cols
        columns_ref[j] = grad[:, at : at + cols]


def slope_kernel(seq, blocks, z_ref, normed_ref, curve_ref, loss_ref, *rest):
    backs, outs, all_ref, sum_ref = rest[:blocks], rest[blocks : 2 * blocks], rest[-2], rest[-1]
    step = pl.program_id(0)
    tokens, width = normed_ref.shape
    count = tokens // seq
    depth = width // blocks

    @pl.when(step == 0)
    def _():
        sum_ref[...] = jnp.zeros_like(sum_ref)
        for k in range(blocks):
            at = lax.rem(z_ref[0] + k, blocks) * depth
            all_ref[:, pl.ds(pl.multiple_of(at, LANES), depth)] = backs[k][...].astype(F32)

    back = all_ref[pl.ds(pl.multiple_of(step * count, count), count), :]
    normed = normed_ref[...].astype(F32).reshape(count, seq, width)
    dots = jnp.sum(normed * back[:, None, :], axis=2, keepdims=True)
    slope = curve_ref[...].reshape(count, seq, 1) * dots
    heavy = (slope * normed).reshape(tokens // 8, 8, width)
    sum_ref[...] += jnp.sum(heavy, axis=0)

    @pl.when(step == pl.num_programs(0) - 1)
    def _():
        all_ref[0:1, :] = jnp.sum(sum_ref[...], axis=0, keepdims=True)
        for k in range(blocks):
            at = lax.rem(z_ref[0] + k, blocks) * depth
            outs[k][:, :depth] = all_ref[0:1, pl.ds(pl.multiple_of(at, LANES), depth)]
            outs[k][:, depth:] = loss_ref[...]


def slope_rows(z, normed, curve, loss, backs, seq):
    tokens, width = normed.shape
    blocks = len(backs)
    queries = tokens // seq
    group = 8 if queries % 8 == 0 else queries
    step_tokens = group * seq
    whole = lambda dims: pl.BlockSpec(dims, lambda i: (0, 0))
    return pl.pallas_call(
        functools.partial(slope_kernel, seq, blocks),
        grid=(queries // group,),
        out_shape=[shape((1, width // blocks + LANES), F32)] * blocks,
        in_specs=[
            SMEM,
            pl.BlockSpec((step_tokens, width), lambda i: (i, 0)),
            pl.BlockSpec((step_tokens, 1), lambda i: (i, 0)),
            whole((1, LANES)),
        ]
        + [whole((queries, width // blocks))] * blocks,
        out_specs=[whole((1, width // blocks + LANES))] * blocks,
        scratch_shapes=[pltpu.VMEM((queries, width), F32), pltpu.VMEM((8, width), F32)],
        cost_estimate=pl.CostEstimate(
            flops=4 * tokens * width, bytes_accessed=2 * tokens * width, transcendentals=0
        ),
        compiler_params=pltpu.CompilerParams(vmem_limit_bytes=44 * MIB),
        name="slope_rows",
    )(z, normed, curve, loss, *backs)


def columns_kernel(n, order_ref, grads_ref, *refs):
    pieces, out_ref, sorted_ref = refs[:n], refs[n], refs[n + 1]
    chunk = grads_ref.shape[1]
    for j in range(sorted_ref.shape[0] // chunk):
        sorted_ref[j * chunk : (j + 1) * chunk, :] = grads_ref[order_ref[j]]
    rows = pieces[0].shape[0]
    total = tn(sorted_ref[0:rows, :], pieces[0][...])
    for k in range(1, n):
        total = total + tn(sorted_ref[k * rows : (k + 1) * rows, :], pieces[k][...])
    out_ref[...] = total.T.astype(BF16)


def finish_kernel(n, place_ref, slope_ref, pool_ref, *refs):
    pieces, out_ref = refs[:n], refs[n]
    cols = pieces[0].shape[1]
    slope = slope_ref[...]
    for k in range(n):
        at = pl.ds(pl.multiple_of(place_ref[k] * cols, LANES), cols)
        out_ref[:, at] = pieces[k][...].astype(F32) + slope * pool_ref[:, at]


def body(hidden_states, positives, negatives, lengths, norm_gain, proj_weight, pool_query, slab):
    queries, seq, width = hidden_states.shape
    depth, proj_width = proj_weight.shape
    n_z, n_g, n_i = lax.axis_size("fsdp"), lax.axis_size("grp"), lax.axis_size("item")
    n_c = 2 if n_i % 2 == 0 else 1
    n_h = n_i // n_c
    n_all = n_z * n_g * n_i
    z, g, i = lax.axis_index("fsdp"), lax.axis_index("grp"), lax.axis_index("item")
    h, c = i // n_c, lax.rem(i, n_c)
    root = math.sqrt(proj_width)
    z_arr = z.reshape(1).astype(jnp.int32)
    steps_z = range(1, n_z)
    steps_i = range(1, n_i)

    def plane_shift(values, dg, dh, dc):
        pairs = []
        for pg in range(n_g):
            for ph in range(n_h):
                for pc in range(n_c):
                    to = ((pg + dg) % n_g) * n_i + ((ph + dh) % n_h) * n_c + (pc + dc) % n_c
                    pairs.append((pg * n_i + ph * n_c + pc, to))
        return lax.ppermute(values, PLANE, pairs)

    def plane_gather(own):
        got = {}
        for dg in range(n_g):
            for dh in range(n_h):
                got[dg, dh, 0] = own if dg == dh == 0 else plane_shift(own, dg, dh, 0)
        for dg in range(n_g):
            for dh in range(n_h):
                for dc in range(1, n_c):
                    got[dg, dh, dc] = plane_shift(got[dg, dh, 0], 0, 0, dc)
        return got

    def source(dg, dh, dc):
        return (
            lax.rem(g - dg + n_g, n_g),
            lax.rem(h - dh + n_h, n_h) * n_c + lax.rem(c - dc + n_c, n_c),
        )

    block_u = jnp.sum(proj_weight.astype(F32) * pool_query[None, :], axis=1).reshape(1, depth)
    u_parts = [block_u] + [shift(block_u, "fsdp", k) for k in steps_z]
    u = jnp.zeros((1, width), F32)
    for k in range(n_z):
        u = lax.dynamic_update_slice(u, u_parts[k], (0, lax.rem(z - k + n_z, n_z) * depth))

    states = hidden_states.reshape(-1, width).astype(F32)
    inv_rms = lax.rsqrt(jnp.mean(states * states, axis=1, keepdims=True) + norm_eps)
    normed = (states * inv_rms * norm_gain.astype(F32)).astype(BF16)

    own = negatives.shape[1] // n_i
    lists = lax.all_to_all(negatives.reshape(queries, n_i, own), "item", 1, 0, tiled=True)
    lists = lists.reshape(n_i * queries, own)
    origin = jnp.stack([lax.rem(i - k + n_i, n_i) for k in range(n_i)] + [i * slab.shape[0]])
    counts = call(
        functools.partial(count_kernel, n_i),
        [shape((n_i * queries, slab.shape[0]), F32)], [origin.astype(jnp.int32), lists], "list_counts", smem=1,
    )[0]
    slab_f32 = slab.astype(F32)
    slab_scale = (
        lax.rsqrt(jnp.mean(slab_f32 * slab_f32, axis=1) + embed_eps) / root / sharpness_divisor
    ).reshape(1, -1)

    token_lengths = jnp.broadcast_to(lengths[:, None], (queries, seq)).reshape(-1, 1)
    *sends, gated, curve = gate_rows(z_arr, normed, u, token_lengths, seq, root, n_z)

    pieces = [sends[0]] + [shift(sends[k], "fsdp", k) for k in steps_z]
    *parts, held = block_product(pieces, proj_weight, False, True)
    parts = [parts[0]] + [shift(parts[k], "fsdp", -k) for k in steps_z]
    row = shape((queries, proj_width), F32)
    pooled, unit, embedded = call(
        functools.partial(embed_kernel, root),
        [row, shape((queries, 1), F32), shape(row.shape, BF16)], parts, "embed",
    )

    pieces = [embedded] + [shift(embedded, "item", k) for k in steps_i]
    wide = (queries, proj_width + LANES)
    parts = call(
        functools.partial(contrast_kernel, n_i),
        [shape(wide, F32)] + [shape(wide, BF16)] * (n_i - 1),
        pieces + [slab, slab_scale, counts], "contrast",
        flops=4 * n_i * queries * slab.shape[0] * proj_width,
    )
    parts = [parts[0]] + [shift(parts[k], "item", -k) for k in steps_i]
    n_plane = n_g * n_i
    cols = proj_width // n_plane
    grad, grad_columns, loss = call(
        functools.partial(grad_kernel, n_i, root),
        [shape(row.shape, BF16), shape((n_all, queries, cols), BF16), shape((1, LANES), F32)],
        parts + [positives, pooled, unit, embedded], "grad_pooled",
    )

    spread = plane_gather(held)
    all_columns = lax.all_to_all(grad_columns, EVERY, 0, 0, tiled=True)
    keys = sorted(spread, key=lambda key: (key[2], key[0], key[1]))
    order = []
    for key in keys:
        from_g, from_i = source(*key)
        for k in range(n_z):
            order.append((lax.rem(z - k + n_z, n_z) * n_g + from_g) * n_i + from_i)
    block_columns = call(
        functools.partial(columns_kernel, len(keys)),
        [shape((depth, cols), BF16)],
        [jnp.stack(order).astype(jnp.int32), all_columns] + [spread[key] for key in keys], "grad_columns",
        flops=2 * n_all * queries * depth * cols, scratch=[pltpu.VMEM((n_all * queries, cols), BF16)], smem=1,
    )[0]
    finished = plane_gather(block_columns)

    pieces = [grad] + [shift(grad, "fsdp", k) for k in steps_z]
    backs = block_product(pieces, proj_weight, True, False)
    backs = [backs[0]] + [shift(backs[k], "fsdp", -k) for k in steps_z]
    slopes = slope_rows(z_arr, normed, curve, loss, backs, seq)
    slope = slopes[0]
    for k in steps_z:
        slope = slope + shift(slopes[k], "fsdp", k)
    slope = slope + sum(shift(slope, "grp", k) for k in range(1, n_g))
    slope = slope + sum(shift(slope, "item", k) for k in steps_i)
    mean_loss = slope[0, depth] / (queries * n_all)
    slope = slope[:, :depth]
    high, low = split_bf16(slope)
    low = lax.reduce_precision(slope - lax.reduce_precision(slope, 8, 7), 8, 7).astype(BF16)
    query_part = jnp.dot(jnp.concatenate([high, low], axis=0), proj_weight, preferred_element_type=F32)
    query_part = jnp.sum(query_part, axis=0, keepdims=True)
    grad_query = query_part + sum(shift(query_part, "fsdp", k) for k in steps_z)

    places = []
    for key in keys:
        from_g, from_i = source(*key)
        places.append(from_g * n_i + from_i)
    grad_proj = call(
        functools.partial(finish_kernel, len(keys)), [shape((depth, proj_width), F32)],
        [jnp.stack(places).astype(jnp.int32), slope.reshape(depth, 1), pool_query.reshape(1, -1)]
        + [finished[key] for key in keys], "finish", smem=1,
    )[0]
    return (grad_proj, grad_query.reshape(proj_width), mean_loss)


def solution(mesh):
    return jax.shard_map(
        body,
        mesh=mesh,
        in_specs=(
            P(("grp", "fsdp", "item"), None, None),
            P(("grp", "fsdp", "item"), None),
            P(("grp", "fsdp", "item"), None),
            P(("grp", "fsdp", "item")),
            P(),
            P("fsdp", None),
            P(),
            P("item", None),
        ),
        out_specs=(P("fsdp", None), P(), P()),
        check_vma=False,
    )
```

```python
import functools
import math

import jax
import jax.numpy as jnp
from jax import lax
from jax.experimental import pallas as pl
from jax.experimental.pallas import tpu as pltpu
from jax.sharding import PartitionSpec as P

sharpness_divisor = 0.05
norm_eps = 1e-05
embed_eps = 1e-06

EVERY = ("fsdp", "grp", "item")
PLANE = ("grp", "item")
F32 = jnp.float32
BF16 = jnp.bfloat16
LANES = 128
MIB = 1024 * 1024
VMEM = pl.BlockSpec(memory_space=pltpu.VMEM)
SMEM = pl.BlockSpec(memory_space=pltpu.SMEM)


def shape(dims, dtype):
    return jax.ShapeDtypeStruct(dims, dtype)


def call(kernel, outs, ins, name, flops=0, scratch=(), smem=0, after=()):
    run = kernel
    if after:
        count = len(ins)

        def run(*refs):
            kernel(*refs[:count], *refs[count + len(after) :])

    moved = sum(math.prod(a.shape) * a.dtype.itemsize for a in list(ins) + list(outs))
    return pl.pallas_call(
        run,
        out_shape=outs,
        in_specs=[SMEM] * smem
        + [VMEM] * (len(ins) - smem)
        + [pl.BlockSpec(memory_space=pl.ANY)] * len(after),
        out_specs=[VMEM] * len(outs),
        scratch_shapes=scratch,
        cost_estimate=pl.CostEstimate(flops=flops, bytes_accessed=moved, transcendentals=0),
        compiler_params=pltpu.CompilerParams(vmem_limit_bytes=44 * MIB),
        name=name,
    )(*ins, *after)


def shift(values, axis, k):
    n = lax.axis_size(axis)
    return lax.ppermute(values, axis, [(i, (i + k) % n) for i in range(n)])


def split_bf16(values):
    high = values.astype(BF16)
    low = (values - high.astype(F32)).astype(BF16)
    return high, low


def nt(left, right):
    return lax.dot_general(left, right, (((1,), (1,)), ((), ())), preferred_element_type=F32)


def tn(left, right):
    return lax.dot_general(left, right, (((0,), (0,)), ((), ())), preferred_element_type=F32)


def norm_kernel(states_ref, gain_ref, normed_ref):
    tokens, width = states_ref.shape
    step = 4 * LANES if width % (4 * LANES) == 0 else width
    for top in range(0, tokens, 32):
        rows = slice(top, top + 32)
        squares = jnp.zeros((32, step), F32)
        for at in range(0, width, step):
            part = states_ref[rows, at : at + step].astype(F32)
            squares = squares + part * part
        inv_rms = lax.rsqrt(jnp.sum(squares, axis=1, keepdims=True) / width + norm_eps)
        for at in range(0, width, step):
            part = states_ref[rows, at : at + step].astype(F32)
            part = part * inv_rms * gain_ref[:, at : at + step]
            normed_ref[rows, at : at + step] = part.astype(BF16)


def norm_rows(states, gain):
    tokens, width = states.shape
    block = 128 if tokens % 128 == 0 else tokens
    rows = pl.BlockSpec((block, width), lambda i: (i, 0))
    return pl.pallas_call(
        norm_kernel,
        grid=(tokens // block,),
        out_shape=shape((tokens, width), BF16),
        in_specs=[rows, pl.BlockSpec((1, width), lambda i: (0, 0))],
        out_specs=rows,
        cost_estimate=pl.CostEstimate(
            flops=6 * tokens * width, bytes_accessed=4 * tokens * width, transcendentals=0
        ),
        compiler_params=pltpu.CompilerParams(vmem_limit_bytes=44 * MIB),
        name="norm_rows",
    )(states, gain)


def gate_kernel(seq, root, blocks, z_ref, normed_ref, u_ref, len_ref, lists_ref, *rest):
    half = blocks // 2
    outs, gated_ref, curve_ref, copy_ref, rows_ref = rest[:half], *rest[half:]
    step = pl.program_id(0)
    tokens, width = normed_ref.shape
    count = tokens // seq
    chunk = 4 * LANES if width % (4 * LANES) == 0 else width
    logits = []
    for top in range(0, tokens, 32):
        total = jnp.zeros((32, chunk), F32)
        for at in range(0, width, chunk):
            part = normed_ref[top : top + 32, at : at + chunk].astype(F32)
            total = total + part * u_ref[:, at : at + chunk]
        logits.append(jnp.sum(total, axis=1, keepdims=True))
    logit = jnp.concatenate(logits, axis=0) / root
    gate = 1.0 / (1.0 + jnp.exp(-logit))
    slot = lax.rem(lax.broadcasted_iota(jnp.int32, (tokens, 1), 0), seq)
    valid = jnp.where(slot < len_ref[...], 1.0, 0.0) / len_ref[...].astype(F32)
    gated = valid * gate
    gated_ref[...] = gated
    curve_ref[...] = gated * (1.0 - gate) / root
    owner = lax.broadcasted_iota(jnp.int32, (tokens, count), 0) // seq
    mine = owner == lax.broadcasted_iota(jnp.int32, (tokens, count), 1)
    high, low = split_bf16(jnp.where(mine, gated, 0.0))
    both = tn(jnp.concatenate([high, low], axis=1), normed_ref[...])
    rows_ref[pl.ds(pl.multiple_of(step * count, count), count), :] = both[:count] + both[count:]

    @pl.when(step == pl.num_programs(0) - 1)
    def _():
        copy_ref[...] = lists_ref[...]
        depth = width // blocks
        place = lax.rem(z_ref[0], half)
        for k in range(half):
            for j in range(2):
                at = (j * half + lax.rem(place + k, half)) * depth
                outs[k][:, j * depth : (j + 1) * depth] = rows_ref[
                    :, pl.ds(pl.multiple_of(at, LANES), depth)
                ].astype(BF16)


def gate_rows(z, normed, u, token_lengths, lists, seq, root, blocks):
    tokens, width = normed.shape
    queries = tokens // seq
    group = 8 if queries % 8 == 0 else queries
    step_tokens = group * seq
    half = blocks // 2
    outs = [shape((queries, width // half), BF16)] * half + [shape((tokens, 1), F32)] * 2
    outs.append(shape(lists.shape, lists.dtype))
    column = pl.BlockSpec((step_tokens, 1), lambda i: (i, 0))
    whole = lambda dims: pl.BlockSpec(dims, lambda i: (0, 0))
    return pl.pallas_call(
        functools.partial(gate_kernel, seq, root, blocks),
        grid=(queries // group,),
        out_shape=outs,
        in_specs=[
            SMEM,
            pl.BlockSpec((step_tokens, width), lambda i: (i, 0)),
            whole((1, width)),
            column,
            whole(lists.shape),
        ],
        out_specs=[whole((queries, width // half))] * half + [column] * 2 + [whole(lists.shape)],
        scratch_shapes=[pltpu.VMEM((queries, width), F32)],
        cost_estimate=pl.CostEstimate(
            flops=4 * tokens * width, bytes_accessed=2 * tokens * width, transcendentals=0
        ),
        compiler_params=pltpu.CompilerParams(vmem_limit_bytes=44 * MIB),
        name="gate_rows",
    )(z, normed, u, token_lengths, lists)


def pack_kernel(*refs):
    rows = refs[0].shape[0]
    for k, ref in enumerate(refs[:-1]):
        refs[-1][k * rows : (k + 1) * rows, :] = ref[...]


def pack(pieces, name):
    rows, width = pieces[0].shape
    return call(pack_kernel, [shape((len(pieces) * rows, width), pieces[0].dtype)], pieces, name)[0]


def forward_kernel(n, packs, side_ref, places_ref, *refs):
    pieces, weight_ref, shares = refs[:n], refs[n], refs[n + 1 : n + 1 + packs]
    outs = refs[n + 1 + packs : 2 * n + 1 + packs]
    mirror_ref, held_ref, away_ref = refs[2 * n + 1 + packs :]
    rows = pieces[0].shape[0]
    depth = weight_ref.shape[0]
    side = side_ref[0]
    for k in range(n):
        part = slice(k * rows, (k + 1) * rows)
        held_ref[part, :] = pieces[k][:, pl.ds(pl.multiple_of(side * depth, LANES), depth)]
        away_ref[part, :] = pieces[k][:, pl.ds(pl.multiple_of((1 - side) * depth, LANES), depth)]
    count = places_ref.shape[0] // packs
    share = shares[0].shape[0] // count
    for p in range(packs):
        for j in range(count):
            at = pl.multiple_of(places_ref[p * count + j] * share, share)
            mirror_ref[pl.ds(at, share), :] = shares[p][j * share : (j + 1) * share, :]
    product = jnp.dot(held_ref[...], weight_ref[...], preferred_element_type=F32)
    product = product + jnp.dot(away_ref[...], mirror_ref[...], preferred_element_type=F32)
    for k in range(n):
        outs[k][...] = product[k * rows : (k + 1) * rows].astype(outs[k].dtype)


def back_kernel(n, side_ref, *refs):
    pieces, weight_ref, mirror_ref, outs = refs[:n], refs[n], refs[n + 1], refs[n + 2 :]
    rows = pieces[0].shape[0]
    depth = weight_ref.shape[0]
    side = side_ref[0]
    stack = jnp.concatenate([p[...] for p in pieces], axis=0)
    own = nt(stack, weight_ref[...]).astype(BF16)
    mirror = nt(stack, mirror_ref[...]).astype(BF16)
    for k in range(n):
        part = slice(k * rows, (k + 1) * rows)
        outs[k][:, pl.ds(pl.multiple_of(side * depth, LANES), depth)] = own[part]
        outs[k][:, pl.ds(pl.multiple_of((1 - side) * depth, LANES), depth)] = mirror[part]


def embed_kernel(root, n, *refs):
    parts, packed = refs[:n], refs[n:-4]
    pooled_ref, unit_ref, embedded_ref, pack_ref = refs[-4:]
    pooled = parts[0][...]
    for part in parts[1:]:
        pooled = pooled + part[...].astype(F32)
    unit = lax.rsqrt(jnp.mean(pooled * pooled, axis=1, keepdims=True) + embed_eps) / root
    pooled_ref[...] = pooled
    unit_ref[...] = unit
    embedded_ref[...] = (pooled * unit).astype(BF16)
    pack_kernel(*packed, pack_ref)


def count_kernel(n, root, base_ref, slab_ref, *refs):
    lists, counts_ref, scale_ref = refs[:n], refs[n], refs[n + 1]
    queries = lists[0].shape[0]
    rows, width = slab_ref.shape
    slab = slab_ref[...].astype(F32)
    high, low = split_bf16(slab * slab)
    ones = jnp.ones((8, width), BF16)
    row_sq = (nt(ones, high) + nt(ones, low))[0:1]
    scale_ref[...] = lax.rsqrt(row_sq / width + embed_eps) / root / sharpness_divisor
    ids = lax.broadcasted_iota(jnp.int32, (queries, LANES), 1)
    for k in range(n):
        own = lists[k][...] - base_ref[0]
        columns = [
            jnp.broadcast_to(own[:, entry : entry + 1], (queries, LANES)) for entry in range(own.shape[1])
        ]
        for at in range(0, rows, LANES):
            total = jnp.zeros(ids.shape, F32)
            for column in columns:
                total = total + jnp.where(column == ids + at, 1.0, 0.0)
            counts_ref[k * queries : (k + 1) * queries, at : at + LANES] = total


def contrast_kernel(n, *refs):
    pieces, (slab_ref, scale_ref, counts_ref), outs = refs[:n], refs[n : n + 3], refs[n + 3 :]
    queries, width = pieces[0].shape
    embedded = jnp.concatenate([p[...] for p in pieces], axis=0)
    slab = slab_ref[...]
    scale = scale_ref[...]
    heavy = counts_ref[...] * jnp.exp(nt(embedded, slab) * scale)
    denom = jnp.sum(heavy, axis=1, keepdims=True)
    grad = jnp.dot((heavy * scale).astype(BF16), slab, preferred_element_type=F32)
    high, low = split_bf16(denom)
    lane = lax.broadcasted_iota(jnp.int32, (queries, LANES), 1)
    for k in range(n):
        part = slice(k * queries, (k + 1) * queries)
        outs[k][:, :width] = grad[part].astype(outs[k].dtype)
        if k == 0:
            tail = jnp.where(lane == 0, denom[part], 0.0)
        else:
            tail = jnp.where(lane == 0, high[part].astype(F32), jnp.where(lane == 1, low[part].astype(F32), 0.0))
        outs[k][:, width:] = tail.astype(outs[k].dtype)


def grad_kernel(n, packed_count, root, *refs):
    parts = refs[:n]
    pos_ref, pooled_ref, unit_ref, embedded_ref = refs[n : n + 4]
    packed = refs[n + 4 : n + 4 + packed_count]
    grad_ref, columns_ref, loss_ref, pack_ref = refs[n + 4 + packed_count :]
    queries, width = pos_ref.shape
    total = parts[0][:, :width]
    denom = jnp.sum(parts[0][:, width:], axis=1, keepdims=True)
    for part in parts[1:]:
        total = total + part[:, :width].astype(F32)
        denom = denom + jnp.sum(part[:, width:].astype(F32), axis=1, keepdims=True)
    positive = pos_ref[...].astype(F32)
    scale = (
        lax.rsqrt(jnp.mean(positive * positive, axis=1, keepdims=True) + embed_eps)
        / root
        / sharpness_divisor
    )
    score = jnp.sum(embedded_ref[...].astype(F32) * positive, axis=1, keepdims=True) * scale
    pos_exp = jnp.exp(score)
    denom = denom + pos_exp
    loss_ref[...] = jnp.broadcast_to(jnp.sum(jnp.log(denom) - score), loss_ref.shape)
    grad_embed = total / denom + (pos_exp / denom - 1.0) * scale * positive
    pooled, unit = pooled_ref[...], unit_ref[...]
    mean_sq = jnp.mean(pooled * pooled, axis=1, keepdims=True)
    radial = jnp.sum(pooled * grad_embed, axis=1, keepdims=True)
    grad = unit * grad_embed - pooled * (radial * unit / (width * (mean_sq + embed_eps)))
    grad = grad.astype(BF16)
    grad_ref[...] = grad
    cols = columns_ref.shape[2]
    places = width // cols
    for j in range(columns_ref.shape[0]):
        at = (j % places) * cols
        columns_ref[j] = grad[:, at : at + cols]
    pack_kernel(*packed, pack_ref)


def slope_kernel(seq, blocks, z_ref, normed_ref, curve_ref, loss_ref, *rest):
    half = blocks // 2
    backs, outs, all_ref, sum_ref = rest[:half], rest[half + 1 : 2 * half + 1], rest[-2], rest[-1]
    step = pl.program_id(0)
    tokens, width = normed_ref.shape
    count = tokens // seq
    depth = width // blocks
    place = lax.rem(z_ref[0], half)

    def block_at(j, k):
        return pl.ds(pl.multiple_of((j * half + lax.rem(place + k, half)) * depth, LANES), depth)

    @pl.when(step == 0)
    def _():
        sum_ref[...] = jnp.zeros_like(sum_ref)
        for k in range(half):
            for j in range(2):
                all_ref[:, block_at(j, k)] = backs[k][:, j * depth : (j + 1) * depth].astype(F32)

    back = all_ref[pl.ds(pl.multiple_of(step * count, count), count), :]
    normed = normed_ref[...].astype(F32).reshape(count, seq, width)
    dots = jnp.sum(normed * back[:, None, :], axis=2, keepdims=True)
    slope = curve_ref[...].reshape(count, seq, 1) * dots
    heavy = (slope * normed).reshape(tokens // 8, 8, width)
    sum_ref[...] += jnp.sum(heavy, axis=0)

    @pl.when(step == pl.num_programs(0) - 1)
    def _():
        all_ref[0:1, :] = jnp.sum(sum_ref[...], axis=0, keepdims=True)
        for k in range(half):
            for j in range(2):
                outs[k][:, j * depth : (j + 1) * depth] = all_ref[0:1, block_at(j, k)]
            outs[k][:, 2 * depth :] = loss_ref[...]


def slope_rows(z, normed, curve, loss, backs, seq, blocks, after):
    tokens, width = normed.shape
    half = blocks // 2
    queries = tokens // seq
    group = 8 if queries % 8 == 0 else queries
    step_tokens = group * seq
    whole = lambda dims: pl.BlockSpec(dims, lambda i: (0, 0))
    return pl.pallas_call(
        functools.partial(slope_kernel, seq, blocks),
        grid=(queries // group,),
        out_shape=[shape((1, width // half + LANES), F32)] * half,
        in_specs=[
            SMEM,
            pl.BlockSpec((step_tokens, width), lambda i: (i, 0)),
            pl.BlockSpec((step_tokens, 1), lambda i: (i, 0)),
            whole((1, LANES)),
        ]
        + [whole((queries, width // half))] * half
        + [pl.BlockSpec(memory_space=pl.ANY)],
        out_specs=[whole((1, width // half + LANES))] * half,
        scratch_shapes=[pltpu.VMEM((queries, width), F32), pltpu.VMEM((8, width), F32)],
        cost_estimate=pl.CostEstimate(
            flops=4 * tokens * width, bytes_accessed=2 * tokens * width, transcendentals=0
        ),
        compiler_params=pltpu.CompilerParams(vmem_limit_bytes=44 * MIB),
        name="slope_rows",
    )(z, normed, curve, loss, *backs, after)


def columns_kernel(n, order_ref, grads_ref, *refs):
    pieces, out_ref, sorted_ref = refs[:n], refs[n], refs[n + 1]
    chunk = grads_ref.shape[1]
    for j in range(sorted_ref.shape[0] // chunk):
        sorted_ref[j * chunk : (j + 1) * chunk, :] = grads_ref[order_ref[j]]
    at = pieces[0].shape[0]
    total = tn(sorted_ref[0:at, :], pieces[0][...])
    for piece in pieces[1:]:
        rows = piece.shape[0]
        total = total + tn(sorted_ref[at : at + rows, :], piece[...])
        at += rows
    out_ref[...] = total.T.astype(BF16)


def finish_kernel(n, place_ref, slope_ref, pool_ref, *refs):
    pieces, out_ref = refs[:n], refs[n]
    cols = pieces[0].shape[1]
    slope = slope_ref[...]
    for k in range(n):
        at = pl.ds(pl.multiple_of(place_ref[k] * cols, LANES), cols)
        out_ref[:, at] = pieces[k][...].astype(F32) + slope * pool_ref[:, at]


def finish(places, slope, pool, pieces):
    rows, cols = pieces[0].shape
    width = pool.shape[1]
    block = 128 if rows % 128 == 0 else rows
    moved = rows * width * 6
    return pl.pallas_call(
        functools.partial(finish_kernel, len(pieces)),
        grid=(rows // block,),
        out_shape=shape((rows, width), F32),
        in_specs=[
            SMEM,
            pl.BlockSpec((block, 1), lambda i: (i, 0)),
            pl.BlockSpec((1, width), lambda i: (0, 0)),
        ]
        + [pl.BlockSpec((block, cols), lambda i: (i, 0))] * len(pieces),
        out_specs=pl.BlockSpec((block, width), lambda i: (i, 0)),
        cost_estimate=pl.CostEstimate(flops=2 * rows * width, bytes_accessed=moved, transcendentals=0),
        compiler_params=pltpu.CompilerParams(vmem_limit_bytes=44 * MIB),
        name="finish",
    )(places, slope, pool, *pieces)


def body(hidden_states, positives, negatives, lengths, norm_gain, proj_weight, pool_query, slab):
    queries, seq, width = hidden_states.shape
    depth, proj_width = proj_weight.shape
    n_z, n_g, n_i = lax.axis_size("fsdp"), lax.axis_size("grp"), lax.axis_size("item")
    assert n_z % 2 == 0
    half = n_z // 2
    n_c = 2 if n_i % 2 == 0 else 1
    n_h = n_i // n_c
    n_plane = n_g * n_i
    n_all = n_z * n_plane
    z, g, i = lax.axis_index("fsdp"), lax.axis_index("grp"), lax.axis_index("item")
    h, c = i // n_c, lax.rem(i, n_c)
    side, member = z // half, lax.rem(z, half)
    root = math.sqrt(proj_width)
    steps_z, steps_i = range(1, n_z), range(1, n_i)

    def ints(*values):
        return jnp.stack([jnp.asarray(v, jnp.int32) for v in values])

    z_arr, side_arr = ints(z), ints(side)

    def plane_shift(values, dg, dh, dc):
        pairs = []
        for pg in range(n_g):
            for ph in range(n_h):
                for pc in range(n_c):
                    to = ((pg + dg) % n_g) * n_i + ((ph + dh) % n_h) * n_c + (pc + dc) % n_c
                    pairs.append((pg * n_i + ph * n_c + pc, to))
        return lax.ppermute(values, PLANE, pairs)

    def half_shift(values, k):
        pairs = [(a, a // half * half + (a % half + k) % half) for a in range(n_z)]
        return lax.ppermute(values, "fsdp", pairs)

    def mirror_shift(values):
        return lax.ppermute(values, "fsdp", [(a, (a + half) % n_z) for a in range(n_z)])

    def source(dg, dh, dc):
        return (
            lax.rem(g - dg + n_g, n_g),
            lax.rem(h - dh + n_h, n_h) * n_c + lax.rem(c - dc + n_c, n_c),
        )

    chips = [(dg, dh) for dg in range(n_g) for dh in range(n_h)]

    share = depth // n_plane
    place = g * n_i + i
    weight_share = lax.dynamic_slice_in_dim(proj_weight, place * share, share, 0)
    far_share = mirror_shift(weight_share)

    block_u = jnp.sum(proj_weight.astype(F32) * pool_query[None, :], axis=1).reshape(1, depth)
    u_parts = [block_u] + [shift(block_u, "fsdp", k) for k in steps_z]
    u = jnp.zeros((1, width), F32)
    for k in range(n_z):
        u = lax.dynamic_update_slice(u, u_parts[k], (0, lax.rem(z - k + n_z, n_z) * depth))

    normed = norm_rows(hidden_states.reshape(-1, width), norm_gain.astype(F32).reshape(1, width))

    chip_shares = [far_share if dg == dh == 0 else plane_shift(far_share, dg, dh, 0) for dg, dh in chips]
    packs = [pack(chip_shares, "pack_shares")]
    packs += [plane_shift(packs[0], 0, 0, dc) for dc in range(1, n_c)]
    share_places = []
    for dc in range(n_c):
        for dg, dh in chips:
            from_g, from_i = source(dg, dh, dc)
            share_places.append(from_g * n_i + from_i)

    token_lengths = jnp.broadcast_to(lengths[:, None], (queries, seq)).reshape(-1, 1)
    *sends, gated, curve, own_lists = gate_rows(
        z_arr, normed, u, token_lengths, negatives, seq, root, n_z
    )

    pieces = [sends[0]] + [half_shift(sends[k], k) for k in range(1, half)]
    lists = [own_lists] + [shift(own_lists, "item", k) for k in steps_i]
    counts, slab_scale = call(
        functools.partial(count_kernel, n_i, root),
        [shape((n_i * queries, slab.shape[0]), F32), shape((1, slab.shape[0]), F32)],
        [ints(i * slab.shape[0]), slab] + lists, "list_counts", smem=1,
    )
    block = shape((half * queries, depth), BF16)
    *parts, mirror, held, away = call(
        functools.partial(forward_kernel, half, n_c),
        [shape((queries, proj_width), F32)]
        + [shape((queries, proj_width), BF16)] * (half - 1)
        + [shape((depth, proj_width), BF16), block, block],
        [side_arr, ints(*share_places)] + pieces + [proj_weight] + packs, "forward",
        flops=4 * half * queries * depth * proj_width, smem=2,
    )
    parts = [parts[0]] + [half_shift(parts[k], -k) for k in range(1, half)]
    near = [held] + [plane_shift(held, 0, dh, 0) for dh in range(1, n_h)]
    other = mirror_shift(away)
    row = shape((queries, proj_width), F32)
    row16 = shape((queries, proj_width), BF16)
    pooled, unit, embedded, near = call(
        functools.partial(embed_kernel, root, half),
        [row, shape((queries, 1), F32), row16, shape((n_h * half * queries, depth), BF16)],
        parts + near, "embed",
    )

    pieces = [embedded] + [shift(embedded, "item", k) for k in steps_i]
    near_far = [plane_shift(near, dg, 0, 0) for dg in range(1, n_g)]
    wide = (queries, proj_width + LANES)
    parts = call(
        functools.partial(contrast_kernel, n_i),
        [shape(wide, F32)] + [shape(wide, BF16)] * (n_i - 1),
        pieces + [slab, slab_scale, counts], "contrast",
        flops=4 * n_i * queries * slab.shape[0] * proj_width, after=[other],
    )
    parts = [parts[0]] + [shift(parts[k], "item", -k) for k in steps_i]
    others = [other] + [plane_shift(other, dg, 0, 0) for dg in range(1, n_g)]
    cols = proj_width // n_plane
    grad, grad_columns, loss, others = call(
        functools.partial(grad_kernel, n_i, n_g, root),
        [
            row16, shape((n_all, queries, cols), BF16), shape((1, LANES), F32),
            shape((n_g * half * queries, depth), BF16),
        ],
        parts + [positives, pooled, unit, embedded] + others, "grad_pooled", after=near_far,
    )

    all_columns = lax.all_to_all(grad_columns, EVERY, 0, 0, tiled=True)
    near_sets = [(near, 0)] + [(near_far[dg - 1], dg) for dg in range(1, n_g)]
    other_sets = [(others, 0)] + [(plane_shift(others, 0, dh, 0), dh) for dh in range(1, n_h)]
    spread, order = [], []
    for dc in range(n_c):
        for array, dg in near_sets:
            spread.append(array if dc == 0 else plane_shift(array, 0, 0, dc))
            order += [(side, k, dg, dh, dc) for dh in range(n_h) for k in range(half)]
        for array, dh in other_sets:
            spread.append(array if dc == 0 else plane_shift(array, 0, 0, dc))
            order += [(1 - side, k, dg, dh, dc) for dg in range(n_g) for k in range(half)]
    ranks = []
    for from_side, k, dg, dh, dc in order:
        from_g, from_i = source(dg, dh, dc)
        from_z = from_side * half + lax.rem(member - k + half, half)
        ranks.append((from_z * n_g + from_g) * n_i + from_i)
    block_columns = call(
        functools.partial(columns_kernel, len(spread)), [shape((depth, cols), BF16)],
        [ints(*ranks), all_columns] + spread, "grad_columns",
        flops=2 * n_all * queries * depth * cols, scratch=[pltpu.VMEM((n_all * queries, cols), BF16)], smem=1,
    )[0]
    finished, places = [], []
    on_chips = [block_columns if dg == dh == 0 else plane_shift(block_columns, dg, dh, 0) for dg, dh in chips]
    for dc in range(n_c):
        for (dg, dh), array in zip(chips, on_chips):
            finished.append(array if dc == 0 else plane_shift(array, 0, 0, dc))
            from_g, from_i = source(dg, dh, dc)
            places.append(from_g * n_i + from_i)

    pieces = [grad] + [half_shift(grad, k) for k in range(1, half)]
    backs = call(
        functools.partial(back_kernel, half), [shape((queries, 2 * depth), BF16)] * half,
        [side_arr] + pieces + [proj_weight, mirror], "backward",
        flops=4 * half * queries * depth * proj_width, smem=1,
    )
    backs = [backs[0]] + [half_shift(backs[k], -k) for k in range(1, half)]
    slopes = slope_rows(z_arr, normed, curve, loss, backs, seq, n_z, block_columns)
    slope = slopes[0]
    for k in range(1, half):
        slope = slope + half_shift(slopes[k], k)
    slope = slope + mirror_shift(slope)
    slope = slope + sum(shift(slope, "grp", k) for k in range(1, n_g))
    slope = slope + sum(shift(slope, "item", k) for k in steps_i)
    mean_loss = slope[0, 2 * depth] / (queries * n_all)
    slope = slope[:, : 2 * depth]
    high = lax.reduce_precision(slope, 8, 7)
    both = jnp.concatenate([high.astype(BF16), (slope - high).astype(BF16)], axis=0)
    my_both = lax.dynamic_slice_in_dim(both, side * depth, depth, 1)
    mirror_both = lax.dynamic_slice_in_dim(both, (1 - side) * depth, depth, 1)
    query_part = jnp.dot(my_both, proj_weight, preferred_element_type=F32)
    query_part = query_part + jnp.dot(mirror_both, mirror, preferred_element_type=F32)
    query_part = jnp.sum(query_part, axis=0, keepdims=True)
    grad_query = query_part + sum(half_shift(query_part, k) for k in range(1, half))

    my_slope = lax.dynamic_slice_in_dim(slope, side * depth, depth, 1).reshape(depth, 1)
    grad_proj = finish(ints(*places), my_slope, pool_query.reshape(1, -1), finished)
    return (grad_proj, grad_query.reshape(proj_width), mean_loss)


def solution(mesh):
    return jax.shard_map(
        body,
        mesh=mesh,
        in_specs=(
            P(("grp", "fsdp", "item"), None, None),
            P(("grp", "fsdp", "item"), None),
            P(("grp", "fsdp", "item"), None),
            P(("grp", "fsdp", "item")),
            P(),
            P("fsdp", None),
            P(),
            P("item", None),
        ),
        out_specs=(P("fsdp", None), P(), P()),
        check_vma=False,
    )
```

```python
import functools
import math

import jax
import jax.numpy as jnp
from jax import lax
from jax.experimental import pallas as pl
from jax.experimental.pallas import tpu as pltpu
from jax.sharding import PartitionSpec as P

sharpness_divisor = 0.05
norm_eps = 1e-05
embed_eps = 1e-06

EVERY = ("fsdp", "grp", "item")
PLANE = ("grp", "item")
F32 = jnp.float32
BF16 = jnp.bfloat16
LANES = 128
MIB = 1024 * 1024
VMEM = pl.BlockSpec(memory_space=pltpu.VMEM)
SMEM = pl.BlockSpec(memory_space=pltpu.SMEM)


def shape(dims, dtype):
    return jax.ShapeDtypeStruct(dims, dtype)


def call(kernel, outs, ins, name, flops=0, scratch=(), smem=0, after=()):
    run = kernel
    if after:
        count = len(ins)

        def run(*refs):
            kernel(*refs[:count], *refs[count + len(after) :])

    moved = sum(math.prod(a.shape) * a.dtype.itemsize for a in list(ins) + list(outs))
    held = sum(math.prod(s.shape) * jnp.dtype(s.dtype).itemsize for s in scratch)
    return pl.pallas_call(
        run,
        out_shape=outs,
        in_specs=[SMEM] * smem
        + [VMEM] * (len(ins) - smem)
        + [pl.BlockSpec(memory_space=pl.ANY)] * len(after),
        out_specs=[VMEM] * len(outs),
        scratch_shapes=scratch,
        cost_estimate=pl.CostEstimate(flops=flops, bytes_accessed=moved, transcendentals=0),
        compiler_params=pltpu.CompilerParams(vmem_limit_bytes=2 * (moved + held) + 6 * MIB),
        name=name,
    )(*ins, *after)


def shift(values, axis, k):
    n = lax.axis_size(axis)
    return lax.ppermute(values, axis, [(i, (i + k) % n) for i in range(n)])


def split_bf16(values):
    high = values.astype(BF16)
    low = (values - high.astype(F32)).astype(BF16)
    return high, low


def nt(left, right):
    return lax.dot_general(left, right, (((1,), (1,)), ((), ())), preferred_element_type=F32)


def tn(left, right):
    return lax.dot_general(left, right, (((0,), (0,)), ((), ())), preferred_element_type=F32)


def norm_kernel(event_ref, states_ref, gain_ref, normed_ref):
    tokens, width = states_ref.shape
    step = 4 * LANES if width % (4 * LANES) == 0 else width
    for top in range(0, tokens, 32):
        rows = slice(top, top + 32)
        squares = jnp.zeros((32, step), F32)
        for at in range(0, width, step):
            part = states_ref[rows, at : at + step].astype(F32)
            squares = squares + part * part
        inv_rms = lax.rsqrt(jnp.sum(squares, axis=1, keepdims=True) / width + norm_eps)
        for at in range(0, width, step):
            part = states_ref[rows, at : at + step].astype(F32)
            part = part * inv_rms * gain_ref[:, at : at + step]
            normed_ref[rows, at : at + step] = part.astype(BF16)


def norm_rows(event, states, gain):
    tokens, width = states.shape
    block = 128 if tokens % 128 == 0 else tokens
    rows = pl.BlockSpec((block, width), lambda i: (i, 0))
    return pl.pallas_call(
        norm_kernel,
        grid=(tokens // block,),
        out_shape=shape((tokens, width), BF16),
        in_specs=[pl.BlockSpec(memory_space=pl.ANY), rows, pl.BlockSpec((1, width), lambda i: (0, 0))],
        out_specs=rows,
        cost_estimate=pl.CostEstimate(
            flops=6 * tokens * width, bytes_accessed=4 * tokens * width, transcendentals=0
        ),
        compiler_params=pltpu.CompilerParams(vmem_limit_bytes=10 * MIB),
        name="norm_rows",
    )(event, states, gain)


def gate_kernel(seq, root, blocks, z_ref, normed_ref, u_ref, len_ref, lists_ref, event_ref, *rest):
    half = blocks // 2
    outs, gated_ref, curve_ref, copy_ref, rows_ref = rest[:half], *rest[half:]
    step = pl.program_id(0)
    tokens, width = normed_ref.shape
    count = tokens // seq
    chunk = 4 * LANES if width % (4 * LANES) == 0 else width
    logits = []
    for top in range(0, tokens, 32):
        total = jnp.zeros((32, chunk), F32)
        for at in range(0, width, chunk):
            part = normed_ref[top : top + 32, at : at + chunk].astype(F32)
            total = total + part * u_ref[:, at : at + chunk]
        logits.append(jnp.sum(total, axis=1, keepdims=True))
    logit = jnp.concatenate(logits, axis=0) / root
    gate = 1.0 / (1.0 + jnp.exp(-logit))
    slot = lax.rem(lax.broadcasted_iota(jnp.int32, (tokens, 1), 0), seq)
    valid = jnp.where(slot < len_ref[...], 1.0, 0.0) / len_ref[...].astype(F32)
    gated = valid * gate
    gated_ref[...] = gated
    curve_ref[...] = gated * (1.0 - gate) / root
    owner = lax.broadcasted_iota(jnp.int32, (tokens, count), 0) // seq
    mine = owner == lax.broadcasted_iota(jnp.int32, (tokens, count), 1)
    high, low = split_bf16(jnp.where(mine, gated, 0.0))
    both = tn(jnp.concatenate([high, low], axis=1), normed_ref[...])
    rows_ref[pl.ds(pl.multiple_of(step * count, count), count), :] = both[:count] + both[count:]

    @pl.when(step == pl.num_programs(0) - 1)
    def _():
        copy_ref[...] = lists_ref[...]
        depth = width // blocks
        place = lax.rem(z_ref[0], half)
        for k in range(half):
            for j in range(2):
                at = (j * half + lax.rem(place + k, half)) * depth
                outs[k][:, j * depth : (j + 1) * depth] = rows_ref[
                    :, pl.ds(pl.multiple_of(at, LANES), depth)
                ].astype(BF16)


def gate_rows(z, normed, u, token_lengths, lists, event, seq, root, blocks):
    tokens, width = normed.shape
    queries = tokens // seq
    group = 16 if queries % 16 == 0 else queries
    step_tokens = group * seq
    half = blocks // 2
    outs = [shape((queries, width // half), BF16)] * half + [shape((tokens, 1), F32)] * 2
    outs.append(shape(lists.shape, lists.dtype))
    column = pl.BlockSpec((step_tokens, 1), lambda i: (i, 0))
    whole = lambda dims: pl.BlockSpec(dims, lambda i: (0, 0))
    return pl.pallas_call(
        functools.partial(gate_kernel, seq, root, blocks),
        grid=(queries // group,),
        out_shape=outs,
        in_specs=[
            SMEM,
            pl.BlockSpec((step_tokens, width), lambda i: (i, 0)),
            whole((1, width)),
            column,
            whole(lists.shape),
            pl.BlockSpec(memory_space=pl.ANY),
        ],
        out_specs=[whole((queries, width // half))] * half + [column] * 2 + [whole(lists.shape)],
        scratch_shapes=[pltpu.VMEM((queries, width), F32)],
        cost_estimate=pl.CostEstimate(
            flops=4 * tokens * width, bytes_accessed=2 * tokens * width, transcendentals=0
        ),
        compiler_params=pltpu.CompilerParams(vmem_limit_bytes=16 * MIB),
        name="gate_rows",
    )(z, normed, u, token_lengths, lists, event)


def pack_kernel(*refs):
    rows = refs[0].shape[0]
    for k, ref in enumerate(refs[:-1]):
        refs[-1][k * rows : (k + 1) * rows, :] = ref[...]


def pack(pieces, name, event):
    rows, width = pieces[0].shape
    out = shape((len(pieces) * rows, width), pieces[0].dtype)
    return call(pack_kernel, [out], pieces, name, after=[event])[0]


def forward_kernel(n, packs, side_ref, places_ref, *refs):
    pieces, weight_ref, shares = refs[:n], refs[n], refs[n + 1 : n + 1 + packs]
    outs = refs[n + 1 + packs : 2 * n + 1 + packs]
    mirror_ref, held_ref, away_ref = refs[2 * n + 1 + packs :]
    rows = pieces[0].shape[0]
    depth = weight_ref.shape[0]
    side = side_ref[0]
    for k in range(n):
        part = slice(k * rows, (k + 1) * rows)
        held_ref[part, :] = pieces[k][:, pl.ds(pl.multiple_of(side * depth, LANES), depth)]
        away_ref[part, :] = pieces[k][:, pl.ds(pl.multiple_of((1 - side) * depth, LANES), depth)]
    count = places_ref.shape[0] // packs
    share = shares[0].shape[0] // count
    for p in range(packs):
        for j in range(count):
            at = pl.multiple_of(places_ref[p * count + j] * share, share)
            mirror_ref[pl.ds(at, share), :] = shares[p][j * share : (j + 1) * share, :]
    product = jnp.dot(held_ref[...], weight_ref[...], preferred_element_type=F32)
    product = product + jnp.dot(away_ref[...], mirror_ref[...], preferred_element_type=F32)
    for k in range(n):
        outs[k][...] = product[k * rows : (k + 1) * rows].astype(outs[k].dtype)


def back_kernel(n, side_ref, *refs):
    pieces, weight_ref, mirror_ref, outs = refs[:n], refs[n], refs[n + 1], refs[n + 2 :]
    rows = pieces[0].shape[0]
    depth = weight_ref.shape[0]
    side = side_ref[0]
    stack = jnp.concatenate([p[...] for p in pieces], axis=0)
    own = nt(stack, weight_ref[...]).astype(BF16)
    mirror = nt(stack, mirror_ref[...]).astype(BF16)
    for k in range(n):
        part = slice(k * rows, (k + 1) * rows)
        outs[k][:, pl.ds(pl.multiple_of(side * depth, LANES), depth)] = own[part]
        outs[k][:, pl.ds(pl.multiple_of((1 - side) * depth, LANES), depth)] = mirror[part]


def embed_kernel(root, n, *refs):
    parts, packed = refs[:n], refs[n:-4]
    pooled_ref, unit_ref, embedded_ref, pack_ref = refs[-4:]
    pooled = parts[0][...]
    for part in parts[1:]:
        pooled = pooled + part[...].astype(F32)
    unit = lax.rsqrt(jnp.mean(pooled * pooled, axis=1, keepdims=True) + embed_eps) / root
    pooled_ref[...] = pooled
    unit_ref[...] = unit
    embedded_ref[...] = (pooled * unit).astype(BF16)
    pack_kernel(*packed, pack_ref)


def count_kernel(n, root, base_ref, slab_ref, *refs):
    lists, counts_ref, scale_ref = refs[:n], refs[n], refs[n + 1]
    queries = lists[0].shape[0]
    rows, width = slab_ref.shape
    slab = slab_ref[...].astype(F32)
    high, low = split_bf16(slab * slab)
    ones = jnp.ones((8, width), BF16)
    row_sq = (nt(ones, high) + nt(ones, low))[0:1]
    scale_ref[...] = lax.rsqrt(row_sq / width + embed_eps) / root / sharpness_divisor
    ids = lax.broadcasted_iota(jnp.int32, (queries, LANES), 1)
    for k in range(n):
        own = lists[k][...] - base_ref[0]
        columns = [
            jnp.broadcast_to(own[:, entry : entry + 1], (queries, LANES)) for entry in range(own.shape[1])
        ]
        for at in range(0, rows, LANES):
            total = jnp.zeros(ids.shape, F32)
            for column in columns:
                total = total + jnp.where(column == ids + at, 1.0, 0.0)
            counts_ref[k * queries : (k + 1) * queries, at : at + LANES] = total


def contrast_kernel(n, *refs):
    pieces, (slab_ref, scale_ref, counts_ref), outs = refs[:n], refs[n : n + 3], refs[n + 3 :]
    queries, width = pieces[0].shape
    embedded = jnp.concatenate([p[...] for p in pieces], axis=0)
    slab = slab_ref[...]
    scale = scale_ref[...]
    heavy = counts_ref[...] * jnp.exp(nt(embedded, slab) * scale)
    denom = jnp.sum(heavy, axis=1, keepdims=True)
    grad = jnp.dot((heavy * scale).astype(BF16), slab, preferred_element_type=F32)
    high, low = split_bf16(denom)
    lane = lax.broadcasted_iota(jnp.int32, (queries, LANES), 1)
    for k in range(n):
        part = slice(k * queries, (k + 1) * queries)
        outs[k][:, :width] = grad[part].astype(outs[k].dtype)
        if k == 0:
            tail = jnp.where(lane == 0, denom[part], 0.0)
        else:
            tail = jnp.where(lane == 0, high[part].astype(F32), jnp.where(lane == 1, low[part].astype(F32), 0.0))
        outs[k][:, width:] = tail.astype(outs[k].dtype)


def grad_kernel(n, packed_count, root, *refs):
    parts = refs[:n]
    pos_ref, pooled_ref, unit_ref, embedded_ref = refs[n : n + 4]
    packed = refs[n + 4 : n + 4 + packed_count]
    grad_ref, columns_ref, loss_ref, pack_ref = refs[n + 4 + packed_count :]
    queries, width = pos_ref.shape
    total = parts[0][:, :width]
    denom = jnp.sum(parts[0][:, width:], axis=1, keepdims=True)
    for part in parts[1:]:
        total = total + part[:, :width].astype(F32)
        denom = denom + jnp.sum(part[:, width:].astype(F32), axis=1, keepdims=True)
    positive = pos_ref[...].astype(F32)
    scale = (
        lax.rsqrt(jnp.mean(positive * positive, axis=1, keepdims=True) + embed_eps)
        / root
        / sharpness_divisor
    )
    score = jnp.sum(embedded_ref[...].astype(F32) * positive, axis=1, keepdims=True) * scale
    pos_exp = jnp.exp(score)
    denom = denom + pos_exp
    loss_ref[...] = jnp.broadcast_to(jnp.sum(jnp.log(denom) - score), loss_ref.shape)
    grad_embed = total / denom + (pos_exp / denom - 1.0) * scale * positive
    pooled, unit = pooled_ref[...], unit_ref[...]
    mean_sq = jnp.mean(pooled * pooled, axis=1, keepdims=True)
    radial = jnp.sum(pooled * grad_embed, axis=1, keepdims=True)
    grad = unit * grad_embed - pooled * (radial * unit / (width * (mean_sq + embed_eps)))
    grad = grad.astype(BF16)
    grad_ref[...] = grad
    cols = columns_ref.shape[2]
    places = width // cols
    for j in range(columns_ref.shape[0]):
        at = (j % places) * cols
        columns_ref[j] = grad[:, at : at + cols]
    pack_kernel(*packed, pack_ref)


def slope_kernel(seq, blocks, z_ref, normed_ref, curve_ref, loss_ref, *rest):
    half = blocks // 2
    backs, out_ref, all_ref, sum_ref = rest[:half], rest[-3], rest[-2], rest[-1]
    step = pl.program_id(0)
    tokens, width = normed_ref.shape
    count = tokens // seq
    depth = width // blocks
    place = lax.rem(z_ref[0], half)

    def block_at(j, k):
        return pl.ds(pl.multiple_of((j * half + lax.rem(place + k, half)) * depth, LANES), depth)

    @pl.when(step == 0)
    def _():
        sum_ref[...] = jnp.zeros_like(sum_ref)
        for k in range(half):
            for j in range(2):
                all_ref[:, block_at(j, k)] = backs[k][:, j * depth : (j + 1) * depth].astype(F32)

    back = all_ref[pl.ds(pl.multiple_of(step * count, count), count), :]
    normed = normed_ref[...].astype(F32).reshape(count, seq, width)
    dots = jnp.sum(normed * back[:, None, :], axis=2, keepdims=True)
    slope = curve_ref[...].reshape(count, seq, 1) * dots
    heavy = (slope * normed).reshape(tokens // 8, 8, width)
    sum_ref[...] += jnp.sum(heavy, axis=0)

    @pl.when(step == pl.num_programs(0) - 1)
    def _():
        total = jnp.sum(sum_ref[...], axis=0, keepdims=True)
        loss = jnp.broadcast_to(loss_ref[...], (7, LANES))
        share = width // out_ref.shape[0]
        for to in range(out_ref.shape[0]):
            out_ref[to, 1:8, :] = loss
            out_ref[to, 0:1, :share] = total[:, to * share : (to + 1) * share]


def slope_rows(z, normed, curve, loss, backs, seq, blocks, devices, after):
    tokens, width = normed.shape
    half = blocks // 2
    queries = tokens // seq
    group = 8 if queries % 8 == 0 else queries
    step_tokens = group * seq
    whole = lambda dims: pl.BlockSpec(dims, lambda i: (0, 0))
    return pl.pallas_call(
        functools.partial(slope_kernel, seq, blocks),
        grid=(queries // group,),
        out_shape=shape((devices, 8, LANES), F32),
        in_specs=[
            SMEM,
            pl.BlockSpec((step_tokens, width), lambda i: (i, 0)),
            pl.BlockSpec((step_tokens, 1), lambda i: (i, 0)),
            whole((1, LANES)),
        ]
        + [whole((queries, width // half))] * half
        + [pl.BlockSpec(memory_space=pl.ANY)],
        out_specs=pl.BlockSpec((devices, 8, LANES), lambda i: (0, 0, 0)),
        scratch_shapes=[pltpu.VMEM((queries, width), F32), pltpu.VMEM((8, width), F32)],
        cost_estimate=pl.CostEstimate(
            flops=4 * tokens * width, bytes_accessed=2 * tokens * width, transcendentals=0
        ),
        compiler_params=pltpu.CompilerParams(vmem_limit_bytes=20 * MIB),
        name="slope_rows",
    )(z, normed, curve, loss, *backs, after)


def columns_kernel(n, order_ref, grads_ref, *refs):
    pieces, out_ref, sorted_ref = refs[:n], refs[n], refs[n + 1]
    chunk = grads_ref.shape[1]
    for j in range(sorted_ref.shape[0] // chunk):
        sorted_ref[j * chunk : (j + 1) * chunk, :] = grads_ref[order_ref[j]]
    at = pieces[0].shape[0]
    total = tn(sorted_ref[0:at, :], pieces[0][...])
    for piece in pieces[1:]:
        rows = piece.shape[0]
        total = total + tn(sorted_ref[at : at + rows, :], piece[...])
        at += rows
    out_ref[...] = total.T.astype(BF16)


def query_kernel(share, place_ref, parts_ref, weight_ref, out_ref, loss_ref):
    total = jnp.sum(parts_ref[...], axis=0)
    loss_ref[...] = total[1:2]
    line = total[0:1]
    high, low = split_bf16(jnp.broadcast_to(line[:, :share], (8, share)))
    weight = weight_ref[pl.ds(pl.multiple_of(place_ref[0] * share, share), share), :]
    part = (
        jnp.dot(high, weight, preferred_element_type=F32)
        + jnp.dot(low, weight, preferred_element_type=F32)
    )[0:1]
    lines = part.shape[1] // LANES
    rows = [part[:, k * LANES : (k + 1) * LANES] for k in range(lines)] + [line]
    rows.append(jnp.zeros((out_ref.shape[1] - lines - 1, LANES), F32))
    out_ref[...] = jnp.broadcast_to(jnp.concatenate(rows, axis=0)[None], out_ref.shape)


def finish_kernel(n, *refs):
    z_ref, place_ref, sums_ref, pool_ref = refs[:4]
    pieces, out_ref, query_ref = refs[4 : 4 + n], refs[-2], refs[-1]
    rows, cols = pieces[0].shape[0] // (place_ref.shape[0] // n), pieces[0].shape[1]
    places = place_ref.shape[0]
    share = rows // places
    lines = query_ref.shape[0]
    query_ref[...] = jnp.sum(sums_ref[:, :lines, :], axis=0)
    for p in range(places):
        line = sums_ref[z_ref[0] * places + p, lines : lines + 1, :share]
        slope = jnp.broadcast_to(line, (LANES, share)).T
        part = slice(p * share, (p + 1) * share)
        for k in range(places):
            piece = pieces[k // (places // n)]
            base = k % (places // n) * rows
            at = pl.ds(pl.multiple_of(place_ref[k] * cols, LANES), cols)
            mine = piece[base + p * share : base + (p + 1) * share, :].astype(F32)
            out_ref[part, at] = mine + slope * pool_ref[:, at]


def body(hidden_states, positives, negatives, lengths, norm_gain, proj_weight, pool_query, slab):
    queries, seq, width = hidden_states.shape
    depth, proj_width = proj_weight.shape
    n_z, n_g, n_i = lax.axis_size("fsdp"), lax.axis_size("grp"), lax.axis_size("item")
    assert n_z % 2 == 0
    half = n_z // 2
    n_c = 2 if n_i % 2 == 0 else 1
    n_h = n_i // n_c
    n_plane = n_g * n_i
    n_all = n_z * n_plane
    z, g, i = lax.axis_index("fsdp"), lax.axis_index("grp"), lax.axis_index("item")
    h, c = i // n_c, lax.rem(i, n_c)
    side, member = z // half, lax.rem(z, half)
    root = math.sqrt(proj_width)
    steps_z, steps_i = range(1, n_z), range(1, n_i)

    def ints(*values):
        return jnp.stack([jnp.asarray(v, jnp.int32) for v in values])

    z_arr, side_arr = ints(z), ints(side)

    def plane_shift(values, dg, dh, dc):
        pairs = []
        for pg in range(n_g):
            for ph in range(n_h):
                for pc in range(n_c):
                    to = ((pg + dg) % n_g) * n_i + ((ph + dh) % n_h) * n_c + (pc + dc) % n_c
                    pairs.append((pg * n_i + ph * n_c + pc, to))
        return lax.ppermute(values, PLANE, pairs)

    def half_shift(values, k):
        pairs = [(a, a // half * half + (a % half + k) % half) for a in range(n_z)]
        return lax.ppermute(values, "fsdp", pairs)

    def mirror_shift(values):
        return lax.ppermute(values, "fsdp", [(a, (a + half) % n_z) for a in range(n_z)])

    def source(dg, dh, dc):
        return (
            lax.rem(g - dg + n_g, n_g),
            lax.rem(h - dh + n_h, n_h) * n_c + lax.rem(c - dc + n_c, n_c),
        )

    chips = [(dg, dh) for dg in range(n_g) for dh in range(n_h)]

    share = depth // n_plane
    place = g * n_i + i
    weight_share = lax.dynamic_slice_in_dim(proj_weight, place * share, share, 0)
    far_share = mirror_shift(weight_share)

    block_u = jnp.sum(proj_weight.astype(F32) * pool_query[None, :], axis=1).reshape(1, depth)
    u_parts = [block_u] + [shift(block_u, "fsdp", k) for k in steps_z]
    u = jnp.zeros((1, width), F32)
    for k in range(n_z):
        u = lax.dynamic_update_slice(u, u_parts[k], (0, lax.rem(z - k + n_z, n_z) * depth))

    normed = norm_rows(u, hidden_states.reshape(-1, width), norm_gain.astype(F32).reshape(1, width))

    far_share = pack([far_share], "far_share", normed)
    chip_shares = [far_share if dg == dh == 0 else plane_shift(far_share, dg, dh, 0) for dg, dh in chips]
    share_places = []
    for dc in range(n_c):
        for dg, dh in chips:
            from_g, from_i = source(dg, dh, dc)
            share_places.append(from_g * n_i + from_i)

    token_lengths = jnp.broadcast_to(lengths[:, None], (queries, seq)).reshape(-1, 1)
    *sends, gated, curve, own_lists = gate_rows(
        z_arr, normed, u, token_lengths, negatives, far_share, seq, root, n_z
    )

    packs = [pack(chip_shares, "pack_shares", gated)]
    packs += [plane_shift(packs[0], 0, 0, dc) for dc in range(1, n_c)]

    pieces = [sends[0]] + [half_shift(sends[k], k) for k in range(1, half)]
    lists = [own_lists] + [shift(own_lists, "item", k) for k in steps_i]
    counts, slab_scale = call(
        functools.partial(count_kernel, n_i, root),
        [shape((n_i * queries, slab.shape[0]), F32), shape((1, slab.shape[0]), F32)],
        [ints(i * slab.shape[0]), slab] + lists, "list_counts", smem=1,
    )
    block = shape((half * queries, depth), BF16)
    *parts, mirror, held, away = call(
        functools.partial(forward_kernel, half, n_c),
        [shape((queries, proj_width), F32)]
        + [shape((queries, proj_width), BF16)] * (half - 1)
        + [shape((depth, proj_width), BF16), block, block],
        [side_arr, ints(*share_places)] + pieces + [proj_weight] + packs, "forward",
        flops=4 * half * queries * depth * proj_width, smem=2, after=[counts],
    )
    parts = [parts[0]] + [half_shift(parts[k], -k) for k in range(1, half)]
    near = [held] + [plane_shift(held, 0, dh, 0) for dh in range(1, n_h)]
    other = mirror_shift(away)
    row = shape((queries, proj_width), F32)
    row16 = shape((queries, proj_width), BF16)
    pooled, unit, embedded, near = call(
        functools.partial(embed_kernel, root, half),
        [row, shape((queries, 1), F32), row16, shape((n_h * half * queries, depth), BF16)],
        parts + near, "embed",
    )

    pieces = [embedded] + [shift(embedded, "item", k) for k in steps_i]
    near_far = [plane_shift(near, dg, 0, 0) for dg in range(1, n_g)]
    wide = (queries, proj_width + LANES)
    parts = call(
        functools.partial(contrast_kernel, n_i),
        [shape(wide, F32)] + [shape(wide, BF16)] * (n_i - 1),
        pieces + [slab, slab_scale, counts], "contrast",
        flops=4 * n_i * queries * slab.shape[0] * proj_width, after=[other],
    )
    parts = [parts[0]] + [shift(parts[k], "item", -k) for k in steps_i]
    near_cores = [plane_shift(near, 0, 0, dc) for dc in range(1, n_c)]
    others = [other] + [plane_shift(other, dg, 0, 0) for dg in range(1, n_g)]
    cols = proj_width // n_plane
    grad, grad_columns, loss, others = call(
        functools.partial(grad_kernel, n_i, n_g, root),
        [
            row16, shape((n_all, queries, cols), BF16), shape((1, LANES), F32),
            shape((n_g * half * queries, depth), BF16),
        ],
        parts + [positives, pooled, unit, embedded] + others, "grad_pooled", after=near_far + near_cores,
    )

    all_columns = lax.all_to_all(grad_columns, EVERY, 0, 0, tiled=True)
    pieces = [grad] + [half_shift(grad, k) for k in range(1, half)]
    backs = call(
        functools.partial(back_kernel, half), [shape((queries, 2 * depth), BF16)] * half,
        [side_arr] + pieces + [proj_weight, mirror], "backward",
        flops=4 * half * queries * depth * proj_width, smem=1,
    )
    own_back = backs[0]
    backs = [backs[0]] + [half_shift(backs[k], -k) for k in range(1, half)]
    near_sets = [(near, 0)] + [(near_far[dg - 1], dg) for dg in range(1, n_g)]
    other_sets = [(others, 0)] + [(plane_shift(others, 0, dh, 0), dh) for dh in range(1, n_h)]
    spread, order = [], []
    for dc in range(n_c):
        for array, dg in near_sets:
            if dc and dg == 0:
                spread.append(near_cores[dc - 1])
            else:
                spread.append(array if dc == 0 else plane_shift(array, 0, 0, dc))
            order += [(side, k, dg, dh, dc) for dh in range(n_h) for k in range(half)]
        for array, dh in other_sets:
            spread.append(array if dc == 0 else plane_shift(array, 0, 0, dc))
            order += [(1 - side, k, dg, dh, dc) for dg in range(n_g) for k in range(half)]
    ranks = []
    for from_side, k, dg, dh, dc in order:
        from_g, from_i = source(dg, dh, dc)
        from_z = from_side * half + lax.rem(member - k + half, half)
        ranks.append((from_z * n_g + from_g) * n_i + from_i)
    block_columns = call(
        functools.partial(columns_kernel, len(spread)), [shape((depth, cols), BF16)],
        [ints(*ranks), all_columns] + spread, "grad_columns",
        flops=2 * n_all * queries * depth * cols, scratch=[pltpu.VMEM((n_all * queries, cols), BF16)], smem=1,
        after=[own_back],
    )[0]
    on_chips = [block_columns if dg == dh == 0 else plane_shift(block_columns, dg, dh, 0) for dg, dh in chips]
    slopes = slope_rows(z_arr, normed, curve, loss, backs, seq, n_z, n_all, block_columns)
    slopes = lax.all_to_all(slopes, EVERY, 0, 0, tiled=True)
    finished = [pack(on_chips, "pack_columns", slopes)]
    finished += [plane_shift(finished[0], 0, 0, dc) for dc in range(1, n_c)]
    lines = proj_width // LANES
    sums, loss_total = call(
        functools.partial(query_kernel, share),
        [shape((n_all, lines // 8 * 8 + 8, LANES), F32), shape((1, LANES), F32)],
        [ints(place), slopes, proj_weight], "slope_sum", smem=1,
    )
    sums = lax.all_to_all(sums, EVERY, 0, 0, tiled=True)
    grad_proj, grad_query = call(
        functools.partial(finish_kernel, len(finished)),
        [shape((depth, proj_width), F32), shape((lines, LANES), F32)],
        [z_arr, ints(*share_places), sums, pool_query.reshape(1, -1)] + finished, "finish", smem=2,
    )
    mean_loss = loss_total[0, 0] / (queries * n_all)
    return (grad_proj, grad_query.reshape(proj_width), mean_loss)


def solution(mesh):
    return jax.shard_map(
        body,
        mesh=mesh,
        in_specs=(
            P(("grp", "fsdp", "item"), None, None),
            P(("grp", "fsdp", "item"), None),
            P(("grp", "fsdp", "item"), None),
            P(("grp", "fsdp", "item")),
            P(),
            P("fsdp", None),
            P(),
            P("item", None),
        ),
        out_specs=(P("fsdp", None), P(), P()),
        check_vma=False,
    )
```

```python
import functools
import math

import jax
import jax.numpy as jnp
from jax import lax
from jax.experimental import pallas as pl
from jax.experimental.pallas import tpu as pltpu
from jax.sharding import PartitionSpec as P

sharpness_divisor = 0.05
norm_eps = 1e-05
embed_eps = 1e-06

EVERY = ("fsdp", "grp", "item")
PLANE = ("grp", "item")
F32 = jnp.float32
BF16 = jnp.bfloat16
LANES = 128
MIB = 1024 * 1024
VMEM = pl.BlockSpec(memory_space=pltpu.VMEM)
SMEM = pl.BlockSpec(memory_space=pltpu.SMEM)


def shape(dims, dtype):
    return jax.ShapeDtypeStruct(dims, dtype)


def call(kernel, outs, ins, name, flops=0, scratch=(), smem=0, kept=0, after=()):
    count, first = len(ins), smem + kept
    copied = ins[first:]
    moved = sum(math.prod(a.shape) * a.dtype.itemsize for a in list(ins) + list(outs))
    held = sum(math.prod(s.shape) * jnp.dtype(s.dtype).itemsize for s in scratch)

    def run(*refs):
        rest = refs[count + len(after) :]
        results, buffers = rest[: len(outs)], rest[len(outs) : len(outs) + len(copied)]
        own, sems = rest[len(outs) + len(copied) : -1], rest[-1]
        copies = [
            pltpu.make_async_copy(src, dst, sems.at[k])
            for k, (src, dst) in enumerate(zip(refs[first:count], buffers))
        ]
        for copy in copies:
            copy.start()
        for copy in copies:
            copy.wait()
        kernel(*refs[:first], *buffers, *results, *own)

    anywhere = pl.BlockSpec(memory_space=pl.ANY)
    return pl.pallas_call(
        run,
        out_shape=outs,
        in_specs=[SMEM] * smem + [VMEM] * kept + [anywhere] * (len(copied) + len(after)),
        out_specs=[VMEM] * len(outs),
        scratch_shapes=[pltpu.VMEM(a.shape, a.dtype) for a in copied]
        + list(scratch)
        + [pltpu.SemaphoreType.DMA((max(len(copied), 1),))],
        cost_estimate=pl.CostEstimate(flops=flops, bytes_accessed=moved, transcendentals=0),
        compiler_params=pltpu.CompilerParams(vmem_limit_bytes=2 * (moved + held) + 6 * MIB),
        name=name,
    )(*ins, *after)


def shift(values, axis, k):
    n = lax.axis_size(axis)
    return lax.ppermute(values, axis, [(i, (i + k) % n) for i in range(n)])


def split_bf16(values):
    high = values.astype(BF16)
    low = (values - high.astype(F32)).astype(BF16)
    return high, low


def nt(left, right):
    return lax.dot_general(left, right, (((1,), (1,)), ((), ())), preferred_element_type=F32)


def tn(left, right):
    return lax.dot_general(left, right, (((0,), (0,)), ((), ())), preferred_element_type=F32)


def norm_kernel(event_ref, states_ref, gain_ref, normed_ref):
    tokens, width = states_ref.shape
    step = 4 * LANES if width % (4 * LANES) == 0 else width
    for top in range(0, tokens, 32):
        rows = slice(top, top + 32)
        squares = jnp.zeros((32, step), F32)
        for at in range(0, width, step):
            part = states_ref[rows, at : at + step].astype(F32)
            squares = squares + part * part
        inv_rms = lax.rsqrt(jnp.sum(squares, axis=1, keepdims=True) / width + norm_eps)
        for at in range(0, width, step):
            part = states_ref[rows, at : at + step].astype(F32)
            part = part * inv_rms * gain_ref[:, at : at + step]
            normed_ref[rows, at : at + step] = part.astype(BF16)


def norm_rows(event, states, gain):
    tokens, width = states.shape
    block = 128 if tokens % 128 == 0 else tokens
    rows = pl.BlockSpec((block, width), lambda i: (i, 0))
    return pl.pallas_call(
        norm_kernel,
        grid=(tokens // block,),
        out_shape=shape((tokens, width), BF16),
        in_specs=[pl.BlockSpec(memory_space=pl.ANY), rows, pl.BlockSpec((1, width), lambda i: (0, 0))],
        out_specs=rows,
        cost_estimate=pl.CostEstimate(
            flops=6 * tokens * width, bytes_accessed=4 * tokens * width, transcendentals=0
        ),
        compiler_params=pltpu.CompilerParams(vmem_limit_bytes=60 * MIB),
        name="norm_rows",
    )(event, states, gain)


def gate_kernel(seq, root, blocks, z_ref, normed_ref, u_ref, len_ref, lists_ref, event_ref, *rest):
    half = blocks // 2
    outs, gated_ref, curve_ref, copies, rows_ref = (
        rest[:half], rest[half], rest[half + 1], rest[half + 2 : -1], rest[-1]
    )
    step = pl.program_id(0)
    tokens, width = normed_ref.shape
    count = tokens // seq
    chunk = 4 * LANES if width % (4 * LANES) == 0 else width
    logits = []
    for top in range(0, tokens, 32):
        total = jnp.zeros((32, chunk), F32)
        for at in range(0, width, chunk):
            part = normed_ref[top : top + 32, at : at + chunk].astype(F32)
            total = total + part * u_ref[:, at : at + chunk]
        logits.append(jnp.sum(total, axis=1, keepdims=True))
    logit = jnp.concatenate(logits, axis=0) / root
    gate = 1.0 / (1.0 + jnp.exp(-logit))
    slot = lax.rem(lax.broadcasted_iota(jnp.int32, (tokens, 1), 0), seq)
    valid = jnp.where(slot < len_ref[...], 1.0, 0.0) / len_ref[...].astype(F32)
    gated = valid * gate
    gated_ref[...] = gated
    curve_ref[...] = gated * (1.0 - gate) / root
    owner = lax.broadcasted_iota(jnp.int32, (tokens, count), 0) // seq
    mine = owner == lax.broadcasted_iota(jnp.int32, (tokens, count), 1)
    high, low = split_bf16(jnp.where(mine, gated, 0.0))
    both = tn(jnp.concatenate([high, low], axis=1), normed_ref[...])
    rows_ref[pl.ds(pl.multiple_of(step * count, count), count), :] = both[:count] + both[count:]

    @pl.when(step == pl.num_programs(0) - 1)
    def _():
        owners = len(copies)
        own = lists_ref.shape[1] // owners
        for k in range(owners):
            picked = jnp.zeros(copies[k].shape, jnp.int32)
            for j in range(owners):
                picked = jnp.where(
                    lax.rem(z_ref[1] + k, owners) == j, lists_ref[:, j * own : (j + 1) * own], picked
                )
            copies[k][...] = picked
        depth = width // blocks
        place = lax.rem(z_ref[0], half)
        for k in range(half):
            for j in range(2):
                at = (j * half + lax.rem(place + k, half)) * depth
                outs[k][:, j * depth : (j + 1) * depth] = rows_ref[
                    :, pl.ds(pl.multiple_of(at, LANES), depth)
                ].astype(BF16)


def gate_rows(z, normed, u, token_lengths, lists, event, seq, root, blocks, owners):
    tokens, width = normed.shape
    queries = tokens // seq
    group = 16 if queries % 16 == 0 else queries
    step_tokens = group * seq
    half = blocks // 2
    outs = [shape((queries, width // half), BF16)] * half + [shape((tokens, 1), F32)] * 2
    outs += [shape((queries, lists.shape[1] // owners), lists.dtype)] * owners
    column = pl.BlockSpec((step_tokens, 1), lambda i: (i, 0))
    whole = lambda dims: pl.BlockSpec(dims, lambda i: (0, 0))
    return pl.pallas_call(
        functools.partial(gate_kernel, seq, root, blocks),
        grid=(queries // group,),
        out_shape=outs,
        in_specs=[
            SMEM,
            pl.BlockSpec((step_tokens, width), lambda i: (i, 0)),
            whole((1, width)),
            column,
            whole(lists.shape),
            pl.BlockSpec(memory_space=pl.ANY),
        ],
        out_specs=[whole((queries, width // half))] * half + [column] * 2
        + [whole((queries, lists.shape[1] // owners))] * owners,
        scratch_shapes=[pltpu.VMEM((queries, width), F32)],
        cost_estimate=pl.CostEstimate(
            flops=4 * tokens * width, bytes_accessed=2 * tokens * width, transcendentals=0
        ),
        compiler_params=pltpu.CompilerParams(vmem_limit_bytes=60 * MIB),
        name="gate_rows",
    )(z, normed, u, token_lengths, lists, event)


def pack_kernel(*refs):
    rows = refs[0].shape[0]
    for k, ref in enumerate(refs[:-1]):
        refs[-1][k * rows : (k + 1) * rows, :] = ref[...]


def pack(pieces, name, event):
    rows, width = pieces[0].shape
    n = len(pieces)

    def run(*refs):
        out_ref, sems = refs[-2], refs[-1]
        copies = [
            pltpu.make_async_copy(refs[k], out_ref.at[pl.ds(k * rows, rows), :], sems.at[k])
            for k in range(n)
        ]
        for copy in copies:
            copy.start()
        for copy in copies:
            copy.wait()

    anywhere = pl.BlockSpec(memory_space=pl.ANY)
    return pl.pallas_call(
        run,
        out_shape=shape((n * rows, width), pieces[0].dtype),
        in_specs=[anywhere] * (n + 1),
        out_specs=anywhere,
        scratch_shapes=[pltpu.SemaphoreType.DMA((n,))],
        cost_estimate=pl.CostEstimate(flops=0, bytes_accessed=4 * n * rows * width, transcendentals=0),
        compiler_params=pltpu.CompilerParams(vmem_limit_bytes=4 * MIB),
        name=name,
    )(*pieces, event)


def forward_kernel(n, packs, side_ref, places_ref, weight_ref, *refs):
    refs = refs[:n] + (weight_ref,) + refs[n:]
    pieces, shares = refs[:n], refs[n + 1 : n + 1 + packs]
    outs = refs[n + 1 + packs : 2 * n + 1 + packs]
    mirror_ref, held_ref, away_ref = refs[2 * n + 1 + packs :]
    rows = pieces[0].shape[0]
    depth = weight_ref.shape[0]
    side = side_ref[0]
    for k in range(n):
        part = slice(k * rows, (k + 1) * rows)
        held_ref[part, :] = pieces[k][:, pl.ds(pl.multiple_of(side * depth, LANES), depth)]
        away_ref[part, :] = pieces[k][:, pl.ds(pl.multiple_of((1 - side) * depth, LANES), depth)]
    count = places_ref.shape[0] // packs
    share = shares[0].shape[0] // count
    for p in range(packs):
        for j in range(count):
            at = pl.multiple_of(places_ref[p * count + j] * share, share)
            mirror_ref[pl.ds(at, share), :] = shares[p][j * share : (j + 1) * share, :]
    product = jnp.dot(held_ref[...], weight_ref[...], preferred_element_type=F32)
    product = product + jnp.dot(away_ref[...], mirror_ref[...], preferred_element_type=F32)
    for k in range(n):
        outs[k][...] = product[k * rows : (k + 1) * rows].astype(outs[k].dtype)


def back_kernel(n, packed, side_ref, weight_ref, mirror_ref, *refs):
    pieces, outs = refs[:n], refs[n + packed : -1]
    pack_kernel(*refs[n : n + packed], refs[-1])
    rows = pieces[0].shape[0]
    depth = weight_ref.shape[0]
    side = side_ref[0]
    stack = jnp.concatenate([p[...] for p in pieces], axis=0)
    own = nt(stack, weight_ref[...]).astype(BF16)
    mirror = nt(stack, mirror_ref[...]).astype(BF16)
    for k in range(n):
        part = slice(k * rows, (k + 1) * rows)
        outs[k][:, pl.ds(pl.multiple_of(side * depth, LANES), depth)] = own[part]
        outs[k][:, pl.ds(pl.multiple_of((1 - side) * depth, LANES), depth)] = mirror[part]


def embed_kernel(root, n, *refs):
    parts, away_ref, packed = refs[:n], refs[n], refs[n + 1 : -5]
    pooled_ref, unit_ref, embedded_ref, pack_ref, pass_ref = refs[-5:]
    pass_ref[...] = away_ref[...]
    pooled = parts[0][...]
    for part in parts[1:]:
        pooled = pooled + part[...].astype(F32)
    unit = lax.rsqrt(jnp.mean(pooled * pooled, axis=1, keepdims=True) + embed_eps) / root
    pooled_ref[...] = pooled
    unit_ref[...] = unit
    embedded_ref[...] = (pooled * unit).astype(BF16)
    pack_kernel(*packed, pack_ref)


def count_kernel(n, root, base_ref, slab_ref, *refs):
    lists, counts_ref, scale_ref = refs[:n], refs[n], refs[n + 1]
    queries = lists[0].shape[0]
    rows, width = slab_ref.shape
    slab = slab_ref[...].astype(F32)
    high, low = split_bf16(slab * slab)
    ones = jnp.ones((8, width), BF16)
    row_sq = (nt(ones, high) + nt(ones, low))[0:1]
    scale_ref[...] = lax.rsqrt(row_sq / width + embed_eps) / root / sharpness_divisor
    ids = lax.broadcasted_iota(jnp.int32, (queries, LANES), 1)
    for k in range(n):
        own = lists[k][...] - base_ref[0]
        columns = [
            jnp.broadcast_to(own[:, entry : entry + 1], (queries, LANES)) for entry in range(own.shape[1])
        ]
        for at in range(0, rows, LANES):
            total = jnp.zeros(ids.shape, F32)
            for column in columns:
                total = total + jnp.where(column == ids + at, 1.0, 0.0)
            counts_ref[k * queries : (k + 1) * queries, at : at + LANES] = total


def contrast_kernel(n, *refs):
    (slab_ref, scale_ref, counts_ref), pieces, outs = refs[:3], refs[3 : n + 3], refs[n + 3 :]
    queries, width = pieces[0].shape
    embedded = jnp.concatenate([p[...] for p in pieces], axis=0)
    slab = slab_ref[...]
    scale = scale_ref[...]
    heavy = counts_ref[...] * jnp.exp(nt(embedded, slab) * scale)
    denom = jnp.sum(heavy, axis=1, keepdims=True)
    grad = jnp.dot((heavy * scale).astype(BF16), slab, preferred_element_type=F32)
    high, low = split_bf16(denom)
    lane = lax.broadcasted_iota(jnp.int32, (queries, LANES), 1)
    for k in range(n):
        part = slice(k * queries, (k + 1) * queries)
        outs[k][:, :width] = grad[part].astype(outs[k].dtype)
        if k == 0:
            tail = jnp.where(lane == 0, denom[part], 0.0)
        else:
            tail = jnp.where(lane == 0, high[part].astype(F32), jnp.where(lane == 1, low[part].astype(F32), 0.0))
        outs[k][:, width:] = tail.astype(outs[k].dtype)


def grad_kernel(n, root, *refs):
    pos_ref, pooled_ref, unit_ref, embedded_ref = refs[:4]
    parts = refs[4 : n + 4]
    grad_ref, columns_ref, loss_ref = refs[n + 4 :]
    queries, width = pos_ref.shape
    total = parts[0][:, :width]
    denom = jnp.sum(parts[0][:, width:], axis=1, keepdims=True)
    for part in parts[1:]:
        total = total + part[:, :width].astype(F32)
        denom = denom + jnp.sum(part[:, width:].astype(F32), axis=1, keepdims=True)
    positive = pos_ref[...].astype(F32)
    scale = (
        lax.rsqrt(jnp.mean(positive * positive, axis=1, keepdims=True) + embed_eps)
        / root
        / sharpness_divisor
    )
    score = jnp.sum(embedded_ref[...].astype(F32) * positive, axis=1, keepdims=True) * scale
    pos_exp = jnp.exp(score)
    denom = denom + pos_exp
    loss_ref[...] = jnp.broadcast_to(jnp.sum(jnp.log(denom) - score), loss_ref.shape)
    grad_embed = total / denom + (pos_exp / denom - 1.0) * scale * positive
    pooled, unit = pooled_ref[...], unit_ref[...]
    mean_sq = jnp.mean(pooled * pooled, axis=1, keepdims=True)
    radial = jnp.sum(pooled * grad_embed, axis=1, keepdims=True)
    grad = unit * grad_embed - pooled * (radial * unit / (width * (mean_sq + embed_eps)))
    grad = grad.astype(BF16)
    grad_ref[...] = grad
    cols = columns_ref.shape[2]
    places = width // cols
    for j in range(columns_ref.shape[0]):
        at = (j % places) * cols
        columns_ref[j] = grad[:, at : at + cols]


def slope_kernel(seq, blocks, plane, z_ref, normed_ref, curve_ref, loss_ref, *rest):
    half = blocks // 2
    backs, (out_ref, all_ref, sum_ref) = rest[:half], rest[-3:]
    step = pl.program_id(0)
    tokens, width = normed_ref.shape
    count = tokens // seq
    depth = width // blocks
    place = lax.rem(z_ref[0], half)

    def block_at(j, k):
        return pl.ds(pl.multiple_of((j * half + lax.rem(place + k, half)) * depth, LANES), depth)

    @pl.when(step == 0)
    def _():
        sum_ref[...] = jnp.zeros_like(sum_ref)
        for k in range(half):
            for j in range(2):
                all_ref[:, block_at(j, k)] = backs[k][:, j * depth : (j + 1) * depth].astype(F32)

    back = all_ref[pl.ds(pl.multiple_of(step * count, count), count), :]
    normed = normed_ref[...].astype(F32).reshape(count, seq, width)
    dots = jnp.sum(normed * back[:, None, :], axis=2, keepdims=True)
    slope = curve_ref[...].reshape(count, seq, 1) * dots
    heavy = (slope * normed).reshape(tokens // 8, 8, width)
    sum_ref[...] += jnp.sum(heavy, axis=0)

    @pl.when(step == pl.num_programs(0) - 1)
    def _():
        total = jnp.sum(sum_ref[...], axis=0, keepdims=True)
        lines = depth // LANES
        devices, height = out_ref.shape[0], out_ref.shape[1]
        loss = jnp.broadcast_to(loss_ref[...], (height - 2 * lines, LANES))
        for member in range(half):
            rows = []
            for j in range(2):
                for line in range(lines):
                    at = (j * half + member) * depth + line * LANES
                    rows.append(total[:, at : at + LANES])
            message = jnp.concatenate(rows + [loss], axis=0)
            for to in range(devices):
                if to // plane % half == member:
                    out_ref[to] = message


def slope_rows(z, normed, curve, loss, backs, seq, blocks, devices, plane):
    tokens, width = normed.shape
    half = blocks // 2
    height = 2 * (width // blocks // LANES) // 8 * 8 + 8
    queries = tokens // seq
    group = 8 if queries % 8 == 0 else queries
    step_tokens = group * seq
    whole = lambda dims: pl.BlockSpec(dims, lambda i: (0, 0))
    return pl.pallas_call(
        functools.partial(slope_kernel, seq, blocks, plane),
        grid=(queries // group,),
        out_shape=shape((devices, height, LANES), F32),
        in_specs=[
            SMEM,
            pl.BlockSpec((step_tokens, width), lambda i: (i, 0)),
            pl.BlockSpec((step_tokens, 1), lambda i: (i, 0)),
            whole((1, LANES)),
        ]
        + [whole((queries, width // half))] * half,
        out_specs=pl.BlockSpec((devices, height, LANES), lambda i: (0, 0, 0)),
        scratch_shapes=[pltpu.VMEM((queries, width), F32), pltpu.VMEM((8, width), F32)],
        cost_estimate=pl.CostEstimate(
            flops=4 * tokens * width, bytes_accessed=2 * tokens * width, transcendentals=0
        ),
        compiler_params=pltpu.CompilerParams(vmem_limit_bytes=60 * MIB),
        name="slope_rows",
    )(z, normed, curve, loss, *backs)


def columns_kernel(n, order_ref, grads_ref, *refs):
    pieces, out_ref, sorted_ref = refs[:n], refs[n], refs[n + 1]
    chunk = grads_ref.shape[1]
    for j in range(sorted_ref.shape[0] // chunk):
        sorted_ref[j * chunk : (j + 1) * chunk, :] = grads_ref[order_ref[j]]
    at = pieces[0].shape[0]
    total = tn(sorted_ref[0:at, :], pieces[0][...])
    for piece in pieces[1:]:
        rows = piece.shape[0]
        total = total + tn(sorted_ref[at : at + rows, :], piece[...])
        at += rows
    out_ref[...] = total.T.astype(BF16)


def query_kernel(side_ref, weight_ref, mirror_ref, parts_ref, part_ref, slope_ref, loss_ref):
    depth = weight_ref.shape[0]
    lines = depth // LANES
    total = jnp.sum(parts_ref[...], axis=0)
    loss_ref[...] = total[2 * lines : 2 * lines + 1]
    side = side_ref[0]
    part = jnp.zeros(part_ref.shape, F32)
    for j in range(2):
        rows = total[j * lines : (j + 1) * lines]
        row = jnp.concatenate([rows[k : k + 1] for k in range(lines)], axis=1)
        high, low = split_bf16(jnp.broadcast_to(row, (8, depth)))

        @pl.when(side == j)
        def _():
            slope_ref[...] = rows

        weight = jnp.where(side == j, weight_ref[...], mirror_ref[...])
        part = part + jnp.dot(high, weight, preferred_element_type=F32)[0:1]
        part = part + jnp.dot(low, weight, preferred_element_type=F32)[0:1]
    part_ref[...] = part


def finish_kernel(n, place_ref, pool_ref, slope_ref, *refs):
    pieces, out_ref = refs[:n], refs[-1]
    places = place_ref.shape[0]
    rows, cols = out_ref.shape[0], pieces[0].shape[1]
    for line in range(rows // LANES):
        part = slice(line * LANES, (line + 1) * LANES)
        slope = jnp.broadcast_to(slope_ref[line : line + 1, :], (LANES, LANES)).T
        for k in range(places):
            base = k % (places // n) * rows + line * LANES
            mine = pieces[k // (places // n)][base : base + LANES, :].astype(F32)
            at = pl.ds(pl.multiple_of(place_ref[k] * cols, LANES), cols)
            out_ref[part, at] = mine + slope * pool_ref[:, at]


def body(hidden_states, positives, negatives, lengths, norm_gain, proj_weight, pool_query, slab):
    queries, seq, width = hidden_states.shape
    depth, proj_width = proj_weight.shape
    n_z, n_g, n_i = lax.axis_size("fsdp"), lax.axis_size("grp"), lax.axis_size("item")
    assert n_z % 2 == 0
    half = n_z // 2
    n_c = 2 if n_i % 2 == 0 else 1
    n_h = n_i // n_c
    n_plane = n_g * n_i
    n_all = n_z * n_plane
    z, g, i = lax.axis_index("fsdp"), lax.axis_index("grp"), lax.axis_index("item")
    h, c = i // n_c, lax.rem(i, n_c)
    side, member = z // half, lax.rem(z, half)
    root = math.sqrt(proj_width)
    steps_z, steps_i = range(1, n_z), range(1, n_i)

    def ints(*values):
        return jnp.stack([jnp.asarray(v, jnp.int32) for v in values])

    z_arr, side_arr = ints(z), ints(side)

    def plane_shift(values, dg, dh, dc):
        pairs = []
        for pg in range(n_g):
            for ph in range(n_h):
                for pc in range(n_c):
                    to = ((pg + dg) % n_g) * n_i + ((ph + dh) % n_h) * n_c + (pc + dc) % n_c
                    pairs.append((pg * n_i + ph * n_c + pc, to))
        return lax.ppermute(values, PLANE, pairs)

    def half_shift(values, k):
        pairs = [(a, a // half * half + (a % half + k) % half) for a in range(n_z)]
        return lax.ppermute(values, "fsdp", pairs)

    def mirror_shift(values):
        return lax.ppermute(values, "fsdp", [(a, (a + half) % n_z) for a in range(n_z)])

    def source(dg, dh, dc):
        return (
            lax.rem(g - dg + n_g, n_g),
            lax.rem(h - dh + n_h, n_h) * n_c + lax.rem(c - dc + n_c, n_c),
        )

    chips = [(dg, dh) for dg in range(n_g) for dh in range(n_h)]

    share = depth // n_plane
    place = g * n_i + i
    weight_share = lax.dynamic_slice_in_dim(proj_weight, place * share, share, 0)
    far_share = mirror_shift(weight_share)

    block_u = jnp.sum(proj_weight.astype(F32) * pool_query[None, :], axis=1).reshape(1, depth)
    u_parts = [block_u] + [shift(block_u, "fsdp", k) for k in steps_z]
    u = jnp.zeros((1, width), F32)
    for k in range(n_z):
        u = lax.dynamic_update_slice(u, u_parts[k], (0, lax.rem(z - k + n_z, n_z) * depth))

    normed = norm_rows(u, hidden_states.reshape(-1, width), norm_gain.astype(F32).reshape(1, width))

    far_share = pack([far_share], "far_share", normed)
    chip_shares = [far_share if dg == dh == 0 else plane_shift(far_share, dg, dh, 0) for dg, dh in chips]
    share_places = []
    for dc in range(n_c):
        for dg, dh in chips:
            from_g, from_i = source(dg, dh, dc)
            share_places.append(from_g * n_i + from_i)

    token_lengths = jnp.broadcast_to(lengths[:, None], (queries, seq)).reshape(-1, 1)
    gate_outs = gate_rows(
        ints(z, i), normed, u, token_lengths, negatives, far_share, seq, root, n_z, n_i
    )
    sends, (gated, curve), lists = gate_outs[:half], gate_outs[half : half + 2], gate_outs[half + 2 :]

    packs = [pack(chip_shares, "pack_shares", gated)]
    packs += [plane_shift(packs[0], 0, 0, dc) for dc in range(1, n_c)]

    pieces = [sends[0]] + [half_shift(sends[k], k) for k in range(1, half)]
    lists = [lists[0]] + [shift(lists[k], "item", k) for k in steps_i]
    counts, slab_scale = call(
        functools.partial(count_kernel, n_i, root),
        [shape((n_i * queries, slab.shape[0]), F32), shape((1, slab.shape[0]), F32)],
        [ints(i * slab.shape[0]), slab] + lists, "list_counts", smem=1, kept=1,
    )
    block = shape((half * queries, depth), BF16)
    *parts, mirror, held, away = call(
        functools.partial(forward_kernel, half, n_c),
        [shape((queries, proj_width), F32)]
        + [shape((queries, proj_width), BF16)] * (half - 1)
        + [shape((depth, proj_width), BF16), block, block],
        [side_arr, ints(*share_places), proj_weight] + pieces + packs, "forward",
        flops=4 * half * queries * depth * proj_width, smem=2, kept=1, after=[counts],
    )
    parts = [parts[0]] + [half_shift(parts[k], -k) for k in range(1, half)]
    near = [held] + [plane_shift(held, 0, dh, 0) for dh in range(1, n_h)]
    row = shape((queries, proj_width), F32)
    row16 = shape((queries, proj_width), BF16)
    pooled, unit, embedded, near, away = call(
        functools.partial(embed_kernel, root, half),
        [row, shape((queries, 1), F32), row16, shape((n_h * half * queries, depth), BF16), block],
        parts + [away] + near, "embed",
    )
    other = mirror_shift(away)

    pieces = [embedded] + [shift(embedded, "item", k) for k in steps_i]
    near_far = [plane_shift(near, dg, 0, 0) for dg in range(1, n_g)]
    wide = (queries, proj_width + LANES)
    parts = call(
        functools.partial(contrast_kernel, n_i),
        [shape(wide, F32)] + [shape(wide, BF16)] * (n_i - 1),
        [slab, slab_scale, counts] + pieces, "contrast",
        flops=4 * n_i * queries * slab.shape[0] * proj_width, kept=3,
    )
    parts = [parts[0]] + [shift(parts[k], "item", -k) for k in steps_i]
    near_cores = [plane_shift(near, 0, 0, dc) for dc in range(1, n_c)]
    near_far_cores = [[plane_shift(array, 0, 0, dc) for array in near_far] for dc in range(1, n_c)]
    others = [other] + [plane_shift(other, dg, 0, 0) for dg in range(1, n_g)]
    cols = proj_width // n_plane
    grad, grad_columns, loss = call(
        functools.partial(grad_kernel, n_i, root),
        [row16, shape((n_all, queries, cols), BF16), shape((1, LANES), F32)],
        [positives, pooled, unit, embedded] + parts, "grad_pooled", kept=4,
        after=near_far + near_cores + sum(near_far_cores, []) + others,
    )

    all_columns = lax.all_to_all(grad_columns, EVERY, 0, 0, tiled=True)
    pieces = [grad] + [half_shift(grad, k) for k in range(1, half)]
    *backs, others = call(
        functools.partial(back_kernel, half, n_g),
        [shape((queries, 2 * depth), BF16)] * half + [shape((n_g * half * queries, depth), BF16)],
        [side_arr, proj_weight, mirror] + pieces + others, "backward",
        flops=4 * half * queries * depth * proj_width, smem=1, kept=2,
    )
    backs = [backs[0]] + [half_shift(backs[k], -k) for k in range(1, half)]
    slopes = slope_rows(ints(z, 0), normed, curve, loss, backs, seq, n_z, n_all, n_plane)
    near_sets = [(near, 0)] + [(near_far[dg - 1], dg) for dg in range(1, n_g)]
    other_sets = [(others, 0)] + [(plane_shift(others, 0, dh, 0), dh) for dh in range(1, n_h)]
    spread, order = [], []
    for dc in range(n_c):
        for array, dg in near_sets:
            spread.append(array if dc == 0 else ([near_cores[dc - 1]] + near_far_cores[dc - 1])[dg])
            order += [(side, k, dg, dh, dc) for dh in range(n_h) for k in range(half)]
        for array, dh in other_sets:
            spread.append(array if dc == 0 else plane_shift(array, 0, 0, dc))
            order += [(1 - side, k, dg, dh, dc) for dg in range(n_g) for k in range(half)]
    ranks = []
    for from_side, k, dg, dh, dc in order:
        from_g, from_i = source(dg, dh, dc)
        from_z = from_side * half + lax.rem(member - k + half, half)
        ranks.append((from_z * n_g + from_g) * n_i + from_i)
    block_columns = call(
        functools.partial(columns_kernel, len(spread)), [shape((depth, cols), BF16)],
        [ints(*ranks), all_columns] + spread, "grad_columns",
        flops=2 * n_all * queries * depth * cols, scratch=[pltpu.VMEM((n_all * queries, cols), BF16)], smem=1,
        after=[slopes],
    )[0]
    on_chips = [block_columns if dg == dh == 0 else plane_shift(block_columns, dg, dh, 0) for dg, dh in chips]
    all_slopes = lax.all_to_all(slopes, EVERY, 0, 0, tiled=True)
    query_part, my_slope, loss_total = call(
        query_kernel,
        [shape((1, proj_width), F32), shape((depth // LANES, LANES), F32), shape((1, LANES), F32)],
        [side_arr, proj_weight, mirror, all_slopes], "slope_sum", smem=1, kept=2,
    )
    finished = [pack(on_chips, "pack_columns", slopes)]
    finished += [plane_shift(finished[0], 0, 0, dc) for dc in range(1, n_c)]
    grad_query = query_part + sum(half_shift(query_part, k) for k in range(1, half))
    grad_proj = call(
        functools.partial(finish_kernel, len(finished)), [shape((depth, proj_width), F32)],
        [ints(*share_places), pool_query.reshape(1, -1), my_slope] + finished, "finish", smem=1, kept=2,
    )[0]
    mean_loss = loss_total[0, 0] / (queries * n_all)
    return (grad_proj, grad_query.reshape(proj_width), mean_loss)


def solution(mesh):
    return jax.shard_map(
        body,
        mesh=mesh,
        in_specs=(
            P(("grp", "fsdp", "item"), None, None),
            P(("grp", "fsdp", "item"), None),
            P(("grp", "fsdp", "item"), None),
            P(("grp", "fsdp", "item")),
            P(),
            P("fsdp", None),
            P(),
            P("item", None),
        ),
        out_specs=(P("fsdp", None), P(), P()),
        check_vma=False,
    )
```

```python
import functools
import math

import jax
import jax.numpy as jnp
from jax import lax
from jax.experimental import pallas as pl
from jax.experimental.pallas import tpu as pltpu
from jax.sharding import PartitionSpec as P

sharpness_divisor = 0.05
norm_eps = 1e-05
embed_eps = 1e-06

EVERY = ("fsdp", "grp", "item")
PLANE = ("grp", "item")
F32 = jnp.float32
BF16 = jnp.bfloat16
LANES = 128
MIB = 1024 * 1024
VMEM = pl.BlockSpec(memory_space=pltpu.VMEM)
SMEM = pl.BlockSpec(memory_space=pltpu.SMEM)


def shape(dims, dtype):
    return jax.ShapeDtypeStruct(dims, dtype)


def call(kernel, outs, ins, name, flops=0, scratch=(), smem=0, after=()):
    count = len(ins)
    moved = sum(math.prod(a.shape) * a.dtype.itemsize for a in list(ins) + list(outs))
    held = sum(math.prod(s.shape) * jnp.dtype(s.dtype).itemsize for s in scratch)

    def run(*refs):
        kernel(*refs[:count], *refs[count + len(after) :])

    return pl.pallas_call(
        run,
        out_shape=outs,
        in_specs=[SMEM] * smem
        + [VMEM] * (count - smem)
        + [pl.BlockSpec(memory_space=pl.ANY)] * len(after),
        out_specs=[VMEM] * len(outs),
        scratch_shapes=list(scratch),
        cost_estimate=pl.CostEstimate(flops=flops, bytes_accessed=moved, transcendentals=0),
        compiler_params=pltpu.CompilerParams(vmem_limit_bytes=2 * (moved + held) + 6 * MIB),
        name=name,
    )(*ins, *after)


def shift(values, axis, k):
    n = lax.axis_size(axis)
    return lax.ppermute(values, axis, [(i, (i + k) % n) for i in range(n)])


def split_bf16(values):
    high = values.astype(BF16)
    low = (values - high.astype(F32)).astype(BF16)
    return high, low


def nt(left, right):
    return lax.dot_general(left, right, (((1,), (1,)), ((), ())), preferred_element_type=F32)


def tn(left, right):
    return lax.dot_general(left, right, (((0,), (0,)), ((), ())), preferred_element_type=F32)


def norm_kernel(states_ref, gain_ref, normed_ref):
    tokens, width = states_ref.shape
    step = 4 * LANES if width % (4 * LANES) == 0 else width
    for top in range(0, tokens, 32):
        rows = slice(top, top + 32)
        squares = jnp.zeros((32, step), F32)
        for at in range(0, width, step):
            part = states_ref[rows, at : at + step].astype(F32)
            squares = squares + part * part
        inv_rms = lax.rsqrt(jnp.sum(squares, axis=1, keepdims=True) / width + norm_eps)
        for at in range(0, width, step):
            part = states_ref[rows, at : at + step].astype(F32)
            part = part * inv_rms * gain_ref[:, at : at + step]
            normed_ref[rows, at : at + step] = part.astype(BF16)


def norm_rows(events, states, gain):
    tokens, width = states.shape
    block = 128 if tokens % 128 == 0 else tokens
    rows = pl.BlockSpec((block, width), lambda i: (i, 0))
    return pl.pallas_call(
        lambda *refs: norm_kernel(*refs[len(events) :]),
        grid=(tokens // block,),
        out_shape=shape((tokens, width), BF16),
        in_specs=[pl.BlockSpec(memory_space=pl.ANY)] * len(events)
        + [rows, pl.BlockSpec((1, width), lambda i: (0, 0))],
        out_specs=rows,
        cost_estimate=pl.CostEstimate(
            flops=6 * tokens * width, bytes_accessed=4 * tokens * width, transcendentals=0
        ),
        compiler_params=pltpu.CompilerParams(vmem_limit_bytes=10 * MIB),
        name="norm_rows",
    )(*events, states, gain)


def gate_kernel(seq, root, blocks, z_ref, normed_ref, u_ref, len_ref, lists_ref, event_ref, *rest):
    half = blocks // 2
    outs, gated_ref, curve_ref, copies, rows_ref = (
        rest[:half], rest[half], rest[half + 1], rest[half + 2 : -1], rest[-1]
    )
    step = pl.program_id(0)
    tokens, width = normed_ref.shape
    count = tokens // seq
    chunk = 4 * LANES if width % (4 * LANES) == 0 else width
    logits = []
    for top in range(0, tokens, 32):
        total = jnp.zeros((32, chunk), F32)
        for at in range(0, width, chunk):
            part = normed_ref[top : top + 32, at : at + chunk].astype(F32)
            total = total + part * u_ref[:, at : at + chunk]
        logits.append(jnp.sum(total, axis=1, keepdims=True))
    logit = jnp.concatenate(logits, axis=0) / root
    gate = 1.0 / (1.0 + jnp.exp(-logit))
    slot = lax.rem(lax.broadcasted_iota(jnp.int32, (tokens, 1), 0), seq)
    valid = jnp.where(slot < len_ref[...], 1.0, 0.0) / len_ref[...].astype(F32)
    gated = valid * gate
    gated_ref[...] = gated
    curve_ref[...] = gated * (1.0 - gate) / root
    owner = lax.broadcasted_iota(jnp.int32, (tokens, count), 0) // seq
    mine = owner == lax.broadcasted_iota(jnp.int32, (tokens, count), 1)
    high, low = split_bf16(jnp.where(mine, gated, 0.0))
    both = tn(jnp.concatenate([high, low], axis=1), normed_ref[...])
    rows_ref[pl.ds(pl.multiple_of(step * count, count), count), :] = both[:count] + both[count:]

    @pl.when(step == pl.num_programs(0) - 1)
    def _():
        owners = len(copies)
        own = lists_ref.shape[1] // owners
        for k in range(owners):
            picked = jnp.zeros(copies[k].shape, jnp.int32)
            for j in range(owners):
                picked = jnp.where(
                    lax.rem(z_ref[1] + k, owners) == j, lists_ref[:, j * own : (j + 1) * own], picked
                )
            copies[k][...] = picked
        depth = width // blocks
        place = lax.rem(z_ref[0], half)
        for k in range(half):
            for j in range(2):
                at = (j * half + lax.rem(place + k, half)) * depth
                outs[k][:, j * depth : (j + 1) * depth] = rows_ref[
                    :, pl.ds(pl.multiple_of(at, LANES), depth)
                ].astype(BF16)


def gate_rows(z, normed, u, token_lengths, lists, event, seq, root, blocks, owners):
    tokens, width = normed.shape
    queries = tokens // seq
    group = 16 if queries % 16 == 0 else queries
    step_tokens = group * seq
    half = blocks // 2
    outs = [shape((queries, width // half), BF16)] * half + [shape((tokens, 1), F32)] * 2
    outs += [shape((queries, lists.shape[1] // owners), lists.dtype)] * owners
    column = pl.BlockSpec((step_tokens, 1), lambda i: (i, 0))
    whole = lambda dims: pl.BlockSpec(dims, lambda i: (0, 0))
    return pl.pallas_call(
        functools.partial(gate_kernel, seq, root, blocks),
        grid=(queries // group,),
        out_shape=outs,
        in_specs=[
            SMEM,
            pl.BlockSpec((step_tokens, width), lambda i: (i, 0)),
            whole((1, width)),
            column,
            whole(lists.shape),
            pl.BlockSpec(memory_space=pl.ANY),
        ],
        out_specs=[whole((queries, width // half))] * half + [column] * 2
        + [whole((queries, lists.shape[1] // owners))] * owners,
        scratch_shapes=[pltpu.VMEM((queries, width), F32)],
        cost_estimate=pl.CostEstimate(
            flops=4 * tokens * width, bytes_accessed=2 * tokens * width, transcendentals=0
        ),
        compiler_params=pltpu.CompilerParams(vmem_limit_bytes=16 * MIB),
        name="gate_rows",
    )(z, normed, u, token_lengths, lists, event)


def pack_kernel(*refs):
    rows = refs[0].shape[0]
    for k, ref in enumerate(refs[:-1]):
        refs[-1][k * rows : (k + 1) * rows, :] = ref[...]


def pack(pieces, name, event):
    rows, width = pieces[0].shape
    out = shape((len(pieces) * rows, width), pieces[0].dtype)
    return call(pack_kernel, [out], pieces, name, after=[event])[0]


def forward_kernel(n, packs, side_ref, places_ref, weight_ref, *refs):
    refs = refs[:n] + (weight_ref,) + refs[n:]
    pieces, shares = refs[:n], refs[n + 1 : n + 1 + packs]
    outs = refs[n + 1 + packs : 2 * n + 1 + packs]
    mirror_ref, held_ref, away_ref = refs[2 * n + 1 + packs :]
    rows = pieces[0].shape[0]
    depth = weight_ref.shape[0]
    side = side_ref[0]
    for k in range(n):
        part = slice(k * rows, (k + 1) * rows)
        held_ref[part, :] = pieces[k][:, pl.ds(pl.multiple_of(side * depth, LANES), depth)]
        away_ref[part, :] = pieces[k][:, pl.ds(pl.multiple_of((1 - side) * depth, LANES), depth)]
    count = places_ref.shape[0] // packs
    share = shares[0].shape[0] // count
    for p in range(packs):
        for j in range(count):
            at = pl.multiple_of(places_ref[p * count + j] * share, share)
            mirror_ref[pl.ds(at, share), :] = shares[p][j * share : (j + 1) * share, :]
    product = jnp.dot(held_ref[...], weight_ref[...], preferred_element_type=F32)
    product = product + jnp.dot(away_ref[...], mirror_ref[...], preferred_element_type=F32)
    for k in range(n):
        outs[k][...] = product[k * rows : (k + 1) * rows].astype(outs[k].dtype)


def back_kernel(n, packed, side_ref, weight_ref, mirror_ref, *refs):
    pieces, outs = refs[:n], refs[n + packed : -1]
    pack_kernel(*refs[n : n + packed], refs[-1])
    rows = pieces[0].shape[0]
    depth = weight_ref.shape[0]
    side = side_ref[0]
    stack = jnp.concatenate([p[...] for p in pieces], axis=0)
    own = nt(stack, weight_ref[...]).astype(BF16)
    mirror = nt(stack, mirror_ref[...]).astype(BF16)
    for k in range(n):
        part = slice(k * rows, (k + 1) * rows)
        outs[k][:, pl.ds(pl.multiple_of(side * depth, LANES), depth)] = own[part]
        outs[k][:, pl.ds(pl.multiple_of((1 - side) * depth, LANES), depth)] = mirror[part]


def embed_kernel(root, n, *refs):
    parts, away_ref, packed = refs[:n], refs[n], refs[n + 1 : -5]
    pooled_ref, unit_ref, embedded_ref, pack_ref, pass_ref = refs[-5:]
    pass_ref[...] = away_ref[...]
    pooled = parts[0][...]
    for part in parts[1:]:
        pooled = pooled + part[...].astype(F32)
    unit = lax.rsqrt(jnp.mean(pooled * pooled, axis=1, keepdims=True) + embed_eps) / root
    pooled_ref[...] = pooled
    unit_ref[...] = unit
    embedded_ref[...] = (pooled * unit).astype(BF16)
    pack_kernel(*packed, pack_ref)


def count_kernel(n, root, base_ref, slab_ref, *refs):
    lists, counts_ref, scale_ref = refs[:n], refs[n], refs[n + 1]
    queries = lists[0].shape[0]
    rows, width = slab_ref.shape
    slab = slab_ref[...].astype(F32)
    high, low = split_bf16(slab * slab)
    ones = jnp.ones((8, width), BF16)
    row_sq = (nt(ones, high) + nt(ones, low))[0:1]
    scale_ref[...] = lax.rsqrt(row_sq / width + embed_eps) / root / sharpness_divisor
    ids = lax.broadcasted_iota(jnp.int32, (queries, LANES), 1)
    for k in range(n):
        own = lists[k][...] - base_ref[0]
        columns = [
            jnp.broadcast_to(own[:, entry : entry + 1], (queries, LANES)) for entry in range(own.shape[1])
        ]
        for at in range(0, rows, LANES):
            total = jnp.zeros(ids.shape, F32)
            for column in columns:
                total = total + jnp.where(column == ids + at, 1.0, 0.0)
            counts_ref[k * queries : (k + 1) * queries, at : at + LANES] = total


def contrast_kernel(n, *refs):
    (slab_ref, scale_ref, counts_ref), pieces, outs = refs[:3], refs[3 : n + 3], refs[n + 3 :]
    queries, width = pieces[0].shape
    embedded = jnp.concatenate([p[...] for p in pieces], axis=0)
    slab = slab_ref[...]
    scale = scale_ref[...]
    heavy = counts_ref[...] * jnp.exp(nt(embedded, slab) * scale)
    denom = jnp.sum(heavy, axis=1, keepdims=True)
    grad = jnp.dot((heavy * scale).astype(BF16), slab, preferred_element_type=F32)
    high, low = split_bf16(denom)
    lane = lax.broadcasted_iota(jnp.int32, (queries, LANES), 1)
    for k in range(n):
        part = slice(k * queries, (k + 1) * queries)
        outs[k][:, :width] = grad[part].astype(outs[k].dtype)
        if k == 0:
            tail = jnp.where(lane == 0, denom[part], 0.0)
        else:
            tail = jnp.where(lane == 0, high[part].astype(F32), jnp.where(lane == 1, low[part].astype(F32), 0.0))
        outs[k][:, width:] = tail.astype(outs[k].dtype)


def grad_kernel(n, root, *refs):
    pos_ref, pooled_ref, unit_ref, embedded_ref = refs[:4]
    parts = refs[4 : n + 4]
    grad_ref, columns_ref, loss_ref = refs[n + 4 :]
    queries, width = pos_ref.shape
    total = parts[0][:, :width]
    denom = jnp.sum(parts[0][:, width:], axis=1, keepdims=True)
    for part in parts[1:]:
        total = total + part[:, :width].astype(F32)
        denom = denom + jnp.sum(part[:, width:].astype(F32), axis=1, keepdims=True)
    positive = pos_ref[...].astype(F32)
    scale = (
        lax.rsqrt(jnp.mean(positive * positive, axis=1, keepdims=True) + embed_eps)
        / root
        / sharpness_divisor
    )
    score = jnp.sum(embedded_ref[...].astype(F32) * positive, axis=1, keepdims=True) * scale
    pos_exp = jnp.exp(score)
    denom = denom + pos_exp
    loss_ref[...] = jnp.broadcast_to(jnp.sum(jnp.log(denom) - score), loss_ref.shape)
    grad_embed = total / denom + (pos_exp / denom - 1.0) * scale * positive
    pooled, unit = pooled_ref[...], unit_ref[...]
    mean_sq = jnp.mean(pooled * pooled, axis=1, keepdims=True)
    radial = jnp.sum(pooled * grad_embed, axis=1, keepdims=True)
    grad = unit * grad_embed - pooled * (radial * unit / (width * (mean_sq + embed_eps)))
    grad = grad.astype(BF16)
    grad_ref[...] = grad
    cols = columns_ref.shape[2]
    places = width // cols
    for j in range(columns_ref.shape[0]):
        at = (j % places) * cols
        columns_ref[j] = grad[:, at : at + cols]


def slope_kernel(seq, blocks, plane, z_ref, normed_ref, curve_ref, loss_ref, *rest):
    half = blocks // 2
    backs, (out_ref, all_ref, sum_ref) = rest[:half], rest[-3:]
    step = pl.program_id(0)
    tokens, width = normed_ref.shape
    count = tokens // seq
    depth = width // blocks
    place = lax.rem(z_ref[0], half)

    def block_at(j, k):
        return pl.ds(pl.multiple_of((j * half + lax.rem(place + k, half)) * depth, LANES), depth)

    @pl.when(step == 0)
    def _():
        sum_ref[...] = jnp.zeros_like(sum_ref)
        for k in range(half):
            for j in range(2):
                all_ref[:, block_at(j, k)] = backs[k][:, j * depth : (j + 1) * depth].astype(F32)

    back = all_ref[pl.ds(pl.multiple_of(step * count, count), count), :]
    normed = normed_ref[...].astype(F32).reshape(count, seq, width)
    dots = jnp.sum(normed * back[:, None, :], axis=2, keepdims=True)
    slope = curve_ref[...].reshape(count, seq, 1) * dots
    heavy = (slope * normed).reshape(tokens // 8, 8, width)
    sum_ref[...] += jnp.sum(heavy, axis=0)

    @pl.when(step == pl.num_programs(0) - 1)
    def _():
        total = jnp.sum(sum_ref[...], axis=0, keepdims=True)
        lines = depth // LANES
        devices, height = out_ref.shape[0], out_ref.shape[1]
        loss = jnp.broadcast_to(loss_ref[...], (height - 2 * lines, LANES))
        for member in range(half):
            rows = []
            for j in range(2):
                for line in range(lines):
                    at = (j * half + member) * depth + line * LANES
                    rows.append(total[:, at : at + LANES])
            message = jnp.concatenate(rows + [loss], axis=0)
            for to in range(devices):
                if to // plane % half == member:
                    out_ref[to] = message


def slope_rows(z, normed, curve, loss, backs, seq, blocks, devices, plane):
    tokens, width = normed.shape
    half = blocks // 2
    height = 2 * (width // blocks // LANES) // 8 * 8 + 8
    queries = tokens // seq
    group = 8 if queries % 8 == 0 else queries
    step_tokens = group * seq
    whole = lambda dims: pl.BlockSpec(dims, lambda i: (0, 0))
    return pl.pallas_call(
        functools.partial(slope_kernel, seq, blocks, plane),
        grid=(queries // group,),
        out_shape=shape((devices, height, LANES), F32),
        in_specs=[
            SMEM,
            pl.BlockSpec((step_tokens, width), lambda i: (i, 0)),
            pl.BlockSpec((step_tokens, 1), lambda i: (i, 0)),
            whole((1, LANES)),
        ]
        + [whole((queries, width // half))] * half,
        out_specs=pl.BlockSpec((devices, height, LANES), lambda i: (0, 0, 0)),
        scratch_shapes=[pltpu.VMEM((queries, width), F32), pltpu.VMEM((8, width), F32)],
        cost_estimate=pl.CostEstimate(
            flops=4 * tokens * width, bytes_accessed=2 * tokens * width, transcendentals=0
        ),
        compiler_params=pltpu.CompilerParams(vmem_limit_bytes=20 * MIB),
        name="slope_rows",
    )(z, normed, curve, loss, *backs)


def columns_kernel(n, order_ref, slopes_ref, grads_ref, *refs):
    pieces, (out_ref, pass_ref, sorted_ref) = refs[:n], refs[n:]
    pass_ref[...] = slopes_ref[...]
    chunk = grads_ref.shape[1]
    for j in range(sorted_ref.shape[0] // chunk):
        sorted_ref[j * chunk : (j + 1) * chunk, :] = grads_ref[order_ref[j]]
    at = pieces[0].shape[0]
    total = tn(sorted_ref[0:at, :], pieces[0][...])
    for piece in pieces[1:]:
        rows = piece.shape[0]
        total = total + tn(sorted_ref[at : at + rows, :], piece[...])
        at += rows
    out_ref[...] = total.T.astype(BF16)


def query_kernel(side_ref, weight_ref, mirror_ref, parts_ref, part_ref, slope_ref, loss_ref):
    depth = weight_ref.shape[0]
    lines = depth // LANES
    total = jnp.sum(parts_ref[...], axis=0)
    loss_ref[...] = total[2 * lines : 2 * lines + 1]
    side = side_ref[0]
    part = jnp.zeros(part_ref.shape, F32)
    for j in range(2):
        rows = total[j * lines : (j + 1) * lines]
        row = jnp.concatenate([rows[k : k + 1] for k in range(lines)], axis=1)
        high, low = split_bf16(jnp.broadcast_to(row, (8, depth)))

        @pl.when(side == j)
        def _():
            slope_ref[...] = rows

        weight = jnp.where(side == j, weight_ref[...], mirror_ref[...])
        part = part + jnp.dot(high, weight, preferred_element_type=F32)[0:1]
        part = part + jnp.dot(low, weight, preferred_element_type=F32)[0:1]
    part_ref[...] = part


def finish_kernel(n, place_ref, pool_ref, slope_ref, *refs):
    pieces, out_ref = refs[:n], refs[-1]
    places = place_ref.shape[0]
    rows, cols = out_ref.shape[0], pieces[0].shape[1]
    for line in range(rows // LANES):
        part = slice(line * LANES, (line + 1) * LANES)
        slope = jnp.broadcast_to(slope_ref[line : line + 1, :], (LANES, LANES)).T
        for k in range(places):
            base = k % (places // n) * rows + line * LANES
            mine = pieces[k // (places // n)][base : base + LANES, :].astype(F32)
            at = pl.ds(pl.multiple_of(place_ref[k] * cols, LANES), cols)
            out_ref[part, at] = mine + slope * pool_ref[:, at]


def body(hidden_states, positives, negatives, lengths, norm_gain, proj_weight, pool_query, slab):
    queries, seq, width = hidden_states.shape
    depth, proj_width = proj_weight.shape
    n_z, n_g, n_i = lax.axis_size("fsdp"), lax.axis_size("grp"), lax.axis_size("item")
    assert n_z % 2 == 0
    half = n_z // 2
    n_c = 2 if n_i % 2 == 0 else 1
    n_h = n_i // n_c
    n_plane = n_g * n_i
    n_all = n_z * n_plane
    z, g, i = lax.axis_index("fsdp"), lax.axis_index("grp"), lax.axis_index("item")
    h, c = i // n_c, lax.rem(i, n_c)
    side, member = z // half, lax.rem(z, half)
    root = math.sqrt(proj_width)
    steps_z, steps_i = range(1, n_z), range(1, n_i)

    def ints(*values):
        return jnp.stack([jnp.asarray(v, jnp.int32) for v in values])

    z_arr, side_arr = ints(z), ints(side)

    def plane_shift(values, dg, dh, dc):
        pairs = []
        for pg in range(n_g):
            for ph in range(n_h):
                for pc in range(n_c):
                    to = ((pg + dg) % n_g) * n_i + ((ph + dh) % n_h) * n_c + (pc + dc) % n_c
                    pairs.append((pg * n_i + ph * n_c + pc, to))
        return lax.ppermute(values, PLANE, pairs)

    def half_shift(values, k):
        pairs = [(a, a // half * half + (a % half + k) % half) for a in range(n_z)]
        return lax.ppermute(values, "fsdp", pairs)

    def mirror_shift(values):
        return lax.ppermute(values, "fsdp", [(a, (a + half) % n_z) for a in range(n_z)])

    def source(dg, dh, dc):
        return (
            lax.rem(g - dg + n_g, n_g),
            lax.rem(h - dh + n_h, n_h) * n_c + lax.rem(c - dc + n_c, n_c),
        )

    chips = [(dg, dh) for dg in range(n_g) for dh in range(n_h)]

    share = depth // n_plane
    place = g * n_i + i
    weight_share = lax.dynamic_slice_in_dim(proj_weight, place * share, share, 0)
    far_share = mirror_shift(weight_share)

    block_u = jnp.sum(proj_weight.astype(F32) * pool_query[None, :], axis=1).reshape(1, depth)
    u_parts = [block_u] + [shift(block_u, "fsdp", k) for k in steps_z]
    u = jnp.zeros((1, width), F32)
    for k in range(n_z):
        u = lax.dynamic_update_slice(u, u_parts[k], (0, lax.rem(z - k + n_z, n_z) * depth))

    share_places = []
    for dc in range(n_c):
        for dg, dh in chips:
            from_g, from_i = source(dg, dh, dc)
            share_places.append(from_g * n_i + from_i)
    share_places = ints(*share_places)
    order = []
    for dc in range(n_c):
        for dg in range(n_g):
            order += [(side, k, dg, dh, dc) for dh in range(n_h) for k in range(half)]
        for dh in range(n_h):
            order += [(1 - side, k, dg, dh, dc) for dg in range(n_g) for k in range(half)]
    ranks = []
    for from_side, k, dg, dh, dc in order:
        from_g, from_i = source(dg, dh, dc)
        from_z = from_side * half + lax.rem(member - k + half, half)
        ranks.append((from_z * n_g + from_g) * n_i + from_i)
    ranks = ints(*ranks)
    both_arr, base_arr = ints(z, i), ints(i * slab.shape[0])
    token_lengths = jnp.broadcast_to(lengths[:, None], (queries, seq)).reshape(-1, 1)
    events = [u, token_lengths, share_places, ranks, both_arr, base_arr, side_arr]
    normed = norm_rows(
        events, hidden_states.reshape(-1, width),
        norm_gain.astype(F32).reshape(1, width)
    )

    far_share = pack([far_share], "far_share", normed)
    chip_shares = [far_share if dg == dh == 0 else plane_shift(far_share, dg, dh, 0) for dg, dh in chips]
    gate_outs = gate_rows(
        both_arr, normed, u, token_lengths, negatives, far_share, seq, root, n_z, n_i
    )
    sends, (gated, curve), lists = gate_outs[:half], gate_outs[half : half + 2], gate_outs[half + 2 :]

    packs = [pack(chip_shares, "pack_shares", gated)]
    packs += [plane_shift(packs[0], 0, 0, dc) for dc in range(1, n_c)]

    pieces = [sends[0]] + [half_shift(sends[k], k) for k in range(1, half)]
    lists = [lists[0]] + [shift(lists[k], "item", k) for k in steps_i]
    counts, slab_scale = call(
        functools.partial(count_kernel, n_i, root),
        [shape((n_i * queries, slab.shape[0]), F32), shape((1, slab.shape[0]), F32)],
        [base_arr, slab] + lists, "list_counts", smem=1,
    )
    block = shape((half * queries, depth), BF16)
    *parts, mirror, held, away = call(
        functools.partial(forward_kernel, half, n_c),
        [shape((queries, proj_width), F32)]
        + [shape((queries, proj_width), BF16)] * (half - 1)
        + [shape((depth, proj_width), BF16), block, block],
        [side_arr, share_places, proj_weight] + pieces + packs, "forward",
        flops=4 * half * queries * depth * proj_width, smem=2, after=[counts],
    )
    parts = [parts[0]] + [half_shift(parts[k], -k) for k in range(1, half)]
    near = [held] + [plane_shift(held, 0, dh, 0) for dh in range(1, n_h)]
    row = shape((queries, proj_width), F32)
    row16 = shape((queries, proj_width), BF16)
    pooled, unit, embedded, near, away = call(
        functools.partial(embed_kernel, root, half),
        [row, shape((queries, 1), F32), row16, shape((n_h * half * queries, depth), BF16), block],
        parts + [away] + near, "embed",
    )
    other = mirror_shift(away)

    pieces = [embedded] + [shift(embedded, "item", k) for k in steps_i]
    near_far = [plane_shift(near, dg, 0, 0) for dg in range(1, n_g)]
    wide = (queries, proj_width + LANES)
    parts = call(
        functools.partial(contrast_kernel, n_i),
        [shape(wide, F32)] + [shape(wide, BF16)] * (n_i - 1),
        [slab, slab_scale, counts] + pieces, "contrast",
        flops=4 * n_i * queries * slab.shape[0] * proj_width,
    )
    parts = [parts[0]] + [shift(parts[k], "item", -k) for k in steps_i]
    near_cores = [plane_shift(near, 0, 0, dc) for dc in range(1, n_c)]
    near_far_cores = [[plane_shift(array, 0, 0, dc) for array in near_far] for dc in range(1, n_c)]
    others = [other] + [plane_shift(other, dg, 0, 0) for dg in range(1, n_g)]
    cols = proj_width // n_plane
    grad, grad_columns, loss = call(
        functools.partial(grad_kernel, n_i, root),
        [row16, shape((n_all, queries, cols), BF16), shape((1, LANES), F32)],
        [positives, pooled, unit, embedded] + parts, "grad_pooled",
        after=near_far + near_cores + sum(near_far_cores, []) + others,
    )

    all_columns = lax.all_to_all(grad_columns, EVERY, 0, 0, tiled=True)
    pieces = [grad] + [half_shift(grad, k) for k in range(1, half)]
    *backs, others = call(
        functools.partial(back_kernel, half, n_g),
        [shape((queries, 2 * depth), BF16)] * half + [shape((n_g * half * queries, depth), BF16)],
        [side_arr, proj_weight, mirror] + pieces + others, "backward",
        flops=4 * half * queries * depth * proj_width, smem=1,
    )
    backs = [backs[0]] + [half_shift(backs[k], -k) for k in range(1, half)]
    slopes = slope_rows(both_arr, normed, curve, loss, backs, seq, n_z, n_all, n_plane)
    across = [plane_shift(others, 0, dh, 0) for dh in range(1, n_h)]
    late = [pack([array], "late", slopes) for array in across]
    spread = []
    for dc in range(n_c):
        if dc == 0:
            spread += [near, *near_far, others, *across]
        else:
            spread += [near_cores[dc - 1], *near_far_cores[dc - 1]]
            spread += [plane_shift(array, 0, 0, dc) for array in [others, *late]]
    block_columns, slopes = call(
        functools.partial(columns_kernel, len(spread)), [shape((depth, cols), BF16), shape(slopes.shape, F32)],
        [ranks, slopes, all_columns] + spread, "grad_columns",
        flops=2 * n_all * queries * depth * cols, scratch=[pltpu.VMEM((n_all * queries, cols), BF16)], smem=1,
    )
    on_chips = [block_columns if dg == dh == 0 else plane_shift(block_columns, dg, dh, 0) for dg, dh in chips]
    all_slopes = lax.all_to_all(slopes, EVERY, 0, 0, tiled=True)
    query_part, my_slope, loss_total = call(
        query_kernel,
        [shape((1, proj_width), F32), shape((depth // LANES, LANES), F32), shape((1, LANES), F32)],
        [side_arr, proj_weight, mirror, all_slopes], "slope_sum", smem=1,
    )
    finished = [pack(on_chips, "pack_columns", all_slopes)]
    finished += [plane_shift(finished[0], 0, 0, dc) for dc in range(1, n_c)]
    grad_query = query_part + sum(half_shift(query_part, k) for k in range(1, half))
    grad_proj = call(
        functools.partial(finish_kernel, len(finished)), [shape((depth, proj_width), F32)],
        [share_places, pool_query.reshape(1, -1), my_slope] + finished, "finish", smem=1,
    )[0]
    mean_loss = loss_total[0, 0] / (queries * n_all)
    return (grad_proj, grad_query.reshape(proj_width), mean_loss)


def solution(mesh):
    return jax.shard_map(
        body,
        mesh=mesh,
        in_specs=(
            P(("grp", "fsdp", "item"), None, None),
            P(("grp", "fsdp", "item"), None),
            P(("grp", "fsdp", "item"), None),
            P(("grp", "fsdp", "item")),
            P(),
            P("fsdp", None),
            P(),
            P("item", None),
        ),
        out_specs=(P("fsdp", None), P(), P()),
        check_vma=False,
    )
```

```python
import functools
import math

import jax
import jax.numpy as jnp
from jax import lax
from jax.experimental import pallas as pl
from jax.experimental.pallas import tpu as pltpu
from jax.sharding import PartitionSpec as P

sharpness_divisor = 0.05
norm_eps = 1e-05
embed_eps = 1e-06

EVERY = ("fsdp", "grp", "item")
PLANE = ("grp", "item")
F32 = jnp.float32
BF16 = jnp.bfloat16
LANES = 128
MIB = 1024 * 1024
VMEM = pl.BlockSpec(memory_space=pltpu.VMEM)
SMEM = pl.BlockSpec(memory_space=pltpu.SMEM)


def shape(dims, dtype):
    return jax.ShapeDtypeStruct(dims, dtype)


def call(kernel, outs, ins, name, flops=0, scratch=(), smem=0, after=()):
    count = len(ins)
    moved = sum(math.prod(a.shape) * a.dtype.itemsize for a in list(ins) + list(outs))
    held = sum(math.prod(s.shape) * jnp.dtype(s.dtype).itemsize for s in scratch)

    def run(*refs):
        kernel(*refs[:count], *refs[count + len(after) :])

    return pl.pallas_call(
        run,
        out_shape=outs,
        in_specs=[SMEM] * smem
        + [VMEM] * (count - smem)
        + [pl.BlockSpec(memory_space=pl.ANY)] * len(after),
        out_specs=[VMEM] * len(outs),
        scratch_shapes=list(scratch),
        cost_estimate=pl.CostEstimate(flops=flops, bytes_accessed=moved, transcendentals=0),
        compiler_params=pltpu.CompilerParams(vmem_limit_bytes=2 * (moved + held) + 6 * MIB),
        name=name,
    )(*ins, *after)


def shift(values, axis, k):
    n = lax.axis_size(axis)
    return lax.ppermute(values, axis, [(i, (i + k) % n) for i in range(n)])


def split_bf16(values):
    high = values.astype(BF16)
    low = (values - high.astype(F32)).astype(BF16)
    return high, low


def nt(left, right):
    return lax.dot_general(left, right, (((1,), (1,)), ((), ())), preferred_element_type=F32)


def tn(left, right):
    return lax.dot_general(left, right, (((0,), (0,)), ((), ())), preferred_element_type=F32)


def norm_kernel(states_ref, gain_ref, normed_ref, token_ref):
    token_ref[...] = jnp.zeros_like(token_ref)
    tokens, width = states_ref.shape
    step = 4 * LANES if width % (4 * LANES) == 0 else width
    for top in range(0, tokens, 32):
        rows = slice(top, top + 32)
        squares = jnp.zeros((32, step), F32)
        for at in range(0, width, step):
            part = states_ref[rows, at : at + step].astype(F32)
            squares = squares + part * part
        inv_rms = lax.rsqrt(jnp.sum(squares, axis=1, keepdims=True) / width + norm_eps)
        for at in range(0, width, step):
            part = states_ref[rows, at : at + step].astype(F32)
            part = part * inv_rms * gain_ref[:, at : at + step]
            normed_ref[rows, at : at + step] = part.astype(BF16)


def norm_rows(events, states, gain):
    tokens, width = states.shape
    block = 128 if tokens % 128 == 0 else tokens
    rows = pl.BlockSpec((block, width), lambda i: (i, 0))
    return pl.pallas_call(
        lambda *refs: norm_kernel(*refs[len(events) :]),
        grid=(tokens // block,),
        out_shape=[shape((tokens, width), BF16), shape((8, LANES), F32)],
        in_specs=[pl.BlockSpec(memory_space=pl.ANY)] * len(events)
        + [rows, pl.BlockSpec((1, width), lambda i: (0, 0))],
        out_specs=[rows, pl.BlockSpec((8, LANES), lambda i: (0, 0))],
        cost_estimate=pl.CostEstimate(
            flops=6 * tokens * width, bytes_accessed=4 * tokens * width, transcendentals=0
        ),
        compiler_params=pltpu.CompilerParams(vmem_limit_bytes=10 * MIB),
        name="norm_rows",
    )(*events, states, gain)


def gate_kernel(seq, root, blocks, z_ref, normed_ref, u_ref, len_ref, lists_ref, event_ref, *rest):
    half = blocks // 2
    outs, gated_ref, curve_ref, copies, rows_ref = (
        rest[:half], rest[half], rest[half + 1], rest[half + 2 : -1], rest[-1]
    )
    step = pl.program_id(0)
    tokens, width = normed_ref.shape
    count = tokens // seq
    chunk = 4 * LANES if width % (4 * LANES) == 0 else width
    logits = []
    for top in range(0, tokens, 32):
        total = jnp.zeros((32, chunk), F32)
        for at in range(0, width, chunk):
            part = normed_ref[top : top + 32, at : at + chunk].astype(F32)
            total = total + part * u_ref[:, at : at + chunk]
        logits.append(jnp.sum(total, axis=1, keepdims=True))
    logit = jnp.concatenate(logits, axis=0) / root
    gate = 1.0 / (1.0 + jnp.exp(-logit))
    slot = lax.rem(lax.broadcasted_iota(jnp.int32, (tokens, 1), 0), seq)
    valid = jnp.where(slot < len_ref[...], 1.0, 0.0) / len_ref[...].astype(F32)
    gated = valid * gate
    gated_ref[...] = gated
    curve_ref[...] = gated * (1.0 - gate) / root
    owner = lax.broadcasted_iota(jnp.int32, (tokens, count), 0) // seq
    mine = owner == lax.broadcasted_iota(jnp.int32, (tokens, count), 1)
    high, low = split_bf16(jnp.where(mine, gated, 0.0))
    both = tn(jnp.concatenate([high, low], axis=1), normed_ref[...])
    rows_ref[pl.ds(pl.multiple_of(step * count, count), count), :] = both[:count] + both[count:]

    @pl.when(step == pl.num_programs(0) - 1)
    def _():
        owners = len(copies)
        own = lists_ref.shape[1] // owners
        for k in range(owners):
            picked = jnp.zeros(copies[k].shape, jnp.int32)
            for j in range(owners):
                picked = jnp.where(
                    lax.rem(z_ref[1] + k, owners) == j, lists_ref[:, j * own : (j + 1) * own], picked
                )
            copies[k][...] = picked
        depth = width // blocks
        place = lax.rem(z_ref[0], half)
        for k in range(half):
            for j in range(2):
                at = (j * half + lax.rem(place + k, half)) * depth
                outs[k][:, j * depth : (j + 1) * depth] = rows_ref[
                    :, pl.ds(pl.multiple_of(at, LANES), depth)
                ].astype(BF16)


def gate_rows(z, normed, u, token_lengths, lists, event, seq, root, blocks, owners):
    tokens, width = normed.shape
    queries = tokens // seq
    group = 16 if queries % 16 == 0 else queries
    step_tokens = group * seq
    half = blocks // 2
    outs = [shape((queries, width // half), BF16)] * half + [shape((tokens, 1), F32)] * 2
    outs += [shape((queries, lists.shape[1] // owners), lists.dtype)] * owners
    column = pl.BlockSpec((step_tokens, 1), lambda i: (i, 0))
    whole = lambda dims: pl.BlockSpec(dims, lambda i: (0, 0))
    return pl.pallas_call(
        functools.partial(gate_kernel, seq, root, blocks),
        grid=(queries // group,),
        out_shape=outs,
        in_specs=[
            SMEM,
            pl.BlockSpec((step_tokens, width), lambda i: (i, 0)),
            whole((1, width)),
            column,
            whole(lists.shape),
            pl.BlockSpec(memory_space=pl.ANY),
        ],
        out_specs=[whole((queries, width // half))] * half + [column] * 2
        + [whole((queries, lists.shape[1] // owners))] * owners,
        scratch_shapes=[pltpu.VMEM((queries, width), F32)],
        cost_estimate=pl.CostEstimate(
            flops=4 * tokens * width, bytes_accessed=2 * tokens * width, transcendentals=0
        ),
        compiler_params=pltpu.CompilerParams(vmem_limit_bytes=16 * MIB),
        name="gate_rows",
    )(z, normed, u, token_lengths, lists, event)


def pack_kernel(*refs):
    rows = refs[0].shape[0]
    for k, ref in enumerate(refs[:-1]):
        refs[-1][k * rows : (k + 1) * rows, :] = ref[...]


def pack(pieces, name, event):
    rows, width = pieces[0].shape
    out = shape((len(pieces) * rows, width), pieces[0].dtype)
    return call(pack_kernel, [out], pieces, name, after=[event])[0]


def pass_kernel(from_ref, to_ref):
    to_ref[...] = from_ref[...]


def passed(values, name, event):
    return call(pass_kernel, [shape(values.shape, values.dtype)], [values], name, after=[event])[0]


def add_kernel(*refs):
    total = refs[0][...]
    for ref in refs[1:-1]:
        total = total + ref[...]
    refs[-1][...] = total


def forward_kernel(n, packs, side_ref, places_ref, weight_ref, *refs):
    refs = refs[:n] + (weight_ref,) + refs[n:]
    pieces, shares = refs[:n], refs[n + 1 : n + 1 + packs]
    outs = refs[n + 1 + packs : 2 * n + 1 + packs]
    mirror_ref, held_ref, away_ref = refs[2 * n + 1 + packs :]
    rows = pieces[0].shape[0]
    depth = weight_ref.shape[0]
    side = side_ref[0]
    for k in range(n):
        part = slice(k * rows, (k + 1) * rows)
        held_ref[part, :] = pieces[k][:, pl.ds(pl.multiple_of(side * depth, LANES), depth)]
        away_ref[part, :] = pieces[k][:, pl.ds(pl.multiple_of((1 - side) * depth, LANES), depth)]
    count = places_ref.shape[0] // packs
    share = shares[0].shape[0] // count
    for p in range(packs):
        for j in range(count):
            at = pl.multiple_of(places_ref[p * count + j] * share, share)
            mirror_ref[pl.ds(at, share), :] = shares[p][j * share : (j + 1) * share, :]
    product = jnp.dot(held_ref[...], weight_ref[...], preferred_element_type=F32)
    product = product + jnp.dot(away_ref[...], mirror_ref[...], preferred_element_type=F32)
    for k in range(n):
        outs[k][...] = product[k * rows : (k + 1) * rows].astype(outs[k].dtype)


def back_kernel(n, packed, side_ref, weight_ref, mirror_ref, *refs):
    pieces, outs = refs[:n], refs[n + packed : -1]
    pack_kernel(*refs[n : n + packed], refs[-1])
    rows = pieces[0].shape[0]
    depth = weight_ref.shape[0]
    side = side_ref[0]
    stack = jnp.concatenate([p[...] for p in pieces], axis=0)
    own = nt(stack, weight_ref[...]).astype(BF16)
    mirror = nt(stack, mirror_ref[...]).astype(BF16)
    for k in range(n):
        part = slice(k * rows, (k + 1) * rows)
        outs[k][:, pl.ds(pl.multiple_of(side * depth, LANES), depth)] = own[part]
        outs[k][:, pl.ds(pl.multiple_of((1 - side) * depth, LANES), depth)] = mirror[part]


def embed_kernel(root, n, *refs):
    parts, away_ref, packed = refs[:n], refs[n], refs[n + 1 : -5]
    pooled_ref, unit_ref, embedded_ref, pack_ref, pass_ref = refs[-5:]
    pass_ref[...] = away_ref[...]
    pooled = parts[0][...]
    for part in parts[1:]:
        pooled = pooled + part[...].astype(F32)
    unit = lax.rsqrt(jnp.mean(pooled * pooled, axis=1, keepdims=True) + embed_eps) / root
    pooled_ref[...] = pooled
    unit_ref[...] = unit
    embedded_ref[...] = (pooled * unit).astype(BF16)
    pack_kernel(*packed, pack_ref)


def count_kernel(n, root, base_ref, slab_ref, *refs):
    lists, counts_ref, scale_ref = refs[:n], refs[n], refs[n + 1]
    queries = lists[0].shape[0]
    rows, width = slab_ref.shape
    slab = slab_ref[...].astype(F32)
    high, low = split_bf16(slab * slab)
    ones = jnp.ones((8, width), BF16)
    row_sq = (nt(ones, high) + nt(ones, low))[0:1]
    scale_ref[...] = lax.rsqrt(row_sq / width + embed_eps) / root / sharpness_divisor
    ids = lax.broadcasted_iota(jnp.int32, (queries, LANES), 1)
    for k in range(n):
        own = lists[k][...] - base_ref[0]
        columns = [
            jnp.broadcast_to(own[:, entry : entry + 1], (queries, LANES)) for entry in range(own.shape[1])
        ]
        for at in range(0, rows, LANES):
            total = jnp.zeros(ids.shape, F32)
            for column in columns:
                total = total + jnp.where(column == ids + at, 1.0, 0.0)
            counts_ref[k * queries : (k + 1) * queries, at : at + LANES] = total


def contrast_kernel(n, *refs):
    (slab_ref, scale_ref, counts_ref), pieces, outs = refs[:3], refs[3 : n + 3], refs[n + 3 :]
    queries, width = pieces[0].shape
    embedded = jnp.concatenate([p[...] for p in pieces], axis=0)
    slab = slab_ref[...]
    scale = scale_ref[...]
    heavy = counts_ref[...] * jnp.exp(nt(embedded, slab) * scale)
    denom = jnp.sum(heavy, axis=1, keepdims=True)
    grad = jnp.dot((heavy * scale).astype(BF16), slab, preferred_element_type=F32)
    high, low = split_bf16(denom)
    lane = lax.broadcasted_iota(jnp.int32, (queries, LANES), 1)
    for k in range(n):
        part = slice(k * queries, (k + 1) * queries)
        outs[k][:, :width] = grad[part].astype(outs[k].dtype)
        if k == 0:
            tail = jnp.where(lane == 0, denom[part], 0.0)
        else:
            tail = jnp.where(lane == 0, high[part].astype(F32), jnp.where(lane == 1, low[part].astype(F32), 0.0))
        outs[k][:, width:] = tail.astype(outs[k].dtype)


def grad_kernel(n, root, *refs):
    pos_ref, pooled_ref, unit_ref, embedded_ref = refs[:4]
    parts = refs[4 : n + 4]
    grad_ref, columns_ref, loss_ref = refs[n + 4 :]
    queries, width = pos_ref.shape
    total = parts[0][:, :width]
    denom = jnp.sum(parts[0][:, width:], axis=1, keepdims=True)
    for part in parts[1:]:
        total = total + part[:, :width].astype(F32)
        denom = denom + jnp.sum(part[:, width:].astype(F32), axis=1, keepdims=True)
    positive = pos_ref[...].astype(F32)
    scale = (
        lax.rsqrt(jnp.mean(positive * positive, axis=1, keepdims=True) + embed_eps)
        / root
        / sharpness_divisor
    )
    score = jnp.sum(embedded_ref[...].astype(F32) * positive, axis=1, keepdims=True) * scale
    pos_exp = jnp.exp(score)
    denom = denom + pos_exp
    loss_ref[...] = jnp.broadcast_to(jnp.sum(jnp.log(denom) - score), loss_ref.shape)
    grad_embed = total / denom + (pos_exp / denom - 1.0) * scale * positive
    pooled, unit = pooled_ref[...], unit_ref[...]
    mean_sq = jnp.mean(pooled * pooled, axis=1, keepdims=True)
    radial = jnp.sum(pooled * grad_embed, axis=1, keepdims=True)
    grad = unit * grad_embed - pooled * (radial * unit / (width * (mean_sq + embed_eps)))
    grad = grad.astype(BF16)
    grad_ref[...] = grad
    cols = columns_ref.shape[2]
    places = width // cols
    for j in range(columns_ref.shape[0]):
        at = (j % places) * cols
        columns_ref[j] = grad[:, at : at + cols]


def slope_kernel(seq, blocks, plane, z_ref, normed_ref, curve_ref, loss_ref, *rest):
    half = blocks // 2
    backs, (out_ref, all_ref, sum_ref) = rest[:half], rest[-3:]
    step = pl.program_id(0)
    tokens, width = normed_ref.shape
    count = tokens // seq
    depth = width // blocks
    place = lax.rem(z_ref[0], half)

    def block_at(j, k):
        return pl.ds(pl.multiple_of((j * half + lax.rem(place + k, half)) * depth, LANES), depth)

    @pl.when(step == 0)
    def _():
        sum_ref[...] = jnp.zeros_like(sum_ref)
        for k in range(half):
            for j in range(2):
                all_ref[:, block_at(j, k)] = backs[k][:, j * depth : (j + 1) * depth].astype(F32)

    back = all_ref[pl.ds(pl.multiple_of(step * count, count), count), :]
    normed = normed_ref[...].astype(F32).reshape(count, seq, width)
    dots = jnp.sum(normed * back[:, None, :], axis=2, keepdims=True)
    slope = curve_ref[...].reshape(count, seq, 1) * dots
    heavy = (slope * normed).reshape(tokens // 8, 8, width)
    sum_ref[...] += jnp.sum(heavy, axis=0)

    @pl.when(step == pl.num_programs(0) - 1)
    def _():
        total = jnp.sum(sum_ref[...], axis=0, keepdims=True)
        lines = depth // LANES
        devices, height = out_ref.shape[0], out_ref.shape[1]
        loss = jnp.broadcast_to(loss_ref[...], (height - 2 * lines, LANES))
        for member in range(half):
            rows = []
            for j in range(2):
                for line in range(lines):
                    at = (j * half + member) * depth + line * LANES
                    rows.append(total[:, at : at + LANES])
            message = jnp.concatenate(rows + [loss], axis=0)
            for to in range(devices):
                if to // plane % half == member:
                    out_ref[to] = message


def slope_rows(z, normed, curve, loss, backs, seq, blocks, devices, plane):
    tokens, width = normed.shape
    half = blocks // 2
    height = 2 * (width // blocks // LANES) // 8 * 8 + 8
    queries = tokens // seq
    group = 8 if queries % 8 == 0 else queries
    step_tokens = group * seq
    whole = lambda dims: pl.BlockSpec(dims, lambda i: (0, 0))
    return pl.pallas_call(
        functools.partial(slope_kernel, seq, blocks, plane),
        grid=(queries // group,),
        out_shape=shape((devices, height, LANES), F32),
        in_specs=[
            SMEM,
            pl.BlockSpec((step_tokens, width), lambda i: (i, 0)),
            pl.BlockSpec((step_tokens, 1), lambda i: (i, 0)),
            whole((1, LANES)),
        ]
        + [whole((queries, width // half))] * half,
        out_specs=pl.BlockSpec((devices, height, LANES), lambda i: (0, 0, 0)),
        scratch_shapes=[pltpu.VMEM((queries, width), F32), pltpu.VMEM((8, width), F32)],
        cost_estimate=pl.CostEstimate(
            flops=4 * tokens * width, bytes_accessed=2 * tokens * width, transcendentals=0
        ),
        compiler_params=pltpu.CompilerParams(vmem_limit_bytes=20 * MIB),
        name="slope_rows",
    )(z, normed, curve, loss, *backs)


def columns_kernel(n, order_ref, grads_ref, *refs):
    pieces, (out_ref, sorted_ref) = refs[:n], refs[n:]
    chunk = grads_ref.shape[1]
    for j in range(sorted_ref.shape[0] // chunk):
        sorted_ref[j * chunk : (j + 1) * chunk, :] = grads_ref[order_ref[j]]
    at = pieces[0].shape[0]
    total = tn(sorted_ref[0:at, :], pieces[0][...])
    for piece in pieces[1:]:
        rows = piece.shape[0]
        total = total + tn(sorted_ref[at : at + rows, :], piece[...])
        at += rows
    out_ref[...] = total.T.astype(BF16)


def query_kernel(side_ref, weight_ref, mirror_ref, parts_ref, part_ref, slope_ref, loss_ref):
    depth = weight_ref.shape[0]
    lines = depth // LANES
    total = jnp.sum(parts_ref[...], axis=0)
    loss_ref[...] = total[2 * lines : 2 * lines + 1]
    side = side_ref[0]
    part = jnp.zeros(part_ref.shape, F32)
    for j in range(2):
        rows = total[j * lines : (j + 1) * lines]
        row = jnp.concatenate([rows[k : k + 1] for k in range(lines)], axis=1)
        high, low = split_bf16(jnp.broadcast_to(row, (8, depth)))

        @pl.when(side == j)
        def _():
            slope_ref[...] = rows

        weight = jnp.where(side == j, weight_ref[...], mirror_ref[...])
        part = part + jnp.dot(high, weight, preferred_element_type=F32)[0:1]
        part = part + jnp.dot(low, weight, preferred_element_type=F32)[0:1]
    part_ref[...] = part


def finish_kernel(n, place_ref, pool_ref, slope_ref, *refs):
    pieces, out_ref, token_ref = refs[:n], refs[-2], refs[-1]
    token_ref[...] = jnp.zeros_like(token_ref)
    places = place_ref.shape[0]
    rows, cols = out_ref.shape[0], pieces[0].shape[1]
    for line in range(rows // LANES):
        part = slice(line * LANES, (line + 1) * LANES)
        slope = jnp.broadcast_to(slope_ref[line : line + 1, :], (LANES, LANES)).T
        for k in range(places):
            base = k % (places // n) * rows + line * LANES
            mine = pieces[k // (places // n)][base : base + LANES, :].astype(F32)
            at = pl.ds(pl.multiple_of(place_ref[k] * cols, LANES), cols)
            out_ref[part, at] = mine + slope * pool_ref[:, at]


def body(hidden_states, positives, negatives, lengths, norm_gain, proj_weight, pool_query, slab):
    queries, seq, width = hidden_states.shape
    depth, proj_width = proj_weight.shape
    n_z, n_g, n_i = lax.axis_size("fsdp"), lax.axis_size("grp"), lax.axis_size("item")
    assert n_z % 2 == 0
    half = n_z // 2
    n_c = 2 if n_i % 2 == 0 else 1
    n_h = n_i // n_c
    n_plane = n_g * n_i
    n_all = n_z * n_plane
    z, g, i = lax.axis_index("fsdp"), lax.axis_index("grp"), lax.axis_index("item")
    h, c = i // n_c, lax.rem(i, n_c)
    side, member = z // half, lax.rem(z, half)
    root = math.sqrt(proj_width)
    steps_z, steps_i = range(1, n_z), range(1, n_i)

    def ints(*values):
        return jnp.stack([jnp.asarray(v, jnp.int32) for v in values])

    z_arr, side_arr = ints(z), ints(side)

    def plane_shift(values, dg, dh, dc):
        pairs = []
        for pg in range(n_g):
            for ph in range(n_h):
                for pc in range(n_c):
                    to = ((pg + dg) % n_g) * n_i + ((ph + dh) % n_h) * n_c + (pc + dc) % n_c
                    pairs.append((pg * n_i + ph * n_c + pc, to))
        return lax.ppermute(values, PLANE, pairs)

    def half_shift(values, k):
        pairs = [(a, a // half * half + (a % half + k) % half) for a in range(n_z)]
        return lax.ppermute(values, "fsdp", pairs)

    def mirror_shift(values):
        return lax.ppermute(values, "fsdp", [(a, (a + half) % n_z) for a in range(n_z)])

    def source(dg, dh, dc):
        return (
            lax.rem(g - dg + n_g, n_g),
            lax.rem(h - dh + n_h, n_h) * n_c + lax.rem(c - dc + n_c, n_c),
        )

    chips = [(dg, dh) for dg in range(n_g) for dh in range(n_h)]

    share = depth // n_plane
    place = g * n_i + i
    weight_share = lax.dynamic_slice_in_dim(proj_weight, place * share, share, 0)
    far_share = mirror_shift(weight_share)

    block_u = jnp.sum(proj_weight.astype(F32) * pool_query[None, :], axis=1).reshape(1, depth)
    u_parts = [block_u] + [shift(block_u, "fsdp", k) for k in steps_z]
    u = jnp.zeros((1, width), F32)
    for k in range(n_z):
        u = lax.dynamic_update_slice(u, u_parts[k], (0, lax.rem(z - k + n_z, n_z) * depth))

    share_places = []
    for dc in range(n_c):
        for dg, dh in chips:
            from_g, from_i = source(dg, dh, dc)
            share_places.append(from_g * n_i + from_i)
    share_places = ints(*share_places)
    order = []
    for dc in range(n_c):
        for dg in range(n_g):
            order += [(side, k, dg, dh, dc) for dh in range(n_h) for k in range(half)]
        for dh in range(n_h):
            order += [(1 - side, k, dg, dh, dc) for dg in range(n_g) for k in range(half)]
    ranks = []
    for from_side, k, dg, dh, dc in order:
        from_g, from_i = source(dg, dh, dc)
        from_z = from_side * half + lax.rem(member - k + half, half)
        ranks.append((from_z * n_g + from_g) * n_i + from_i)
    ranks = ints(*ranks)
    both_arr, base_arr = ints(z, i), ints(i * slab.shape[0])
    token_lengths = jnp.broadcast_to(lengths[:, None], (queries, seq)).reshape(-1, 1)
    events = [u, token_lengths, share_places, ranks, both_arr, base_arr, side_arr]
    normed, normed_token = norm_rows(
        events, hidden_states.reshape(-1, width),
        norm_gain.astype(F32).reshape(1, width)
    )

    far_share = pack([far_share], "far_share", normed_token)
    chip_shares = [far_share if dg == dh == 0 else plane_shift(far_share, dg, dh, 0) for dg, dh in chips]
    gate_outs = gate_rows(
        both_arr, normed, u, token_lengths, negatives, far_share, seq, root, n_z, n_i
    )
    sends, (gated, curve), lists = gate_outs[:half], gate_outs[half : half + 2], gate_outs[half + 2 :]

    packs = [pack(chip_shares, "pack_shares", gated)]
    packs += [plane_shift(packs[0], 0, 0, dc) for dc in range(1, n_c)]

    pieces = [sends[0]] + [half_shift(sends[k], k) for k in range(1, half)]
    lists = [lists[0]] + [shift(lists[k], "item", k) for k in steps_i]
    counts, slab_scale = call(
        functools.partial(count_kernel, n_i, root),
        [shape((n_i * queries, slab.shape[0]), F32), shape((1, slab.shape[0]), F32)],
        [base_arr, slab] + lists, "list_counts", smem=1,
    )
    block = shape((half * queries, depth), BF16)
    *parts, mirror, held, away = call(
        functools.partial(forward_kernel, half, n_c),
        [shape((queries, proj_width), F32)]
        + [shape((queries, proj_width), BF16)] * (half - 1)
        + [shape((depth, proj_width), BF16), block, block],
        [side_arr, share_places, proj_weight] + pieces + packs, "forward",
        flops=4 * half * queries * depth * proj_width, smem=2, after=[counts],
    )
    parts = [parts[0]] + [half_shift(parts[k], -k) for k in range(1, half)]
    near = [held] + [plane_shift(held, 0, dh, 0) for dh in range(1, n_h)]
    row = shape((queries, proj_width), F32)
    row16 = shape((queries, proj_width), BF16)
    pooled, unit, embedded, near, away = call(
        functools.partial(embed_kernel, root, half),
        [row, shape((queries, 1), F32), row16, shape((n_h * half * queries, depth), BF16), block],
        parts + [away] + near, "embed",
    )
    other = mirror_shift(away)

    pieces = [embedded] + [shift(embedded, "item", k) for k in steps_i]
    near_far = [plane_shift(near, dg, 0, 0) for dg in range(1, n_g)]
    wide = (queries, proj_width + LANES)
    parts = call(
        functools.partial(contrast_kernel, n_i),
        [shape(wide, F32)] + [shape(wide, BF16)] * (n_i - 1),
        [slab, slab_scale, counts] + pieces, "contrast",
        flops=4 * n_i * queries * slab.shape[0] * proj_width,
    )
    parts = [parts[0]] + [shift(parts[k], "item", -k) for k in steps_i]
    near_cores = [plane_shift(near, 0, 0, dc) for dc in range(1, n_c)]
    near_far_cores = [[plane_shift(array, 0, 0, dc) for array in near_far] for dc in range(1, n_c)]
    others = [other] + [plane_shift(other, dg, 0, 0) for dg in range(1, n_g)]
    cols = proj_width // n_plane
    grad, grad_columns, loss = call(
        functools.partial(grad_kernel, n_i, root),
        [row16, shape((n_all, queries, cols), BF16), shape((1, LANES), F32)],
        [positives, pooled, unit, embedded] + parts, "grad_pooled",
        after=near_far + near_cores + sum(near_far_cores, []) + others,
    )

    pieces = [grad] + [half_shift(grad, k) for k in range(1, half)]
    *backs, others = call(
        functools.partial(back_kernel, half, n_g),
        [shape((queries, 2 * depth), BF16)] * half + [shape((n_g * half * queries, depth), BF16)],
        [side_arr, proj_weight, mirror] + pieces + others, "backward",
        flops=4 * half * queries * depth * proj_width, smem=1,
    )
    backs = [backs[0]] + [half_shift(backs[k], -k) for k in range(1, half)]
    all_columns = lax.all_to_all(
        passed(grad_columns, "columns_out", backs[-1]), EVERY, 0, 0, tiled=True
    )
    slopes = slope_rows(both_arr, normed, curve, loss, backs, seq, n_z, n_all, n_plane)
    across = [plane_shift(others, 0, dh, 0) for dh in range(1, n_h)]
    late = [pack([array], "late", slopes) for array in across]
    spread = []
    for dc in range(n_c):
        if dc == 0:
            spread += [near, *near_far, others, *across]
        else:
            spread += [near_cores[dc - 1], *near_far_cores[dc - 1]]
            spread += [plane_shift(array, 0, 0, dc) for array in [others, *late]]
    block_columns = call(
        functools.partial(columns_kernel, len(spread)), [shape((depth, cols), BF16)],
        [ranks, all_columns] + spread, "grad_columns",
        flops=2 * n_all * queries * depth * cols, scratch=[pltpu.VMEM((n_all * queries, cols), BF16)], smem=1,
    )[0]
    on_chips = [block_columns if dg == dh == 0 else plane_shift(block_columns, dg, dh, 0) for dg, dh in chips]
    slopes = passed(slopes, "slopes_out", on_chips[1 % len(on_chips)])
    all_slopes = lax.all_to_all(slopes, EVERY, 0, 0, tiled=True)
    query_part, my_slope, loss_total = call(
        query_kernel,
        [shape((1, proj_width), F32), shape((depth // LANES, LANES), F32), shape((1, LANES), F32)],
        [side_arr, proj_weight, mirror, all_slopes], "slope_sum", smem=1,
    )
    finished = [pack(on_chips, "pack_columns", slopes)]
    finished += [plane_shift(finished[0], 0, 0, dc) for dc in range(1, n_c)]
    query_parts = [query_part] + [half_shift(query_part, k) for k in range(1, half)]
    grad_proj, finish_token = call(
        functools.partial(finish_kernel, len(finished)),
        [shape((depth, proj_width), F32), shape((8, LANES), F32)],
        [share_places, pool_query.reshape(1, -1), my_slope] + finished, "finish", smem=1,
    )
    grad_query = call(
        add_kernel, [shape((1, proj_width), F32)], query_parts, "query_sum", after=[finish_token]
    )[0]
    mean_loss = loss_total[0, 0] / (queries * n_all)
    return (grad_proj, grad_query.reshape(proj_width), mean_loss)


def solution(mesh):
    return jax.shard_map(
        body,
        mesh=mesh,
        in_specs=(
            P(("grp", "fsdp", "item"), None, None),
            P(("grp", "fsdp", "item"), None),
            P(("grp", "fsdp", "item"), None),
            P(("grp", "fsdp", "item")),
            P(),
            P("fsdp", None),
            P(),
            P("item", None),
        ),
        out_specs=(P("fsdp", None), P(), P()),
        check_vma=False,
    )
```

```python
import functools
import math

import jax
import jax.numpy as jnp
from jax import lax
from jax.experimental import pallas as pl
from jax.experimental.pallas import tpu as pltpu
from jax.sharding import PartitionSpec as P

sharpness_divisor = 0.05
norm_eps = 1e-05
embed_eps = 1e-06

EVERY = ("fsdp", "grp", "item")
PLANE = ("grp", "item")
F32 = jnp.float32
BF16 = jnp.bfloat16
LANES = 128
MIB = 1024 * 1024
VMEM = pl.BlockSpec(memory_space=pltpu.VMEM)
SMEM = pl.BlockSpec(memory_space=pltpu.SMEM)


def shape(dims, dtype):
    return jax.ShapeDtypeStruct(dims, dtype)


def copying(kernel, smem, shapes):
    n = len(shapes)

    def run(*refs):
        sources, buffers, sems = refs[smem : smem + n], refs[-n - 1 : -1], refs[-1]
        copies = [
            pltpu.make_async_copy(sources[k], buffers[k], sems.at[k]) for k in range(n)
        ]
        for copy in copies:
            copy.start()
        for copy in copies:
            copy.wait()
        kernel(*refs[:smem], *buffers, *refs[smem + n : -n - 1])

    return run


def call(kernel, outs, ins, name, flops=0, scratch=(), smem=0, after=(), copy=False):
    count = len(ins)
    if copy:
        shapes = [pltpu.VMEM(a.shape, a.dtype) for a in ins[smem:]]
        kernel = copying(kernel, smem, shapes)
        scratch = [*scratch, *shapes, pltpu.SemaphoreType.DMA((len(shapes),))]
    moved = sum(math.prod(a.shape) * a.dtype.itemsize for a in list(ins) + list(outs))
    held = 0 if copy else sum(math.prod(s.shape) * jnp.dtype(s.dtype).itemsize for s in scratch)

    def run(*refs):
        kernel(*refs[:count], *refs[count + len(after) :])

    return pl.pallas_call(
        run,
        out_shape=outs,
        in_specs=[SMEM] * smem
        + [pl.BlockSpec(memory_space=pl.ANY) if copy else VMEM] * (count - smem)
        + [pl.BlockSpec(memory_space=pl.ANY)] * len(after),
        out_specs=[VMEM] * len(outs),
        scratch_shapes=list(scratch),
        cost_estimate=pl.CostEstimate(flops=flops, bytes_accessed=moved, transcendentals=0),
        compiler_params=pltpu.CompilerParams(vmem_limit_bytes=2 * (moved + held) + 6 * MIB),
        name=name,
    )(*ins, *after)


def shift(values, axis, k):
    n = lax.axis_size(axis)
    return lax.ppermute(values, axis, [(i, (i + k) % n) for i in range(n)])


def split_bf16(values):
    high = values.astype(BF16)
    low = (values - high.astype(F32)).astype(BF16)
    return high, low


def nt(left, right):
    return lax.dot_general(left, right, (((1,), (1,)), ((), ())), preferred_element_type=F32)


def tn(left, right):
    return lax.dot_general(left, right, (((0,), (0,)), ((), ())), preferred_element_type=F32)


def u_kernel(weight_ref, pool_ref, u_ref):
    pool = jnp.broadcast_to(pool_ref[...], (8, pool_ref.shape[1]))
    high = pool.astype(BF16)
    low, last = split_bf16(pool - high.astype(F32))
    weight = weight_ref[...]
    u_ref[...] = (nt(high, weight) + nt(low, weight) + nt(last, weight))[0:1]


def gate_kernel(seq, root, blocks, z_ref, states_ref, gain_ref, u_ref, len_ref, lists_ref, *rest):
    half = blocks // 2
    outs, normed_ref, gated_ref, curve_ref, copies, rows_ref = (
        rest[:half], rest[half], rest[half + 1], rest[half + 2], rest[half + 3 : -1], rest[-1]
    )
    step = pl.program_id(0)
    tokens, width = states_ref.shape
    count = tokens // seq
    chunk = 4 * LANES if width % (4 * LANES) == 0 else width
    logits = []
    for top in range(0, tokens, 32):
        rows = slice(top, top + 32)
        squares = jnp.zeros((32, chunk), F32)
        for at in range(0, width, chunk):
            part = states_ref[rows, at : at + chunk].astype(F32)
            squares = squares + part * part
        inv_rms = lax.rsqrt(jnp.sum(squares, axis=1, keepdims=True) / width + norm_eps)
        total = jnp.zeros((32, chunk), F32)
        for at in range(0, width, chunk):
            part = states_ref[rows, at : at + chunk].astype(F32)
            part = (part * inv_rms * gain_ref[:, at : at + chunk]).astype(BF16)
            normed_ref[rows, at : at + chunk] = part
            total = total + part.astype(F32) * u_ref[:, at : at + chunk]
        logits.append(jnp.sum(total, axis=1, keepdims=True))
    logit = jnp.concatenate(logits, axis=0) / root
    gate = 1.0 / (1.0 + jnp.exp(-logit))
    slot = lax.rem(lax.broadcasted_iota(jnp.int32, (tokens, 1), 0), seq)
    valid = jnp.where(slot < len_ref[...], 1.0, 0.0) / len_ref[...].astype(F32)
    gated = valid * gate
    gated_ref[...] = gated
    curve_ref[...] = gated * (1.0 - gate) / root
    owner = lax.broadcasted_iota(jnp.int32, (tokens, count), 0) // seq
    mine = owner == lax.broadcasted_iota(jnp.int32, (tokens, count), 1)
    high, low = split_bf16(jnp.where(mine, gated, 0.0))
    both = tn(jnp.concatenate([high, low], axis=1), normed_ref[...])
    rows_ref[pl.ds(pl.multiple_of(step * count, count), count), :] = both[:count] + both[count:]

    @pl.when(step == pl.num_programs(0) - 1)
    def _():
        owners = len(copies)
        own = lists_ref.shape[1] // owners
        for k in range(owners):
            picked = jnp.zeros(copies[k].shape, jnp.int32)
            for j in range(owners):
                picked = jnp.where(
                    lax.rem(z_ref[1] + k, owners) == j, lists_ref[:, j * own : (j + 1) * own], picked
                )
            copies[k][...] = picked
        depth = width // blocks
        place = lax.rem(z_ref[0], half)
        for k in range(half):
            for j in range(2):
                at = (j * half + lax.rem(place + k, half)) * depth
                outs[k][:, j * depth : (j + 1) * depth] = rows_ref[
                    :, pl.ds(pl.multiple_of(at, LANES), depth)
                ].astype(BF16)


def gate_rows(z, states, gain, u, token_lengths, lists, events, seq, root, blocks, owners):
    tokens, width = states.shape
    queries = tokens // seq
    group = 16 if queries % 16 == 0 else queries
    step_tokens = group * seq
    half = blocks // 2
    outs = [shape((queries, width // half), BF16)] * half
    outs += [shape((tokens, width), BF16)] + [shape((tokens, 1), F32)] * 2
    outs += [shape((queries, lists.shape[1] // owners), lists.dtype)] * owners
    column = pl.BlockSpec((step_tokens, 1), lambda i: (i, 0))
    rows = pl.BlockSpec((step_tokens, width), lambda i: (i, 0))
    inputs = [z, states, gain, u, token_lengths, lists]

    def run(*refs):
        gate_kernel(seq, root, blocks, *refs[: len(inputs)], *refs[len(inputs) + len(events) :])

    whole = lambda dims: pl.BlockSpec(dims, lambda i: (0, 0))
    return pl.pallas_call(
        run,
        grid=(queries // group,),
        out_shape=outs,
        in_specs=[
            SMEM,
            rows,
            whole((1, width)),
            whole((1, width)),
            column,
            whole(lists.shape),
        ]
        + [pl.BlockSpec(memory_space=pl.ANY)] * len(events),
        out_specs=[whole((queries, width // half))] * half + [rows] + [column] * 2
        + [whole((queries, lists.shape[1] // owners))] * owners,
        scratch_shapes=[pltpu.VMEM((queries, width), F32)],
        cost_estimate=pl.CostEstimate(
            flops=10 * tokens * width, bytes_accessed=4 * tokens * width, transcendentals=0
        ),
        compiler_params=pltpu.CompilerParams(vmem_limit_bytes=20 * MIB),
        name="gate_rows",
    )(*inputs, *events)


def pack_kernel(*refs):
    rows = refs[0].shape[0]
    for k, ref in enumerate(refs[:-1]):
        refs[-1][k * rows : (k + 1) * rows, :] = ref[...]


def pack(pieces, name, event):
    rows, width = pieces[0].shape
    out = shape((len(pieces) * rows, width), pieces[0].dtype)
    return call(pack_kernel, [out], pieces, name, after=[event])[0]


def pass_kernel(from_ref, to_ref):
    to_ref[...] = from_ref[...]


def passed(values, name, event):
    return call(pass_kernel, [shape(values.shape, values.dtype)], [values], name, after=[event])[0]


def add_kernel(*refs):
    total = refs[0][...]
    for ref in refs[1:-1]:
        total = total + ref[...]
    refs[-1][...] = total


def forward_kernel(n, packs, side_ref, places_ref, weight_ref, *refs):
    refs = refs[:n] + (weight_ref,) + refs[n:]
    pieces, shares = refs[:n], refs[n + 1 : n + 1 + packs]
    outs = refs[n + 1 + packs : 2 * n + 1 + packs]
    mirror_ref, held_ref, away_ref = refs[2 * n + 1 + packs :]
    rows = pieces[0].shape[0]
    depth = weight_ref.shape[0]
    side = side_ref[0]
    for k in range(n):
        part = slice(k * rows, (k + 1) * rows)
        held_ref[part, :] = pieces[k][:, pl.ds(pl.multiple_of(side * depth, LANES), depth)]
        away_ref[part, :] = pieces[k][:, pl.ds(pl.multiple_of((1 - side) * depth, LANES), depth)]
    count = places_ref.shape[0] // packs
    share = shares[0].shape[0] // count
    for p in range(packs):
        for j in range(count):
            at = pl.multiple_of(places_ref[p * count + j] * share, share)
            mirror_ref[pl.ds(at, share), :] = shares[p][j * share : (j + 1) * share, :]
    product = jnp.dot(held_ref[...], weight_ref[...], preferred_element_type=F32)
    product = product + jnp.dot(away_ref[...], mirror_ref[...], preferred_element_type=F32)
    for k in range(n):
        outs[k][...] = product[k * rows : (k + 1) * rows].astype(outs[k].dtype)


def back_kernel(n, packed, side_ref, weight_ref, mirror_ref, *refs):
    pieces, outs = refs[:n], refs[n + packed : -1]
    pack_kernel(*refs[n : n + packed], refs[-1])
    rows = pieces[0].shape[0]
    depth = weight_ref.shape[0]
    side = side_ref[0]
    stack = jnp.concatenate([p[...] for p in pieces], axis=0)
    own = nt(stack, weight_ref[...]).astype(BF16)
    mirror = nt(stack, mirror_ref[...]).astype(BF16)
    for k in range(n):
        part = slice(k * rows, (k + 1) * rows)
        outs[k][:, pl.ds(pl.multiple_of(side * depth, LANES), depth)] = own[part]
        outs[k][:, pl.ds(pl.multiple_of((1 - side) * depth, LANES), depth)] = mirror[part]


def embed_kernel(root, n, *refs):
    parts, away_ref, packed = refs[:n], refs[n], refs[n + 1 : -5]
    pooled_ref, unit_ref, embedded_ref, pack_ref, pass_ref = refs[-5:]
    pass_ref[...] = away_ref[...]
    pooled = parts[0][...]
    for part in parts[1:]:
        pooled = pooled + part[...].astype(F32)
    unit = lax.rsqrt(jnp.mean(pooled * pooled, axis=1, keepdims=True) + embed_eps) / root
    pooled_ref[...] = pooled
    unit_ref[...] = unit
    embedded_ref[...] = (pooled * unit).astype(BF16)
    pack_kernel(*packed, pack_ref)


def count_kernel(n, root, base_ref, slab_ref, *refs):
    lists, counts_ref, scale_ref = refs[:n], refs[n], refs[n + 1]
    queries = lists[0].shape[0]
    rows, width = slab_ref.shape
    slab = slab_ref[...].astype(F32)
    high, low = split_bf16(slab * slab)
    ones = jnp.ones((8, width), BF16)
    row_sq = (nt(ones, high) + nt(ones, low))[0:1]
    scale_ref[...] = lax.rsqrt(row_sq / width + embed_eps) / root / sharpness_divisor
    ids = lax.broadcasted_iota(jnp.int32, (queries, LANES), 1)
    for k in range(n):
        own = lists[k][...] - base_ref[0]
        columns = [
            jnp.broadcast_to(own[:, entry : entry + 1], (queries, LANES)) for entry in range(own.shape[1])
        ]
        for at in range(0, rows, LANES):
            total = jnp.zeros(ids.shape, F32)
            for column in columns:
                total = total + jnp.where(column == ids + at, 1.0, 0.0)
            counts_ref[k * queries : (k + 1) * queries, at : at + LANES] = total


def contrast_kernel(n, *refs):
    (slab_ref, scale_ref, counts_ref), pieces, outs = refs[:3], refs[3 : n + 3], refs[n + 3 :]
    queries, width = pieces[0].shape
    embedded = jnp.concatenate([p[...] for p in pieces], axis=0)
    slab = slab_ref[...]
    scale = scale_ref[...]
    heavy = counts_ref[...] * jnp.exp(nt(embedded, slab) * scale)
    denom = jnp.sum(heavy, axis=1, keepdims=True)
    grad = jnp.dot((heavy * scale).astype(BF16), slab, preferred_element_type=F32)
    high, low = split_bf16(denom)
    lane = lax.broadcasted_iota(jnp.int32, (queries, LANES), 1)
    for k in range(n):
        part = slice(k * queries, (k + 1) * queries)
        outs[k][:, :width] = grad[part].astype(outs[k].dtype)
        if k == 0:
            tail = jnp.where(lane == 0, denom[part], 0.0)
        else:
            tail = jnp.where(lane == 0, high[part].astype(F32), jnp.where(lane == 1, low[part].astype(F32), 0.0))
        outs[k][:, width:] = tail.astype(outs[k].dtype)


def grad_kernel(n, root, *refs):
    pos_ref, pooled_ref, unit_ref, embedded_ref = refs[:4]
    parts = refs[4 : n + 4]
    grad_ref, columns_ref, loss_ref = refs[n + 4 :]
    queries, width = pos_ref.shape
    total = parts[0][:, :width]
    denom = jnp.sum(parts[0][:, width:], axis=1, keepdims=True)
    for part in parts[1:]:
        total = total + part[:, :width].astype(F32)
        denom = denom + jnp.sum(part[:, width:].astype(F32), axis=1, keepdims=True)
    positive = pos_ref[...].astype(F32)
    scale = (
        lax.rsqrt(jnp.mean(positive * positive, axis=1, keepdims=True) + embed_eps)
        / root
        / sharpness_divisor
    )
    score = jnp.sum(embedded_ref[...].astype(F32) * positive, axis=1, keepdims=True) * scale
    pos_exp = jnp.exp(score)
    denom = denom + pos_exp
    loss_ref[...] = jnp.broadcast_to(jnp.sum(jnp.log(denom) - score), loss_ref.shape)
    grad_embed = total / denom + (pos_exp / denom - 1.0) * scale * positive
    pooled, unit = pooled_ref[...], unit_ref[...]
    mean_sq = jnp.mean(pooled * pooled, axis=1, keepdims=True)
    radial = jnp.sum(pooled * grad_embed, axis=1, keepdims=True)
    grad = unit * grad_embed - pooled * (radial * unit / (width * (mean_sq + embed_eps)))
    grad = grad.astype(BF16)
    grad_ref[...] = grad
    cols = columns_ref.shape[2]
    places = width // cols
    for j in range(columns_ref.shape[0]):
        at = (j % places) * cols
        columns_ref[j] = grad[:, at : at + cols]


def slope_kernel(seq, blocks, z_ref, normed_ref, curve_ref, loss_ref, *rest):
    half = blocks // 2
    backs, outs, (all_ref, sum_ref) = rest[:half], rest[half : 2 * half], rest[-2:]
    step = pl.program_id(0)
    tokens, width = normed_ref.shape
    count = tokens // seq
    depth = width // blocks
    place = lax.rem(z_ref[0], half)

    def block_at(j, k):
        return pl.ds(pl.multiple_of((j * half + lax.rem(place + k, half)) * depth, LANES), depth)

    @pl.when(step == 0)
    def _():
        sum_ref[...] = jnp.zeros_like(sum_ref)
        for k in range(half):
            for j in range(2):
                all_ref[:, block_at(j, k)] = backs[k][:, j * depth : (j + 1) * depth].astype(F32)

    back = all_ref[pl.ds(pl.multiple_of(step * count, count), count), :]
    normed = normed_ref[...].astype(F32).reshape(count, seq, width)
    dots = jnp.sum(normed * back[:, None, :], axis=2, keepdims=True)
    slope = curve_ref[...].reshape(count, seq, 1) * dots
    heavy = (slope * normed).reshape(tokens // 8, 8, width)
    sum_ref[...] += jnp.sum(heavy, axis=0)

    @pl.when(step == pl.num_programs(0) - 1)
    def _():
        total = jnp.sum(sum_ref[...], axis=0, keepdims=True)
        lines = depth // LANES
        height = outs[0].shape[0]
        loss = jnp.broadcast_to(loss_ref[...], (height - 2 * lines, LANES))
        all_ref[0:1, :] = total
        for k in range(half):
            for j in range(2):
                row = all_ref[0:1, block_at(j, k)]
                for line in range(lines):
                    outs[k][j * lines + line : j * lines + line + 1, :] = row[
                        :, line * LANES : (line + 1) * LANES
                    ]
            outs[k][2 * lines :, :] = loss


def slope_rows(z, normed, curve, loss, backs, seq, blocks):
    tokens, width = normed.shape
    half = blocks // 2
    height = 2 * (width // blocks // LANES) // 8 * 8 + 8
    queries = tokens // seq
    group = 8 if queries % 8 == 0 else queries
    step_tokens = group * seq
    whole = lambda dims: pl.BlockSpec(dims, lambda i: (0, 0))
    return pl.pallas_call(
        functools.partial(slope_kernel, seq, blocks),
        grid=(queries // group,),
        out_shape=[shape((height, LANES), F32)] * half,
        in_specs=[
            SMEM,
            pl.BlockSpec((step_tokens, width), lambda i: (i, 0)),
            pl.BlockSpec((step_tokens, 1), lambda i: (i, 0)),
            whole((1, LANES)),
        ]
        + [whole((queries, width // half))] * half,
        out_specs=[whole((height, LANES))] * half,
        scratch_shapes=[pltpu.VMEM((queries, width), F32), pltpu.VMEM((8, width), F32)],
        cost_estimate=pl.CostEstimate(
            flops=4 * tokens * width, bytes_accessed=2 * tokens * width, transcendentals=0
        ),
        compiler_params=pltpu.CompilerParams(vmem_limit_bytes=20 * MIB),
        name="slope_rows",
    )(z, normed, curve, loss, *backs)


def columns_kernel(n, order_ref, grads_ref, *refs):
    pieces, (out_ref, sorted_ref) = refs[:n], refs[n:]
    chunk = grads_ref.shape[1]
    for j in range(sorted_ref.shape[0] // chunk):
        sorted_ref[j * chunk : (j + 1) * chunk, :] = grads_ref[order_ref[j]]
    at = pieces[0].shape[0]
    total = tn(sorted_ref[0:at, :], pieces[0][...])
    for piece in pieces[1:]:
        rows = piece.shape[0]
        total = total + tn(sorted_ref[at : at + rows, :], piece[...])
        at += rows
    out_ref[...] = total.T.astype(BF16)


def query_kernel(side_ref, weight_ref, mirror_ref, parts_ref, part_ref, slope_ref, loss_ref):
    depth = weight_ref.shape[0]
    lines = depth // LANES
    total = parts_ref[...]
    loss_ref[...] = total[2 * lines : 2 * lines + 1]
    side = side_ref[0]
    part = jnp.zeros(part_ref.shape, F32)
    for j in range(2):
        rows = total[j * lines : (j + 1) * lines]
        row = jnp.concatenate([rows[k : k + 1] for k in range(lines)], axis=1)
        high, low = split_bf16(jnp.broadcast_to(row, (8, depth)))

        @pl.when(side == j)
        def _():
            slope_ref[...] = rows

        weight = jnp.where(side == j, weight_ref[...], mirror_ref[...])
        part = part + jnp.dot(high, weight, preferred_element_type=F32)[0:1]
        part = part + jnp.dot(low, weight, preferred_element_type=F32)[0:1]
    part_ref[...] = part


def finish_kernel(n, place_ref, pool_ref, slope_ref, *refs):
    pieces, out_ref, token_ref = refs[:n], refs[-2], refs[-1]
    token_ref[...] = jnp.zeros_like(token_ref)
    places = place_ref.shape[0]
    rows, cols = out_ref.shape[0], pieces[0].shape[1]
    for line in range(rows // LANES):
        part = slice(line * LANES, (line + 1) * LANES)
        slope = jnp.broadcast_to(slope_ref[line : line + 1, :], (LANES, LANES)).T
        for k in range(places):
            base = k % (places // n) * rows + line * LANES
            mine = pieces[k // (places // n)][base : base + LANES, :].astype(F32)
            at = pl.ds(pl.multiple_of(place_ref[k] * cols, LANES), cols)
            out_ref[part, at] = mine + slope * pool_ref[:, at]


def body(hidden_states, positives, negatives, lengths, norm_gain, proj_weight, pool_query, slab):
    queries, seq, width = hidden_states.shape
    depth, proj_width = proj_weight.shape
    n_z, n_g, n_i = lax.axis_size("fsdp"), lax.axis_size("grp"), lax.axis_size("item")
    assert n_z % 2 == 0
    half = n_z // 2
    n_c = 2 if n_i % 2 == 0 else 1
    n_h = n_i // n_c
    n_plane = n_g * n_i
    n_all = n_z * n_plane
    z, g, i = lax.axis_index("fsdp"), lax.axis_index("grp"), lax.axis_index("item")
    h, c = i // n_c, lax.rem(i, n_c)
    side, member = z // half, lax.rem(z, half)
    root = math.sqrt(proj_width)
    steps_z, steps_i = range(1, n_z), range(1, n_i)

    def ints(*values):
        return jnp.stack([jnp.asarray(v, jnp.int32) for v in values])

    z_arr, side_arr = ints(z), ints(side)

    def plane_shift(values, dg, dh, dc):
        pairs = []
        for pg in range(n_g):
            for ph in range(n_h):
                for pc in range(n_c):
                    to = ((pg + dg) % n_g) * n_i + ((ph + dh) % n_h) * n_c + (pc + dc) % n_c
                    pairs.append((pg * n_i + ph * n_c + pc, to))
        return lax.ppermute(values, PLANE, pairs)

    def half_shift(values, k):
        pairs = [(a, a // half * half + (a % half + k) % half) for a in range(n_z)]
        return lax.ppermute(values, "fsdp", pairs)

    def mirror_shift(values):
        return lax.ppermute(values, "fsdp", [(a, (a + half) % n_z) for a in range(n_z)])

    def source(dg, dh, dc):
        return (
            lax.rem(g - dg + n_g, n_g),
            lax.rem(h - dh + n_h, n_h) * n_c + lax.rem(c - dc + n_c, n_c),
        )

    chips = [(dg, dh) for dg in range(n_g) for dh in range(n_h)]

    share = depth // n_plane
    place = g * n_i + i
    weight_share = lax.dynamic_slice_in_dim(proj_weight, place * share, share, 0)
    far_share = mirror_shift(weight_share)

    block_u = call(
        u_kernel, [shape((1, depth), F32)], [proj_weight, pool_query.reshape(1, -1)], "block_u",
        after=[weight_share],
    )[0]
    u_parts = [block_u] + [shift(block_u, "fsdp", k) for k in steps_z]
    u = jnp.zeros((1, width), F32)
    for k in range(n_z):
        u = lax.dynamic_update_slice(u, u_parts[k], (0, lax.rem(z - k + n_z, n_z) * depth))

    share_places = []
    for dc in range(n_c):
        for dg, dh in chips:
            from_g, from_i = source(dg, dh, dc)
            share_places.append(from_g * n_i + from_i)
    share_places = ints(*share_places)
    order = []
    for dc in range(n_c):
        for dg in range(n_g):
            order += [(side, k, dg, dh, dc) for dh in range(n_h) for k in range(half)]
        for dh in range(n_h):
            order += [(1 - side, k, dg, dh, dc) for dg in range(n_g) for k in range(half)]
    ranks = []
    for from_side, k, dg, dh, dc in order:
        from_g, from_i = source(dg, dh, dc)
        from_z = from_side * half + lax.rem(member - k + half, half)
        ranks.append((from_z * n_g + from_g) * n_i + from_i)
    ranks = ints(*ranks)
    both_arr, base_arr = ints(z, i), ints(i * slab.shape[0])
    token_lengths = jnp.broadcast_to(lengths[:, None], (queries, seq)).reshape(-1, 1)
    events = [far_share, share_places, ranks, base_arr, side_arr]
    chip_shares = [far_share if dg == dh == 0 else plane_shift(far_share, dg, dh, 0) for dg, dh in chips]
    gate_outs = gate_rows(
        both_arr, hidden_states.reshape(-1, width), norm_gain.astype(F32).reshape(1, width), u,
        token_lengths, negatives, events, seq, root, n_z, n_i,
    )
    sends, (normed, gated, curve), lists = gate_outs[:half], gate_outs[half : half + 3], gate_outs[half + 3 :]
    packs = [pack(chip_shares, "pack_shares", gated)]
    packs += [plane_shift(packs[0], 0, 0, dc) for dc in range(1, n_c)]

    pieces = [sends[0]] + [half_shift(sends[k], k) for k in range(1, half)]
    lists = [lists[0]] + [shift(lists[k], "item", k) for k in steps_i]
    counts, slab_scale = call(
        functools.partial(count_kernel, n_i, root),
        [shape((n_i * queries, slab.shape[0]), F32), shape((1, slab.shape[0]), F32)],
        [base_arr, slab] + lists, "list_counts", smem=1,
    )
    block = shape((half * queries, depth), BF16)
    *parts, mirror, held, away = call(
        functools.partial(forward_kernel, half, n_c),
        [shape((queries, proj_width), F32)]
        + [shape((queries, proj_width), BF16)] * (half - 1)
        + [shape((depth, proj_width), BF16), block, block],
        [side_arr, share_places, proj_weight] + pieces + packs, "forward",
        flops=4 * half * queries * depth * proj_width, smem=2, after=[counts],
    )
    parts = [parts[0]] + [half_shift(parts[k], -k) for k in range(1, half)]
    near = [held] + [plane_shift(held, 0, dh, 0) for dh in range(1, n_h)]
    row = shape((queries, proj_width), F32)
    row16 = shape((queries, proj_width), BF16)
    pooled, unit, embedded, near, away = call(
        functools.partial(embed_kernel, root, half),
        [row, shape((queries, 1), F32), row16, shape((n_h * half * queries, depth), BF16), block],
        parts + [away] + near, "embed",
    )
    other = mirror_shift(away)

    pieces = [embedded] + [shift(embedded, "item", k) for k in steps_i]
    near_far = [plane_shift(near, dg, 0, 0) for dg in range(1, n_g)]
    wide = (queries, proj_width + LANES)
    parts = call(
        functools.partial(contrast_kernel, n_i),
        [shape(wide, F32)] + [shape(wide, BF16)] * (n_i - 1),
        [slab, slab_scale, counts] + pieces, "contrast",
        flops=4 * n_i * queries * slab.shape[0] * proj_width,
    )
    parts = [parts[0]] + [shift(parts[k], "item", -k) for k in steps_i]
    near_cores = [plane_shift(near, 0, 0, dc) for dc in range(1, n_c)]
    near_far_cores = [[plane_shift(array, 0, 0, dc) for array in near_far] for dc in range(1, n_c)]
    others = [other] + [plane_shift(other, dg, 0, 0) for dg in range(1, n_g)]
    cols = proj_width // n_plane
    grad, grad_columns, loss = call(
        functools.partial(grad_kernel, n_i, root),
        [row16, shape((n_all, queries, cols), BF16), shape((1, LANES), F32)],
        [positives, pooled, unit, embedded] + parts, "grad_pooled",
        after=near_far + near_cores + sum(near_far_cores, []) + others,
    )

    pieces = [grad] + [half_shift(grad, k) for k in range(1, half)]
    *backs, others = call(
        functools.partial(back_kernel, half, n_g),
        [shape((queries, 2 * depth), BF16)] * half + [shape((n_g * half * queries, depth), BF16)],
        [side_arr, proj_weight, mirror] + pieces + others, "backward",
        flops=4 * half * queries * depth * proj_width, smem=1,
    )
    backs = [backs[0]] + [half_shift(backs[k], -k) for k in range(1, half)]
    all_columns = lax.all_to_all(
        passed(grad_columns, "columns_out", backs[-1]), EVERY, 0, 0, tiled=True
    )
    slopes = slope_rows(both_arr, normed, curve, loss, backs, seq, n_z)
    across = [plane_shift(others, 0, dh, 0) for dh in range(1, n_h)]
    late = [pack([array], "late", slopes[0]) for array in across]
    spread = []
    for dc in range(n_c):
        if dc == 0:
            spread += [near, *near_far, others, *across]
        else:
            spread += [near_cores[dc - 1], *near_far_cores[dc - 1]]
            spread += [plane_shift(array, 0, 0, dc) for array in [others, *late]]
    block_columns = call(
        functools.partial(columns_kernel, len(spread)), [shape((depth, cols), BF16)],
        [ranks, all_columns] + spread, "grad_columns",
        flops=2 * n_all * queries * depth * cols, scratch=[pltpu.VMEM((n_all * queries, cols), BF16)], smem=1, copy=True,
    )[0]
    on_chips = [block_columns if dg == dh == 0 else plane_shift(block_columns, dg, dh, 0) for dg, dh in chips]
    def total(parts, name):
        return call(add_kernel, [shape(parts[0].shape, F32)], parts, name)[0]

    slopes = [passed(array, "slopes_out", block_columns) for array in slopes]
    slope = total([slopes[0]] + [half_shift(slopes[k], k) for k in range(1, half)], "sum_half")
    slope = total([slope, mirror_shift(slope)], "sum_mirror")
    for axis, size in ((0, n_g), (1, n_h), (2, n_c)):
        if size > 1:
            moves = [[k if a == axis else 0 for a in range(3)] for k in range(1, size)]
            slope = total([slope] + [plane_shift(slope, *move) for move in moves], "sum_plane")
    query_part, my_slope, loss_total = call(
        query_kernel,
        [shape((1, proj_width), F32), shape((depth // LANES, LANES), F32), shape((1, LANES), F32)],
        [side_arr, proj_weight, mirror, slope], "slope_sum", smem=1,
    )
    finished = [pack(on_chips, "pack_columns", slope)]
    finished += [plane_shift(finished[0], 0, 0, dc) for dc in range(1, n_c)]
    query_parts = [query_part] + [half_shift(query_part, k) for k in range(1, half)]
    grad_proj, finish_token = call(
        functools.partial(finish_kernel, len(finished)),
        [shape((depth, proj_width), F32), shape((8, LANES), F32)],
        [share_places, pool_query.reshape(1, -1), my_slope] + finished, "finish", smem=1,
    )
    grad_query = call(
        add_kernel, [shape((1, proj_width), F32)], query_parts, "query_sum", after=[finish_token]
    )[0]
    mean_loss = loss_total[0, 0] / (queries * n_all)
    return (grad_proj, grad_query.reshape(proj_width), mean_loss)


def solution(mesh):
    return jax.shard_map(
        body,
        mesh=mesh,
        in_specs=(
            P(("grp", "fsdp", "item"), None, None),
            P(("grp", "fsdp", "item"), None),
            P(("grp", "fsdp", "item"), None),
            P(("grp", "fsdp", "item")),
            P(),
            P("fsdp", None),
            P(),
            P("item", None),
        ),
        out_specs=(P("fsdp", None), P(), P()),
        check_vma=False,
    )
```

```python
import functools
import math

import jax
import jax.numpy as jnp
from jax import lax
from jax.experimental import pallas as pl
from jax.experimental.pallas import tpu as pltpu
from jax.sharding import PartitionSpec as P

sharpness_divisor = 0.05
norm_eps = 1e-05
embed_eps = 1e-06

EVERY = ("fsdp", "grp", "item")
PLANE = ("grp", "item")
F32 = jnp.float32
BF16 = jnp.bfloat16
LANES = 128
MIB = 1024 * 1024
VMEM = pl.BlockSpec(memory_space=pltpu.VMEM)
SMEM = pl.BlockSpec(memory_space=pltpu.SMEM)


def shape(dims, dtype):
    return jax.ShapeDtypeStruct(dims, dtype)


def copying(kernel, smem, shapes):
    n = len(shapes)

    def run(*refs):
        sources, buffers, sems = refs[smem : smem + n], refs[-n - 1 : -1], refs[-1]
        copies = [
            pltpu.make_async_copy(sources[k], buffers[k], sems.at[k]) for k in range(n)
        ]
        for copy in copies:
            copy.start()
        for copy in copies:
            copy.wait()
        kernel(*refs[:smem], *buffers, *refs[smem + n : -n - 1])

    return run


def call(kernel, outs, ins, name, flops=0, scratch=(), smem=0, after=(), copy=False):
    count = len(ins)
    if copy:
        shapes = [pltpu.VMEM(a.shape, a.dtype) for a in ins[smem:]]
        kernel = copying(kernel, smem, shapes)
        scratch = [*scratch, *shapes, pltpu.SemaphoreType.DMA((len(shapes),))]
    moved = sum(math.prod(a.shape) * a.dtype.itemsize for a in list(ins) + list(outs))
    held = 0 if copy else sum(math.prod(s.shape) * jnp.dtype(s.dtype).itemsize for s in scratch)

    def run(*refs):
        kernel(*refs[:count], *refs[count + len(after) :])

    return pl.pallas_call(
        run,
        out_shape=outs,
        in_specs=[SMEM] * smem
        + [pl.BlockSpec(memory_space=pl.ANY) if copy else VMEM] * (count - smem)
        + [pl.BlockSpec(memory_space=pl.ANY)] * len(after),
        out_specs=[VMEM] * len(outs),
        scratch_shapes=list(scratch),
        cost_estimate=pl.CostEstimate(flops=flops, bytes_accessed=moved, transcendentals=0),
        compiler_params=pltpu.CompilerParams(
            vmem_limit_bytes=(4 if copy else 2) * (moved + held) + (12 if copy else 6) * MIB
        ),
        name=name,
    )(*ins, *after)


def shift(values, axis, k):
    n = lax.axis_size(axis)
    return lax.ppermute(values, axis, [(i, (i + k) % n) for i in range(n)])


def split_bf16(values):
    high = values.astype(BF16)
    low = (values - high.astype(F32)).astype(BF16)
    return high, low


def nt(left, right):
    return lax.dot_general(left, right, (((1,), (1,)), ((), ())), preferred_element_type=F32)


def tn(left, right):
    return lax.dot_general(left, right, (((0,), (0,)), ((), ())), preferred_element_type=F32)


def u_kernel(weight_ref, pool_ref, u_ref):
    pool = jnp.broadcast_to(pool_ref[...], (8, pool_ref.shape[1]))
    high = pool.astype(BF16)
    low, last = split_bf16(pool - high.astype(F32))
    weight = weight_ref[...]
    u_ref[...] = (nt(high, weight) + nt(low, weight) + nt(last, weight))[0:1]


def gate_kernel(seq, root, blocks, z_ref, states_ref, gain_ref, u_ref, len_ref, lists_ref, *rest):
    half = blocks // 2
    outs, normed_ref, gated_ref, curve_ref, copies, rows_ref = (
        rest[:half], rest[half], rest[half + 1], rest[half + 2], rest[half + 3 : -1], rest[-1]
    )
    step = pl.program_id(0)
    tokens, width = states_ref.shape
    count = tokens // seq
    chunk = 4 * LANES if width % (4 * LANES) == 0 else width
    logits = []
    for top in range(0, tokens, 32):
        rows = slice(top, top + 32)
        squares = jnp.zeros((32, chunk), F32)
        for at in range(0, width, chunk):
            part = states_ref[rows, at : at + chunk].astype(F32)
            squares = squares + part * part
        inv_rms = lax.rsqrt(jnp.sum(squares, axis=1, keepdims=True) / width + norm_eps)
        total = jnp.zeros((32, chunk), F32)
        for at in range(0, width, chunk):
            part = states_ref[rows, at : at + chunk].astype(F32)
            part = (part * inv_rms * gain_ref[:, at : at + chunk]).astype(BF16)
            normed_ref[rows, at : at + chunk] = part
            total = total + part.astype(F32) * u_ref[:, at : at + chunk]
        logits.append(jnp.sum(total, axis=1, keepdims=True))
    logit = jnp.concatenate(logits, axis=0) / root
    gate = 1.0 / (1.0 + jnp.exp(-logit))
    slot = lax.rem(lax.broadcasted_iota(jnp.int32, (tokens, 1), 0), seq)
    valid = jnp.where(slot < len_ref[...], 1.0, 0.0) / len_ref[...].astype(F32)
    gated = valid * gate
    gated_ref[...] = gated
    curve_ref[...] = gated * (1.0 - gate) / root
    owner = lax.broadcasted_iota(jnp.int32, (tokens, count), 0) // seq
    mine = owner == lax.broadcasted_iota(jnp.int32, (tokens, count), 1)
    high, low = split_bf16(jnp.where(mine, gated, 0.0))
    both = tn(jnp.concatenate([high, low], axis=1), normed_ref[...])
    rows_ref[pl.ds(pl.multiple_of(step * count, count), count), :] = both[:count] + both[count:]

    @pl.when(step == pl.num_programs(0) - 1)
    def _():
        owners = len(copies)
        own = lists_ref.shape[1] // owners
        for k in range(owners):
            picked = jnp.zeros(copies[k].shape, jnp.int32)
            for j in range(owners):
                picked = jnp.where(
                    lax.rem(z_ref[1] + k, owners) == j, lists_ref[:, j * own : (j + 1) * own], picked
                )
            copies[k][...] = picked
        depth = width // blocks
        place = lax.rem(z_ref[0], half)
        for k in range(half):
            for j in range(2):
                at = (j * half + lax.rem(place + k, half)) * depth
                outs[k][:, j * depth : (j + 1) * depth] = rows_ref[
                    :, pl.ds(pl.multiple_of(at, LANES), depth)
                ].astype(BF16)


def gate_rows(z, states, gain, u, token_lengths, lists, events, seq, root, blocks, owners):
    tokens, width = states.shape
    queries = tokens // seq
    group = 16 if queries % 16 == 0 else queries
    step_tokens = group * seq
    half = blocks // 2
    outs = [shape((queries, width // half), BF16)] * half
    outs += [shape((tokens, width), BF16)] + [shape((tokens, 1), F32)] * 2
    outs += [shape((queries, lists.shape[1] // owners), lists.dtype)] * owners
    column = pl.BlockSpec((step_tokens, 1), lambda i: (i, 0))
    rows = pl.BlockSpec((step_tokens, width), lambda i: (i, 0))
    inputs = [z, states, gain, u, token_lengths, lists]

    def run(*refs):
        gate_kernel(seq, root, blocks, *refs[: len(inputs)], *refs[len(inputs) + len(events) :])

    whole = lambda dims: pl.BlockSpec(dims, lambda i: (0, 0))
    return pl.pallas_call(
        run,
        grid=(queries // group,),
        out_shape=outs,
        in_specs=[
            SMEM,
            rows,
            whole((1, width)),
            whole((1, width)),
            column,
            whole(lists.shape),
        ]
        + [pl.BlockSpec(memory_space=pl.ANY)] * len(events),
        out_specs=[whole((queries, width // half))] * half + [rows] + [column] * 2
        + [whole((queries, lists.shape[1] // owners))] * owners,
        scratch_shapes=[pltpu.VMEM((queries, width), F32)],
        cost_estimate=pl.CostEstimate(
            flops=10 * tokens * width, bytes_accessed=4 * tokens * width, transcendentals=0
        ),
        compiler_params=pltpu.CompilerParams(vmem_limit_bytes=50 * MIB),
        name="gate_rows",
    )(*inputs, *events)


def pack_kernel(*refs):
    rows = refs[0].shape[0]
    for k, ref in enumerate(refs[:-1]):
        refs[-1][k * rows : (k + 1) * rows, :] = ref[...]


def pack(pieces, name, event):
    rows, width = pieces[0].shape
    out = shape((len(pieces) * rows, width), pieces[0].dtype)
    return call(pack_kernel, [out], pieces, name, after=[event])[0]


def pass_kernel(from_ref, to_ref):
    to_ref[...] = from_ref[...]


def passed(values, name, event):
    return call(pass_kernel, [shape(values.shape, values.dtype)], [values], name, after=[event])[0]


def add_kernel(*refs):
    total = refs[0][...]
    for ref in refs[1:-1]:
        total = total + ref[...]
    refs[-1][...] = total


def forward_kernel(n, packs, side_ref, places_ref, weight_ref, *refs):
    refs = refs[:n] + (weight_ref,) + refs[n:]
    pieces, shares = refs[:n], refs[n + 1 : n + 1 + packs]
    outs = refs[n + 1 + packs : 2 * n + 1 + packs]
    mirror_ref, held_ref, away_ref = refs[2 * n + 1 + packs :]
    rows = pieces[0].shape[0]
    depth = weight_ref.shape[0]
    side = side_ref[0]
    for k in range(n):
        part = slice(k * rows, (k + 1) * rows)
        held_ref[part, :] = pieces[k][:, pl.ds(pl.multiple_of(side * depth, LANES), depth)]
        away_ref[part, :] = pieces[k][:, pl.ds(pl.multiple_of((1 - side) * depth, LANES), depth)]
    count = places_ref.shape[0] // packs
    share = shares[0].shape[0] // count
    for p in range(packs):
        for j in range(count):
            at = pl.multiple_of(places_ref[p * count + j] * share, share)
            mirror_ref[pl.ds(at, share), :] = shares[p][j * share : (j + 1) * share, :]
    product = jnp.dot(held_ref[...], weight_ref[...], preferred_element_type=F32)
    product = product + jnp.dot(away_ref[...], mirror_ref[...], preferred_element_type=F32)
    for k in range(n):
        outs[k][...] = product[k * rows : (k + 1) * rows].astype(outs[k].dtype)


def back_kernel(n, packed, side_ref, weight_ref, mirror_ref, *refs):
    pieces, outs = refs[:n], refs[n + packed : -1]
    pack_kernel(*refs[n : n + packed], refs[-1])
    rows = pieces[0].shape[0]
    depth = weight_ref.shape[0]
    side = side_ref[0]
    stack = jnp.concatenate([p[...] for p in pieces], axis=0)
    own = nt(stack, weight_ref[...]).astype(BF16)
    mirror = nt(stack, mirror_ref[...]).astype(BF16)
    for k in range(n):
        part = slice(k * rows, (k + 1) * rows)
        outs[k][:, pl.ds(pl.multiple_of(side * depth, LANES), depth)] = own[part]
        outs[k][:, pl.ds(pl.multiple_of((1 - side) * depth, LANES), depth)] = mirror[part]


def embed_kernel(root, n, *refs):
    parts, away_ref, packed = refs[:n], refs[n], refs[n + 1 : -5]
    pooled_ref, unit_ref, embedded_ref, pack_ref, pass_ref = refs[-5:]
    pass_ref[...] = away_ref[...]
    pooled = parts[0][...]
    for part in parts[1:]:
        pooled = pooled + part[...].astype(F32)
    unit = lax.rsqrt(jnp.mean(pooled * pooled, axis=1, keepdims=True) + embed_eps) / root
    pooled_ref[...] = pooled
    unit_ref[...] = unit
    embedded_ref[...] = (pooled * unit).astype(BF16)
    pack_kernel(*packed, pack_ref)


def count_kernel(n, root, base_ref, slab_ref, *refs):
    lists, counts_ref, scale_ref = refs[:n], refs[n], refs[n + 1]
    queries = lists[0].shape[0]
    rows, width = slab_ref.shape
    slab = slab_ref[...].astype(F32)
    high, low = split_bf16(slab * slab)
    ones = jnp.ones((8, width), BF16)
    row_sq = (nt(ones, high) + nt(ones, low))[0:1]
    scale_ref[...] = lax.rsqrt(row_sq / width + embed_eps) / root / sharpness_divisor
    ids = lax.broadcasted_iota(jnp.int32, (queries, LANES), 1)
    for k in range(n):
        own = lists[k][...] - base_ref[0]
        columns = [
            jnp.broadcast_to(own[:, entry : entry + 1], (queries, LANES)) for entry in range(own.shape[1])
        ]
        for at in range(0, rows, LANES):
            total = jnp.zeros(ids.shape, F32)
            for column in columns:
                total = total + jnp.where(column == ids + at, 1.0, 0.0)
            counts_ref[k * queries : (k + 1) * queries, at : at + LANES] = total


def contrast_kernel(n, *refs):
    (slab_ref, scale_ref, counts_ref), pieces, outs = refs[:3], refs[3 : n + 3], refs[n + 3 :]
    queries, width = pieces[0].shape
    embedded = jnp.concatenate([p[...] for p in pieces], axis=0)
    slab = slab_ref[...]
    scale = scale_ref[...]
    heavy = counts_ref[...] * jnp.exp(nt(embedded, slab) * scale)
    denom = jnp.sum(heavy, axis=1, keepdims=True)
    grad = jnp.dot((heavy * scale).astype(BF16), slab, preferred_element_type=F32)
    high, low = split_bf16(denom)
    lane = lax.broadcasted_iota(jnp.int32, (queries, LANES), 1)
    for k in range(n):
        part = slice(k * queries, (k + 1) * queries)
        outs[k][:, :width] = grad[part].astype(outs[k].dtype)
        if k == 0:
            tail = jnp.where(lane == 0, denom[part], 0.0)
        else:
            tail = jnp.where(lane == 0, high[part].astype(F32), jnp.where(lane == 1, low[part].astype(F32), 0.0))
        outs[k][:, width:] = tail.astype(outs[k].dtype)


def grad_kernel(n, root, *refs):
    pos_ref, pooled_ref, unit_ref, embedded_ref = refs[:4]
    parts = refs[4 : n + 4]
    grad_ref, columns_ref, loss_ref = refs[n + 4 :]
    queries, width = pos_ref.shape
    total = parts[0][:, :width]
    denom = jnp.sum(parts[0][:, width:], axis=1, keepdims=True)
    for part in parts[1:]:
        total = total + part[:, :width].astype(F32)
        denom = denom + jnp.sum(part[:, width:].astype(F32), axis=1, keepdims=True)
    positive = pos_ref[...].astype(F32)
    scale = (
        lax.rsqrt(jnp.mean(positive * positive, axis=1, keepdims=True) + embed_eps)
        / root
        / sharpness_divisor
    )
    score = jnp.sum(embedded_ref[...].astype(F32) * positive, axis=1, keepdims=True) * scale
    pos_exp = jnp.exp(score)
    denom = denom + pos_exp
    loss_ref[...] = jnp.broadcast_to(jnp.sum(jnp.log(denom) - score), loss_ref.shape)
    grad_embed = total / denom + (pos_exp / denom - 1.0) * scale * positive
    pooled, unit = pooled_ref[...], unit_ref[...]
    mean_sq = jnp.mean(pooled * pooled, axis=1, keepdims=True)
    radial = jnp.sum(pooled * grad_embed, axis=1, keepdims=True)
    grad = unit * grad_embed - pooled * (radial * unit / (width * (mean_sq + embed_eps)))
    grad = grad.astype(BF16)
    grad_ref[...] = grad
    cols = columns_ref.shape[2]
    places = width // cols
    for j in range(columns_ref.shape[0]):
        at = (j % places) * cols
        columns_ref[j] = grad[:, at : at + cols]


def slope_kernel(seq, blocks, z_ref, normed_ref, curve_ref, loss_ref, *rest):
    half = blocks // 2
    backs, outs, (all_ref, sum_ref) = rest[:half], rest[half : 2 * half], rest[-2:]
    step = pl.program_id(0)
    tokens, width = normed_ref.shape
    count = tokens // seq
    depth = width // blocks
    place = lax.rem(z_ref[0], half)

    def block_at(j, k):
        return pl.ds(pl.multiple_of((j * half + lax.rem(place + k, half)) * depth, LANES), depth)

    @pl.when(step == 0)
    def _():
        sum_ref[...] = jnp.zeros_like(sum_ref)
        for k in range(half):
            for j in range(2):
                all_ref[:, block_at(j, k)] = backs[k][:, j * depth : (j + 1) * depth].astype(F32)

    back = all_ref[pl.ds(pl.multiple_of(step * count, count), count), :]
    normed = normed_ref[...].astype(F32).reshape(count, seq, width)
    dots = jnp.sum(normed * back[:, None, :], axis=2, keepdims=True)
    slope = curve_ref[...].reshape(count, seq, 1) * dots
    heavy = (slope * normed).reshape(tokens // 8, 8, width)
    sum_ref[...] += jnp.sum(heavy, axis=0)

    @pl.when(step == pl.num_programs(0) - 1)
    def _():
        total = jnp.sum(sum_ref[...], axis=0, keepdims=True)
        lines = depth // LANES
        height = outs[0].shape[0]
        loss = jnp.broadcast_to(loss_ref[...], (height - 2 * lines, LANES))
        all_ref[0:1, :] = total
        for k in range(half):
            for j in range(2):
                row = all_ref[0:1, block_at(j, k)]
                for line in range(lines):
                    outs[k][j * lines + line : j * lines + line + 1, :] = row[
                        :, line * LANES : (line + 1) * LANES
                    ]
            outs[k][2 * lines :, :] = loss


def slope_rows(z, normed, curve, loss, backs, seq, blocks):
    tokens, width = normed.shape
    half = blocks // 2
    height = 2 * (width // blocks // LANES) // 8 * 8 + 8
    queries = tokens // seq
    group = 8 if queries % 8 == 0 else queries
    step_tokens = group * seq
    whole = lambda dims: pl.BlockSpec(dims, lambda i: (0, 0))
    return pl.pallas_call(
        functools.partial(slope_kernel, seq, blocks),
        grid=(queries // group,),
        out_shape=[shape((height, LANES), F32)] * half,
        in_specs=[
            SMEM,
            pl.BlockSpec((step_tokens, width), lambda i: (i, 0)),
            pl.BlockSpec((step_tokens, 1), lambda i: (i, 0)),
            whole((1, LANES)),
        ]
        + [whole((queries, width // half))] * half,
        out_specs=[whole((height, LANES))] * half,
        scratch_shapes=[pltpu.VMEM((queries, width), F32), pltpu.VMEM((8, width), F32)],
        cost_estimate=pl.CostEstimate(
            flops=4 * tokens * width, bytes_accessed=2 * tokens * width, transcendentals=0
        ),
        compiler_params=pltpu.CompilerParams(vmem_limit_bytes=20 * MIB),
        name="slope_rows",
    )(z, normed, curve, loss, *backs)


def columns_kernel(n, order_ref, grads_ref, *refs):
    pieces, (out_ref, sorted_ref) = refs[:n], refs[n:]
    chunk = grads_ref.shape[1]
    for j in range(sorted_ref.shape[0] // chunk):
        sorted_ref[j * chunk : (j + 1) * chunk, :] = grads_ref[order_ref[j]]
    at = pieces[0].shape[0]
    total = tn(sorted_ref[0:at, :], pieces[0][...])
    for piece in pieces[1:]:
        rows = piece.shape[0]
        total = total + tn(sorted_ref[at : at + rows, :], piece[...])
        at += rows
    out_ref[...] = total.T.astype(BF16)


def query_kernel(side_ref, weight_ref, mirror_ref, parts_ref, part_ref, slope_ref, loss_ref):
    depth = weight_ref.shape[0]
    lines = depth // LANES
    total = parts_ref[...]
    loss_ref[...] = total[2 * lines : 2 * lines + 1]
    side = side_ref[0]
    part = jnp.zeros(part_ref.shape, F32)
    for j in range(2):
        rows = total[j * lines : (j + 1) * lines]
        row = jnp.concatenate([rows[k : k + 1] for k in range(lines)], axis=1)
        high, low = split_bf16(jnp.broadcast_to(row, (8, depth)))

        @pl.when(side == j)
        def _():
            slope_ref[...] = rows

        weight = jnp.where(side == j, weight_ref[...], mirror_ref[...])
        part = part + jnp.dot(high, weight, preferred_element_type=F32)[0:1]
        part = part + jnp.dot(low, weight, preferred_element_type=F32)[0:1]
    part_ref[...] = part


def finish_kernel(n, place_ref, pool_ref, slope_ref, *refs):
    pieces, out_ref, token_ref = refs[:n], refs[-2], refs[-1]
    token_ref[...] = jnp.zeros_like(token_ref)
    places = place_ref.shape[0]
    rows, cols = out_ref.shape[0], pieces[0].shape[1]
    for line in range(rows // LANES):
        part = slice(line * LANES, (line + 1) * LANES)
        slope = jnp.broadcast_to(slope_ref[line : line + 1, :], (LANES, LANES)).T
        for k in range(places):
            base = k % (places // n) * rows + line * LANES
            mine = pieces[k // (places // n)][base : base + LANES, :].astype(F32)
            at = pl.ds(pl.multiple_of(place_ref[k] * cols, LANES), cols)
            out_ref[part, at] = mine + slope * pool_ref[:, at]


def body(hidden_states, positives, negatives, lengths, norm_gain, proj_weight, pool_query, slab):
    queries, seq, width = hidden_states.shape
    depth, proj_width = proj_weight.shape
    n_z, n_g, n_i = lax.axis_size("fsdp"), lax.axis_size("grp"), lax.axis_size("item")
    assert n_z % 2 == 0
    half = n_z // 2
    n_c = 2 if n_i % 2 == 0 else 1
    n_h = n_i // n_c
    n_plane = n_g * n_i
    n_all = n_z * n_plane
    z, g, i = lax.axis_index("fsdp"), lax.axis_index("grp"), lax.axis_index("item")
    h, c = i // n_c, lax.rem(i, n_c)
    side, member = z // half, lax.rem(z, half)
    root = math.sqrt(proj_width)
    steps_z, steps_i = range(1, n_z), range(1, n_i)

    def ints(*values):
        return jnp.stack([jnp.asarray(v, jnp.int32) for v in values])

    z_arr, side_arr = ints(z), ints(side)

    def plane_shift(values, dg, dh, dc):
        pairs = []
        for pg in range(n_g):
            for ph in range(n_h):
                for pc in range(n_c):
                    to = ((pg + dg) % n_g) * n_i + ((ph + dh) % n_h) * n_c + (pc + dc) % n_c
                    pairs.append((pg * n_i + ph * n_c + pc, to))
        return lax.ppermute(values, PLANE, pairs)

    def half_shift(values, k):
        pairs = [(a, a // half * half + (a % half + k) % half) for a in range(n_z)]
        return lax.ppermute(values, "fsdp", pairs)

    def mirror_shift(values):
        return lax.ppermute(values, "fsdp", [(a, (a + half) % n_z) for a in range(n_z)])

    def source(dg, dh, dc):
        return (
            lax.rem(g - dg + n_g, n_g),
            lax.rem(h - dh + n_h, n_h) * n_c + lax.rem(c - dc + n_c, n_c),
        )

    chips = [(dg, dh) for dg in range(n_g) for dh in range(n_h)]

    share = depth // n_plane
    place = g * n_i + i
    weight_share = lax.dynamic_slice_in_dim(proj_weight, place * share, share, 0)
    far_share = mirror_shift(weight_share)

    block_u = call(
        u_kernel, [shape((1, depth), F32)], [proj_weight, pool_query.reshape(1, -1)], "block_u",
        after=[weight_share],
    )[0]
    u_parts = [block_u] + [shift(block_u, "fsdp", k) for k in steps_z]
    u = jnp.zeros((1, width), F32)
    for k in range(n_z):
        u = lax.dynamic_update_slice(u, u_parts[k], (0, lax.rem(z - k + n_z, n_z) * depth))

    share_places = []
    for dc in range(n_c):
        for dg, dh in chips:
            from_g, from_i = source(dg, dh, dc)
            share_places.append(from_g * n_i + from_i)
    share_places = ints(*share_places)
    order = []
    for dc in range(n_c):
        for dg in range(n_g):
            order += [(side, k, dg, dh, dc) for dh in range(n_h) for k in range(half)]
        for dh in range(n_h):
            order += [(1 - side, k, dg, dh, dc) for dg in range(n_g) for k in range(half)]
    ranks = []
    for from_side, k, dg, dh, dc in order:
        from_g, from_i = source(dg, dh, dc)
        from_z = from_side * half + lax.rem(member - k + half, half)
        ranks.append((from_z * n_g + from_g) * n_i + from_i)
    ranks = ints(*ranks)
    both_arr, base_arr = ints(z, i), ints(i * slab.shape[0])
    token_lengths = jnp.broadcast_to(lengths[:, None], (queries, seq)).reshape(-1, 1)
    events = [far_share, share_places, ranks, base_arr, side_arr]
    chip_shares = [far_share if dg == dh == 0 else plane_shift(far_share, dg, dh, 0) for dg, dh in chips]
    gate_outs = gate_rows(
        both_arr, hidden_states.reshape(-1, width), norm_gain.astype(F32).reshape(1, width), u,
        token_lengths, negatives, events, seq, root, n_z, n_i,
    )
    sends, (normed, gated, curve), lists = gate_outs[:half], gate_outs[half : half + 3], gate_outs[half + 3 :]
    packs = [pack(chip_shares, "pack_shares", gated)]
    packs += [plane_shift(packs[0], 0, 0, dc) for dc in range(1, n_c)]

    pieces = [sends[0]] + [half_shift(sends[k], k) for k in range(1, half)]
    lists = [lists[0]] + [shift(lists[k], "item", k) for k in steps_i]
    counts, slab_scale = call(
        functools.partial(count_kernel, n_i, root),
        [shape((n_i * queries, slab.shape[0]), F32), shape((1, slab.shape[0]), F32)],
        [base_arr, slab] + lists, "list_counts", smem=1,
    )
    block = shape((half * queries, depth), BF16)
    *parts, mirror, held, away = call(
        functools.partial(forward_kernel, half, n_c),
        [shape((queries, proj_width), F32)]
        + [shape((queries, proj_width), BF16)] * (half - 1)
        + [shape((depth, proj_width), BF16), block, block],
        [side_arr, share_places, proj_weight] + pieces + packs, "forward",
        flops=4 * half * queries * depth * proj_width, smem=2, after=[counts],
    )
    parts = [parts[0]] + [half_shift(parts[k], -k) for k in range(1, half)]
    near = [held] + [plane_shift(held, 0, dh, 0) for dh in range(1, n_h)]
    row = shape((queries, proj_width), F32)
    row16 = shape((queries, proj_width), BF16)
    pooled, unit, embedded, near, away = call(
        functools.partial(embed_kernel, root, half),
        [row, shape((queries, 1), F32), row16, shape((n_h * half * queries, depth), BF16), block],
        parts + [away] + near, "embed",
    )
    other = mirror_shift(away)

    pieces = [embedded] + [shift(embedded, "item", k) for k in steps_i]
    near_far = [plane_shift(near, dg, 0, 0) for dg in range(1, n_g)]
    near_cores = [plane_shift(near, 0, 0, dc) for dc in range(1, n_c)]
    wide = (queries, proj_width + LANES)
    parts = call(
        functools.partial(contrast_kernel, n_i),
        [shape(wide, F32)] + [shape(wide, BF16)] * (n_i - 1),
        [slab, slab_scale, counts] + pieces, "contrast",
        flops=4 * n_i * queries * slab.shape[0] * proj_width, after=near_cores,
    )
    near_far_late = [passed(array, "near_far", parts[0]) for array in near_far]
    parts = [parts[0]] + [shift(parts[k], "item", -k) for k in steps_i]
    near_far_cores = [[plane_shift(array, 0, 0, dc) for array in near_far_late] for dc in range(1, n_c)]
    other = passed(other, "other", parts[1 % n_i])
    others = [other] + [plane_shift(other, dg, 0, 0) for dg in range(1, n_g)]
    cols = proj_width // n_plane
    grad, grad_columns, loss = call(
        functools.partial(grad_kernel, n_i, root),
        [row16, shape((n_all, queries, cols), BF16), shape((1, LANES), F32)],
        [positives, pooled, unit, embedded] + parts, "grad_pooled",
    )

    pieces = [grad] + [half_shift(grad, k) for k in range(1, half)]
    *backs, others = call(
        functools.partial(back_kernel, half, n_g),
        [shape((queries, 2 * depth), BF16)] * half + [shape((n_g * half * queries, depth), BF16)],
        [side_arr, proj_weight, mirror] + pieces + others, "backward",
        flops=4 * half * queries * depth * proj_width, smem=1, after=near_cores + sum(near_far_cores, []),
    )
    backs = [backs[0]] + [half_shift(backs[k], -k) for k in range(1, half)]
    all_columns = lax.all_to_all(
        passed(grad_columns, "columns_out", backs[-1]), EVERY, 0, 0, tiled=True
    )
    slopes = slope_rows(both_arr, normed, curve, loss, backs, seq, n_z)
    def total(parts, name):
        return call(add_kernel, [shape(parts[0].shape, F32)], parts, name)[0]

    slope = total([slopes[0]] + [half_shift(slopes[k], k) for k in range(1, half)], "sum_half")
    across = [plane_shift(others, 0, dh, 0) for dh in range(1, n_h)]
    late = [pack([array], "late", slopes[0]) for array in across]
    spread = []
    for dc in range(n_c):
        if dc == 0:
            spread += [near, *near_far, others, *across]
        else:
            spread += [near_cores[dc - 1], *near_far_cores[dc - 1]]
            spread += [plane_shift(array, 0, 0, dc) for array in [others, *late]]
    block_columns = call(
        functools.partial(columns_kernel, len(spread)), [shape((depth, cols), BF16)],
        [ranks, all_columns] + spread, "grad_columns",
        flops=2 * n_all * queries * depth * cols, scratch=[pltpu.VMEM((n_all * queries, cols), BF16)], smem=1, copy=True, after=[slope],
    )[0]
    on_chips = [block_columns if dg == dh == 0 else plane_shift(block_columns, dg, dh, 0) for dg, dh in chips]
    slope = passed(slope, "slope_out", block_columns)
    slope = total([slope, mirror_shift(slope)], "sum_mirror")
    for axis, size in ((0, n_g), (1, n_h), (2, n_c)):
        if size > 1:
            moves = [[k if a == axis else 0 for a in range(3)] for k in range(1, size)]
            slope = total([slope] + [plane_shift(slope, *move) for move in moves], "sum_plane")
    query_part, my_slope, loss_total = call(
        query_kernel,
        [shape((1, proj_width), F32), shape((depth // LANES, LANES), F32), shape((1, LANES), F32)],
        [side_arr, proj_weight, mirror, slope], "slope_sum", smem=1,
    )
    finished = [pack(on_chips, "pack_columns", slope)]
    finished += [plane_shift(finished[0], 0, 0, dc) for dc in range(1, n_c)]
    query_parts = [query_part] + [half_shift(query_part, k) for k in range(1, half)]
    grad_proj, finish_token = call(
        functools.partial(finish_kernel, len(finished)),
        [shape((depth, proj_width), F32), shape((8, LANES), F32)],
        [share_places, pool_query.reshape(1, -1), my_slope] + finished, "finish", smem=1,
    )
    grad_query = call(
        add_kernel, [shape((1, proj_width), F32)], query_parts, "query_sum", after=[finish_token]
    )[0]
    mean_loss = loss_total[0, 0] / (queries * n_all)
    return (grad_proj, grad_query.reshape(proj_width), mean_loss)


def solution(mesh):
    return jax.shard_map(
        body,
        mesh=mesh,
        in_specs=(
            P(("grp", "fsdp", "item"), None, None),
            P(("grp", "fsdp", "item"), None),
            P(("grp", "fsdp", "item"), None),
            P(("grp", "fsdp", "item")),
            P(),
            P("fsdp", None),
            P(),
            P("item", None),
        ),
        out_specs=(P("fsdp", None), P(), P()),
        check_vma=False,
    )
```

```python
import functools
import math

import jax
import jax.numpy as jnp
from jax import lax
from jax.experimental import pallas as pl
from jax.experimental.pallas import tpu as pltpu
from jax.sharding import PartitionSpec as P

sharpness_divisor = 0.05
norm_eps = 1e-05
embed_eps = 1e-06

EVERY = ("fsdp", "grp", "item")
PLANE = ("grp", "item")
F32 = jnp.float32
BF16 = jnp.bfloat16
LANES = 128
MIB = 1024 * 1024
VMEM = pl.BlockSpec(memory_space=pltpu.VMEM)
SMEM = pl.BlockSpec(memory_space=pltpu.SMEM)


def shape(dims, dtype):
    return jax.ShapeDtypeStruct(dims, dtype)


def copying(kernel, smem, shapes):
    n = len(shapes)

    def run(*refs):
        sources, buffers, sems = refs[smem : smem + n], refs[-n - 1 : -1], refs[-1]
        copies = [
            pltpu.make_async_copy(sources[k], buffers[k], sems.at[k]) for k in range(n)
        ]
        for copy in copies:
            copy.start()
        for copy in copies:
            copy.wait()
        kernel(*refs[:smem], *buffers, *refs[smem + n : -n - 1])

    return run


def call(kernel, outs, ins, name, flops=0, scratch=(), smem=0, after=(), copy=False, streamed=False):
    count = len(ins)
    if copy:
        shapes = [pltpu.VMEM(a.shape, a.dtype) for a in ins[smem:]]
        kernel = copying(kernel, smem, shapes)
        scratch = [*scratch, *shapes, pltpu.SemaphoreType.DMA((len(shapes),))]
    moved = sum(math.prod(a.shape) * a.dtype.itemsize for a in list(ins) + list(outs))
    held = 0 if copy or streamed else sum(math.prod(s.shape) * jnp.dtype(s.dtype).itemsize for s in scratch)

    def run(*refs):
        kernel(*refs[:count], *refs[count + len(after) :])

    return pl.pallas_call(
        run,
        out_shape=outs,
        in_specs=[SMEM] * smem
        + [pl.BlockSpec(memory_space=pl.ANY) if copy else VMEM] * (count - smem)
        + [pl.BlockSpec(memory_space=pl.ANY)] * len(after),
        out_specs=([pl.BlockSpec(memory_space=pl.ANY)] if streamed else [VMEM]) + [VMEM] * (len(outs) - 1),
        scratch_shapes=list(scratch),
        cost_estimate=pl.CostEstimate(flops=flops, bytes_accessed=moved, transcendentals=0),
        compiler_params=pltpu.CompilerParams(
            vmem_limit_bytes=61 * MIB if copy else 2 * (moved + held) + 6 * MIB
        ),
        name=name,
    )(*ins, *after)


def shift(values, axis, k):
    n = lax.axis_size(axis)
    return lax.ppermute(values, axis, [(i, (i + k) % n) for i in range(n)])


def split_bf16(values):
    high = values.astype(BF16)
    low = (values - high.astype(F32)).astype(BF16)
    return high, low


def nt(left, right):
    return lax.dot_general(left, right, (((1,), (1,)), ((), ())), preferred_element_type=F32)


def tn(left, right):
    return lax.dot_general(left, right, (((0,), (0,)), ((), ())), preferred_element_type=F32)


def u_kernel(weight_ref, pool_ref, u_ref):
    pool = jnp.broadcast_to(pool_ref[...], (8, pool_ref.shape[1]))
    high = pool.astype(BF16)
    low, last = split_bf16(pool - high.astype(F32))
    weight = weight_ref[...]
    u_ref[...] = (nt(high, weight) + nt(low, weight) + nt(last, weight))[0:1]


def gate_kernel(seq, root, blocks, z_ref, states_ref, gain_ref, u_ref, len_ref, lists_ref, *rest):
    half = blocks // 2
    outs, normed_ref, gated_ref, curve_ref, copies, rows_ref = (
        rest[:half], rest[half], rest[half + 1], rest[half + 2], rest[half + 3 : -1], rest[-1]
    )
    step = pl.program_id(0)
    tokens, width = states_ref.shape
    count = tokens // seq
    chunk = 4 * LANES if width % (4 * LANES) == 0 else width
    logits = []
    for top in range(0, tokens, 32):
        rows = slice(top, top + 32)
        squares = jnp.zeros((32, chunk), F32)
        for at in range(0, width, chunk):
            part = states_ref[rows, at : at + chunk].astype(F32)
            squares = squares + part * part
        inv_rms = lax.rsqrt(jnp.sum(squares, axis=1, keepdims=True) / width + norm_eps)
        total = jnp.zeros((32, chunk), F32)
        for at in range(0, width, chunk):
            part = states_ref[rows, at : at + chunk].astype(F32)
            part = (part * inv_rms * gain_ref[:, at : at + chunk]).astype(BF16)
            normed_ref[rows, at : at + chunk] = part
            total = total + part.astype(F32) * u_ref[:, at : at + chunk]
        logits.append(jnp.sum(total, axis=1, keepdims=True))
    logit = jnp.concatenate(logits, axis=0) / root
    gate = 1.0 / (1.0 + jnp.exp(-logit))
    slot = lax.rem(lax.broadcasted_iota(jnp.int32, (tokens, 1), 0), seq)
    valid = jnp.where(slot < len_ref[...], 1.0, 0.0) / len_ref[...].astype(F32)
    gated = valid * gate
    gated_ref[...] = gated
    curve_ref[...] = gated * (1.0 - gate) / root
    owner = lax.broadcasted_iota(jnp.int32, (tokens, count), 0) // seq
    mine = owner == lax.broadcasted_iota(jnp.int32, (tokens, count), 1)
    high, low = split_bf16(jnp.where(mine, gated, 0.0))
    both = tn(jnp.concatenate([high, low], axis=1), normed_ref[...])
    rows_ref[pl.ds(pl.multiple_of(step * count, count), count), :] = both[:count] + both[count:]

    @pl.when(step == pl.num_programs(0) - 1)
    def _():
        owners = len(copies)
        own = lists_ref.shape[1] // owners
        for k in range(owners):
            picked = jnp.zeros(copies[k].shape, jnp.int32)
            for j in range(owners):
                picked = jnp.where(
                    lax.rem(z_ref[1] + k, owners) == j, lists_ref[:, j * own : (j + 1) * own], picked
                )
            copies[k][...] = picked
        depth = width // blocks
        place = lax.rem(z_ref[0], half)
        for k in range(half):
            for j in range(2):
                at = (j * half + lax.rem(place + k, half)) * depth
                outs[k][:, j * depth : (j + 1) * depth] = rows_ref[
                    :, pl.ds(pl.multiple_of(at, LANES), depth)
                ].astype(BF16)


def gate_rows(z, states, gain, u, token_lengths, lists, events, seq, root, blocks, owners):
    tokens, width = states.shape
    queries = tokens // seq
    group = 16 if queries % 16 == 0 else queries
    step_tokens = group * seq
    half = blocks // 2
    outs = [shape((queries, width // half), BF16)] * half
    outs += [shape((tokens, width), BF16)] + [shape((tokens, 1), F32)] * 2
    outs += [shape((queries, lists.shape[1] // owners), lists.dtype)] * owners
    column = pl.BlockSpec((step_tokens, 1), lambda i: (i, 0))
    rows = pl.BlockSpec((step_tokens, width), lambda i: (i, 0))
    inputs = [z, states, gain, u, token_lengths, lists]

    def run(*refs):
        gate_kernel(seq, root, blocks, *refs[: len(inputs)], *refs[len(inputs) + len(events) :])

    whole = lambda dims: pl.BlockSpec(dims, lambda i: (0, 0))
    return pl.pallas_call(
        run,
        grid=(queries // group,),
        out_shape=outs,
        in_specs=[
            SMEM,
            rows,
            whole((1, width)),
            whole((1, width)),
            column,
            whole(lists.shape),
        ]
        + [pl.BlockSpec(memory_space=pl.ANY)] * len(events),
        out_specs=[whole((queries, width // half))] * half + [rows] + [column] * 2
        + [whole((queries, lists.shape[1] // owners))] * owners,
        scratch_shapes=[pltpu.VMEM((queries, width), F32)],
        cost_estimate=pl.CostEstimate(
            flops=10 * tokens * width, bytes_accessed=4 * tokens * width, transcendentals=0
        ),
        compiler_params=pltpu.CompilerParams(vmem_limit_bytes=50 * MIB),
        name="gate_rows",
    )(*inputs, *events)


def pack_kernel(*refs):
    rows = refs[0].shape[0]
    for k, ref in enumerate(refs[:-1]):
        refs[-1][k * rows : (k + 1) * rows, :] = ref[...]


def pack_copies(n, *refs):
    out_ref, sems = refs[-2], refs[-1]
    rows = refs[0].shape[0]
    copies = [
        pltpu.make_async_copy(refs[k], out_ref.at[pl.ds(k * rows, rows), :], sems.at[k]) for k in range(n)
    ]
    for copy in copies:
        copy.start()
    for copy in copies:
        copy.wait()


def pack(pieces, name, event, copy=False):
    rows, width = pieces[0].shape
    n = len(pieces)
    out = shape((n * rows, width), pieces[0].dtype)
    if copy:
        anywhere = pl.BlockSpec(memory_space=pl.ANY)
        return pl.pallas_call(
            functools.partial(pack_copies, n),
            out_shape=out,
            in_specs=[anywhere] * (n + 1),
            out_specs=anywhere,
            scratch_shapes=[pltpu.SemaphoreType.DMA((n,))],
            cost_estimate=pl.CostEstimate(flops=0, bytes_accessed=4 * n * rows * width, transcendentals=0),
            compiler_params=pltpu.CompilerParams(vmem_limit_bytes=4 * MIB),
            name=name,
        )(*pieces, event)
    return call(pack_kernel, [out], pieces, name, after=[event])[0]


def pass_kernel(from_ref, to_ref):
    to_ref[...] = from_ref[...]


def passed(values, name, event):
    return call(pass_kernel, [shape(values.shape, values.dtype)], [values], name, after=[event])[0]


def add_kernel(*refs):
    total = refs[0][...]
    for ref in refs[1:-1]:
        total = total + ref[...]
    refs[-1][...] = total


def forward_kernel(n, packs, side_ref, places_ref, weight_ref, *refs):
    refs = refs[:n] + (weight_ref,) + refs[n:]
    pieces, shares = refs[:n], refs[n + 1 : n + 1 + packs]
    outs = refs[n + 1 + packs : 2 * n + 1 + packs]
    mirror_ref, held_ref, away_ref = refs[2 * n + 1 + packs :]
    rows = pieces[0].shape[0]
    depth = weight_ref.shape[0]
    side = side_ref[0]
    for k in range(n):
        part = slice(k * rows, (k + 1) * rows)
        held_ref[part, :] = pieces[k][:, pl.ds(pl.multiple_of(side * depth, LANES), depth)]
        away_ref[part, :] = pieces[k][:, pl.ds(pl.multiple_of((1 - side) * depth, LANES), depth)]
    count = places_ref.shape[0] // packs
    share = shares[0].shape[0] // count
    for p in range(packs):
        for j in range(count):
            at = pl.multiple_of(places_ref[p * count + j] * share, share)
            mirror_ref[pl.ds(at, share), :] = shares[p][j * share : (j + 1) * share, :]
    product = jnp.dot(held_ref[...], weight_ref[...], preferred_element_type=F32)
    product = product + jnp.dot(away_ref[...], mirror_ref[...], preferred_element_type=F32)
    for k in range(n):
        outs[k][...] = product[k * rows : (k + 1) * rows].astype(outs[k].dtype)


def back_kernel(n, packed, side_ref, weight_ref, mirror_ref, *refs):
    pieces, outs = refs[:n], refs[n + packed : -1]
    pack_kernel(*refs[n : n + packed], refs[-1])
    rows = pieces[0].shape[0]
    depth = weight_ref.shape[0]
    side = side_ref[0]
    stack = jnp.concatenate([p[...] for p in pieces], axis=0)
    own = nt(stack, weight_ref[...]).astype(BF16)
    mirror = nt(stack, mirror_ref[...]).astype(BF16)
    for k in range(n):
        part = slice(k * rows, (k + 1) * rows)
        outs[k][:, pl.ds(pl.multiple_of(side * depth, LANES), depth)] = own[part]
        outs[k][:, pl.ds(pl.multiple_of((1 - side) * depth, LANES), depth)] = mirror[part]


def embed_kernel(root, n, *refs):
    parts, away_ref, packed = refs[:n], refs[n], refs[n + 1 : -5]
    pooled_ref, unit_ref, embedded_ref, pack_ref, pass_ref = refs[-5:]
    pass_ref[...] = away_ref[...]
    pooled = parts[0][...]
    for part in parts[1:]:
        pooled = pooled + part[...].astype(F32)
    unit = lax.rsqrt(jnp.mean(pooled * pooled, axis=1, keepdims=True) + embed_eps) / root
    pooled_ref[...] = pooled
    unit_ref[...] = unit
    embedded_ref[...] = (pooled * unit).astype(BF16)
    pack_kernel(*packed, pack_ref)


def count_kernel(n, root, base_ref, slab_ref, *refs):
    lists, counts_ref, scale_ref = refs[:n], refs[n], refs[n + 1]
    queries = lists[0].shape[0]
    rows, width = slab_ref.shape
    slab = slab_ref[...].astype(F32)
    high, low = split_bf16(slab * slab)
    ones = jnp.ones((8, width), BF16)
    row_sq = (nt(ones, high) + nt(ones, low))[0:1]
    scale_ref[...] = lax.rsqrt(row_sq / width + embed_eps) / root / sharpness_divisor
    ids = lax.broadcasted_iota(jnp.int32, (queries, LANES), 1)
    for k in range(n):
        own = lists[k][...] - base_ref[0]
        columns = [
            jnp.broadcast_to(own[:, entry : entry + 1], (queries, LANES)) for entry in range(own.shape[1])
        ]
        for at in range(0, rows, LANES):
            total = jnp.zeros(ids.shape, F32)
            for column in columns:
                total = total + jnp.where(column == ids + at, 1.0, 0.0)
            counts_ref[k * queries : (k + 1) * queries, at : at + LANES] = total


def contrast_kernel(n, *refs):
    (slab_ref, scale_ref, counts_ref), pieces, outs = refs[:3], refs[3 : n + 3], refs[n + 3 :]
    queries, width = pieces[0].shape
    embedded = jnp.concatenate([p[...] for p in pieces], axis=0)
    slab = slab_ref[...]
    scale = scale_ref[...]
    heavy = counts_ref[...] * jnp.exp(nt(embedded, slab) * scale)
    denom = jnp.sum(heavy, axis=1, keepdims=True)
    grad = jnp.dot((heavy * scale).astype(BF16), slab, preferred_element_type=F32)
    high, low = split_bf16(denom)
    lane = lax.broadcasted_iota(jnp.int32, (queries, LANES), 1)
    for k in range(n):
        part = slice(k * queries, (k + 1) * queries)
        outs[k][:, :width] = grad[part].astype(outs[k].dtype)
        if k == 0:
            tail = jnp.where(lane == 0, denom[part], 0.0)
        else:
            tail = jnp.where(lane == 0, high[part].astype(F32), jnp.where(lane == 1, low[part].astype(F32), 0.0))
        outs[k][:, width:] = tail.astype(outs[k].dtype)


def grad_kernel(n, root, *refs):
    pos_ref, pooled_ref, unit_ref, embedded_ref = refs[:4]
    parts = refs[4 : n + 4]
    grad_ref, columns_ref, loss_ref = refs[n + 4 :]
    queries, width = pos_ref.shape
    total = parts[0][:, :width]
    denom = jnp.sum(parts[0][:, width:], axis=1, keepdims=True)
    for part in parts[1:]:
        total = total + part[:, :width].astype(F32)
        denom = denom + jnp.sum(part[:, width:].astype(F32), axis=1, keepdims=True)
    positive = pos_ref[...].astype(F32)
    scale = (
        lax.rsqrt(jnp.mean(positive * positive, axis=1, keepdims=True) + embed_eps)
        / root
        / sharpness_divisor
    )
    score = jnp.sum(embedded_ref[...].astype(F32) * positive, axis=1, keepdims=True) * scale
    pos_exp = jnp.exp(score)
    denom = denom + pos_exp
    loss_ref[...] = jnp.broadcast_to(jnp.sum(jnp.log(denom) - score), loss_ref.shape)
    grad_embed = total / denom + (pos_exp / denom - 1.0) * scale * positive
    pooled, unit = pooled_ref[...], unit_ref[...]
    mean_sq = jnp.mean(pooled * pooled, axis=1, keepdims=True)
    radial = jnp.sum(pooled * grad_embed, axis=1, keepdims=True)
    grad = unit * grad_embed - pooled * (radial * unit / (width * (mean_sq + embed_eps)))
    grad = grad.astype(BF16)
    grad_ref[...] = grad
    cols = columns_ref.shape[2]
    places = width // cols
    for j in range(columns_ref.shape[0]):
        at = (j % places) * cols
        columns_ref[j] = grad[:, at : at + cols]


def slope_kernel(seq, blocks, z_ref, normed_ref, curve_ref, loss_ref, *rest):
    half = blocks // 2
    backs, outs, (all_ref, sum_ref) = rest[:half], rest[half : 2 * half], rest[-2:]
    step = pl.program_id(0)
    tokens, width = normed_ref.shape
    count = tokens // seq
    depth = width // blocks
    place = lax.rem(z_ref[0], half)

    def block_at(j, k):
        return pl.ds(pl.multiple_of((j * half + lax.rem(place + k, half)) * depth, LANES), depth)

    @pl.when(step == 0)
    def _():
        sum_ref[...] = jnp.zeros_like(sum_ref)
        for k in range(half):
            for j in range(2):
                all_ref[:, block_at(j, k)] = backs[k][:, j * depth : (j + 1) * depth].astype(F32)

    back = all_ref[pl.ds(pl.multiple_of(step * count, count), count), :]
    normed = normed_ref[...].astype(F32).reshape(count, seq, width)
    dots = jnp.sum(normed * back[:, None, :], axis=2, keepdims=True)
    slope = curve_ref[...].reshape(count, seq, 1) * dots
    heavy = (slope * normed).reshape(tokens // 8, 8, width)
    sum_ref[...] += jnp.sum(heavy, axis=0)

    @pl.when(step == pl.num_programs(0) - 1)
    def _():
        total = jnp.sum(sum_ref[...], axis=0, keepdims=True)
        lines = depth // LANES
        height = outs[0].shape[0]
        loss = jnp.broadcast_to(loss_ref[...], (height - 2 * lines, LANES))
        all_ref[0:1, :] = total
        for k in range(half):
            for j in range(2):
                row = all_ref[0:1, block_at(j, k)]
                for line in range(lines):
                    outs[k][j * lines + line : j * lines + line + 1, :] = row[
                        :, line * LANES : (line + 1) * LANES
                    ]
            outs[k][2 * lines :, :] = loss


def slope_rows(z, normed, curve, loss, backs, seq, blocks):
    tokens, width = normed.shape
    half = blocks // 2
    height = 2 * (width // blocks // LANES) // 8 * 8 + 8
    queries = tokens // seq
    group = 8 if queries % 8 == 0 else queries
    step_tokens = group * seq
    whole = lambda dims: pl.BlockSpec(dims, lambda i: (0, 0))
    return pl.pallas_call(
        functools.partial(slope_kernel, seq, blocks),
        grid=(queries // group,),
        out_shape=[shape((height, LANES), F32)] * half,
        in_specs=[
            SMEM,
            pl.BlockSpec((step_tokens, width), lambda i: (i, 0)),
            pl.BlockSpec((step_tokens, 1), lambda i: (i, 0)),
            whole((1, LANES)),
        ]
        + [whole((queries, width // half))] * half,
        out_specs=[whole((height, LANES))] * half,
        scratch_shapes=[pltpu.VMEM((queries, width), F32), pltpu.VMEM((8, width), F32)],
        cost_estimate=pl.CostEstimate(
            flops=4 * tokens * width, bytes_accessed=2 * tokens * width, transcendentals=0
        ),
        compiler_params=pltpu.CompilerParams(vmem_limit_bytes=20 * MIB),
        name="slope_rows",
    )(z, normed, curve, loss, *backs)


def columns_kernel(n, order_ref, grads_ref, *refs):
    pieces, (out_ref, sorted_ref) = refs[:n], refs[n:]
    chunk = grads_ref.shape[1]
    for j in range(sorted_ref.shape[0] // chunk):
        sorted_ref[j * chunk : (j + 1) * chunk, :] = grads_ref[order_ref[j]]
    at = pieces[0].shape[0]
    total = tn(sorted_ref[0:at, :], pieces[0][...])
    for piece in pieces[1:]:
        rows = piece.shape[0]
        total = total + tn(sorted_ref[at : at + rows, :], piece[...])
        at += rows
    out_ref[...] = total.T.astype(BF16)


def query_kernel(side_ref, weight_ref, mirror_ref, parts_ref, part_ref, slope_ref, loss_ref):
    depth = weight_ref.shape[0]
    lines = depth // LANES
    total = parts_ref[...]
    loss_ref[...] = total[2 * lines : 2 * lines + 1]
    side = side_ref[0]
    part = jnp.zeros(part_ref.shape, F32)
    for j in range(2):
        rows = total[j * lines : (j + 1) * lines]
        row = jnp.concatenate([rows[k : k + 1] for k in range(lines)], axis=1)
        high, low = split_bf16(jnp.broadcast_to(row, (8, depth)))

        @pl.when(side == j)
        def _():
            slope_ref[...] = rows

        weight = jnp.where(side == j, weight_ref[...], mirror_ref[...])
        part = part + jnp.dot(high, weight, preferred_element_type=F32)[0:1]
        part = part + jnp.dot(low, weight, preferred_element_type=F32)[0:1]
    part_ref[...] = part


def finish_kernel(n, place_ref, pool_ref, slope_ref, *refs):
    pieces, result_ref, token_ref, out_ref, sems = refs[:n], *refs[n:]
    token_ref[...] = jnp.zeros_like(token_ref)
    places = place_ref.shape[0]
    rows, cols = out_ref.shape[0], pieces[0].shape[1]
    copies = []
    for line in range(rows // LANES):
        part = pl.ds(line * LANES, LANES)
        slope = jnp.broadcast_to(slope_ref[line : line + 1, :], (LANES, LANES)).T
        for k in range(places):
            base = k % (places // n) * rows + line * LANES
            mine = pieces[k // (places // n)][base : base + LANES, :].astype(F32)
            at = pl.ds(pl.multiple_of(place_ref[k] * cols, LANES), cols)
            out_ref[part, at] = mine + slope * pool_ref[:, at]
        copies.append(
            pltpu.make_async_copy(out_ref.at[part, :], result_ref.at[part, :], sems.at[line])
        )
        copies[-1].start()
    for copy in copies:
        copy.wait()


def body(hidden_states, positives, negatives, lengths, norm_gain, proj_weight, pool_query, slab):
    queries, seq, width = hidden_states.shape
    depth, proj_width = proj_weight.shape
    n_z, n_g, n_i = lax.axis_size("fsdp"), lax.axis_size("grp"), lax.axis_size("item")
    assert n_z % 2 == 0
    half = n_z // 2
    n_c = 2 if n_i % 2 == 0 else 1
    n_h = n_i // n_c
    n_plane = n_g * n_i
    n_all = n_z * n_plane
    z, g, i = lax.axis_index("fsdp"), lax.axis_index("grp"), lax.axis_index("item")
    h, c = i // n_c, lax.rem(i, n_c)
    side, member = z // half, lax.rem(z, half)
    root = math.sqrt(proj_width)
    steps_z, steps_i = range(1, n_z), range(1, n_i)

    def ints(*values):
        return jnp.stack([jnp.asarray(v, jnp.int32) for v in values])

    z_arr, side_arr = ints(z), ints(side)

    def plane_shift(values, dg, dh, dc):
        pairs = []
        for pg in range(n_g):
            for ph in range(n_h):
                for pc in range(n_c):
                    to = ((pg + dg) % n_g) * n_i + ((ph + dh) % n_h) * n_c + (pc + dc) % n_c
                    pairs.append((pg * n_i + ph * n_c + pc, to))
        return lax.ppermute(values, PLANE, pairs)

    def half_shift(values, k):
        pairs = [(a, a // half * half + (a % half + k) % half) for a in range(n_z)]
        return lax.ppermute(values, "fsdp", pairs)

    def mirror_shift(values):
        return lax.ppermute(values, "fsdp", [(a, (a + half) % n_z) for a in range(n_z)])

    def source(dg, dh, dc):
        return (
            lax.rem(g - dg + n_g, n_g),
            lax.rem(h - dh + n_h, n_h) * n_c + lax.rem(c - dc + n_c, n_c),
        )

    chips = [(dg, dh) for dg in range(n_g) for dh in range(n_h)]

    share = depth // n_plane
    place = g * n_i + i
    weight_share = lax.dynamic_slice_in_dim(proj_weight, place * share, share, 0)
    far_share = mirror_shift(weight_share)

    block_u = call(
        u_kernel, [shape((1, depth), F32)], [proj_weight, pool_query.reshape(1, -1)], "block_u",
        after=[weight_share],
    )[0]
    u_parts = [block_u] + [shift(block_u, "fsdp", k) for k in steps_z]
    u = jnp.zeros((1, width), F32)
    for k in range(n_z):
        u = lax.dynamic_update_slice(u, u_parts[k], (0, lax.rem(z - k + n_z, n_z) * depth))

    share_places = []
    for dc in range(n_c):
        for dg, dh in chips:
            from_g, from_i = source(dg, dh, dc)
            share_places.append(from_g * n_i + from_i)
    share_places = ints(*share_places)
    order = []
    for dc in range(n_c):
        for dg in range(n_g):
            order += [(side, k, dg, dh, dc) for dh in range(n_h) for k in range(half)]
        for dh in range(n_h):
            order += [(1 - side, k, dg, dh, dc) for dg in range(n_g) for k in range(half)]
    ranks = []
    for from_side, k, dg, dh, dc in order:
        from_g, from_i = source(dg, dh, dc)
        from_z = from_side * half + lax.rem(member - k + half, half)
        ranks.append((from_z * n_g + from_g) * n_i + from_i)
    ranks = ints(*ranks)
    both_arr, base_arr = ints(z, i), ints(i * slab.shape[0])
    token_lengths = jnp.broadcast_to(lengths[:, None], (queries, seq)).reshape(-1, 1)
    events = [far_share, share_places, ranks, base_arr, side_arr]
    chip_shares = [far_share if dg == dh == 0 else plane_shift(far_share, dg, dh, 0) for dg, dh in chips]
    gate_outs = gate_rows(
        both_arr, hidden_states.reshape(-1, width), norm_gain.astype(F32).reshape(1, width), u,
        token_lengths, negatives, events, seq, root, n_z, n_i,
    )
    sends, (normed, gated, curve), lists = gate_outs[:half], gate_outs[half : half + 3], gate_outs[half + 3 :]
    packs = [pack(chip_shares, "pack_shares", gated)]
    packs += [plane_shift(packs[0], 0, 0, dc) for dc in range(1, n_c)]

    pieces = [sends[0]] + [half_shift(sends[k], k) for k in range(1, half)]
    lists = [lists[0]] + [shift(lists[k], "item", k) for k in steps_i]
    counts, slab_scale = call(
        functools.partial(count_kernel, n_i, root),
        [shape((n_i * queries, slab.shape[0]), F32), shape((1, slab.shape[0]), F32)],
        [base_arr, slab] + lists, "list_counts", smem=1,
    )
    block = shape((half * queries, depth), BF16)
    *parts, mirror, held, away = call(
        functools.partial(forward_kernel, half, n_c),
        [shape((queries, proj_width), F32)]
        + [shape((queries, proj_width), BF16)] * (half - 1)
        + [shape((depth, proj_width), BF16), block, block],
        [side_arr, share_places, proj_weight] + pieces + packs, "forward",
        flops=4 * half * queries * depth * proj_width, smem=2, after=[counts],
    )
    parts = [parts[0]] + [half_shift(parts[k], -k) for k in range(1, half)]
    near = [held] + [plane_shift(held, 0, dh, 0) for dh in range(1, n_h)]
    row = shape((queries, proj_width), F32)
    row16 = shape((queries, proj_width), BF16)
    pooled, unit, embedded, near, away = call(
        functools.partial(embed_kernel, root, half),
        [row, shape((queries, 1), F32), row16, shape((n_h * half * queries, depth), BF16), block],
        parts + [away] + near, "embed",
    )
    other = mirror_shift(away)

    pieces = [embedded] + [shift(embedded, "item", k) for k in steps_i]
    near_far = [plane_shift(near, dg, 0, 0) for dg in range(1, n_g)]
    near_cores = [plane_shift(near, 0, 0, dc) for dc in range(1, n_c)]
    wide = (queries, proj_width + LANES)
    parts = call(
        functools.partial(contrast_kernel, n_i),
        [shape(wide, F32)] + [shape(wide, BF16)] * (n_i - 1),
        [slab, slab_scale, counts] + pieces, "contrast",
        flops=4 * n_i * queries * slab.shape[0] * proj_width, after=near_cores,
    )
    near_far_late = [passed(array, "near_far", parts[0]) for array in near_far]
    parts = [parts[0]] + [shift(parts[k], "item", -k) for k in steps_i]
    near_far_cores = [[plane_shift(array, 0, 0, dc) for array in near_far_late] for dc in range(1, n_c)]
    other = passed(other, "other", parts[1 % n_i])
    others = [other] + [plane_shift(other, dg, 0, 0) for dg in range(1, n_g)]
    cols = proj_width // n_plane
    grad, grad_columns, loss = call(
        functools.partial(grad_kernel, n_i, root),
        [row16, shape((n_all, queries, cols), BF16), shape((1, LANES), F32)],
        [positives, pooled, unit, embedded] + parts, "grad_pooled",
    )

    pieces = [grad] + [half_shift(grad, k) for k in range(1, half)]
    *backs, others = call(
        functools.partial(back_kernel, half, n_g),
        [shape((queries, 2 * depth), BF16)] * half + [shape((n_g * half * queries, depth), BF16)],
        [side_arr, proj_weight, mirror] + pieces + others, "backward",
        flops=4 * half * queries * depth * proj_width, smem=1, after=near_cores + sum(near_far_cores, []),
    )
    backs = [backs[0]] + [half_shift(backs[k], -k) for k in range(1, half)]
    all_columns = lax.all_to_all(
        passed(grad_columns, "columns_out", backs[-1]), EVERY, 0, 0, tiled=True
    )
    slopes = slope_rows(both_arr, normed, curve, loss, backs, seq, n_z)
    def total(parts, name):
        return call(add_kernel, [shape(parts[0].shape, F32)], parts, name)[0]

    across = [plane_shift(others, 0, dh, 0) for dh in range(1, n_h)]
    late = [pack([array], "late", slopes[0]) for array in across]
    spread = []
    for dc in range(n_c):
        if dc == 0:
            spread += [near, *near_far, others, *across]
        else:
            spread += [near_cores[dc - 1], *near_far_cores[dc - 1]]
            spread += [plane_shift(array, 0, 0, dc) for array in [others, *late]]
    block_columns = call(
        functools.partial(columns_kernel, len(spread)), [shape((depth, cols), BF16)],
        [ranks, all_columns] + spread, "grad_columns",
        flops=2 * n_all * queries * depth * cols, scratch=[pltpu.VMEM((n_all * queries, cols), BF16)], smem=1, copy=True,
    )[0]
    on_chips = [block_columns if dg == dh == 0 else plane_shift(block_columns, dg, dh, 0) for dg, dh in chips]
    slopes = [passed(array, "slope_out", block_columns) for array in slopes]
    stage = [slopes[0]]
    for k in range(half):
        for flip in (0, 1):
            if k or flip:
                pairs = [(a, (a // half + flip) % 2 * half + (a % half + k) % half) for a in range(n_z)]
                stage.append(lax.ppermute(slopes[k], "fsdp", pairs))
    slope = total(stage, "sum_line")
    if n_g > 1:
        slope = total([slope] + [shift(slope, "grp", k) for k in range(1, n_g)], "sum_groups")
    if n_i > 1:
        slope = total([slope] + [shift(slope, "item", k) for k in steps_i], "sum_items")
    query_part, my_slope, loss_total = call(
        query_kernel,
        [shape((1, proj_width), F32), shape((depth // LANES, LANES), F32), shape((1, LANES), F32)],
        [side_arr, proj_weight, mirror, slope], "slope_sum", smem=1,
    )
    finished = [pack(on_chips, "pack_columns", slope, True)]
    finished += [plane_shift(finished[0], 0, 0, dc) for dc in range(1, n_c)]
    query_parts = [query_part] + [half_shift(query_part, k) for k in range(1, half)]
    grad_proj, finish_token = call(
        functools.partial(finish_kernel, len(finished)),
        [shape((depth, proj_width), F32), shape((8, LANES), F32)],
        [share_places, pool_query.reshape(1, -1), my_slope] + finished, "finish", smem=1, streamed=True,
        scratch=[pltpu.VMEM((depth, proj_width), F32), pltpu.SemaphoreType.DMA((depth // LANES,))],
    )
    grad_query = call(
        add_kernel, [shape((1, proj_width), F32)], query_parts, "query_sum", after=[finish_token]
    )[0]
    mean_loss = loss_total[0, 0] / (queries * n_all)
    return (grad_proj, grad_query.reshape(proj_width), mean_loss)


def solution(mesh):
    return jax.shard_map(
        body,
        mesh=mesh,
        in_specs=(
            P(("grp", "fsdp", "item"), None, None),
            P(("grp", "fsdp", "item"), None),
            P(("grp", "fsdp", "item"), None),
            P(("grp", "fsdp", "item")),
            P(),
            P("fsdp", None),
            P(),
            P("item", None),
        ),
        out_specs=(P("fsdp", None), P(), P()),
        check_vma=False,
    )
```

```python
import functools
import math

import jax
import jax.numpy as jnp
from jax import lax
from jax.experimental import pallas as pl
from jax.experimental.pallas import tpu as pltpu
from jax.sharding import PartitionSpec as P

sharpness_divisor = 0.05
norm_eps = 1e-05
embed_eps = 1e-06

EVERY = ("fsdp", "grp", "item")
PLANE = ("grp", "item")
F32 = jnp.float32
BF16 = jnp.bfloat16
LANES = 128
MIB = 1024 * 1024
VMEM = pl.BlockSpec(memory_space=pltpu.VMEM)
SMEM = pl.BlockSpec(memory_space=pltpu.SMEM)


def shape(dims, dtype):
    return jax.ShapeDtypeStruct(dims, dtype)


def copying(kernel, smem, shapes):
    n = len(shapes)

    def run(*refs):
        sources, buffers, sems = refs[smem : smem + n], refs[-n - 1 : -1], refs[-1]
        copies = [
            pltpu.make_async_copy(sources[k], buffers[k], sems.at[k]) for k in range(n)
        ]
        for copy in copies:
            copy.start()
        for copy in copies:
            copy.wait()
        kernel(*refs[:smem], *buffers, *refs[smem + n : -n - 1])

    return run


def call(kernel, outs, ins, name, flops=0, scratch=(), smem=0, after=(), copy=False, streamed=False):
    count = len(ins)
    if copy:
        shapes = [pltpu.VMEM(a.shape, a.dtype) for a in ins[smem:]]
        kernel = copying(kernel, smem, shapes)
        scratch = [*scratch, *shapes, pltpu.SemaphoreType.DMA((len(shapes),))]
    moved = sum(math.prod(a.shape) * a.dtype.itemsize for a in list(ins) + list(outs))
    held = 0 if copy or streamed else sum(math.prod(s.shape) * jnp.dtype(s.dtype).itemsize for s in scratch)

    def run(*refs):
        kernel(*refs[:count], *refs[count + len(after) :])

    return pl.pallas_call(
        run,
        out_shape=outs,
        in_specs=[SMEM] * smem
        + [pl.BlockSpec(memory_space=pl.ANY) if copy else VMEM] * (count - smem)
        + [pl.BlockSpec(memory_space=pl.ANY)] * len(after),
        out_specs=([pl.BlockSpec(memory_space=pl.ANY)] if streamed else [VMEM]) + [VMEM] * (len(outs) - 1),
        scratch_shapes=list(scratch),
        cost_estimate=pl.CostEstimate(flops=flops, bytes_accessed=moved, transcendentals=0),
        compiler_params=pltpu.CompilerParams(
            vmem_limit_bytes=61 * MIB if copy else 2 * (moved + held) + 6 * MIB
        ),
        name=name,
    )(*ins, *after)


def shift(values, axis, k):
    n = lax.axis_size(axis)
    return lax.ppermute(values, axis, [(i, (i + k) % n) for i in range(n)])


def split_bf16(values):
    high = values.astype(BF16)
    low = (values - high.astype(F32)).astype(BF16)
    return high, low


def nt(left, right):
    return lax.dot_general(left, right, (((1,), (1,)), ((), ())), preferred_element_type=F32)


def tn(left, right):
    return lax.dot_general(left, right, (((0,), (0,)), ((), ())), preferred_element_type=F32)


def u_kernel(weight_ref, pool_ref, u_ref):
    pool = jnp.broadcast_to(pool_ref[...], (8, pool_ref.shape[1]))
    high = pool.astype(BF16)
    low, last = split_bf16(pool - high.astype(F32))
    weight = weight_ref[...]
    u_ref[...] = (nt(high, weight) + nt(low, weight) + nt(last, weight))[0:1]


def gate_kernel(seq, root, blocks, z_ref, states_ref, gain_ref, u_ref, len_ref, lists_ref, *rest):
    half = blocks // 2
    outs, normed_ref, gated_ref, curve_ref, copies, rows_ref = (
        rest[:half], rest[half], rest[half + 1], rest[half + 2], rest[half + 3 : -1], rest[-1]
    )
    step = pl.program_id(0)
    tokens, width = states_ref.shape
    count = tokens // seq
    chunk = 4 * LANES if width % (4 * LANES) == 0 else width
    logits = []
    for top in range(0, tokens, 32):
        rows = slice(top, top + 32)
        squares = jnp.zeros((32, chunk), F32)
        for at in range(0, width, chunk):
            part = states_ref[rows, at : at + chunk].astype(F32)
            squares = squares + part * part
        inv_rms = lax.rsqrt(jnp.sum(squares, axis=1, keepdims=True) / width + norm_eps)
        total = jnp.zeros((32, chunk), F32)
        for at in range(0, width, chunk):
            part = states_ref[rows, at : at + chunk].astype(F32)
            part = (part * inv_rms * gain_ref[:, at : at + chunk]).astype(BF16)
            normed_ref[rows, at : at + chunk] = part
            total = total + part.astype(F32) * u_ref[:, at : at + chunk]
        logits.append(jnp.sum(total, axis=1, keepdims=True))
    logit = jnp.concatenate(logits, axis=0) / root
    gate = 1.0 / (1.0 + jnp.exp(-logit))
    slot = lax.rem(lax.broadcasted_iota(jnp.int32, (tokens, 1), 0), seq)
    valid = jnp.where(slot < len_ref[...], 1.0, 0.0) / len_ref[...].astype(F32)
    gated = valid * gate
    gated_ref[...] = gated
    curve_ref[...] = gated * (1.0 - gate) / root
    owner = lax.broadcasted_iota(jnp.int32, (tokens, count), 0) // seq
    mine = owner == lax.broadcasted_iota(jnp.int32, (tokens, count), 1)
    high, low = split_bf16(jnp.where(mine, gated, 0.0))
    both = tn(jnp.concatenate([high, low], axis=1), normed_ref[...])
    rows_ref[pl.ds(pl.multiple_of(step * count, count), count), :] = both[:count] + both[count:]

    @pl.when(step == pl.num_programs(0) - 1)
    def _():
        owners = len(copies)
        own = lists_ref.shape[1] // owners
        for k in range(owners):
            picked = jnp.zeros(copies[k].shape, jnp.int32)
            for j in range(owners):
                picked = jnp.where(
                    lax.rem(z_ref[1] + k, owners) == j, lists_ref[:, j * own : (j + 1) * own], picked
                )
            copies[k][...] = picked
        depth = width // blocks
        place = lax.rem(z_ref[0], half)
        for k in range(half):
            for j in range(2):
                at = (j * half + lax.rem(place + k, half)) * depth
                outs[k][:, j * depth : (j + 1) * depth] = rows_ref[
                    :, pl.ds(pl.multiple_of(at, LANES), depth)
                ].astype(BF16)


def gate_rows(z, states, gain, u, token_lengths, lists, events, seq, root, blocks, owners):
    tokens, width = states.shape
    queries = tokens // seq
    group = 16 if queries % 16 == 0 else queries
    step_tokens = group * seq
    half = blocks // 2
    outs = [shape((queries, width // half), BF16)] * half
    outs += [shape((tokens, width), BF16)] + [shape((tokens, 1), F32)] * 2
    outs += [shape((queries, lists.shape[1] // owners), lists.dtype)] * owners
    column = pl.BlockSpec((step_tokens, 1), lambda i: (i, 0))
    rows = pl.BlockSpec((step_tokens, width), lambda i: (i, 0))
    inputs = [z, states, gain, u, token_lengths, lists]

    def run(*refs):
        gate_kernel(seq, root, blocks, *refs[: len(inputs)], *refs[len(inputs) + len(events) :])

    whole = lambda dims: pl.BlockSpec(dims, lambda i: (0, 0))
    return pl.pallas_call(
        run,
        grid=(queries // group,),
        out_shape=outs,
        in_specs=[
            SMEM,
            rows,
            whole((1, width)),
            whole((1, width)),
            column,
            whole(lists.shape),
        ]
        + [pl.BlockSpec(memory_space=pl.ANY)] * len(events),
        out_specs=[whole((queries, width // half))] * half + [rows] + [column] * 2
        + [whole((queries, lists.shape[1] // owners))] * owners,
        scratch_shapes=[pltpu.VMEM((queries, width), F32)],
        cost_estimate=pl.CostEstimate(
            flops=10 * tokens * width, bytes_accessed=4 * tokens * width, transcendentals=0
        ),
        compiler_params=pltpu.CompilerParams(vmem_limit_bytes=50 * MIB),
        name="gate_rows",
    )(*inputs, *events)


def pack_kernel(*refs):
    rows = refs[0].shape[0]
    for k, ref in enumerate(refs[:-1]):
        refs[-1][k * rows : (k + 1) * rows, :] = ref[...]


def pack_copies(n, *refs):
    out_ref, sems = refs[-2], refs[-1]
    rows = refs[0].shape[0]
    copies = [
        pltpu.make_async_copy(refs[k], out_ref.at[pl.ds(k * rows, rows), :], sems.at[k]) for k in range(n)
    ]
    for copy in copies:
        copy.start()
    for copy in copies:
        copy.wait()


def pack(pieces, name, event, copy=False):
    rows, width = pieces[0].shape
    n = len(pieces)
    out = shape((n * rows, width), pieces[0].dtype)
    if copy:
        anywhere = pl.BlockSpec(memory_space=pl.ANY)
        return pl.pallas_call(
            functools.partial(pack_copies, n),
            out_shape=out,
            in_specs=[anywhere] * (n + 1),
            out_specs=anywhere,
            scratch_shapes=[pltpu.SemaphoreType.DMA((n,))],
            cost_estimate=pl.CostEstimate(flops=0, bytes_accessed=4 * n * rows * width, transcendentals=0),
            compiler_params=pltpu.CompilerParams(vmem_limit_bytes=4 * MIB),
            name=name,
        )(*pieces, event)
    return call(pack_kernel, [out], pieces, name, after=[event])[0]


def pass_kernel(from_ref, to_ref):
    to_ref[...] = from_ref[...]


def passed(values, name, event):
    return call(pass_kernel, [shape(values.shape, values.dtype)], [values], name, after=[event])[0]


def add_kernel(*refs):
    total = refs[0][...]
    for ref in refs[1:-1]:
        total = total + ref[...]
    refs[-1][...] = total


def forward_kernel(n, packs, side_ref, places_ref, weight_ref, *refs):
    refs = refs[:n] + (weight_ref,) + refs[n:]
    pieces, shares = refs[:n], refs[n + 1 : n + 1 + packs]
    outs = refs[n + 1 + packs : 2 * n + 1 + packs]
    mirror_ref, held_ref, away_ref = refs[2 * n + 1 + packs :]
    rows = pieces[0].shape[0]
    depth = weight_ref.shape[0]
    side = side_ref[0]
    for k in range(n):
        part = slice(k * rows, (k + 1) * rows)
        held_ref[part, :] = pieces[k][:, pl.ds(pl.multiple_of(side * depth, LANES), depth)]
        away_ref[part, :] = pieces[k][:, pl.ds(pl.multiple_of((1 - side) * depth, LANES), depth)]
    count = places_ref.shape[0] // packs
    share = shares[0].shape[0] // count
    for p in range(packs):
        for j in range(count):
            at = pl.multiple_of(places_ref[p * count + j] * share, share)
            mirror_ref[pl.ds(at, share), :] = shares[p][j * share : (j + 1) * share, :]
    product = jnp.dot(held_ref[...], weight_ref[...], preferred_element_type=F32)
    product = product + jnp.dot(away_ref[...], mirror_ref[...], preferred_element_type=F32)
    for k in range(n):
        outs[k][...] = product[k * rows : (k + 1) * rows].astype(outs[k].dtype)


def back_kernel(n, packed, side_ref, weight_ref, mirror_ref, *refs):
    pieces, outs = refs[:n], refs[n + packed : -1]
    pack_kernel(*refs[n : n + packed], refs[-1])
    rows = pieces[0].shape[0]
    depth = weight_ref.shape[0]
    side = side_ref[0]
    stack = jnp.concatenate([p[...] for p in pieces], axis=0)
    own = nt(stack, weight_ref[...]).astype(BF16)
    mirror = nt(stack, mirror_ref[...]).astype(BF16)
    for k in range(n):
        part = slice(k * rows, (k + 1) * rows)
        outs[k][:, pl.ds(pl.multiple_of(side * depth, LANES), depth)] = own[part]
        outs[k][:, pl.ds(pl.multiple_of((1 - side) * depth, LANES), depth)] = mirror[part]


def embed_kernel(root, n, *refs):
    parts, away_ref, packed = refs[:n], refs[n], refs[n + 1 : -5]
    pooled_ref, unit_ref, embedded_ref, pack_ref, pass_ref = refs[-5:]
    pass_ref[...] = away_ref[...]
    pooled = parts[0][...]
    for part in parts[1:]:
        pooled = pooled + part[...].astype(F32)
    unit = lax.rsqrt(jnp.mean(pooled * pooled, axis=1, keepdims=True) + embed_eps) / root
    pooled_ref[...] = pooled
    unit_ref[...] = unit
    embedded_ref[...] = (pooled * unit).astype(BF16)
    pack_kernel(*packed, pack_ref)


def count_kernel(n, root, base_ref, slab_ref, *refs):
    lists, counts_ref, scale_ref = refs[:n], refs[n], refs[n + 1]
    queries = lists[0].shape[0]
    rows, width = slab_ref.shape
    slab = slab_ref[...].astype(F32)
    high, low = split_bf16(slab * slab)
    ones = jnp.ones((8, width), BF16)
    row_sq = (nt(ones, high) + nt(ones, low))[0:1]
    scale_ref[...] = lax.rsqrt(row_sq / width + embed_eps) / root / sharpness_divisor
    ids = lax.broadcasted_iota(jnp.int32, (queries, LANES), 1)
    for k in range(n):
        own = lists[k][...] - base_ref[0]
        columns = [
            jnp.broadcast_to(own[:, entry : entry + 1], (queries, LANES)) for entry in range(own.shape[1])
        ]
        for at in range(0, rows, LANES):
            total = jnp.zeros(ids.shape, F32)
            for column in columns:
                total = total + jnp.where(column == ids + at, 1.0, 0.0)
            counts_ref[k * queries : (k + 1) * queries, at : at + LANES] = total


def contrast_kernel(n, *refs):
    (slab_ref, scale_ref, counts_ref), pieces, outs = refs[:3], refs[3 : n + 3], refs[n + 3 :]
    queries, width = pieces[0].shape
    embedded = jnp.concatenate([p[...] for p in pieces], axis=0)
    slab = slab_ref[...]
    scale = scale_ref[...]
    heavy = counts_ref[...] * jnp.exp(nt(embedded, slab) * scale)
    denom = jnp.sum(heavy, axis=1, keepdims=True)
    grad = jnp.dot((heavy * scale).astype(BF16), slab, preferred_element_type=F32)
    high, low = split_bf16(denom)
    lane = lax.broadcasted_iota(jnp.int32, (queries, LANES), 1)
    for k in range(n):
        part = slice(k * queries, (k + 1) * queries)
        outs[k][:, :width] = grad[part].astype(outs[k].dtype)
        if k == 0:
            tail = jnp.where(lane == 0, denom[part], 0.0)
        else:
            tail = jnp.where(lane == 0, high[part].astype(F32), jnp.where(lane == 1, low[part].astype(F32), 0.0))
        outs[k][:, width:] = tail.astype(outs[k].dtype)


def grad_kernel(n, root, *refs):
    pos_ref, pooled_ref, unit_ref, embedded_ref = refs[:4]
    parts = refs[4 : n + 4]
    grad_ref, columns_ref, loss_ref = refs[n + 4 :]
    queries, width = pos_ref.shape
    total = parts[0][:, :width]
    denom = jnp.sum(parts[0][:, width:], axis=1, keepdims=True)
    for part in parts[1:]:
        total = total + part[:, :width].astype(F32)
        denom = denom + jnp.sum(part[:, width:].astype(F32), axis=1, keepdims=True)
    positive = pos_ref[...].astype(F32)
    scale = (
        lax.rsqrt(jnp.mean(positive * positive, axis=1, keepdims=True) + embed_eps)
        / root
        / sharpness_divisor
    )
    score = jnp.sum(embedded_ref[...].astype(F32) * positive, axis=1, keepdims=True) * scale
    pos_exp = jnp.exp(score)
    denom = denom + pos_exp
    loss_ref[...] = jnp.broadcast_to(jnp.sum(jnp.log(denom) - score), loss_ref.shape)
    grad_embed = total / denom + (pos_exp / denom - 1.0) * scale * positive
    pooled, unit = pooled_ref[...], unit_ref[...]
    mean_sq = jnp.mean(pooled * pooled, axis=1, keepdims=True)
    radial = jnp.sum(pooled * grad_embed, axis=1, keepdims=True)
    grad = unit * grad_embed - pooled * (radial * unit / (width * (mean_sq + embed_eps)))
    grad = grad.astype(BF16)
    grad_ref[...] = grad
    cols = columns_ref.shape[2]
    places = width // cols
    for j in range(columns_ref.shape[0]):
        at = (j % places) * cols
        columns_ref[j] = grad[:, at : at + cols]


def slope_kernel(seq, blocks, z_ref, normed_ref, curve_ref, loss_ref, *rest):
    half = blocks // 2
    backs, outs, (all_ref, sum_ref) = rest[:half], rest[half : 2 * half], rest[-2:]
    step = pl.program_id(0)
    tokens, width = normed_ref.shape
    count = tokens // seq
    depth = width // blocks
    place = lax.rem(z_ref[0], half)

    def block_at(j, k):
        return pl.ds(pl.multiple_of((j * half + lax.rem(place + k, half)) * depth, LANES), depth)

    @pl.when(step == 0)
    def _():
        sum_ref[...] = jnp.zeros_like(sum_ref)
        for k in range(half):
            for j in range(2):
                all_ref[:, block_at(j, k)] = backs[k][:, j * depth : (j + 1) * depth].astype(F32)

    back = all_ref[pl.ds(pl.multiple_of(step * count, count), count), :]
    normed = normed_ref[...].astype(F32).reshape(count, seq, width)
    dots = jnp.sum(normed * back[:, None, :], axis=2, keepdims=True)
    slope = curve_ref[...].reshape(count, seq, 1) * dots
    heavy = (slope * normed).reshape(tokens // 8, 8, width)
    sum_ref[...] += jnp.sum(heavy, axis=0)

    @pl.when(step == pl.num_programs(0) - 1)
    def _():
        total = jnp.sum(sum_ref[...], axis=0, keepdims=True)
        lines = depth // LANES
        height = outs[0].shape[0]
        loss = jnp.broadcast_to(loss_ref[...], (height - 2 * lines, LANES))
        all_ref[0:1, :] = total
        for k in range(half):
            for j in range(2):
                row = all_ref[0:1, block_at(j, k)]
                for line in range(lines):
                    outs[k][j * lines + line : j * lines + line + 1, :] = row[
                        :, line * LANES : (line + 1) * LANES
                    ]
            outs[k][2 * lines :, :] = loss


def slope_rows(z, normed, curve, loss, backs, seq, blocks):
    tokens, width = normed.shape
    half = blocks // 2
    height = 2 * (width // blocks // LANES) // 8 * 8 + 8
    queries = tokens // seq
    group = 8 if queries % 8 == 0 else queries
    step_tokens = group * seq
    whole = lambda dims: pl.BlockSpec(dims, lambda i: (0, 0))
    return pl.pallas_call(
        functools.partial(slope_kernel, seq, blocks),
        grid=(queries // group,),
        out_shape=[shape((height, LANES), F32)] * half,
        in_specs=[
            SMEM,
            pl.BlockSpec((step_tokens, width), lambda i: (i, 0)),
            pl.BlockSpec((step_tokens, 1), lambda i: (i, 0)),
            whole((1, LANES)),
        ]
        + [whole((queries, width // half))] * half,
        out_specs=[whole((height, LANES))] * half,
        scratch_shapes=[pltpu.VMEM((queries, width), F32), pltpu.VMEM((8, width), F32)],
        cost_estimate=pl.CostEstimate(
            flops=4 * tokens * width, bytes_accessed=2 * tokens * width, transcendentals=0
        ),
        compiler_params=pltpu.CompilerParams(vmem_limit_bytes=20 * MIB),
        name="slope_rows",
    )(z, normed, curve, loss, *backs)


def columns_kernel(n, order_ref, grads_ref, *refs):
    pieces, (out_ref, sorted_ref) = refs[:n], refs[n:]
    chunk = grads_ref.shape[1]
    for j in range(sorted_ref.shape[0] // chunk):
        sorted_ref[j * chunk : (j + 1) * chunk, :] = grads_ref[order_ref[j]]
    at = pieces[0].shape[0]
    total = tn(sorted_ref[0:at, :], pieces[0][...])
    for piece in pieces[1:]:
        rows = piece.shape[0]
        total = total + tn(sorted_ref[at : at + rows, :], piece[...])
        at += rows
    out_ref[...] = total.T.astype(BF16)


def query_kernel(side_ref, weight_ref, mirror_ref, parts_ref, part_ref, slope_ref, loss_ref):
    depth = weight_ref.shape[0]
    lines = depth // LANES
    total = parts_ref[...]
    loss_ref[...] = total[2 * lines : 2 * lines + 1]
    side = side_ref[0]
    part = jnp.zeros(part_ref.shape, F32)
    for j in range(2):
        rows = total[j * lines : (j + 1) * lines]
        row = jnp.concatenate([rows[k : k + 1] for k in range(lines)], axis=1)
        high, low = split_bf16(jnp.broadcast_to(row, (8, depth)))

        @pl.when(side == j)
        def _():
            slope_ref[...] = rows

        weight = jnp.where(side == j, weight_ref[...], mirror_ref[...])
        part = part + jnp.dot(high, weight, preferred_element_type=F32)[0:1]
        part = part + jnp.dot(low, weight, preferred_element_type=F32)[0:1]
    part_ref[...] = part


def finish_kernel(n, place_ref, pool_ref, slope_ref, *refs):
    pieces, result_ref, token_ref, out_ref, sems = refs[:n], *refs[n:]
    token_ref[...] = jnp.zeros_like(token_ref)
    places = place_ref.shape[0]
    rows, cols = out_ref.shape[0], pieces[0].shape[1]
    copies = []
    for line in range(rows // LANES):
        part = pl.ds(line * LANES, LANES)
        slope = jnp.broadcast_to(slope_ref[line : line + 1, :], (LANES, LANES)).T
        for k in range(places):
            base = k % (places // n) * rows + line * LANES
            mine = pieces[k // (places // n)][base : base + LANES, :].astype(F32)
            at = pl.ds(pl.multiple_of(place_ref[k] * cols, LANES), cols)
            out_ref[part, at] = mine + slope * pool_ref[:, at]
        copies.append(
            pltpu.make_async_copy(out_ref.at[part, :], result_ref.at[part, :], sems.at[line])
        )
        copies[-1].start()
    for copy in copies:
        copy.wait()


def body(hidden_states, positives, negatives, lengths, norm_gain, proj_weight, pool_query, slab):
    queries, seq, width = hidden_states.shape
    depth, proj_width = proj_weight.shape
    n_z, n_g, n_i = lax.axis_size("fsdp"), lax.axis_size("grp"), lax.axis_size("item")
    assert n_z % 2 == 0
    half = n_z // 2
    n_c = 2 if n_i % 2 == 0 else 1
    n_h = n_i // n_c
    n_plane = n_g * n_i
    n_all = n_z * n_plane
    z, g, i = lax.axis_index("fsdp"), lax.axis_index("grp"), lax.axis_index("item")
    h, c = i // n_c, lax.rem(i, n_c)
    side, member = z // half, lax.rem(z, half)
    root = math.sqrt(proj_width)
    steps_z, steps_i = range(1, n_z), range(1, n_i)

    def ints(*values):
        return jnp.stack([jnp.asarray(v, jnp.int32) for v in values])

    z_arr, side_arr = ints(z), ints(side)

    def plane_shift(values, dg, dh, dc):
        pairs = []
        for pg in range(n_g):
            for ph in range(n_h):
                for pc in range(n_c):
                    to = ((pg + dg) % n_g) * n_i + ((ph + dh) % n_h) * n_c + (pc + dc) % n_c
                    pairs.append((pg * n_i + ph * n_c + pc, to))
        return lax.ppermute(values, PLANE, pairs)

    def half_shift(values, k):
        pairs = [(a, a // half * half + (a % half + k) % half) for a in range(n_z)]
        return lax.ppermute(values, "fsdp", pairs)

    def mirror_shift(values):
        return lax.ppermute(values, "fsdp", [(a, (a + half) % n_z) for a in range(n_z)])

    def source(dg, dh, dc):
        return (
            lax.rem(g - dg + n_g, n_g),
            lax.rem(h - dh + n_h, n_h) * n_c + lax.rem(c - dc + n_c, n_c),
        )

    chips = [(dg, dh) for dg in range(n_g) for dh in range(n_h)]

    share = depth // n_plane
    place = g * n_i + i
    weight_share = lax.dynamic_slice_in_dim(proj_weight, place * share, share, 0)
    far_share = mirror_shift(weight_share)

    block_u = call(
        u_kernel, [shape((1, depth), F32)], [proj_weight, pool_query.reshape(1, -1)], "block_u",
        after=[weight_share],
    )[0]
    u_parts = [block_u] + [shift(block_u, "fsdp", k) for k in steps_z]
    u = jnp.zeros((1, width), F32)
    for k in range(n_z):
        u = lax.dynamic_update_slice(u, u_parts[k], (0, lax.rem(z - k + n_z, n_z) * depth))

    share_places = []
    for dc in range(n_c):
        for dg, dh in chips:
            from_g, from_i = source(dg, dh, dc)
            share_places.append(from_g * n_i + from_i)
    share_places = ints(*share_places)
    order = []
    for dc in range(n_c):
        for dg in range(n_g):
            order += [(side, k, dg, dh, dc) for dh in range(n_h) for k in range(half)]
        for dh in range(n_h):
            order += [(1 - side, k, dg, dh, dc) for dg in range(n_g) for k in range(half)]
    ranks = []
    for from_side, k, dg, dh, dc in order:
        from_g, from_i = source(dg, dh, dc)
        from_z = from_side * half + lax.rem(member - k + half, half)
        ranks.append((from_z * n_g + from_g) * n_i + from_i)
    ranks = ints(*ranks)
    both_arr, base_arr = ints(z, i), ints(i * slab.shape[0])
    token_lengths = jnp.broadcast_to(lengths[:, None], (queries, seq)).reshape(-1, 1)
    events = [far_share, share_places, ranks, base_arr, side_arr]
    chip_shares = [far_share if dg == dh == 0 else plane_shift(far_share, dg, dh, 0) for dg, dh in chips]
    gate_outs = gate_rows(
        both_arr, hidden_states.reshape(-1, width), norm_gain.astype(F32).reshape(1, width), u,
        token_lengths, negatives, events, seq, root, n_z, n_i,
    )
    sends, (normed, gated, curve), lists = gate_outs[:half], gate_outs[half : half + 3], gate_outs[half + 3 :]
    packs = [pack(chip_shares, "pack_shares", gated)]
    packs += [plane_shift(packs[0], 0, 0, dc) for dc in range(1, n_c)]

    pieces = [sends[0]] + [half_shift(sends[k], k) for k in range(1, half)]
    lists = [lists[0]] + [shift(lists[k], "item", k) for k in steps_i]
    counts, slab_scale = call(
        functools.partial(count_kernel, n_i, root),
        [shape((n_i * queries, slab.shape[0]), F32), shape((1, slab.shape[0]), F32)],
        [base_arr, slab] + lists, "list_counts", smem=1,
    )
    block = shape((half * queries, depth), BF16)
    *parts, mirror, held, away = call(
        functools.partial(forward_kernel, half, n_c),
        [shape((queries, proj_width), F32)]
        + [shape((queries, proj_width), BF16)] * (half - 1)
        + [shape((depth, proj_width), BF16), block, block],
        [side_arr, share_places, proj_weight] + pieces + packs, "forward",
        flops=4 * half * queries * depth * proj_width, smem=2, after=[counts],
    )
    parts = [parts[0]] + [half_shift(parts[k], -k) for k in range(1, half)]
    near = [held] + [plane_shift(held, 0, dh, 0) for dh in range(1, n_h)]
    row = shape((queries, proj_width), F32)
    row16 = shape((queries, proj_width), BF16)
    pooled, unit, embedded, near, away = call(
        functools.partial(embed_kernel, root, half),
        [row, shape((queries, 1), F32), row16, shape((n_h * half * queries, depth), BF16), block],
        parts + [away] + near, "embed",
    )
    other = mirror_shift(away)

    pieces = [embedded] + [shift(embedded, "item", k) for k in steps_i]
    near_far = [plane_shift(near, dg, 0, 0) for dg in range(1, n_g)]
    near_cores = [plane_shift(near, 0, 0, dc) for dc in range(1, n_c)]
    wide = (queries, proj_width + LANES)
    parts = call(
        functools.partial(contrast_kernel, n_i),
        [shape(wide, F32)] + [shape(wide, BF16)] * (n_i - 1),
        [slab, slab_scale, counts] + pieces, "contrast",
        flops=4 * n_i * queries * slab.shape[0] * proj_width, after=near_cores,
    )
    near_far_late = [passed(array, "near_far", parts[0]) for array in near_far]
    parts = [parts[0]] + [shift(parts[k], "item", -k) for k in steps_i]
    near_far_cores = [[plane_shift(array, 0, 0, dc) for array in near_far_late] for dc in range(1, n_c)]
    other = passed(other, "other", parts[1 % n_i])
    others = [other] + [plane_shift(other, dg, 0, 0) for dg in range(1, n_g)]
    cols = proj_width // n_plane
    grad, grad_columns, loss = call(
        functools.partial(grad_kernel, n_i, root),
        [row16, shape((n_all, queries, cols), BF16), shape((1, LANES), F32)],
        [positives, pooled, unit, embedded] + parts, "grad_pooled",
    )

    pieces = [grad] + [half_shift(grad, k) for k in range(1, half)]
    *backs, others = call(
        functools.partial(back_kernel, half, n_g),
        [shape((queries, 2 * depth), BF16)] * half + [shape((n_g * half * queries, depth), BF16)],
        [side_arr, proj_weight, mirror] + pieces + others, "backward",
        flops=4 * half * queries * depth * proj_width, smem=1, after=near_cores + sum(near_far_cores, []),
    )
    backs = [backs[0]] + [half_shift(backs[k], -k) for k in range(1, half)]
    all_columns = lax.all_to_all(
        passed(grad_columns, "columns_out", backs[-1]), EVERY, 0, 0, tiled=True
    )
    slopes = slope_rows(both_arr, normed, curve, loss, backs, seq, n_z)
    def total(parts, name):
        return call(add_kernel, [shape(parts[0].shape, F32)], parts, name)[0]

    slope = total([slopes[0]] + [half_shift(slopes[k], k) for k in range(1, half)], "sum_half")
    across = [plane_shift(others, 0, dh, 0) for dh in range(1, n_h)]
    late = [pack([array], "late", slopes[0]) for array in across]
    spread = []
    for dc in range(n_c):
        if dc == 0:
            spread += [near, *near_far, others, *across]
        else:
            spread += [near_cores[dc - 1], *near_far_cores[dc - 1]]
            spread += [plane_shift(array, 0, 0, dc) for array in [others, *late]]
    block_columns = call(
        functools.partial(columns_kernel, len(spread)), [shape((depth, cols), BF16)],
        [ranks, all_columns] + spread, "grad_columns",
        flops=2 * n_all * queries * depth * cols, scratch=[pltpu.VMEM((n_all * queries, cols), BF16)], smem=1, copy=True, after=[slope],
    )[0]
    on_chips = [block_columns if dg == dh == 0 else plane_shift(block_columns, dg, dh, 0) for dg, dh in chips]
    slope = passed(slope, "slope_out", block_columns)
    slope = total([slope, mirror_shift(slope)], "sum_mirror")
    if n_g > 1:
        slope = total([slope] + [shift(slope, "grp", k) for k in range(1, n_g)], "sum_groups")
    if n_i > 1:
        slope = total([slope] + [shift(slope, "item", k) for k in steps_i], "sum_items")
    query_part, my_slope, loss_total = call(
        query_kernel,
        [shape((1, proj_width), F32), shape((depth // LANES, LANES), F32), shape((1, LANES), F32)],
        [side_arr, proj_weight, mirror, slope], "slope_sum", smem=1,
    )
    finished = [pack(on_chips, "pack_columns", slope, True)]
    finished += [plane_shift(finished[0], 0, 0, dc) for dc in range(1, n_c)]
    query_parts = [query_part] + [half_shift(query_part, k) for k in range(1, half)]
    grad_proj, finish_token = call(
        functools.partial(finish_kernel, len(finished)),
        [shape((depth, proj_width), F32), shape((8, LANES), F32)],
        [share_places, pool_query.reshape(1, -1), my_slope] + finished, "finish", smem=1, streamed=True,
        scratch=[pltpu.VMEM((depth, proj_width), F32), pltpu.SemaphoreType.DMA((depth // LANES,))],
    )
    grad_query = call(
        add_kernel, [shape((1, proj_width), F32)], query_parts, "query_sum", after=[finish_token]
    )[0]
    mean_loss = loss_total[0, 0] / (queries * n_all)
    return (grad_proj, grad_query.reshape(proj_width), mean_loss)


def solution(mesh):
    return jax.shard_map(
        body,
        mesh=mesh,
        in_specs=(
            P(("grp", "fsdp", "item"), None, None),
            P(("grp", "fsdp", "item"), None),
            P(("grp", "fsdp", "item"), None),
            P(("grp", "fsdp", "item")),
            P(),
            P("fsdp", None),
            P(),
            P("item", None),
        ),
        out_specs=(P("fsdp", None), P(), P()),
        check_vma=False,
    )
```

```python
import functools
import math

import jax
import jax.numpy as jnp
from jax import lax
from jax.experimental import pallas as pl
from jax.experimental.pallas import tpu as pltpu
from jax.sharding import PartitionSpec as P

sharpness_divisor = 0.05
norm_eps = 1e-05
embed_eps = 1e-06

EVERY = ("fsdp", "grp", "item")
PLANE = ("grp", "item")
F32 = jnp.float32
BF16 = jnp.bfloat16
LANES = 128
MIB = 1024 * 1024
VMEM = pl.BlockSpec(memory_space=pltpu.VMEM)
SMEM = pl.BlockSpec(memory_space=pltpu.SMEM)


def shape(dims, dtype):
    return jax.ShapeDtypeStruct(dims, dtype)


def copying(kernel, smem, shapes):
    n = len(shapes)

    def run(*refs):
        sources, buffers, sems = refs[smem : smem + n], refs[-n - 1 : -1], refs[-1]
        copies = [
            pltpu.make_async_copy(sources[k], buffers[k], sems.at[k]) for k in range(n)
        ]
        for copy in copies:
            copy.start()
        kernel(copies, *refs[:smem], *buffers, *refs[smem + n : -n - 1])

    return run


def call(kernel, outs, ins, name, flops=0, scratch=(), smem=0, after=(), copy=False, streamed=False):
    count = len(ins)
    if copy:
        shapes = [pltpu.VMEM(a.shape, a.dtype) for a in ins[smem:]]
        kernel = copying(kernel, smem, shapes)
        scratch = [*scratch, *shapes, pltpu.SemaphoreType.DMA((len(shapes),))]
    moved = sum(math.prod(a.shape) * a.dtype.itemsize for a in list(ins) + list(outs))
    held = 0 if copy or streamed else sum(math.prod(s.shape) * jnp.dtype(s.dtype).itemsize for s in scratch)

    def run(*refs):
        kernel(*refs[:count], *refs[count + len(after) :])

    return pl.pallas_call(
        run,
        out_shape=outs,
        in_specs=[SMEM] * smem
        + [pl.BlockSpec(memory_space=pl.ANY) if copy else VMEM] * (count - smem)
        + [pl.BlockSpec(memory_space=pl.ANY)] * len(after),
        out_specs=([pl.BlockSpec(memory_space=pl.ANY)] if streamed else [VMEM]) + [VMEM] * (len(outs) - 1),
        scratch_shapes=list(scratch),
        cost_estimate=pl.CostEstimate(flops=flops, bytes_accessed=moved, transcendentals=0),
        compiler_params=pltpu.CompilerParams(
            vmem_limit_bytes=61 * MIB if copy else 2 * (moved + held) + 6 * MIB
        ),
        name=name,
    )(*ins, *after)


def shift(values, axis, k):
    n = lax.axis_size(axis)
    return lax.ppermute(values, axis, [(i, (i + k) % n) for i in range(n)])


def split_bf16(values):
    high = values.astype(BF16)
    low = (values - high.astype(F32)).astype(BF16)
    return high, low


def nt(left, right):
    return lax.dot_general(left, right, (((1,), (1,)), ((), ())), preferred_element_type=F32)


def tn(left, right):
    return lax.dot_general(left, right, (((0,), (0,)), ((), ())), preferred_element_type=F32)


def u_kernel(weight_ref, pool_ref, u_ref):
    pool = jnp.broadcast_to(pool_ref[...], (8, pool_ref.shape[1]))
    high = pool.astype(BF16)
    low, last = split_bf16(pool - high.astype(F32))
    weight = weight_ref[...]
    u_ref[...] = (nt(high, weight) + nt(low, weight) + nt(last, weight))[0:1]


def gate_kernel(seq, root, blocks, z_ref, states_ref, gain_ref, u_ref, len_ref, lists_ref, *rest):
    half = blocks // 2
    outs, normed_ref, gated_ref, curve_ref, copies, rows_ref = (
        rest[:half], rest[half], rest[half + 1], rest[half + 2], rest[half + 3 : -1], rest[-1]
    )
    step = pl.program_id(0)
    tokens, width = states_ref.shape
    count = tokens // seq
    chunk = 4 * LANES if width % (4 * LANES) == 0 else width
    logits = []
    for top in range(0, tokens, 32):
        rows = slice(top, top + 32)
        squares = jnp.zeros((32, chunk), F32)
        for at in range(0, width, chunk):
            part = states_ref[rows, at : at + chunk].astype(F32)
            squares = squares + part * part
        inv_rms = lax.rsqrt(jnp.sum(squares, axis=1, keepdims=True) / width + norm_eps)
        total = jnp.zeros((32, chunk), F32)
        for at in range(0, width, chunk):
            part = states_ref[rows, at : at + chunk].astype(F32)
            part = (part * inv_rms * gain_ref[:, at : at + chunk]).astype(BF16)
            normed_ref[rows, at : at + chunk] = part
            total = total + part.astype(F32) * u_ref[:, at : at + chunk]
        logits.append(jnp.sum(total, axis=1, keepdims=True))
    logit = jnp.concatenate(logits, axis=0) / root
    gate = 1.0 / (1.0 + jnp.exp(-logit))
    slot = lax.rem(lax.broadcasted_iota(jnp.int32, (tokens, 1), 0), seq)
    valid = jnp.where(slot < len_ref[...], 1.0, 0.0) / len_ref[...].astype(F32)
    gated = valid * gate
    gated_ref[...] = gated
    curve_ref[...] = gated * (1.0 - gate) / root
    owner = lax.broadcasted_iota(jnp.int32, (tokens, count), 0) // seq
    mine = owner == lax.broadcasted_iota(jnp.int32, (tokens, count), 1)
    high, low = split_bf16(jnp.where(mine, gated, 0.0))
    both = tn(jnp.concatenate([high, low], axis=1), normed_ref[...])
    rows_ref[pl.ds(pl.multiple_of(step * count, count), count), :] = both[:count] + both[count:]

    @pl.when(step == pl.num_programs(0) - 1)
    def _():
        owners = len(copies)
        own = lists_ref.shape[1] // owners
        for k in range(owners):
            picked = jnp.zeros(copies[k].shape, jnp.int32)
            for j in range(owners):
                picked = jnp.where(
                    lax.rem(z_ref[1] + k, owners) == j, lists_ref[:, j * own : (j + 1) * own], picked
                )
            copies[k][...] = picked
        depth = width // blocks
        place = lax.rem(z_ref[0], half)
        for k in range(half):
            for j in range(2):
                at = (j * half + lax.rem(place + k, half)) * depth
                outs[k][:, j * depth : (j + 1) * depth] = rows_ref[
                    :, pl.ds(pl.multiple_of(at, LANES), depth)
                ].astype(BF16)


def gate_rows(z, states, gain, u, token_lengths, lists, events, seq, root, blocks, owners):
    tokens, width = states.shape
    queries = tokens // seq
    group = 16 if queries % 16 == 0 else queries
    step_tokens = group * seq
    half = blocks // 2
    outs = [shape((queries, width // half), BF16)] * half
    outs += [shape((tokens, width), BF16)] + [shape((tokens, 1), F32)] * 2
    outs += [shape((queries, lists.shape[1] // owners), lists.dtype)] * owners
    column = pl.BlockSpec((step_tokens, 1), lambda i: (i, 0))
    rows = pl.BlockSpec((step_tokens, width), lambda i: (i, 0))
    inputs = [z, states, gain, u, token_lengths, lists]

    def run(*refs):
        gate_kernel(seq, root, blocks, *refs[: len(inputs)], *refs[len(inputs) + len(events) :])

    whole = lambda dims: pl.BlockSpec(dims, lambda i: (0, 0))
    return pl.pallas_call(
        run,
        grid=(queries // group,),
        out_shape=outs,
        in_specs=[
            SMEM,
            rows,
            whole((1, width)),
            whole((1, width)),
            column,
            whole(lists.shape),
        ]
        + [pl.BlockSpec(memory_space=pl.ANY)] * len(events),
        out_specs=[whole((queries, width // half))] * half + [rows] + [column] * 2
        + [whole((queries, lists.shape[1] // owners))] * owners,
        scratch_shapes=[pltpu.VMEM((queries, width), F32)],
        cost_estimate=pl.CostEstimate(
            flops=10 * tokens * width, bytes_accessed=4 * tokens * width, transcendentals=0
        ),
        compiler_params=pltpu.CompilerParams(vmem_limit_bytes=50 * MIB),
        name="gate_rows",
    )(*inputs, *events)


def pack_kernel(*refs):
    rows = refs[0].shape[0]
    for k, ref in enumerate(refs[:-1]):
        refs[-1][k * rows : (k + 1) * rows, :] = ref[...]


def pack_copies(n, *refs):
    out_ref, sems = refs[-2], refs[-1]
    rows = refs[0].shape[0]
    copies = [
        pltpu.make_async_copy(refs[k], out_ref.at[pl.ds(k * rows, rows), :], sems.at[k]) for k in range(n)
    ]
    for copy in copies:
        copy.start()
    for copy in copies:
        copy.wait()


def pack(pieces, name, event, copy=False):
    rows, width = pieces[0].shape
    n = len(pieces)
    out = shape((n * rows, width), pieces[0].dtype)
    if copy:
        anywhere = pl.BlockSpec(memory_space=pl.ANY)
        return pl.pallas_call(
            functools.partial(pack_copies, n),
            out_shape=out,
            in_specs=[anywhere] * (n + 1),
            out_specs=anywhere,
            scratch_shapes=[pltpu.SemaphoreType.DMA((n,))],
            cost_estimate=pl.CostEstimate(flops=0, bytes_accessed=4 * n * rows * width, transcendentals=0),
            compiler_params=pltpu.CompilerParams(vmem_limit_bytes=4 * MIB),
            name=name,
        )(*pieces, event)
    return call(pack_kernel, [out], pieces, name, after=[event])[0]


def pass_kernel(from_ref, to_ref):
    to_ref[...] = from_ref[...]


def passed(values, name, event):
    return call(pass_kernel, [shape(values.shape, values.dtype)], [values], name, after=[event])[0]


def add_kernel(*refs):
    total = refs[0][...]
    for ref in refs[1:-1]:
        total = total + ref[...]
    refs[-1][...] = total


def forward_kernel(n, packs, side_ref, places_ref, weight_ref, *refs):
    refs = refs[:n] + (weight_ref,) + refs[n:]
    pieces, shares = refs[:n], refs[n + 1 : n + 1 + packs]
    outs = refs[n + 1 + packs : 2 * n + 1 + packs]
    mirror_ref, held_ref, away_ref = refs[2 * n + 1 + packs :]
    rows = pieces[0].shape[0]
    depth = weight_ref.shape[0]
    side = side_ref[0]
    for k in range(n):
        part = slice(k * rows, (k + 1) * rows)
        held_ref[part, :] = pieces[k][:, pl.ds(pl.multiple_of(side * depth, LANES), depth)]
        away_ref[part, :] = pieces[k][:, pl.ds(pl.multiple_of((1 - side) * depth, LANES), depth)]
    count = places_ref.shape[0] // packs
    share = shares[0].shape[0] // count
    for p in range(packs):
        for j in range(count):
            at = pl.multiple_of(places_ref[p * count + j] * share, share)
            mirror_ref[pl.ds(at, share), :] = shares[p][j * share : (j + 1) * share, :]
    product = jnp.dot(held_ref[...], weight_ref[...], preferred_element_type=F32)
    product = product + jnp.dot(away_ref[...], mirror_ref[...], preferred_element_type=F32)
    for k in range(n):
        outs[k][...] = product[k * rows : (k + 1) * rows].astype(outs[k].dtype)


def back_kernel(n, packed, side_ref, weight_ref, mirror_ref, *refs):
    pieces, outs = refs[:n], refs[n + packed : -1]
    pack_kernel(*refs[n : n + packed], refs[-1])
    rows = pieces[0].shape[0]
    depth = weight_ref.shape[0]
    side = side_ref[0]
    stack = jnp.concatenate([p[...] for p in pieces], axis=0)
    own = nt(stack, weight_ref[...]).astype(BF16)
    mirror = nt(stack, mirror_ref[...]).astype(BF16)
    for k in range(n):
        part = slice(k * rows, (k + 1) * rows)
        outs[k][:, pl.ds(pl.multiple_of(side * depth, LANES), depth)] = own[part]
        outs[k][:, pl.ds(pl.multiple_of((1 - side) * depth, LANES), depth)] = mirror[part]


def embed_kernel(root, n, *refs):
    parts, away_ref, packed = refs[:n], refs[n], refs[n + 1 : -5]
    pooled_ref, unit_ref, embedded_ref, pack_ref, pass_ref = refs[-5:]
    pass_ref[...] = away_ref[...]
    pooled = parts[0][...]
    for part in parts[1:]:
        pooled = pooled + part[...].astype(F32)
    unit = lax.rsqrt(jnp.mean(pooled * pooled, axis=1, keepdims=True) + embed_eps) / root
    pooled_ref[...] = pooled
    unit_ref[...] = unit
    embedded_ref[...] = (pooled * unit).astype(BF16)
    pack_kernel(*packed, pack_ref)


def count_kernel(n, root, base_ref, slab_ref, *refs):
    lists, counts_ref, scale_ref = refs[:n], refs[n], refs[n + 1]
    queries = lists[0].shape[0]
    rows, width = slab_ref.shape
    slab = slab_ref[...].astype(F32)
    high, low = split_bf16(slab * slab)
    ones = jnp.ones((8, width), BF16)
    row_sq = (nt(ones, high) + nt(ones, low))[0:1]
    scale_ref[...] = lax.rsqrt(row_sq / width + embed_eps) / root / sharpness_divisor
    ids = lax.broadcasted_iota(jnp.int32, (queries, LANES), 1)
    for k in range(n):
        own = lists[k][...] - base_ref[0]
        columns = [
            jnp.broadcast_to(own[:, entry : entry + 1], (queries, LANES)) for entry in range(own.shape[1])
        ]
        for at in range(0, rows, LANES):
            total = jnp.zeros(ids.shape, F32)
            for column in columns:
                total = total + jnp.where(column == ids + at, 1.0, 0.0)
            counts_ref[k * queries : (k + 1) * queries, at : at + LANES] = total


def contrast_kernel(n, *refs):
    (slab_ref, scale_ref, counts_ref), pieces, outs = refs[:3], refs[3 : n + 3], refs[n + 3 :]
    queries, width = pieces[0].shape
    embedded = jnp.concatenate([p[...] for p in pieces], axis=0)
    slab = slab_ref[...]
    scale = scale_ref[...]
    heavy = counts_ref[...] * jnp.exp(nt(embedded, slab) * scale)
    denom = jnp.sum(heavy, axis=1, keepdims=True)
    grad = jnp.dot((heavy * scale).astype(BF16), slab, preferred_element_type=F32)
    high, low = split_bf16(denom)
    lane = lax.broadcasted_iota(jnp.int32, (queries, LANES), 1)
    for k in range(n):
        part = slice(k * queries, (k + 1) * queries)
        outs[k][:, :width] = grad[part].astype(outs[k].dtype)
        if k == 0:
            tail = jnp.where(lane == 0, denom[part], 0.0)
        else:
            tail = jnp.where(lane == 0, high[part].astype(F32), jnp.where(lane == 1, low[part].astype(F32), 0.0))
        outs[k][:, width:] = tail.astype(outs[k].dtype)


def grad_kernel(n, root, *refs):
    pos_ref, pooled_ref, unit_ref, embedded_ref = refs[:4]
    parts = refs[4 : n + 4]
    grad_ref, columns_ref, loss_ref = refs[n + 4 :]
    queries, width = pos_ref.shape
    total = parts[0][:, :width]
    denom = jnp.sum(parts[0][:, width:], axis=1, keepdims=True)
    for part in parts[1:]:
        total = total + part[:, :width].astype(F32)
        denom = denom + jnp.sum(part[:, width:].astype(F32), axis=1, keepdims=True)
    positive = pos_ref[...].astype(F32)
    scale = (
        lax.rsqrt(jnp.mean(positive * positive, axis=1, keepdims=True) + embed_eps)
        / root
        / sharpness_divisor
    )
    score = jnp.sum(embedded_ref[...].astype(F32) * positive, axis=1, keepdims=True) * scale
    pos_exp = jnp.exp(score)
    denom = denom + pos_exp
    loss_ref[...] = jnp.broadcast_to(jnp.sum(jnp.log(denom) - score), loss_ref.shape)
    grad_embed = total / denom + (pos_exp / denom - 1.0) * scale * positive
    pooled, unit = pooled_ref[...], unit_ref[...]
    mean_sq = jnp.mean(pooled * pooled, axis=1, keepdims=True)
    radial = jnp.sum(pooled * grad_embed, axis=1, keepdims=True)
    grad = unit * grad_embed - pooled * (radial * unit / (width * (mean_sq + embed_eps)))
    grad = grad.astype(BF16)
    grad_ref[...] = grad
    cols = columns_ref.shape[2]
    places = width // cols
    for j in range(columns_ref.shape[0]):
        at = (j % places) * cols
        columns_ref[j] = grad[:, at : at + cols]


def slope_kernel(seq, blocks, z_ref, normed_ref, curve_ref, loss_ref, *rest):
    half = blocks // 2
    backs, outs, (all_ref, sum_ref) = rest[:half], rest[half : 2 * half], rest[-2:]
    step = pl.program_id(0)
    tokens, width = normed_ref.shape
    count = tokens // seq
    depth = width // blocks
    place = lax.rem(z_ref[0], half)

    def block_at(j, k):
        return pl.ds(pl.multiple_of((j * half + lax.rem(place + k, half)) * depth, LANES), depth)

    @pl.when(step == 0)
    def _():
        sum_ref[...] = jnp.zeros_like(sum_ref)
        for k in range(half):
            for j in range(2):
                all_ref[:, block_at(j, k)] = backs[k][:, j * depth : (j + 1) * depth].astype(F32)

    back = all_ref[pl.ds(pl.multiple_of(step * count, count), count), :]
    normed = normed_ref[...].astype(F32).reshape(count, seq, width)
    dots = jnp.sum(normed * back[:, None, :], axis=2, keepdims=True)
    slope = curve_ref[...].reshape(count, seq, 1) * dots
    heavy = (slope * normed).reshape(tokens // 8, 8, width)
    sum_ref[...] += jnp.sum(heavy, axis=0)

    @pl.when(step == pl.num_programs(0) - 1)
    def _():
        total = jnp.sum(sum_ref[...], axis=0, keepdims=True)
        lines = depth // LANES
        height = outs[0].shape[0]
        loss = jnp.broadcast_to(loss_ref[...], (height - 2 * lines, LANES))
        all_ref[0:1, :] = total
        for k in range(half):
            for j in range(2):
                row = all_ref[0:1, block_at(j, k)]
                for line in range(lines):
                    outs[k][j * lines + line : j * lines + line + 1, :] = row[
                        :, line * LANES : (line + 1) * LANES
                    ]
            outs[k][2 * lines :, :] = loss


def slope_rows(z, normed, curve, loss, backs, seq, blocks):
    tokens, width = normed.shape
    half = blocks // 2
    height = 2 * (width // blocks // LANES) // 8 * 8 + 8
    queries = tokens // seq
    group = 8 if queries % 8 == 0 else queries
    step_tokens = group * seq
    whole = lambda dims: pl.BlockSpec(dims, lambda i: (0, 0))
    return pl.pallas_call(
        functools.partial(slope_kernel, seq, blocks),
        grid=(queries // group,),
        out_shape=[shape((height, LANES), F32)] * half,
        in_specs=[
            SMEM,
            pl.BlockSpec((step_tokens, width), lambda i: (i, 0)),
            pl.BlockSpec((step_tokens, 1), lambda i: (i, 0)),
            whole((1, LANES)),
        ]
        + [whole((queries, width // half))] * half,
        out_specs=[whole((height, LANES))] * half,
        scratch_shapes=[pltpu.VMEM((queries, width), F32), pltpu.VMEM((8, width), F32)],
        cost_estimate=pl.CostEstimate(
            flops=4 * tokens * width, bytes_accessed=2 * tokens * width, transcendentals=0
        ),
        compiler_params=pltpu.CompilerParams(vmem_limit_bytes=20 * MIB),
        name="slope_rows",
    )(z, normed, curve, loss, *backs)


def columns_kernel(n, copies, order_ref, grads_ref, *refs):
    pieces, (out_ref, sorted_ref) = refs[:n], refs[n:]
    chunk = grads_ref.shape[1]
    copies[0].wait()
    for j in range(sorted_ref.shape[0] // chunk):
        sorted_ref[j * chunk : (j + 1) * chunk, :] = grads_ref[order_ref[j]]
    at = pieces[0].shape[0]
    copies[1].wait()
    total = tn(sorted_ref[0:at, :], pieces[0][...])
    for k, piece in enumerate(pieces[1:]):
        rows = piece.shape[0]
        copies[k + 2].wait()
        total = total + tn(sorted_ref[at : at + rows, :], piece[...])
        at += rows
    out_ref[...] = total.T.astype(BF16)


def query_kernel(side_ref, weight_ref, mirror_ref, parts_ref, part_ref, slope_ref, loss_ref):
    depth = weight_ref.shape[0]
    lines = depth // LANES
    total = parts_ref[...]
    loss_ref[...] = total[2 * lines : 2 * lines + 1]
    side = side_ref[0]
    part = jnp.zeros(part_ref.shape, F32)
    for j in range(2):
        rows = total[j * lines : (j + 1) * lines]
        row = jnp.concatenate([rows[k : k + 1] for k in range(lines)], axis=1)
        high, low = split_bf16(jnp.broadcast_to(row, (8, depth)))

        @pl.when(side == j)
        def _():
            slope_ref[...] = rows

        weight = jnp.where(side == j, weight_ref[...], mirror_ref[...])
        part = part + jnp.dot(high, weight, preferred_element_type=F32)[0:1]
        part = part + jnp.dot(low, weight, preferred_element_type=F32)[0:1]
    part_ref[...] = part


def finish_kernel(n, place_ref, pool_ref, slope_ref, *refs):
    pieces, result_ref, token_ref, out_ref, sems = refs[:n], *refs[n:]
    token_ref[...] = jnp.zeros_like(token_ref)
    places = place_ref.shape[0]
    rows, cols = out_ref.shape[0], pieces[0].shape[1]
    copies = []
    for line in range(rows // LANES):
        part = pl.ds(line * LANES, LANES)
        slope = jnp.broadcast_to(slope_ref[line : line + 1, :], (LANES, LANES)).T
        for k in range(places):
            base = k % (places // n) * rows + line * LANES
            mine = pieces[k // (places // n)][base : base + LANES, :].astype(F32)
            at = pl.ds(pl.multiple_of(place_ref[k] * cols, LANES), cols)
            out_ref[part, at] = mine + slope * pool_ref[:, at]
        copies.append(
            pltpu.make_async_copy(out_ref.at[part, :], result_ref.at[part, :], sems.at[line])
        )
        copies[-1].start()
    for copy in copies:
        copy.wait()


def body(hidden_states, positives, negatives, lengths, norm_gain, proj_weight, pool_query, slab):
    queries, seq, width = hidden_states.shape
    depth, proj_width = proj_weight.shape
    n_z, n_g, n_i = lax.axis_size("fsdp"), lax.axis_size("grp"), lax.axis_size("item")
    assert n_z % 2 == 0
    half = n_z // 2
    n_c = 2 if n_i % 2 == 0 else 1
    n_h = n_i // n_c
    n_plane = n_g * n_i
    n_all = n_z * n_plane
    z, g, i = lax.axis_index("fsdp"), lax.axis_index("grp"), lax.axis_index("item")
    h, c = i // n_c, lax.rem(i, n_c)
    side, member = z // half, lax.rem(z, half)
    root = math.sqrt(proj_width)
    steps_z, steps_i = range(1, n_z), range(1, n_i)

    def ints(*values):
        return jnp.stack([jnp.asarray(v, jnp.int32) for v in values])

    z_arr, side_arr = ints(z), ints(side)

    def plane_shift(values, dg, dh, dc):
        pairs = []
        for pg in range(n_g):
            for ph in range(n_h):
                for pc in range(n_c):
                    to = ((pg + dg) % n_g) * n_i + ((ph + dh) % n_h) * n_c + (pc + dc) % n_c
                    pairs.append((pg * n_i + ph * n_c + pc, to))
        return lax.ppermute(values, PLANE, pairs)

    def half_shift(values, k):
        pairs = [(a, a // half * half + (a % half + k) % half) for a in range(n_z)]
        return lax.ppermute(values, "fsdp", pairs)

    def mirror_shift(values):
        return lax.ppermute(values, "fsdp", [(a, (a + half) % n_z) for a in range(n_z)])

    def source(dg, dh, dc):
        return (
            lax.rem(g - dg + n_g, n_g),
            lax.rem(h - dh + n_h, n_h) * n_c + lax.rem(c - dc + n_c, n_c),
        )

    chips = [(dg, dh) for dg in range(n_g) for dh in range(n_h)]

    share = depth // n_plane
    place = g * n_i + i
    weight_share = lax.dynamic_slice_in_dim(proj_weight, place * share, share, 0)
    far_share = mirror_shift(weight_share)

    block_u = call(
        u_kernel, [shape((1, depth), F32)], [proj_weight, pool_query.reshape(1, -1)], "block_u",
        after=[weight_share],
    )[0]
    u_parts = [block_u] + [shift(block_u, "fsdp", k) for k in steps_z]
    u = jnp.zeros((1, width), F32)
    for k in range(n_z):
        u = lax.dynamic_update_slice(u, u_parts[k], (0, lax.rem(z - k + n_z, n_z) * depth))

    share_places = []
    for dc in range(n_c):
        for dg, dh in chips:
            from_g, from_i = source(dg, dh, dc)
            share_places.append(from_g * n_i + from_i)
    share_places = ints(*share_places)
    order = []
    for dc in range(n_c):
        for dg in range(n_g):
            order += [(side, k, dg, dh, dc) for dh in range(n_h) for k in range(half)]
        for dh in range(n_h):
            order += [(1 - side, k, dg, dh, dc) for dg in range(n_g) for k in range(half)]
    ranks = []
    for from_side, k, dg, dh, dc in order:
        from_g, from_i = source(dg, dh, dc)
        from_z = from_side * half + lax.rem(member - k + half, half)
        ranks.append((from_z * n_g + from_g) * n_i + from_i)
    ranks = ints(*ranks)
    both_arr, base_arr = ints(z, i), ints(i * slab.shape[0])
    token_lengths = jnp.broadcast_to(lengths[:, None], (queries, seq)).reshape(-1, 1)
    events = [far_share, share_places, ranks, base_arr, side_arr]
    chip_shares = [far_share if dg == dh == 0 else plane_shift(far_share, dg, dh, 0) for dg, dh in chips]
    gate_outs = gate_rows(
        both_arr, hidden_states.reshape(-1, width), norm_gain.astype(F32).reshape(1, width), u,
        token_lengths, negatives, events, seq, root, n_z, n_i,
    )
    sends, (normed, gated, curve), lists = gate_outs[:half], gate_outs[half : half + 3], gate_outs[half + 3 :]
    packs = [pack(chip_shares, "pack_shares", gated)]
    packs += [plane_shift(packs[0], 0, 0, dc) for dc in range(1, n_c)]

    pieces = [sends[0]] + [half_shift(sends[k], k) for k in range(1, half)]
    lists = [lists[0]] + [shift(lists[k], "item", k) for k in steps_i]
    counts, slab_scale = call(
        functools.partial(count_kernel, n_i, root),
        [shape((n_i * queries, slab.shape[0]), F32), shape((1, slab.shape[0]), F32)],
        [base_arr, slab] + lists, "list_counts", smem=1,
    )
    block = shape((half * queries, depth), BF16)
    *parts, mirror, held, away = call(
        functools.partial(forward_kernel, half, n_c),
        [shape((queries, proj_width), F32)]
        + [shape((queries, proj_width), BF16)] * (half - 1)
        + [shape((depth, proj_width), BF16), block, block],
        [side_arr, share_places, proj_weight] + pieces + packs, "forward",
        flops=4 * half * queries * depth * proj_width, smem=2, after=[counts],
    )
    parts = [parts[0]] + [half_shift(parts[k], -k) for k in range(1, half)]
    near = [held] + [plane_shift(held, 0, dh, 0) for dh in range(1, n_h)]
    row = shape((queries, proj_width), F32)
    row16 = shape((queries, proj_width), BF16)
    pooled, unit, embedded, near, away = call(
        functools.partial(embed_kernel, root, half),
        [row, shape((queries, 1), F32), row16, shape((n_h * half * queries, depth), BF16), block],
        parts + [away] + near, "embed",
    )
    other = mirror_shift(away)

    pieces = [embedded] + [shift(embedded, "item", k) for k in steps_i]
    near_far = [plane_shift(near, dg, 0, 0) for dg in range(1, n_g)]
    near_cores = [plane_shift(near, 0, 0, dc) for dc in range(1, n_c)]
    wide = (queries, proj_width + LANES)
    parts = call(
        functools.partial(contrast_kernel, n_i),
        [shape(wide, F32)] + [shape(wide, BF16)] * (n_i - 1),
        [slab, slab_scale, counts] + pieces, "contrast",
        flops=4 * n_i * queries * slab.shape[0] * proj_width, after=near_cores,
    )
    near_far_late = [passed(array, "near_far", parts[0]) for array in near_far]
    parts = [parts[0]] + [shift(parts[k], "item", -k) for k in steps_i]
    near_far_cores = [[plane_shift(array, 0, 0, dc) for array in near_far_late] for dc in range(1, n_c)]
    other = passed(other, "other", parts[1 % n_i])
    others = [other] + [plane_shift(other, dg, 0, 0) for dg in range(1, n_g)]
    cols = proj_width // n_plane
    grad, grad_columns, loss = call(
        functools.partial(grad_kernel, n_i, root),
        [row16, shape((n_all, queries, cols), BF16), shape((1, LANES), F32)],
        [positives, pooled, unit, embedded] + parts, "grad_pooled",
    )

    pieces = [grad] + [half_shift(grad, k) for k in range(1, half)]
    *backs, others = call(
        functools.partial(back_kernel, half, n_g),
        [shape((queries, 2 * depth), BF16)] * half + [shape((n_g * half * queries, depth), BF16)],
        [side_arr, proj_weight, mirror] + pieces + others, "backward",
        flops=4 * half * queries * depth * proj_width, smem=1, after=near_cores + sum(near_far_cores, []),
    )
    backs = [backs[0]] + [half_shift(backs[k], -k) for k in range(1, half)]
    all_columns = lax.all_to_all(
        passed(grad_columns, "columns_out", backs[-1]), EVERY, 0, 0, tiled=True
    )
    slopes = slope_rows(both_arr, normed, curve, loss, backs, seq, n_z)
    def total(parts, name):
        return call(add_kernel, [shape(parts[0].shape, F32)], parts, name)[0]

    own_slope = slopes[0]
    if n_g > 1:
        slopes = [total([a] + [shift(a, "grp", k) for k in range(1, n_g)], "sum_groups") for a in slopes]
    across = [plane_shift(others, 0, dh, 0) for dh in range(1, n_h)]
    late = [pack([array], "late", own_slope) for array in across]
    spread = []
    for dc in range(n_c):
        if dc == 0:
            spread += [near, *near_far, others, *across]
        else:
            spread += [near_cores[dc - 1], *near_far_cores[dc - 1]]
            spread += [plane_shift(array, 0, 0, dc) for array in [others, *late]]
    block_columns = call(
        functools.partial(columns_kernel, len(spread)), [shape((depth, cols), BF16)],
        [ranks, all_columns] + spread, "grad_columns",
        flops=2 * n_all * queries * depth * cols, scratch=[pltpu.VMEM((n_all * queries, cols), BF16)], smem=1, copy=True, after=slopes,
    )[0]
    on_chips = [block_columns if dg == dh == 0 else plane_shift(block_columns, dg, dh, 0) for dg, dh in chips]
    slopes = [passed(array, "slope_out", block_columns) for array in slopes]
    slope = total([slopes[0]] + [half_shift(slopes[k], k) for k in range(1, half)], "sum_half")
    slope = total([slope, mirror_shift(slope)], "sum_mirror")
    if n_i > 1:
        slope = total([slope] + [shift(slope, "item", k) for k in steps_i], "sum_items")
    query_part, my_slope, loss_total = call(
        query_kernel,
        [shape((1, proj_width), F32), shape((depth // LANES, LANES), F32), shape((1, LANES), F32)],
        [side_arr, proj_weight, mirror, slope], "slope_sum", smem=1,
    )
    finished = [pack(on_chips, "pack_columns", slope, True)]
    finished += [plane_shift(finished[0], 0, 0, dc) for dc in range(1, n_c)]
    query_parts = [query_part] + [half_shift(query_part, k) for k in range(1, half)]
    grad_proj, finish_token = call(
        functools.partial(finish_kernel, len(finished)),
        [shape((depth, proj_width), F32), shape((8, LANES), F32)],
        [share_places, pool_query.reshape(1, -1), my_slope] + finished, "finish", smem=1, streamed=True,
        scratch=[pltpu.VMEM((depth, proj_width), F32), pltpu.SemaphoreType.DMA((depth // LANES,))],
    )
    grad_query = call(
        add_kernel, [shape((1, proj_width), F32)], query_parts, "query_sum", after=[finish_token]
    )[0]
    mean_loss = loss_total[0, 0] / (queries * n_all)
    return (grad_proj, grad_query.reshape(proj_width), mean_loss)


def solution(mesh):
    return jax.shard_map(
        body,
        mesh=mesh,
        in_specs=(
            P(("grp", "fsdp", "item"), None, None),
            P(("grp", "fsdp", "item"), None),
            P(("grp", "fsdp", "item"), None),
            P(("grp", "fsdp", "item")),
            P(),
            P("fsdp", None),
            P(),
            P("item", None),
        ),
        out_specs=(P("fsdp", None), P(), P()),
        check_vma=False,
    )
```

```python
import functools
import math

import jax
import jax.numpy as jnp
from jax import lax
from jax.experimental import pallas as pl
from jax.experimental.pallas import tpu as pltpu
from jax.sharding import PartitionSpec as P

sharpness_divisor = 0.05
norm_eps = 1e-05
embed_eps = 1e-06

EVERY = ("fsdp", "grp", "item")
PLANE = ("grp", "item")
F32 = jnp.float32
BF16 = jnp.bfloat16
LANES = 128
MIB = 1024 * 1024
VMEM = pl.BlockSpec(memory_space=pltpu.VMEM)
SMEM = pl.BlockSpec(memory_space=pltpu.SMEM)


def shape(dims, dtype):
    return jax.ShapeDtypeStruct(dims, dtype)


def copying(kernel, smem, shapes):
    n = len(shapes)

    def run(*refs):
        sources, buffers, sems = refs[smem : smem + n], refs[-n - 1 : -1], refs[-1]
        copies = [
            pltpu.make_async_copy(sources[k], buffers[k], sems.at[k]) for k in range(n)
        ]
        for copy in copies:
            copy.start()
        kernel(copies, *refs[:smem], *buffers, *refs[smem + n : -n - 1])

    return run


def call(kernel, outs, ins, name, flops=0, scratch=(), smem=0, after=(), copy=False, streamed=False):
    count = len(ins)
    if copy:
        shapes = [pltpu.VMEM(a.shape, a.dtype) for a in ins[smem:]]
        kernel = copying(kernel, smem, shapes)
        scratch = [*scratch, *shapes, pltpu.SemaphoreType.DMA((len(shapes),))]
    moved = sum(math.prod(a.shape) * a.dtype.itemsize for a in list(ins) + list(outs))
    held = 0 if copy or streamed else sum(math.prod(s.shape) * jnp.dtype(s.dtype).itemsize for s in scratch)

    def run(*refs):
        kernel(*refs[:count], *refs[count + len(after) :])

    return pl.pallas_call(
        run,
        out_shape=outs,
        in_specs=[SMEM] * smem
        + [pl.BlockSpec(memory_space=pl.ANY) if copy else VMEM] * (count - smem)
        + [pl.BlockSpec(memory_space=pl.ANY)] * len(after),
        out_specs=([pl.BlockSpec(memory_space=pl.ANY)] if streamed else [VMEM]) + [VMEM] * (len(outs) - 1),
        scratch_shapes=list(scratch),
        cost_estimate=pl.CostEstimate(flops=flops, bytes_accessed=moved, transcendentals=0),
        compiler_params=pltpu.CompilerParams(
            vmem_limit_bytes=61 * MIB if copy else 2 * (moved + held) + 6 * MIB
        ),
        name=name,
    )(*ins, *after)


def shift(values, axis, k):
    n = lax.axis_size(axis)
    return lax.ppermute(values, axis, [(i, (i + k) % n) for i in range(n)])


def split_bf16(values):
    high = values.astype(BF16)
    low = (values - high.astype(F32)).astype(BF16)
    return high, low


def nt(left, right):
    return lax.dot_general(left, right, (((1,), (1,)), ((), ())), preferred_element_type=F32)


def tn(left, right):
    return lax.dot_general(left, right, (((0,), (0,)), ((), ())), preferred_element_type=F32)


def u_kernel(weight_ref, pool_ref, u_ref):
    pool = jnp.broadcast_to(pool_ref[...], (8, pool_ref.shape[1]))
    high = pool.astype(BF16)
    low, last = split_bf16(pool - high.astype(F32))
    weight = weight_ref[...]
    u_ref[...] = (nt(high, weight) + nt(low, weight) + nt(last, weight))[0:1]


def gate_kernel(seq, root, blocks, z_ref, states_ref, gain_ref, u_ref, len_ref, lists_ref, *rest):
    half = blocks // 2
    outs, normed_ref, gated_ref, curve_ref, copies, rows_ref = (
        rest[:half], rest[half], rest[half + 1], rest[half + 2], rest[half + 3 : -1], rest[-1]
    )
    step = pl.program_id(0)
    tokens, width = states_ref.shape
    count = tokens // seq
    chunk = 4 * LANES if width % (4 * LANES) == 0 else width
    logits = []
    for top in range(0, tokens, 32):
        rows = slice(top, top + 32)
        squares = jnp.zeros((32, chunk), F32)
        for at in range(0, width, chunk):
            part = states_ref[rows, at : at + chunk].astype(F32)
            squares = squares + part * part
        inv_rms = lax.rsqrt(jnp.sum(squares, axis=1, keepdims=True) / width + norm_eps)
        total = jnp.zeros((32, chunk), F32)
        for at in range(0, width, chunk):
            part = states_ref[rows, at : at + chunk].astype(F32)
            part = (part * inv_rms * gain_ref[:, at : at + chunk]).astype(BF16)
            normed_ref[rows, at : at + chunk] = part
            total = total + part.astype(F32) * u_ref[:, at : at + chunk]
        logits.append(jnp.sum(total, axis=1, keepdims=True))
    logit = jnp.concatenate(logits, axis=0) / root
    gate = 1.0 / (1.0 + jnp.exp(-logit))
    slot = lax.rem(lax.broadcasted_iota(jnp.int32, (tokens, 1), 0), seq)
    valid = jnp.where(slot < len_ref[...], 1.0, 0.0) / len_ref[...].astype(F32)
    gated = valid * gate
    gated_ref[...] = gated
    curve_ref[...] = gated * (1.0 - gate) / root
    owner = lax.broadcasted_iota(jnp.int32, (tokens, count), 0) // seq
    mine = owner == lax.broadcasted_iota(jnp.int32, (tokens, count), 1)
    high, low = split_bf16(jnp.where(mine, gated, 0.0))
    both = tn(jnp.concatenate([high, low], axis=1), normed_ref[...])
    rows_ref[pl.ds(pl.multiple_of(step * count, count), count), :] = both[:count] + both[count:]

    @pl.when(step == pl.num_programs(0) - 1)
    def _():
        owners = len(copies)
        own = lists_ref.shape[1] // owners
        for k in range(owners):
            picked = jnp.zeros(copies[k].shape, jnp.int32)
            for j in range(owners):
                picked = jnp.where(
                    lax.rem(z_ref[1] + k, owners) == j, lists_ref[:, j * own : (j + 1) * own], picked
                )
            copies[k][...] = picked
        depth = width // blocks
        place = lax.rem(z_ref[0], half)
        for k in range(half):
            for j in range(2):
                at = (j * half + lax.rem(place + k, half)) * depth
                outs[k][:, j * depth : (j + 1) * depth] = rows_ref[
                    :, pl.ds(pl.multiple_of(at, LANES), depth)
                ].astype(BF16)


def gate_rows(z, states, gain, u, token_lengths, lists, events, seq, root, blocks, owners):
    tokens, width = states.shape
    queries = tokens // seq
    group = 8 if queries % 8 == 0 else queries
    step_tokens = group * seq
    half = blocks // 2
    outs = [shape((queries, width // half), BF16)] * half
    outs += [shape((tokens, width), BF16)] + [shape((tokens, 1), F32)] * 2
    outs += [shape((queries, lists.shape[1] // owners), lists.dtype)] * owners
    column = pl.BlockSpec((step_tokens, 1), lambda i: (i, 0))
    rows = pl.BlockSpec((step_tokens, width), lambda i: (i, 0))
    inputs = [z, states, gain, u, token_lengths, lists]

    def run(*refs):
        gate_kernel(seq, root, blocks, *refs[: len(inputs)], *refs[len(inputs) + len(events) :])

    whole = lambda dims: pl.BlockSpec(dims, lambda i: (0, 0))
    return pl.pallas_call(
        run,
        grid=(queries // group,),
        out_shape=outs,
        in_specs=[
            SMEM,
            rows,
            whole((1, width)),
            whole((1, width)),
            column,
            whole(lists.shape),
        ]
        + [pl.BlockSpec(memory_space=pl.ANY)] * len(events),
        out_specs=[whole((queries, width // half))] * half + [rows] + [column] * 2
        + [whole((queries, lists.shape[1] // owners))] * owners,
        scratch_shapes=[pltpu.VMEM((queries, width), F32)],
        cost_estimate=pl.CostEstimate(
            flops=10 * tokens * width, bytes_accessed=4 * tokens * width, transcendentals=0
        ),
        compiler_params=pltpu.CompilerParams(vmem_limit_bytes=50 * MIB),
        name="gate_rows",
    )(*inputs, *events)


def pack_kernel(*refs):
    rows = refs[0].shape[0]
    for k, ref in enumerate(refs[:-1]):
        refs[-1][k * rows : (k + 1) * rows, :] = ref[...]


def pack_copies(n, *refs):
    out_ref, sems = refs[-2], refs[-1]
    rows = refs[0].shape[0]
    copies = [
        pltpu.make_async_copy(refs[k], out_ref.at[pl.ds(k * rows, rows), :], sems.at[k]) for k in range(n)
    ]
    for copy in copies:
        copy.start()
    for copy in copies:
        copy.wait()


def pack(pieces, name, event, copy=False):
    rows, width = pieces[0].shape
    n = len(pieces)
    out = shape((n * rows, width), pieces[0].dtype)
    if copy:
        anywhere = pl.BlockSpec(memory_space=pl.ANY)
        return pl.pallas_call(
            functools.partial(pack_copies, n),
            out_shape=out,
            in_specs=[anywhere] * (n + 1),
            out_specs=anywhere,
            scratch_shapes=[pltpu.SemaphoreType.DMA((n,))],
            cost_estimate=pl.CostEstimate(flops=0, bytes_accessed=4 * n * rows * width, transcendentals=0),
            compiler_params=pltpu.CompilerParams(vmem_limit_bytes=4 * MIB),
            name=name,
        )(*pieces, event)
    return call(pack_kernel, [out], pieces, name, after=[event])[0]


def pass_kernel(from_ref, to_ref):
    to_ref[...] = from_ref[...]


def passed(values, name, event):
    return call(pass_kernel, [shape(values.shape, values.dtype)], [values], name, after=[event])[0]


def add_kernel(*refs):
    total = refs[0][...]
    for ref in refs[1:-1]:
        total = total + ref[...]
    refs[-1][...] = total


def forward_kernel(n, packs, side_ref, places_ref, weight_ref, *refs):
    refs = refs[:n] + (weight_ref,) + refs[n:]
    pieces, shares = refs[:n], refs[n + 1 : n + 1 + packs]
    outs = refs[n + 1 + packs : 2 * n + 1 + packs]
    mirror_ref, held_ref, away_ref = refs[2 * n + 1 + packs :]
    rows = pieces[0].shape[0]
    depth = weight_ref.shape[0]
    side = side_ref[0]
    for k in range(n):
        part = slice(k * rows, (k + 1) * rows)
        held_ref[part, :] = pieces[k][:, pl.ds(pl.multiple_of(side * depth, LANES), depth)]
        away_ref[part, :] = pieces[k][:, pl.ds(pl.multiple_of((1 - side) * depth, LANES), depth)]
    count = places_ref.shape[0] // packs
    share = shares[0].shape[0] // count
    for p in range(packs):
        for j in range(count):
            at = pl.multiple_of(places_ref[p * count + j] * share, share)
            mirror_ref[pl.ds(at, share), :] = shares[p][j * share : (j + 1) * share, :]
    product = jnp.dot(held_ref[...], weight_ref[...], preferred_element_type=F32)
    product = product + jnp.dot(away_ref[...], mirror_ref[...], preferred_element_type=F32)
    for k in range(n):
        outs[k][...] = product[k * rows : (k + 1) * rows].astype(outs[k].dtype)


def back_kernel(n, packed, side_ref, weight_ref, mirror_ref, *refs):
    pieces, outs = refs[:n], refs[n + packed : -1]
    pack_kernel(*refs[n : n + packed], refs[-1])
    rows = pieces[0].shape[0]
    depth = weight_ref.shape[0]
    side = side_ref[0]
    stack = jnp.concatenate([p[...] for p in pieces], axis=0)
    own = nt(stack, weight_ref[...]).astype(BF16)
    mirror = nt(stack, mirror_ref[...]).astype(BF16)
    for k in range(n):
        part = slice(k * rows, (k + 1) * rows)
        outs[k][:, pl.ds(pl.multiple_of(side * depth, LANES), depth)] = own[part]
        outs[k][:, pl.ds(pl.multiple_of((1 - side) * depth, LANES), depth)] = mirror[part]


def embed_kernel(root, n, *refs):
    parts, away_ref, packed = refs[:n], refs[n], refs[n + 1 : -5]
    pooled_ref, unit_ref, embedded_ref, pack_ref, pass_ref = refs[-5:]
    pass_ref[...] = away_ref[...]
    pooled = parts[0][...]
    for part in parts[1:]:
        pooled = pooled + part[...].astype(F32)
    unit = lax.rsqrt(jnp.mean(pooled * pooled, axis=1, keepdims=True) + embed_eps) / root
    pooled_ref[...] = pooled
    unit_ref[...] = unit
    embedded_ref[...] = (pooled * unit).astype(BF16)
    pack_kernel(*packed, pack_ref)


def count_kernel(n, root, base_ref, slab_ref, *refs):
    lists, counts_ref, scale_ref = refs[:n], refs[n], refs[n + 1]
    queries = lists[0].shape[0]
    rows, width = slab_ref.shape
    slab = slab_ref[...].astype(F32)
    high, low = split_bf16(slab * slab)
    ones = jnp.ones((8, width), BF16)
    row_sq = (nt(ones, high) + nt(ones, low))[0:1]
    scale_ref[...] = lax.rsqrt(row_sq / width + embed_eps) / root / sharpness_divisor
    ids = lax.broadcasted_iota(jnp.int32, (queries, LANES), 1)
    for k in range(n):
        own = lists[k][...] - base_ref[0]
        columns = [
            jnp.broadcast_to(own[:, entry : entry + 1], (queries, LANES)) for entry in range(own.shape[1])
        ]
        for at in range(0, rows, LANES):
            total = jnp.zeros(ids.shape, F32)
            for column in columns:
                total = total + jnp.where(column == ids + at, 1.0, 0.0)
            counts_ref[k * queries : (k + 1) * queries, at : at + LANES] = total


def contrast_kernel(n, *refs):
    (slab_ref, scale_ref, counts_ref), pieces, outs = refs[:3], refs[3 : n + 3], refs[n + 3 :]
    queries, width = pieces[0].shape
    embedded = jnp.concatenate([p[...] for p in pieces], axis=0)
    slab = slab_ref[...]
    scale = scale_ref[...]
    heavy = counts_ref[...] * jnp.exp(nt(embedded, slab) * scale)
    denom = jnp.sum(heavy, axis=1, keepdims=True)
    grad = jnp.dot((heavy * scale).astype(BF16), slab, preferred_element_type=F32)
    high, low = split_bf16(denom)
    lane = lax.broadcasted_iota(jnp.int32, (queries, LANES), 1)
    for k in range(n):
        part = slice(k * queries, (k + 1) * queries)
        outs[k][:, :width] = grad[part].astype(outs[k].dtype)
        if k == 0:
            tail = jnp.where(lane == 0, denom[part], 0.0)
        else:
            tail = jnp.where(lane == 0, high[part].astype(F32), jnp.where(lane == 1, low[part].astype(F32), 0.0))
        outs[k][:, width:] = tail.astype(outs[k].dtype)


def grad_kernel(n, root, *refs):
    pos_ref, pooled_ref, unit_ref, embedded_ref = refs[:4]
    parts = refs[4 : n + 4]
    grad_ref, columns_ref, loss_ref = refs[n + 4 :]
    queries, width = pos_ref.shape
    total = parts[0][:, :width]
    denom = jnp.sum(parts[0][:, width:], axis=1, keepdims=True)
    for part in parts[1:]:
        total = total + part[:, :width].astype(F32)
        denom = denom + jnp.sum(part[:, width:].astype(F32), axis=1, keepdims=True)
    positive = pos_ref[...].astype(F32)
    scale = (
        lax.rsqrt(jnp.mean(positive * positive, axis=1, keepdims=True) + embed_eps)
        / root
        / sharpness_divisor
    )
    score = jnp.sum(embedded_ref[...].astype(F32) * positive, axis=1, keepdims=True) * scale
    pos_exp = jnp.exp(score)
    denom = denom + pos_exp
    loss_ref[...] = jnp.broadcast_to(jnp.sum(jnp.log(denom) - score), loss_ref.shape)
    grad_embed = total / denom + (pos_exp / denom - 1.0) * scale * positive
    pooled, unit = pooled_ref[...], unit_ref[...]
    mean_sq = jnp.mean(pooled * pooled, axis=1, keepdims=True)
    radial = jnp.sum(pooled * grad_embed, axis=1, keepdims=True)
    grad = unit * grad_embed - pooled * (radial * unit / (width * (mean_sq + embed_eps)))
    grad = grad.astype(BF16)
    grad_ref[...] = grad
    cols = columns_ref.shape[2]
    places = width // cols
    for j in range(columns_ref.shape[0]):
        at = (j % places) * cols
        columns_ref[j] = grad[:, at : at + cols]


def slope_kernel(seq, blocks, z_ref, normed_ref, curve_ref, loss_ref, *rest):
    half = blocks // 2
    backs, outs, (all_ref, sum_ref) = rest[:half], rest[half : 2 * half], rest[-2:]
    step = pl.program_id(0)
    tokens, width = normed_ref.shape
    count = tokens // seq
    depth = width // blocks
    place = lax.rem(z_ref[0], half)

    def block_at(j, k):
        return pl.ds(pl.multiple_of((j * half + lax.rem(place + k, half)) * depth, LANES), depth)

    @pl.when(step == 0)
    def _():
        sum_ref[...] = jnp.zeros_like(sum_ref)
        for k in range(half):
            for j in range(2):
                all_ref[:, block_at(j, k)] = backs[k][:, j * depth : (j + 1) * depth].astype(F32)

    back = all_ref[pl.ds(pl.multiple_of(step * count, count), count), :]
    normed = normed_ref[...].astype(F32).reshape(count, seq, width)
    dots = jnp.sum(normed * back[:, None, :], axis=2, keepdims=True)
    slope = curve_ref[...].reshape(count, seq, 1) * dots
    heavy = (slope * normed).reshape(tokens // 8, 8, width)
    sum_ref[...] += jnp.sum(heavy, axis=0)

    @pl.when(step == pl.num_programs(0) - 1)
    def _():
        total = jnp.sum(sum_ref[...], axis=0, keepdims=True)
        lines = depth // LANES
        height = outs[0].shape[0]
        loss = jnp.broadcast_to(loss_ref[...], (height - 2 * lines, LANES))
        all_ref[0:1, :] = total
        for k in range(half):
            for j in range(2):
                row = all_ref[0:1, block_at(j, k)]
                for line in range(lines):
                    outs[k][j * lines + line : j * lines + line + 1, :] = row[
                        :, line * LANES : (line + 1) * LANES
                    ]
            outs[k][2 * lines :, :] = loss


def slope_rows(z, normed, curve, loss, backs, seq, blocks):
    tokens, width = normed.shape
    half = blocks // 2
    height = 2 * (width // blocks // LANES) // 8 * 8 + 8
    queries = tokens // seq
    group = 8 if queries % 8 == 0 else queries
    step_tokens = group * seq
    whole = lambda dims: pl.BlockSpec(dims, lambda i: (0, 0))
    return pl.pallas_call(
        functools.partial(slope_kernel, seq, blocks),
        grid=(queries // group,),
        out_shape=[shape((height, LANES), F32)] * half,
        in_specs=[
            SMEM,
            pl.BlockSpec((step_tokens, width), lambda i: (i, 0)),
            pl.BlockSpec((step_tokens, 1), lambda i: (i, 0)),
            whole((1, LANES)),
        ]
        + [whole((queries, width // half))] * half,
        out_specs=[whole((height, LANES))] * half,
        scratch_shapes=[pltpu.VMEM((queries, width), F32), pltpu.VMEM((8, width), F32)],
        cost_estimate=pl.CostEstimate(
            flops=4 * tokens * width, bytes_accessed=2 * tokens * width, transcendentals=0
        ),
        compiler_params=pltpu.CompilerParams(vmem_limit_bytes=20 * MIB),
        name="slope_rows",
    )(z, normed, curve, loss, *backs)


def columns_kernel(n, copies, order_ref, grads_ref, *refs):
    pieces, (out_ref, sorted_ref) = refs[:n], refs[n:]
    chunk = grads_ref.shape[1]
    copies[0].wait()
    for j in range(sorted_ref.shape[0] // chunk):
        sorted_ref[j * chunk : (j + 1) * chunk, :] = grads_ref[order_ref[j]]
    at = pieces[0].shape[0]
    copies[1].wait()
    total = tn(sorted_ref[0:at, :], pieces[0][...])
    for k, piece in enumerate(pieces[1:]):
        rows = piece.shape[0]
        copies[k + 2].wait()
        total = total + tn(sorted_ref[at : at + rows, :], piece[...])
        at += rows
    out_ref[...] = total.T.astype(BF16)


def query_kernel(side_ref, weight_ref, mirror_ref, parts_ref, part_ref, slope_ref, loss_ref):
    depth = weight_ref.shape[0]
    lines = depth // LANES
    total = parts_ref[...]
    loss_ref[...] = total[2 * lines : 2 * lines + 1]
    side = side_ref[0]
    part = jnp.zeros(part_ref.shape, F32)
    for j in range(2):
        rows = total[j * lines : (j + 1) * lines]
        row = jnp.concatenate([rows[k : k + 1] for k in range(lines)], axis=1)
        high, low = split_bf16(jnp.broadcast_to(row, (8, depth)))

        @pl.when(side == j)
        def _():
            slope_ref[...] = rows

        weight = jnp.where(side == j, weight_ref[...], mirror_ref[...])
        part = part + jnp.dot(high, weight, preferred_element_type=F32)[0:1]
        part = part + jnp.dot(low, weight, preferred_element_type=F32)[0:1]
    part_ref[...] = part


def finish_kernel(n, place_ref, pool_ref, slope_ref, *refs):
    pieces, result_ref, token_ref, out_ref, sems = refs[:n], *refs[n:]
    token_ref[...] = jnp.zeros_like(token_ref)
    places = place_ref.shape[0]
    rows, cols = out_ref.shape[0], pieces[0].shape[1]
    copies = []
    for line in range(rows // LANES):
        part = pl.ds(line * LANES, LANES)
        slope = jnp.broadcast_to(slope_ref[line : line + 1, :], (LANES, LANES)).T
        for k in range(places):
            base = k % (places // n) * rows + line * LANES
            mine = pieces[k // (places // n)][base : base + LANES, :].astype(F32)
            at = pl.ds(pl.multiple_of(place_ref[k] * cols, LANES), cols)
            out_ref[part, at] = mine + slope * pool_ref[:, at]
        copies.append(
            pltpu.make_async_copy(out_ref.at[part, :], result_ref.at[part, :], sems.at[line])
        )
        copies[-1].start()
    for copy in copies:
        copy.wait()


def body(hidden_states, positives, negatives, lengths, norm_gain, proj_weight, pool_query, slab):
    queries, seq, width = hidden_states.shape
    depth, proj_width = proj_weight.shape
    n_z, n_g, n_i = lax.axis_size("fsdp"), lax.axis_size("grp"), lax.axis_size("item")
    assert n_z % 2 == 0
    half = n_z // 2
    n_c = 2 if n_i % 2 == 0 else 1
    n_h = n_i // n_c
    n_plane = n_g * n_i
    n_all = n_z * n_plane
    z, g, i = lax.axis_index("fsdp"), lax.axis_index("grp"), lax.axis_index("item")
    h, c = i // n_c, lax.rem(i, n_c)
    side, member = z // half, lax.rem(z, half)
    root = math.sqrt(proj_width)
    steps_z, steps_i = range(1, n_z), range(1, n_i)

    def ints(*values):
        return jnp.stack([jnp.asarray(v, jnp.int32) for v in values])

    z_arr, side_arr = ints(z), ints(side)

    def plane_shift(values, dg, dh, dc):
        pairs = []
        for pg in range(n_g):
            for ph in range(n_h):
                for pc in range(n_c):
                    to = ((pg + dg) % n_g) * n_i + ((ph + dh) % n_h) * n_c + (pc + dc) % n_c
                    pairs.append((pg * n_i + ph * n_c + pc, to))
        return lax.ppermute(values, PLANE, pairs)

    def half_shift(values, k):
        pairs = [(a, a // half * half + (a % half + k) % half) for a in range(n_z)]
        return lax.ppermute(values, "fsdp", pairs)

    def mirror_shift(values):
        return lax.ppermute(values, "fsdp", [(a, (a + half) % n_z) for a in range(n_z)])

    def source(dg, dh, dc):
        return (
            lax.rem(g - dg + n_g, n_g),
            lax.rem(h - dh + n_h, n_h) * n_c + lax.rem(c - dc + n_c, n_c),
        )

    chips = [(dg, dh) for dg in range(n_g) for dh in range(n_h)]

    share = depth // n_plane
    place = g * n_i + i
    weight_share = lax.dynamic_slice_in_dim(proj_weight, place * share, share, 0)
    far_share = mirror_shift(weight_share)

    block_u = call(
        u_kernel, [shape((1, depth), F32)], [proj_weight, pool_query.reshape(1, -1)], "block_u",
        after=[weight_share],
    )[0]
    u_parts = [block_u] + [shift(block_u, "fsdp", k) for k in steps_z]
    u = jnp.zeros((1, width), F32)
    for k in range(n_z):
        u = lax.dynamic_update_slice(u, u_parts[k], (0, lax.rem(z - k + n_z, n_z) * depth))

    share_places = []
    for dc in range(n_c):
        for dg, dh in chips:
            from_g, from_i = source(dg, dh, dc)
            share_places.append(from_g * n_i + from_i)
    share_places = ints(*share_places)
    order = []
    for dc in range(n_c):
        for dg in range(n_g):
            order += [(side, k, dg, dh, dc) for dh in range(n_h) for k in range(half)]
        for dh in range(n_h):
            order += [(1 - side, k, dg, dh, dc) for dg in range(n_g) for k in range(half)]
    ranks = []
    for from_side, k, dg, dh, dc in order:
        from_g, from_i = source(dg, dh, dc)
        from_z = from_side * half + lax.rem(member - k + half, half)
        ranks.append((from_z * n_g + from_g) * n_i + from_i)
    ranks = ints(*ranks)
    both_arr, base_arr = ints(z, i), ints(i * slab.shape[0])
    token_lengths = jnp.broadcast_to(lengths[:, None], (queries, seq)).reshape(-1, 1)
    events = [far_share, share_places, ranks, base_arr, side_arr]
    chip_shares = [far_share if dg == dh == 0 else plane_shift(far_share, dg, dh, 0) for dg, dh in chips]
    gate_outs = gate_rows(
        both_arr, hidden_states.reshape(-1, width), norm_gain.astype(F32).reshape(1, width), u,
        token_lengths, negatives, events, seq, root, n_z, n_i,
    )
    sends, (normed, gated, curve), lists = gate_outs[:half], gate_outs[half : half + 3], gate_outs[half + 3 :]
    packs = [pack(chip_shares, "pack_shares", gated)]
    packs += [plane_shift(packs[0], 0, 0, dc) for dc in range(1, n_c)]

    pieces = [sends[0]] + [half_shift(sends[k], k) for k in range(1, half)]
    lists = [lists[0]] + [shift(lists[k], "item", k) for k in steps_i]
    counts, slab_scale = call(
        functools.partial(count_kernel, n_i, root),
        [shape((n_i * queries, slab.shape[0]), F32), shape((1, slab.shape[0]), F32)],
        [base_arr, slab] + lists, "list_counts", smem=1,
    )
    block = shape((half * queries, depth), BF16)
    *parts, mirror, held, away = call(
        functools.partial(forward_kernel, half, n_c),
        [shape((queries, proj_width), F32)]
        + [shape((queries, proj_width), BF16)] * (half - 1)
        + [shape((depth, proj_width), BF16), block, block],
        [side_arr, share_places, proj_weight] + pieces + packs, "forward",
        flops=4 * half * queries * depth * proj_width, smem=2, after=[counts],
    )
    parts = [parts[0]] + [half_shift(parts[k], -k) for k in range(1, half)]
    near = [held] + [plane_shift(held, 0, dh, 0) for dh in range(1, n_h)]
    row = shape((queries, proj_width), F32)
    row16 = shape((queries, proj_width), BF16)
    pooled, unit, embedded, near, away = call(
        functools.partial(embed_kernel, root, half),
        [row, shape((queries, 1), F32), row16, shape((n_h * half * queries, depth), BF16), block],
        parts + [away] + near, "embed",
    )
    other = mirror_shift(away)

    pieces = [embedded] + [shift(embedded, "item", k) for k in steps_i]
    near_far = [plane_shift(near, dg, 0, 0) for dg in range(1, n_g)]
    near_cores = [plane_shift(near, 0, 0, dc) for dc in range(1, n_c)]
    wide = (queries, proj_width + LANES)
    parts = call(
        functools.partial(contrast_kernel, n_i),
        [shape(wide, F32)] + [shape(wide, BF16)] * (n_i - 1),
        [slab, slab_scale, counts] + pieces, "contrast",
        flops=4 * n_i * queries * slab.shape[0] * proj_width, after=near_cores,
    )
    near_far_late = [passed(array, "near_far", parts[0]) for array in near_far]
    parts = [parts[0]] + [shift(parts[k], "item", -k) for k in steps_i]
    near_far_cores = [[plane_shift(array, 0, 0, dc) for array in near_far_late] for dc in range(1, n_c)]
    other = passed(other, "other", parts[1 % n_i])
    others = [other] + [plane_shift(other, dg, 0, 0) for dg in range(1, n_g)]
    cols = proj_width // n_plane
    grad, grad_columns, loss = call(
        functools.partial(grad_kernel, n_i, root),
        [row16, shape((n_all, queries, cols), BF16), shape((1, LANES), F32)],
        [positives, pooled, unit, embedded] + parts, "grad_pooled",
    )

    pieces = [grad] + [half_shift(grad, k) for k in range(1, half)]
    *backs, others = call(
        functools.partial(back_kernel, half, n_g),
        [shape((queries, 2 * depth), BF16)] * half + [shape((n_g * half * queries, depth), BF16)],
        [side_arr, proj_weight, mirror] + pieces + others, "backward",
        flops=4 * half * queries * depth * proj_width, smem=1, after=near_cores + sum(near_far_cores, []),
    )
    backs = [backs[0]] + [half_shift(backs[k], -k) for k in range(1, half)]
    all_columns = lax.all_to_all(
        passed(grad_columns, "columns_out", backs[-1]), EVERY, 0, 0, tiled=True
    )
    slopes = slope_rows(both_arr, normed, curve, loss, backs, seq, n_z)
    def total(parts, name):
        return call(add_kernel, [shape(parts[0].shape, F32)], parts, name)[0]

    own_slope = slopes[0]
    if n_g > 1:
        slopes = [total([a] + [shift(a, "grp", k) for k in range(1, n_g)], "sum_groups") for a in slopes]
    across = [plane_shift(others, 0, dh, 0) for dh in range(1, n_h)]
    late = [pack([array], "late", own_slope) for array in across]
    spread = []
    for dc in range(n_c):
        if dc == 0:
            spread += [near, *near_far, others, *across]
        else:
            spread += [near_cores[dc - 1], *near_far_cores[dc - 1]]
            spread += [plane_shift(array, 0, 0, dc) for array in [others, *late]]
    block_columns = call(
        functools.partial(columns_kernel, len(spread)), [shape((depth, cols), BF16)],
        [ranks, all_columns] + spread, "grad_columns",
        flops=2 * n_all * queries * depth * cols, scratch=[pltpu.VMEM((n_all * queries, cols), BF16)], smem=1, copy=True, after=slopes,
    )[0]
    on_chips = [block_columns if dg == dh == 0 else plane_shift(block_columns, dg, dh, 0) for dg, dh in chips]
    slopes = [passed(array, "slope_out", block_columns) for array in slopes]
    slope = total([slopes[0]] + [half_shift(slopes[k], k) for k in range(1, half)], "sum_half")
    slope = total([slope, mirror_shift(slope)], "sum_mirror")
    if n_i > 1:
        slope = total([slope] + [shift(slope, "item", k) for k in steps_i], "sum_items")
    query_part, my_slope, loss_total = call(
        query_kernel,
        [shape((1, proj_width), F32), shape((depth // LANES, LANES), F32), shape((1, LANES), F32)],
        [side_arr, proj_weight, mirror, slope], "slope_sum", smem=1,
    )
    finished = [pack(on_chips, "pack_columns", slope, True)]
    finished += [plane_shift(finished[0], 0, 0, dc) for dc in range(1, n_c)]
    query_parts = [query_part] + [half_shift(query_part, k) for k in range(1, half)]
    grad_proj, finish_token = call(
        functools.partial(finish_kernel, len(finished)),
        [shape((depth, proj_width), F32), shape((8, LANES), F32)],
        [share_places, pool_query.reshape(1, -1), my_slope] + finished, "finish", smem=1, streamed=True,
        scratch=[pltpu.VMEM((depth, proj_width), F32), pltpu.SemaphoreType.DMA((depth // LANES,))],
    )
    grad_query = call(
        add_kernel, [shape((1, proj_width), F32)], query_parts, "query_sum", after=[finish_token]
    )[0]
    mean_loss = loss_total[0, 0] / (queries * n_all)
    return (grad_proj, grad_query.reshape(proj_width), mean_loss)


def solution(mesh):
    return jax.shard_map(
        body,
        mesh=mesh,
        in_specs=(
            P(("grp", "fsdp", "item"), None, None),
            P(("grp", "fsdp", "item"), None),
            P(("grp", "fsdp", "item"), None),
            P(("grp", "fsdp", "item")),
            P(),
            P("fsdp", None),
            P(),
            P("item", None),
        ),
        out_specs=(P("fsdp", None), P(), P()),
        check_vma=False,
    )
```

```python
import functools
import math

import jax
import jax.numpy as jnp
from jax import lax
from jax.experimental import pallas as pl
from jax.experimental.pallas import tpu as pltpu
from jax.sharding import PartitionSpec as P

sharpness_divisor = 0.05
norm_eps = 1e-05
embed_eps = 1e-06

EVERY = ("fsdp", "grp", "item")
PLANE = ("grp", "item")
F32 = jnp.float32
BF16 = jnp.bfloat16
LANES = 128
MIB = 1024 * 1024
VMEM = pl.BlockSpec(memory_space=pltpu.VMEM)
SMEM = pl.BlockSpec(memory_space=pltpu.SMEM)


def shape(dims, dtype):
    return jax.ShapeDtypeStruct(dims, dtype)


def copying(kernel, smem, shapes):
    n = len(shapes)

    def run(*refs):
        sources, buffers, sems = refs[smem : smem + n], refs[-n - 1 : -1], refs[-1]
        copies = [
            pltpu.make_async_copy(sources[k], buffers[k], sems.at[k]) for k in range(n)
        ]
        for copy in copies:
            copy.start()
        kernel(copies, *refs[:smem], *buffers, *refs[smem + n : -n - 1])

    return run


def call(kernel, outs, ins, name, flops=0, scratch=(), smem=0, after=(), copy=False, streamed=False):
    count = len(ins)
    if copy:
        shapes = [pltpu.VMEM(a.shape, a.dtype) for a in ins[smem:]]
        kernel = copying(kernel, smem, shapes)
        scratch = [*scratch, *shapes, pltpu.SemaphoreType.DMA((len(shapes),))]
    moved = sum(math.prod(a.shape) * a.dtype.itemsize for a in list(ins) + list(outs))
    held = 0 if copy or streamed else sum(math.prod(s.shape) * jnp.dtype(s.dtype).itemsize for s in scratch)

    def run(*refs):
        kernel(*refs[:count], *refs[count + len(after) :])

    return pl.pallas_call(
        run,
        out_shape=outs,
        in_specs=[SMEM] * smem
        + [pl.BlockSpec(memory_space=pl.ANY) if copy else VMEM] * (count - smem)
        + [pl.BlockSpec(memory_space=pl.ANY)] * len(after),
        out_specs=([pl.BlockSpec(memory_space=pl.ANY)] if streamed else [VMEM]) + [VMEM] * (len(outs) - 1),
        scratch_shapes=list(scratch),
        cost_estimate=pl.CostEstimate(flops=flops, bytes_accessed=moved, transcendentals=0),
        compiler_params=pltpu.CompilerParams(
            vmem_limit_bytes=61 * MIB if copy else 2 * (moved + held) + 6 * MIB
        ),
        name=name,
    )(*ins, *after)


def shift(values, axis, k):
    n = lax.axis_size(axis)
    return lax.ppermute(values, axis, [(i, (i + k) % n) for i in range(n)])


def split_bf16(values):
    high = values.astype(BF16)
    low = (values - high.astype(F32)).astype(BF16)
    return high, low


def nt(left, right):
    return lax.dot_general(left, right, (((1,), (1,)), ((), ())), preferred_element_type=F32)


def tn(left, right):
    return lax.dot_general(left, right, (((0,), (0,)), ((), ())), preferred_element_type=F32)


def u_kernel(weight_ref, pool_ref, u_ref):
    pool = jnp.broadcast_to(pool_ref[...], (8, pool_ref.shape[1]))
    high = pool.astype(BF16)
    low, last = split_bf16(pool - high.astype(F32))
    weight = weight_ref[...]
    u_ref[...] = (nt(high, weight) + nt(low, weight) + nt(last, weight))[0:1]


def gate_kernel(seq, root, blocks, z_ref, states_ref, gain_ref, u_ref, len_ref, lists_ref, *rest):
    half = blocks // 2
    outs, normed_ref, gated_ref, curve_ref, copies, rows_ref = (
        rest[:half], rest[half], rest[half + 1], rest[half + 2], rest[half + 3 : -1], rest[-1]
    )
    step = pl.program_id(0)
    tokens, width = states_ref.shape
    count = tokens // seq
    chunk = 4 * LANES if width % (4 * LANES) == 0 else width
    logits = []
    for top in range(0, tokens, 32):
        rows = slice(top, top + 32)
        squares = jnp.zeros((32, chunk), F32)
        for at in range(0, width, chunk):
            part = states_ref[rows, at : at + chunk].astype(F32)
            squares = squares + part * part
        inv_rms = lax.rsqrt(jnp.sum(squares, axis=1, keepdims=True) / width + norm_eps)
        total = jnp.zeros((32, chunk), F32)
        for at in range(0, width, chunk):
            part = states_ref[rows, at : at + chunk].astype(F32)
            part = (part * inv_rms * gain_ref[:, at : at + chunk]).astype(BF16)
            normed_ref[rows, at : at + chunk] = part
            total = total + part.astype(F32) * u_ref[:, at : at + chunk]
        logits.append(jnp.sum(total, axis=1, keepdims=True))
    logit = jnp.concatenate(logits, axis=0) / root
    gate = 1.0 / (1.0 + jnp.exp(-logit))
    slot = lax.rem(lax.broadcasted_iota(jnp.int32, (tokens, 1), 0), seq)
    valid = jnp.where(slot < len_ref[...], 1.0, 0.0) / len_ref[...].astype(F32)
    gated = valid * gate
    gated_ref[...] = gated
    curve_ref[...] = gated * (1.0 - gate) / root
    owner = lax.broadcasted_iota(jnp.int32, (tokens, count), 0) // seq
    mine = owner == lax.broadcasted_iota(jnp.int32, (tokens, count), 1)
    high, low = split_bf16(jnp.where(mine, gated, 0.0))
    both = tn(jnp.concatenate([high, low], axis=1), normed_ref[...])
    rows_ref[pl.ds(pl.multiple_of(step * count, count), count), :] = both[:count] + both[count:]

    @pl.when(step == pl.num_programs(0) - 1)
    def _():
        owners = len(copies)
        own = lists_ref.shape[1] // owners
        for k in range(owners):
            picked = jnp.zeros(copies[k].shape, jnp.int32)
            for j in range(owners):
                picked = jnp.where(
                    lax.rem(z_ref[1] + k, owners) == j, lists_ref[:, j * own : (j + 1) * own], picked
                )
            copies[k][...] = picked
        depth = width // blocks
        place = lax.rem(z_ref[0], half)
        for k in range(half):
            for j in range(2):
                at = (j * half + lax.rem(place + k, half)) * depth
                outs[k][:, j * depth : (j + 1) * depth] = rows_ref[
                    :, pl.ds(pl.multiple_of(at, LANES), depth)
                ].astype(BF16)


def gate_rows(z, states, gain, u, token_lengths, lists, events, seq, root, blocks, owners):
    tokens, width = states.shape
    queries = tokens // seq
    group = 16 if queries % 16 == 0 else queries
    step_tokens = group * seq
    half = blocks // 2
    outs = [shape((queries, width // half), BF16)] * half
    outs += [shape((tokens, width), BF16)] + [shape((tokens, 1), F32)] * 2
    outs += [shape((queries, lists.shape[1] // owners), lists.dtype)] * owners
    column = pl.BlockSpec((step_tokens, 1), lambda i: (i, 0))
    rows = pl.BlockSpec((step_tokens, width), lambda i: (i, 0))
    inputs = [z, states, gain, u, token_lengths, lists]

    def run(*refs):
        gate_kernel(seq, root, blocks, *refs[: len(inputs)], *refs[len(inputs) + len(events) :])

    whole = lambda dims: pl.BlockSpec(dims, lambda i: (0, 0))
    return pl.pallas_call(
        run,
        grid=(queries // group,),
        out_shape=outs,
        in_specs=[
            SMEM,
            rows,
            whole((1, width)),
            whole((1, width)),
            column,
            whole(lists.shape),
        ]
        + [pl.BlockSpec(memory_space=pl.ANY)] * len(events),
        out_specs=[whole((queries, width // half))] * half + [rows] + [column] * 2
        + [whole((queries, lists.shape[1] // owners))] * owners,
        scratch_shapes=[pltpu.VMEM((queries, width), F32)],
        cost_estimate=pl.CostEstimate(
            flops=10 * tokens * width, bytes_accessed=4 * tokens * width, transcendentals=0
        ),
        compiler_params=pltpu.CompilerParams(vmem_limit_bytes=50 * MIB),
        name="gate_rows",
    )(*inputs, *events)


def pack_kernel(*refs):
    rows = refs[0].shape[0]
    for k, ref in enumerate(refs[:-1]):
        refs[-1][k * rows : (k + 1) * rows, :] = ref[...]


def pack_copies(n, *refs):
    out_ref, sems = refs[-2], refs[-1]
    rows = refs[0].shape[0]
    copies = [
        pltpu.make_async_copy(refs[k], out_ref.at[pl.ds(k * rows, rows), :], sems.at[k]) for k in range(n)
    ]
    for copy in copies:
        copy.start()
    for copy in copies:
        copy.wait()


def pack(pieces, name, event, copy=False):
    rows, width = pieces[0].shape
    n = len(pieces)
    out = shape((n * rows, width), pieces[0].dtype)
    if copy:
        anywhere = pl.BlockSpec(memory_space=pl.ANY)
        return pl.pallas_call(
            functools.partial(pack_copies, n),
            out_shape=out,
            in_specs=[anywhere] * (n + 1),
            out_specs=anywhere,
            scratch_shapes=[pltpu.SemaphoreType.DMA((n,))],
            cost_estimate=pl.CostEstimate(flops=0, bytes_accessed=4 * n * rows * width, transcendentals=0),
            compiler_params=pltpu.CompilerParams(vmem_limit_bytes=4 * MIB),
            name=name,
        )(*pieces, event)
    return call(pack_kernel, [out], pieces, name, after=[event])[0]


def pass_kernel(from_ref, to_ref):
    to_ref[...] = from_ref[...]


def passed(values, name, event):
    return call(pass_kernel, [shape(values.shape, values.dtype)], [values], name, after=[event])[0]


def add_kernel(*refs):
    total = refs[0][...]
    for ref in refs[1:-1]:
        total = total + ref[...]
    refs[-1][...] = total


def forward_kernel(n, packs, side_ref, places_ref, weight_ref, *refs):
    refs = refs[:n] + (weight_ref,) + refs[n:]
    pieces, shares = refs[:n], refs[n + 1 : n + 1 + packs]
    outs = refs[n + 1 + packs : 2 * n + 1 + packs]
    mirror_ref, held_ref, away_ref = refs[2 * n + 1 + packs :]
    rows = pieces[0].shape[0]
    depth = weight_ref.shape[0]
    side = side_ref[0]
    for k in range(n):
        part = slice(k * rows, (k + 1) * rows)
        held_ref[part, :] = pieces[k][:, pl.ds(pl.multiple_of(side * depth, LANES), depth)]
        away_ref[part, :] = pieces[k][:, pl.ds(pl.multiple_of((1 - side) * depth, LANES), depth)]
    count = places_ref.shape[0] // packs
    share = shares[0].shape[0] // count
    for p in range(packs):
        for j in range(count):
            at = pl.multiple_of(places_ref[p * count + j] * share, share)
            mirror_ref[pl.ds(at, share), :] = shares[p][j * share : (j + 1) * share, :]
    product = jnp.dot(held_ref[...], weight_ref[...], preferred_element_type=F32)
    product = product + jnp.dot(away_ref[...], mirror_ref[...], preferred_element_type=F32)
    for k in range(n):
        outs[k][...] = product[k * rows : (k + 1) * rows].astype(outs[k].dtype)


def back_kernel(n, packed, side_ref, weight_ref, mirror_ref, *refs):
    pieces, outs = refs[:n], refs[n + packed : -1]
    pack_kernel(*refs[n : n + packed], refs[-1])
    rows = pieces[0].shape[0]
    depth = weight_ref.shape[0]
    side = side_ref[0]
    stack = jnp.concatenate([p[...] for p in pieces], axis=0)
    own = nt(stack, weight_ref[...]).astype(BF16)
    mirror = nt(stack, mirror_ref[...]).astype(BF16)
    for k in range(n):
        part = slice(k * rows, (k + 1) * rows)
        outs[k][:, pl.ds(pl.multiple_of(side * depth, LANES), depth)] = own[part]
        outs[k][:, pl.ds(pl.multiple_of((1 - side) * depth, LANES), depth)] = mirror[part]


def embed_kernel(root, n, *refs):
    parts, away_ref, packed = refs[:n], refs[n], refs[n + 1 : -5]
    pooled_ref, unit_ref, embedded_ref, pack_ref, pass_ref = refs[-5:]
    pass_ref[...] = away_ref[...]
    pooled = parts[0][...]
    for part in parts[1:]:
        pooled = pooled + part[...].astype(F32)
    unit = lax.rsqrt(jnp.mean(pooled * pooled, axis=1, keepdims=True) + embed_eps) / root
    pooled_ref[...] = pooled
    unit_ref[...] = unit
    embedded_ref[...] = (pooled * unit).astype(BF16)
    pack_kernel(*packed, pack_ref)


def count_kernel(n, root, base_ref, slab_ref, *refs):
    lists, counts_ref, scale_ref = refs[:n], refs[n], refs[n + 1]
    queries = lists[0].shape[0]
    rows, width = slab_ref.shape
    slab = slab_ref[...].astype(F32)
    high, low = split_bf16(slab * slab)
    ones = jnp.ones((8, width), BF16)
    row_sq = (nt(ones, high) + nt(ones, low))[0:1]
    scale_ref[...] = lax.rsqrt(row_sq / width + embed_eps) / root / sharpness_divisor
    ids = lax.broadcasted_iota(jnp.int32, (queries, LANES), 1)
    for k in range(n):
        own = lists[k][...] - base_ref[0]
        columns = [
            jnp.broadcast_to(own[:, entry : entry + 1], (queries, LANES)) for entry in range(own.shape[1])
        ]
        for at in range(0, rows, LANES):
            total = jnp.zeros(ids.shape, F32)
            for column in columns:
                total = total + jnp.where(column == ids + at, 1.0, 0.0)
            counts_ref[k * queries : (k + 1) * queries, at : at + LANES] = total


def contrast_kernel(n, *refs):
    (slab_ref, scale_ref, counts_ref), pieces, outs = refs[:3], refs[3 : n + 3], refs[n + 3 :]
    queries, width = pieces[0].shape
    embedded = jnp.concatenate([p[...] for p in pieces], axis=0)
    slab = slab_ref[...]
    scale = scale_ref[...]
    heavy = counts_ref[...] * jnp.exp(nt(embedded, slab) * scale)
    denom = jnp.sum(heavy, axis=1, keepdims=True)
    grad = jnp.dot((heavy * scale).astype(BF16), slab, preferred_element_type=F32)
    high, low = split_bf16(denom)
    lane = lax.broadcasted_iota(jnp.int32, (queries, LANES), 1)
    for k in range(n):
        part = slice(k * queries, (k + 1) * queries)
        outs[k][:, :width] = grad[part].astype(outs[k].dtype)
        if k == 0:
            tail = jnp.where(lane == 0, denom[part], 0.0)
        else:
            tail = jnp.where(lane == 0, high[part].astype(F32), jnp.where(lane == 1, low[part].astype(F32), 0.0))
        outs[k][:, width:] = tail.astype(outs[k].dtype)


def grad_kernel(n, root, *refs):
    pos_ref, pooled_ref, unit_ref, embedded_ref = refs[:4]
    parts = refs[4 : n + 4]
    grad_ref, columns_ref, loss_ref = refs[n + 4 :]
    queries, width = pos_ref.shape
    total = parts[0][:, :width]
    denom = jnp.sum(parts[0][:, width:], axis=1, keepdims=True)
    for part in parts[1:]:
        total = total + part[:, :width].astype(F32)
        denom = denom + jnp.sum(part[:, width:].astype(F32), axis=1, keepdims=True)
    positive = pos_ref[...].astype(F32)
    scale = (
        lax.rsqrt(jnp.mean(positive * positive, axis=1, keepdims=True) + embed_eps)
        / root
        / sharpness_divisor
    )
    score = jnp.sum(embedded_ref[...].astype(F32) * positive, axis=1, keepdims=True) * scale
    pos_exp = jnp.exp(score)
    denom = denom + pos_exp
    loss_ref[...] = jnp.broadcast_to(jnp.sum(jnp.log(denom) - score), loss_ref.shape)
    grad_embed = total / denom + (pos_exp / denom - 1.0) * scale * positive
    pooled, unit = pooled_ref[...], unit_ref[...]
    mean_sq = jnp.mean(pooled * pooled, axis=1, keepdims=True)
    radial = jnp.sum(pooled * grad_embed, axis=1, keepdims=True)
    grad = unit * grad_embed - pooled * (radial * unit / (width * (mean_sq + embed_eps)))
    grad = grad.astype(BF16)
    grad_ref[...] = grad
    cols = columns_ref.shape[2]
    places = width // cols
    for j in range(columns_ref.shape[0]):
        at = (j % places) * cols
        columns_ref[j] = grad[:, at : at + cols]


def slope_kernel(seq, blocks, z_ref, normed_ref, curve_ref, loss_ref, *rest):
    half = blocks // 2
    backs, outs, (all_ref, sum_ref) = rest[:half], rest[half : 2 * half], rest[-2:]
    step = pl.program_id(0)
    tokens, width = normed_ref.shape
    count = tokens // seq
    depth = width // blocks
    place = lax.rem(z_ref[0], half)

    def block_at(j, k):
        return pl.ds(pl.multiple_of((j * half + lax.rem(place + k, half)) * depth, LANES), depth)

    @pl.when(step == 0)
    def _():
        sum_ref[...] = jnp.zeros_like(sum_ref)
        for k in range(half):
            for j in range(2):
                all_ref[:, block_at(j, k)] = backs[k][:, j * depth : (j + 1) * depth].astype(F32)

    back = all_ref[pl.ds(pl.multiple_of(step * count, count), count), :]
    normed = normed_ref[...].astype(F32).reshape(count, seq, width)
    dots = jnp.sum(normed * back[:, None, :], axis=2, keepdims=True)
    slope = curve_ref[...].reshape(count, seq, 1) * dots
    heavy = (slope * normed).reshape(tokens // 8, 8, width)
    sum_ref[...] += jnp.sum(heavy, axis=0)

    @pl.when(step == pl.num_programs(0) - 1)
    def _():
        total = jnp.sum(sum_ref[...], axis=0, keepdims=True)
        lines = depth // LANES
        height = outs[0].shape[0]
        loss = jnp.broadcast_to(loss_ref[...], (height - 2 * lines, LANES))
        all_ref[0:1, :] = total
        for k in range(half):
            for j in range(2):
                row = all_ref[0:1, block_at(j, k)]
                for line in range(lines):
                    outs[k][j * lines + line : j * lines + line + 1, :] = row[
                        :, line * LANES : (line + 1) * LANES
                    ]
            outs[k][2 * lines :, :] = loss


def slope_rows(z, normed, curve, loss, backs, seq, blocks):
    tokens, width = normed.shape
    half = blocks // 2
    height = 2 * (width // blocks // LANES) // 8 * 8 + 8
    queries = tokens // seq
    group = 16 if queries % 16 == 0 else queries
    step_tokens = group * seq
    whole = lambda dims: pl.BlockSpec(dims, lambda i: (0, 0))
    return pl.pallas_call(
        functools.partial(slope_kernel, seq, blocks),
        grid=(queries // group,),
        out_shape=[shape((height, LANES), F32)] * half,
        in_specs=[
            SMEM,
            pl.BlockSpec((step_tokens, width), lambda i: (i, 0)),
            pl.BlockSpec((step_tokens, 1), lambda i: (i, 0)),
            whole((1, LANES)),
        ]
        + [whole((queries, width // half))] * half,
        out_specs=[whole((height, LANES))] * half,
        scratch_shapes=[pltpu.VMEM((queries, width), F32), pltpu.VMEM((8, width), F32)],
        cost_estimate=pl.CostEstimate(
            flops=4 * tokens * width, bytes_accessed=2 * tokens * width, transcendentals=0
        ),
        compiler_params=pltpu.CompilerParams(vmem_limit_bytes=32 * MIB),
        name="slope_rows",
    )(z, normed, curve, loss, *backs)


def columns_kernel(n, copies, order_ref, grads_ref, *refs):
    pieces, (out_ref, sorted_ref) = refs[:n], refs[n:]
    chunk = grads_ref.shape[1]
    copies[0].wait()
    for j in range(sorted_ref.shape[0] // chunk):
        sorted_ref[j * chunk : (j + 1) * chunk, :] = grads_ref[order_ref[j]]
    at = pieces[0].shape[0]
    copies[1].wait()
    total = tn(sorted_ref[0:at, :], pieces[0][...])
    for k, piece in enumerate(pieces[1:]):
        rows = piece.shape[0]
        copies[k + 2].wait()
        total = total + tn(sorted_ref[at : at + rows, :], piece[...])
        at += rows
    out_ref[...] = total.T.astype(BF16)


def query_kernel(side_ref, weight_ref, mirror_ref, parts_ref, part_ref, slope_ref, loss_ref):
    depth = weight_ref.shape[0]
    lines = depth // LANES
    total = parts_ref[...]
    loss_ref[...] = total[2 * lines : 2 * lines + 1]
    side = side_ref[0]
    part = jnp.zeros(part_ref.shape, F32)
    for j in range(2):
        rows = total[j * lines : (j + 1) * lines]
        row = jnp.concatenate([rows[k : k + 1] for k in range(lines)], axis=1)
        high, low = split_bf16(jnp.broadcast_to(row, (8, depth)))

        @pl.when(side == j)
        def _():
            slope_ref[...] = rows

        weight = jnp.where(side == j, weight_ref[...], mirror_ref[...])
        part = part + jnp.dot(high, weight, preferred_element_type=F32)[0:1]
        part = part + jnp.dot(low, weight, preferred_element_type=F32)[0:1]
    part_ref[...] = part


def finish_kernel(n, place_ref, pool_ref, slope_ref, *refs):
    pieces, result_ref, token_ref, out_ref, sems = refs[:n], *refs[n:]
    token_ref[...] = jnp.zeros_like(token_ref)
    places = place_ref.shape[0]
    rows, cols = out_ref.shape[0], pieces[0].shape[1]
    copies = []
    for line in range(rows // LANES):
        part = pl.ds(line * LANES, LANES)
        slope = jnp.broadcast_to(slope_ref[line : line + 1, :], (LANES, LANES)).T
        for k in range(places):
            base = k % (places // n) * rows + line * LANES
            mine = pieces[k // (places // n)][base : base + LANES, :].astype(F32)
            at = pl.ds(pl.multiple_of(place_ref[k] * cols, LANES), cols)
            out_ref[part, at] = mine + slope * pool_ref[:, at]
        copies.append(
            pltpu.make_async_copy(out_ref.at[part, :], result_ref.at[part, :], sems.at[line])
        )
        copies[-1].start()
    for copy in copies:
        copy.wait()


def body(hidden_states, positives, negatives, lengths, norm_gain, proj_weight, pool_query, slab):
    queries, seq, width = hidden_states.shape
    depth, proj_width = proj_weight.shape
    n_z, n_g, n_i = lax.axis_size("fsdp"), lax.axis_size("grp"), lax.axis_size("item")
    assert n_z % 2 == 0
    half = n_z // 2
    n_c = 2 if n_i % 2 == 0 else 1
    n_h = n_i // n_c
    n_plane = n_g * n_i
    n_all = n_z * n_plane
    z, g, i = lax.axis_index("fsdp"), lax.axis_index("grp"), lax.axis_index("item")
    h, c = i // n_c, lax.rem(i, n_c)
    side, member = z // half, lax.rem(z, half)
    root = math.sqrt(proj_width)
    steps_z, steps_i = range(1, n_z), range(1, n_i)

    def ints(*values):
        return jnp.stack([jnp.asarray(v, jnp.int32) for v in values])

    z_arr, side_arr = ints(z), ints(side)

    def plane_shift(values, dg, dh, dc):
        pairs = []
        for pg in range(n_g):
            for ph in range(n_h):
                for pc in range(n_c):
                    to = ((pg + dg) % n_g) * n_i + ((ph + dh) % n_h) * n_c + (pc + dc) % n_c
                    pairs.append((pg * n_i + ph * n_c + pc, to))
        return lax.ppermute(values, PLANE, pairs)

    def half_shift(values, k):
        pairs = [(a, a // half * half + (a % half + k) % half) for a in range(n_z)]
        return lax.ppermute(values, "fsdp", pairs)

    def mirror_shift(values):
        return lax.ppermute(values, "fsdp", [(a, (a + half) % n_z) for a in range(n_z)])

    def source(dg, dh, dc):
        return (
            lax.rem(g - dg + n_g, n_g),
            lax.rem(h - dh + n_h, n_h) * n_c + lax.rem(c - dc + n_c, n_c),
        )

    chips = [(dg, dh) for dg in range(n_g) for dh in range(n_h)]

    share = depth // n_plane
    place = g * n_i + i
    weight_share = lax.dynamic_slice_in_dim(proj_weight, place * share, share, 0)
    far_share = mirror_shift(weight_share)

    block_u = call(
        u_kernel, [shape((1, depth), F32)], [proj_weight, pool_query.reshape(1, -1)], "block_u",
        after=[weight_share],
    )[0]
    u_parts = [block_u] + [shift(block_u, "fsdp", k) for k in steps_z]
    u = jnp.zeros((1, width), F32)
    for k in range(n_z):
        u = lax.dynamic_update_slice(u, u_parts[k], (0, lax.rem(z - k + n_z, n_z) * depth))

    share_places = []
    for dc in range(n_c):
        for dg, dh in chips:
            from_g, from_i = source(dg, dh, dc)
            share_places.append(from_g * n_i + from_i)
    share_places = ints(*share_places)
    order = []
    for dc in range(n_c):
        for dg in range(n_g):
            order += [(side, k, dg, dh, dc) for dh in range(n_h) for k in range(half)]
        for dh in range(n_h):
            order += [(1 - side, k, dg, dh, dc) for dg in range(n_g) for k in range(half)]
    ranks = []
    for from_side, k, dg, dh, dc in order:
        from_g, from_i = source(dg, dh, dc)
        from_z = from_side * half + lax.rem(member - k + half, half)
        ranks.append((from_z * n_g + from_g) * n_i + from_i)
    ranks = ints(*ranks)
    both_arr, base_arr = ints(z, i), ints(i * slab.shape[0])
    token_lengths = jnp.broadcast_to(lengths[:, None], (queries, seq)).reshape(-1, 1)
    events = [far_share, share_places, ranks, base_arr, side_arr]
    chip_shares = [far_share if dg == dh == 0 else plane_shift(far_share, dg, dh, 0) for dg, dh in chips]
    gate_outs = gate_rows(
        both_arr, hidden_states.reshape(-1, width), norm_gain.astype(F32).reshape(1, width), u,
        token_lengths, negatives, events, seq, root, n_z, n_i,
    )
    sends, (normed, gated, curve), lists = gate_outs[:half], gate_outs[half : half + 3], gate_outs[half + 3 :]
    packs = [pack(chip_shares, "pack_shares", gated)]
    packs += [plane_shift(packs[0], 0, 0, dc) for dc in range(1, n_c)]

    pieces = [sends[0]] + [half_shift(sends[k], k) for k in range(1, half)]
    lists = [lists[0]] + [shift(lists[k], "item", k) for k in steps_i]
    counts, slab_scale = call(
        functools.partial(count_kernel, n_i, root),
        [shape((n_i * queries, slab.shape[0]), F32), shape((1, slab.shape[0]), F32)],
        [base_arr, slab] + lists, "list_counts", smem=1,
    )
    block = shape((half * queries, depth), BF16)
    *parts, mirror, held, away = call(
        functools.partial(forward_kernel, half, n_c),
        [shape((queries, proj_width), F32)]
        + [shape((queries, proj_width), BF16)] * (half - 1)
        + [shape((depth, proj_width), BF16), block, block],
        [side_arr, share_places, proj_weight] + pieces + packs, "forward",
        flops=4 * half * queries * depth * proj_width, smem=2, after=[counts],
    )
    parts = [parts[0]] + [half_shift(parts[k], -k) for k in range(1, half)]
    near = [held] + [plane_shift(held, 0, dh, 0) for dh in range(1, n_h)]
    row = shape((queries, proj_width), F32)
    row16 = shape((queries, proj_width), BF16)
    pooled, unit, embedded, near, away = call(
        functools.partial(embed_kernel, root, half),
        [row, shape((queries, 1), F32), row16, shape((n_h * half * queries, depth), BF16), block],
        parts + [away] + near, "embed",
    )
    other = mirror_shift(away)

    pieces = [embedded] + [shift(embedded, "item", k) for k in steps_i]
    near_far = [plane_shift(near, dg, 0, 0) for dg in range(1, n_g)]
    near_cores = [plane_shift(near, 0, 0, dc) for dc in range(1, n_c)]
    wide = (queries, proj_width + LANES)
    parts = call(
        functools.partial(contrast_kernel, n_i),
        [shape(wide, F32)] + [shape(wide, BF16)] * (n_i - 1),
        [slab, slab_scale, counts] + pieces, "contrast",
        flops=4 * n_i * queries * slab.shape[0] * proj_width, after=near_cores,
    )
    near_far_late = [passed(array, "near_far", parts[0]) for array in near_far]
    parts = [parts[0]] + [shift(parts[k], "item", -k) for k in steps_i]
    near_far_cores = [[plane_shift(array, 0, 0, dc) for array in near_far_late] for dc in range(1, n_c)]
    other = passed(other, "other", parts[1 % n_i])
    others = [other] + [plane_shift(other, dg, 0, 0) for dg in range(1, n_g)]
    cols = proj_width // n_plane
    grad, grad_columns, loss = call(
        functools.partial(grad_kernel, n_i, root),
        [row16, shape((n_all, queries, cols), BF16), shape((1, LANES), F32)],
        [positives, pooled, unit, embedded] + parts, "grad_pooled",
    )

    pieces = [grad] + [half_shift(grad, k) for k in range(1, half)]
    *backs, others = call(
        functools.partial(back_kernel, half, n_g),
        [shape((queries, 2 * depth), BF16)] * half + [shape((n_g * half * queries, depth), BF16)],
        [side_arr, proj_weight, mirror] + pieces + others, "backward",
        flops=4 * half * queries * depth * proj_width, smem=1, after=near_cores + sum(near_far_cores, []),
    )
    backs = [backs[0]] + [half_shift(backs[k], -k) for k in range(1, half)]
    all_columns = lax.all_to_all(
        passed(grad_columns, "columns_out", backs[-1]), EVERY, 0, 0, tiled=True
    )
    slopes = slope_rows(both_arr, normed, curve, loss, backs, seq, n_z)
    def total(parts, name):
        return call(add_kernel, [shape(parts[0].shape, F32)], parts, name)[0]

    own_slope = slopes[0]
    if n_g > 1:
        slopes = [total([a] + [shift(a, "grp", k) for k in range(1, n_g)], "sum_groups") for a in slopes]
    across = [plane_shift(others, 0, dh, 0) for dh in range(1, n_h)]
    late = [pack([array], "late", own_slope) for array in across]
    spread = []
    for dc in range(n_c):
        if dc == 0:
            spread += [near, *near_far, others, *across]
        else:
            spread += [near_cores[dc - 1], *near_far_cores[dc - 1]]
            spread += [plane_shift(array, 0, 0, dc) for array in [others, *late]]
    block_columns = call(
        functools.partial(columns_kernel, len(spread)), [shape((depth, cols), BF16)],
        [ranks, all_columns] + spread, "grad_columns",
        flops=2 * n_all * queries * depth * cols, scratch=[pltpu.VMEM((n_all * queries, cols), BF16)], smem=1, copy=True, after=slopes,
    )[0]
    on_chips = [block_columns if dg == dh == 0 else plane_shift(block_columns, dg, dh, 0) for dg, dh in chips]
    slopes = [passed(array, "slope_out", block_columns) for array in slopes]
    slope = total([slopes[0]] + [half_shift(slopes[k], k) for k in range(1, half)], "sum_half")
    slope = total([slope, mirror_shift(slope)], "sum_mirror")
    if n_i > 1:
        slope = total([slope] + [shift(slope, "item", k) for k in steps_i], "sum_items")
    query_part, my_slope, loss_total = call(
        query_kernel,
        [shape((1, proj_width), F32), shape((depth // LANES, LANES), F32), shape((1, LANES), F32)],
        [side_arr, proj_weight, mirror, slope], "slope_sum", smem=1,
    )
    finished = [pack(on_chips, "pack_columns", slope, True)]
    finished += [plane_shift(finished[0], 0, 0, dc) for dc in range(1, n_c)]
    query_parts = [query_part] + [half_shift(query_part, k) for k in range(1, half)]
    grad_proj, finish_token = call(
        functools.partial(finish_kernel, len(finished)),
        [shape((depth, proj_width), F32), shape((8, LANES), F32)],
        [share_places, pool_query.reshape(1, -1), my_slope] + finished, "finish", smem=1, streamed=True,
        scratch=[pltpu.VMEM((depth, proj_width), F32), pltpu.SemaphoreType.DMA((depth // LANES,))],
    )
    grad_query = call(
        add_kernel, [shape((1, proj_width), F32)], query_parts, "query_sum", after=[finish_token]
    )[0]
    mean_loss = loss_total[0, 0] / (queries * n_all)
    return (grad_proj, grad_query.reshape(proj_width), mean_loss)


def solution(mesh):
    return jax.shard_map(
        body,
        mesh=mesh,
        in_specs=(
            P(("grp", "fsdp", "item"), None, None),
            P(("grp", "fsdp", "item"), None),
            P(("grp", "fsdp", "item"), None),
            P(("grp", "fsdp", "item")),
            P(),
            P("fsdp", None),
            P(),
            P("item", None),
        ),
        out_specs=(P("fsdp", None), P(), P()),
        check_vma=False,
    )
```
